32 devices in a mesh: rows: 8 (over z, x), depth: 4 (over y, core).
Axes of the slice: x: 2, y: 2, z: 4, core: 2. Of those that a mesh axis runs over, the one named last changes fastest.
Arguments:
- block_input: bfloat16 [4096, 768], P(('rows', 'depth')), may hold values from -6 to 6
- history: bfloat16 [4, 4096, 768], P('depth', 'rows'), may hold values from -6 to 6
- cotangent: bfloat16 [4096, 768], P(('rows', 'depth')), may hold values from -6 to 6
- token_mask: int32 [4096], P(('rows', 'depth')), may hold values from 0 to 1, as said below
- qkv_weight: bfloat16 [768, 2304], P(('rows', 'depth')), may hold values from -0.21875 to 0.21875
- out_weight: bfloat16 [768, 768], P(('rows', 'depth')), may hold values from -1.5 to 1.5
- up_weight: bfloat16 [768, 3072], P(('rows', 'depth')), may hold values from -0.21875 to 0.21875
- down_weight: bfloat16 [3072, 768], P(('rows', 'depth')), may hold values from -0.109375 to 0.109375
- norm_params: float32 [4, 768], P(None, ('rows', 'depth')), may hold values from -1 to 1
- depth_weights: float32 [5], replicated, may hold values from 0.2 to 1
Outputs:
- output: bfloat16 [4096, 768], P(('rows', 'depth'))
- input_grad: bfloat16 [4096, 768], P(('rows', 'depth'))
- history_grad: bfloat16 [4, 4096, 768], P('depth', 'rows')
- qkv_gradient: float32 [768, 2304], P(('rows', 'depth'))
- out_gradient: float32 [768, 768], P(('rows', 'depth'))
- up_gradient: float32 [768, 3072], P(('rows', 'depth'))
- down_gradient: float32 [3072, 768], P(('rows', 'depth'))
- norm_gradient: float32 [4, 768], P(None, ('rows', 'depth'))
- depth_gradient: float32 [5], replicated
The draws below stay inside these ranges and needn't reach their ends.
Inputs may be any that keep to these rules, and one draw needn't show every extreme that they name: `token_mask`: the first row is 1.
All inputs are finite; a program needn't handle non-finite values.
Results may differ from the reference program's by a relative error of at most 0.035.
Values may be sent and summed in bfloat16 or wider, within the bound.
A program may use at most 192 MiB of HBM per device.

```python
import jax
import jax.numpy as jnp
from jax import lax

D = 768
HEADS = 12
HD = 64
FF = 3072
HIST = 4
SEQ = 512
TOKENS = 4096
N_ROWS = 8


def draw_token_mask(key, part):
    key = jax.random.fold_in(key, 5)
    index = jnp.arange(TOKENS, dtype=jnp.int32)
    limit = 300 + 650 * index // TOKENS
    sample = jax.random.randint(key, (TOKENS,), 0, 1000, dtype=jnp.int32)
    keep = (sample < limit).astype(jnp.int32)
    return keep.at[0].set(1)


def level_of(rng, dims, split, smallest, largest):
    level = 1.0
    for dim, shards_of in split:
        draws = jax.random.uniform(jax.random.fold_in(jax.random.fold_in(rng, 6), dim), (shards_of,), jnp.float32, smallest / len(split), largest / len(split))
        level = level * jnp.repeat(jnp.exp(draws), dims[dim] // shards_of).reshape((-1,) + (1,) * (len(dims) - 1 - dim))
    return level


def gaussian(own_key, extent, width, bound, split=(), kind=jnp.bfloat16):
    level = level_of(own_key, extent, split, -0.22, 0.18) if split else 1.0
    values = jax.random.normal(own_key, extent, jnp.float32) * width * level
    return jnp.minimum(jnp.maximum(values, -bound), bound).astype(kind)


def setup_inputs(seed: int = 0) -> dict:
    arg_keys = jax.random.split(jax.random.key(seed), 11)
    block_input = gaussian(arg_keys[0], (TOKENS, D), 1.0, 6.0, ((0, 32),))
    history = gaussian(arg_keys[1], (HIST, TOKENS, D), 1.0, 6.0, ((0, 4), (1, 8)))
    cotangent = gaussian(arg_keys[2], (TOKENS, D), 1.0, 6.0, ((0, 32),))
    token_mask = draw_token_mask(jax.random.fold_in(arg_keys[10], 71), 0)
    qkv_weight = gaussian(arg_keys[4], (D, 3 * D), D ** -0.5, 0.21875, ((0, 32),))
    out_weight = gaussian(arg_keys[5], (D, D), 16 ** -0.5, 1.5, ((0, 32),))
    up_weight = gaussian(arg_keys[6], (D, FF), D ** -0.5, 0.21875, ((0, 32),))
    down_weight = gaussian(arg_keys[7], (FF, D), FF ** -0.5, 0.109375, ((0, 32),))
    norm_params = gaussian(arg_keys[8], (4, D), 0.2, 1.0, ((1, 32),), jnp.float32)
    depth_weights = jnp.clip(jax.random.uniform(arg_keys[9], (HIST + 1,), jnp.float32, 0.2, 1.0), 0.2, 1.0)
    return {"block_input": block_input, "history": history, "cotangent": cotangent, "token_mask": token_mask, "qkv_weight": qkv_weight, "out_weight": out_weight, "up_weight": up_weight, "down_weight": down_weight, "norm_params": norm_params, "depth_weights": depth_weights}


@jax.custom_vjp
def low(v):
    return lax.optimization_barrier(v.astype(jnp.bfloat16)).astype(jnp.float32)

@jax.custom_vjp
def low_back(v):
    return v

def low_keep(v):
    return (low(v), None)

def low_pass(kept, grad):
    return (grad,)

def back_keep(v):
    return (v, None)

def back_low(kept, grad):
    return (low(grad),)
low.defvjp(low_keep, low_pass)
low_back.defvjp(back_keep, back_low)
HIGHEST = lax.Precision.HIGHEST

def norm_rows(value, gain, shift):
    center = value - lax.optimization_barrier(jnp.mean(value, axis=-1, keepdims=True))
    spread = lax.optimization_barrier(jnp.mean(center * center, axis=-1, keepdims=True))
    return center * lax.rsqrt(spread + 1e-05) * (1.0 + gain) + shift

def rotate(value, place):
    half = HD // 2
    freq = 10000.0 ** (-jnp.arange(half, dtype=jnp.float32) / half)
    angle = place.astype(jnp.float32)[:, None] * freq[None, :]
    cosine = jnp.cos(angle)[:, None, :]
    sine = jnp.sin(angle)[:, None, :]
    first = value[..., :half]
    second = value[..., half:]
    return jnp.concatenate([first * cosine - second * sine, second * cosine + first * sine], axis=-1)

def attend(query, keys, values):
    block = min(512, SEQ)
    number = SEQ // block
    blocks = query.reshape(number, block, HEADS, HD)
    starts = jnp.arange(number, dtype=jnp.int32) * block
    key_place = jnp.arange(SEQ, dtype=jnp.int32)

    def one_block(item):
        rows_part, start = item
        scores = low_back(jnp.einsum('qhd,khd->hqk', rows_part, keys, precision=HIGHEST) * HD ** (-0.5))
        query_place = start + jnp.arange(block, dtype=jnp.int32)
        allowed = query_place[:, None] >= key_place[None, :]
        scores = jnp.where(allowed[None], scores, -1e+30)
        peak = lax.optimization_barrier(jnp.max(scores, axis=-1, keepdims=True))
        probs = jnp.exp(scores - peak)
        probs = probs / lax.optimization_barrier(jnp.sum(probs, axis=-1, keepdims=True))
        return jnp.einsum('hqk,khd->qhd', low(probs), values, precision=HIGHEST)
    result = lax.map(jax.checkpoint(one_block), (blocks, starts))
    return result.reshape(SEQ, HEADS * HD)

def one_sequence(rows_in, stored, qkv_weight, out_weight, up_weight, down_weight, norm_params, depth_weights):
    place = jnp.arange(SEQ, dtype=jnp.int32)
    first = low(norm_rows(rows_in, norm_params[0], norm_params[1]))
    projected = low_back(jnp.dot(first, qkv_weight, precision=HIGHEST))
    query = low(rotate(projected[:, :D].reshape(SEQ, HEADS, HD), place))
    keys = low(rotate(projected[:, D:2 * D].reshape(SEQ, HEADS, HD), place))
    values = low(projected[:, 2 * D:].reshape(SEQ, HEADS, HD))
    mixed = low(low_back(attend(query, keys, values)))
    branch = low_back(jnp.dot(mixed, out_weight, precision=HIGHEST))
    middle = rows_in + branch
    second = low(norm_rows(middle, norm_params[2], norm_params[3]))
    upper = low_back(jnp.dot(second, up_weight, precision=HIGHEST))
    active = low(jax.nn.gelu(upper))
    lower = low_back(jnp.dot(active, down_weight, precision=HIGHEST))
    block_out = middle + lower
    return lax.optimization_barrier(jnp.sum(depth_weights[:HIST][:, None, None] * stored, axis=0)) + depth_weights[HIST] * block_out

def forward(block_input, history, qkv_weight, out_weight, up_weight, down_weight, norm_params, depth_weights):
    seqs = block_input.reshape(N_ROWS, SEQ, D)
    stored = jnp.swapaxes(history.reshape(HIST, N_ROWS, SEQ, D), 0, 1)

    def per_sequence(item):
        return one_sequence(item[0], item[1], qkv_weight, out_weight, up_weight, down_weight, norm_params, depth_weights)
    result = lax.map(jax.checkpoint(per_sequence), (seqs, stored))
    return result.reshape(TOKENS, D)

def reference(block_input, history, cotangent, token_mask, qkv_weight, out_weight, up_weight, down_weight, norm_params, depth_weights):
    maskf = token_mask.astype(jnp.float32)
    total = jnp.sum(maskf)
    grad_out = maskf[:, None] * cotangent.astype(jnp.float32) * (TOKENS / total)
    inputs = (block_input.astype(jnp.float32), history.astype(jnp.float32), qkv_weight.astype(jnp.float32), out_weight.astype(jnp.float32), up_weight.astype(jnp.float32), down_weight.astype(jnp.float32), norm_params, depth_weights)
    result, pull = jax.vjp(forward, *inputs)
    grads = pull(grad_out)
    return (result.astype(jnp.bfloat16), grads[0].astype(jnp.bfloat16), grads[1].astype(jnp.bfloat16), grads[2], grads[3], grads[4], grads[5], grads[6], grads[7])
```

```python
import functools

import jax
import jax.numpy as jnp
import numpy as np
from jax import lax
from jax.experimental import pallas as pl
from jax.experimental.pallas import tpu as pltpu
from jax.sharding import PartitionSpec as P

HEADS = 12
HD = 64


def norm_rows(value, gain, shift):
    center = value - jnp.mean(value, axis=-1, keepdims=True)
    spread = jnp.mean(center * center, axis=-1, keepdims=True)
    return center * lax.rsqrt(spread + 1e-05) * (1.0 + gain) + shift


def rotate(value, place, sign):
    half = value.shape[-1] // 2
    freq = 10000.0 ** (-jnp.arange(half, dtype=jnp.float32) / half)
    angle = place.astype(jnp.float32)[:, None] * freq[None, :]
    cosine = jnp.cos(angle)[:, None, :]
    sine = jnp.sin(angle)[:, None, :] * sign
    first = value[..., :half]
    second = value[..., half:]
    return jnp.concatenate(
        [first * cosine - second * sine, second * cosine + first * sine], axis=-1
    )


def block_scores(query, key_block, start, query_place, scale):
    block_len = key_block.shape[0]
    scores = (
        jnp.einsum("qhd,khd->hqk", query, key_block, preferred_element_type=jnp.float32) * scale
    )
    key_place = start + jnp.arange(block_len, dtype=jnp.int32)
    allowed = query_place[:, None] >= key_place[None, :]
    return (scores, allowed)


def local(
    block_input,
    history,
    cotangent,
    token_mask,
    qkv_weight,
    out_weight,
    up_weight,
    down_weight,
    norm_params,
    depth_weights,
):
    rows_tok, width = block_input.shape
    depth_count = lax.axis_size("depth")
    device_count = lax.axis_size("rows") * depth_count
    place_depth = lax.axis_index("depth")
    heads = HEADS
    head_size = HD
    scale = head_size ** (-0.5)
    seq_len = rows_tok * depth_count
    slot_count = history.shape[0]
    hist_total = slot_count * depth_count
    wide_qkv, wide_out, wide_up, wide_down, wide_norms = (
        lax.all_gather(qkv_weight, ("rows", "depth"), axis=0, tiled=True),
        lax.all_gather(out_weight, ("rows", "depth"), axis=0, tiled=True),
        lax.all_gather(up_weight, ("rows", "depth"), axis=0, tiled=True),
        lax.all_gather(down_weight, ("rows", "depth"), axis=0, tiled=True),
        lax.all_gather(
            norm_params.astype(jnp.bfloat16), ("rows", "depth"), axis=1, tiled=True
        ).astype(norm_params.dtype),
    )
    total = lax.psum(jnp.sum(token_mask), ("rows", "depth")).astype(jnp.float32)
    loss_scale = rows_tok * device_count / total
    float_input = block_input.astype(jnp.float32)
    place = place_depth * rows_tok + jnp.arange(rows_tok, dtype=jnp.int32)
    first = norm_rows(float_input, wide_norms[0], wide_norms[1]).astype(jnp.bfloat16)
    projected = jnp.dot(first, wide_qkv, preferred_element_type=jnp.float32)
    query = rotate(projected[:, :width].reshape(rows_tok, heads, head_size), place, 1.0).astype(
        jnp.bfloat16
    )
    keys = rotate(projected[:, width : 2 * width].reshape(rows_tok, heads, head_size), place, 1.0)
    keys = keys.astype(jnp.bfloat16).reshape(rows_tok, width)
    values = projected[:, 2 * width :].astype(jnp.bfloat16)
    all_keys, all_values = (
        lax.all_gather(keys, "depth", axis=0, tiled=True),
        lax.all_gather(values, "depth", axis=0, tiled=True),
    )
    block_len = min(512, seq_len)
    block_count = seq_len // block_len
    key_blocks = all_keys.reshape(block_count, block_len, heads, head_size)
    value_blocks = all_values.reshape(block_count, block_len, heads, head_size)
    starts = jnp.arange(block_count, dtype=jnp.int32) * block_len

    def peak_step(carry, item):
        peak, weight_sum = carry
        key_block, value_block, start = item
        scores, allowed = block_scores(query, key_block, start, place, scale)
        scores = jnp.where(allowed[None], scores, -1e30)
        new_peak = jnp.maximum(peak, jnp.max(scores, axis=-1))
        weight_sum = weight_sum * jnp.exp(peak - new_peak) + jnp.sum(
            jnp.exp(scores - new_peak[..., None]), axis=-1
        )
        return ((new_peak, weight_sum), None)

    start_carry = (
        jnp.full((heads, rows_tok), -1e30, jnp.float32),
        jnp.zeros((heads, rows_tok), jnp.float32),
    )
    (peak, weight_sum), _ = lax.scan(peak_step, start_carry, (key_blocks, value_blocks, starts))
    log_total = peak + jnp.log(weight_sum)

    def value_step(running, item):
        key_block, value_block, start = item
        scores, allowed = block_scores(query, key_block, start, place, scale)
        probs = jnp.where(allowed[None], jnp.exp(scores - log_total[..., None]), 0.0)
        running = running + jnp.einsum(
            "hqk,khd->qhd",
            probs.astype(jnp.bfloat16),
            value_block,
            preferred_element_type=jnp.float32,
        )
        return (running, None)

    running, _ = lax.scan(
        value_step,
        jnp.zeros((rows_tok, heads, head_size), jnp.float32),
        (key_blocks, value_blocks, starts),
    )
    mixed = running.reshape(rows_tok, width)
    mixed_low = mixed.astype(jnp.bfloat16)
    middle = float_input + jnp.dot(mixed_low, wide_out, preferred_element_type=jnp.float32)
    second = norm_rows(middle, wide_norms[2], wide_norms[3]).astype(jnp.bfloat16)
    upper = jnp.dot(second, wide_up, preferred_element_type=jnp.float32)
    active = jax.nn.gelu(upper).astype(jnp.bfloat16)
    block_out = middle + jnp.dot(active, wide_down, preferred_element_type=jnp.float32)
    own_alpha = lax.dynamic_slice_in_dim(depth_weights, place_depth * slot_count, slot_count)
    partial_mix = jnp.sum(own_alpha[:, None, None] * history.astype(jnp.float32), axis=0)
    mixture = lax.psum_scatter(
        partial_mix.astype(jnp.bfloat16), "depth", scatter_dimension=0, tiled=True
    ).astype(jnp.float32)
    output = (mixture + depth_weights[hist_total] * block_out).astype(jnp.bfloat16)
    grad_out = token_mask.astype(jnp.float32)[:, None] * cotangent.astype(jnp.float32) * loss_scale
    last_term = jnp.sum(grad_out * block_out)
    index_all = jnp.arange(hist_total + 1, dtype=jnp.int32)
    grad_rows = lax.all_gather(grad_out.astype(jnp.bfloat16), "depth", axis=0, tiled=True).astype(
        grad_out.dtype
    )
    history_grad = (own_alpha[:, None, None] * grad_rows[None]).astype(jnp.bfloat16)
    hist_terms = jnp.sum(history.astype(jnp.float32) * grad_rows[None], axis=(1, 2))
    own_index = place_depth * slot_count + jnp.arange(slot_count, dtype=jnp.int32)
    alpha_terms = jnp.sum(
        jnp.where(index_all[None, :] == own_index[:, None], hist_terms[:, None], 0.0), axis=0
    )
    alpha_terms = alpha_terms + jnp.where(index_all == hist_total, last_term, 0.0)
    depth_gradient = lax.psum(alpha_terms, ("rows", "depth"))
    wide_qkv, wide_out, wide_up, wide_down, wide_norms = (
        lax.all_gather(qkv_weight, ("rows", "depth"), axis=0, tiled=True),
        lax.all_gather(out_weight, ("rows", "depth"), axis=0, tiled=True),
        lax.all_gather(up_weight, ("rows", "depth"), axis=0, tiled=True),
        lax.all_gather(down_weight, ("rows", "depth"), axis=0, tiled=True),
        lax.all_gather(
            norm_params.astype(jnp.bfloat16), ("rows", "depth"), axis=1, tiled=True
        ).astype(norm_params.dtype),
    )
    block_grad = depth_weights[hist_total] * grad_out
    lower_grad = block_grad.astype(jnp.bfloat16)
    down_gradient = jnp.dot(active.T, lower_grad, preferred_element_type=jnp.float32)
    active_grad = jnp.dot(lower_grad, wide_down.T, preferred_element_type=jnp.float32)
    _, gelu_pull = jax.vjp(jax.nn.gelu, upper)
    upper_grad = gelu_pull(active_grad)[0].astype(jnp.bfloat16)
    up_gradient = jnp.dot(second.T, upper_grad, preferred_element_type=jnp.float32)
    second_grad = jnp.dot(upper_grad, wide_up.T, preferred_element_type=jnp.float32)
    _, norm_pull = jax.vjp(norm_rows, middle, wide_norms[2], wide_norms[3])
    middle_part, gain_two, shift_two = norm_pull(second_grad)
    middle_grad = block_grad + middle_part
    branch_grad = middle_grad.astype(jnp.bfloat16)
    out_gradient = jnp.dot(mixed_low.T, branch_grad, preferred_element_type=jnp.float32)
    mixed_grad = jnp.dot(branch_grad, wide_out.T, preferred_element_type=jnp.float32).astype(
        jnp.bfloat16
    )
    delta = jnp.sum(
        (mixed_grad.astype(jnp.float32) * mixed).reshape(rows_tok, heads, head_size), axis=-1
    ).T
    mixed_heads = mixed_grad.reshape(rows_tok, heads, head_size)

    def score_grads(
        query_rows, grad_rows, lse_rows, delta_rows, key_block, value_block, query_place, start
    ):
        scores, allowed = block_scores(query_rows, key_block, start, query_place, scale)
        probs = jnp.where(allowed[None], jnp.exp(scores - lse_rows[..., None]), 0.0)
        prob_grad = jnp.einsum(
            "qhd,khd->hqk", grad_rows, value_block, preferred_element_type=jnp.float32
        )
        score_grad = (probs * (prob_grad - delta_rows[..., None])).astype(jnp.bfloat16)
        return (probs, score_grad)

    def grad_step(query_total, item):
        key_block, value_block, start = item
        probs, score_grad = score_grads(
            query, mixed_heads, log_total, delta, key_block, value_block, place, start
        )
        query_total = (
            query_total
            + jnp.einsum("hqk,khd->qhd", score_grad, key_block, preferred_element_type=jnp.float32)
            * scale
        )
        key_part = (
            jnp.einsum("hqk,qhd->khd", score_grad, query, preferred_element_type=jnp.float32)
            * scale
        )
        value_part = jnp.einsum(
            "hqk,qhd->khd",
            probs.astype(jnp.bfloat16),
            mixed_heads,
            preferred_element_type=jnp.float32,
        )
        return (query_total, (key_part, value_part))

    query_total, (key_parts, value_parts) = lax.scan(
        grad_step,
        jnp.zeros((rows_tok, heads, head_size), jnp.float32),
        (key_blocks, value_blocks, starts),
    )
    key_sum, value_sum = (
        lax.psum_scatter(
            key_parts.reshape(seq_len, width).astype(jnp.bfloat16),
            "depth",
            scatter_dimension=0,
            tiled=True,
        ).astype(jnp.float32),
        lax.psum_scatter(
            value_parts.reshape(seq_len, width).astype(jnp.bfloat16),
            "depth",
            scatter_dimension=0,
            tiled=True,
        ).astype(jnp.float32),
    )
    query_grad = rotate(query_total, place, -1.0).reshape(rows_tok, width)
    key_grad = rotate(key_sum.reshape(rows_tok, heads, head_size), place, -1.0).reshape(
        rows_tok, width
    )
    projected_grad = jnp.concatenate([query_grad, key_grad, value_sum], axis=1).astype(jnp.bfloat16)
    qkv_gradient = jnp.dot(first.T, projected_grad, preferred_element_type=jnp.float32)
    first_grad = jnp.dot(projected_grad, wide_qkv.T, preferred_element_type=jnp.float32)
    _, first_pull = jax.vjp(norm_rows, float_input, wide_norms[0], wide_norms[1])
    input_part, gain_one, shift_one = first_pull(first_grad)
    input_grad = (middle_grad + input_part).astype(jnp.bfloat16)
    norms_full = jnp.stack([gain_one, shift_one, gain_two, shift_two])
    qkv_gradient, out_gradient, up_gradient, down_gradient, norm_gradient = (
        lax.psum_scatter(qkv_gradient, ("rows", "depth"), scatter_dimension=0, tiled=True),
        lax.psum_scatter(out_gradient, ("rows", "depth"), scatter_dimension=0, tiled=True),
        lax.psum_scatter(up_gradient, ("rows", "depth"), scatter_dimension=0, tiled=True),
        lax.psum_scatter(down_gradient, ("rows", "depth"), scatter_dimension=0, tiled=True),
        lax.psum_scatter(norms_full, ("rows", "depth"), scatter_dimension=1, tiled=True),
    )
    return (
        output,
        input_grad,
        history_grad,
        qkv_gradient,
        out_gradient,
        up_gradient,
        down_gradient,
        norm_gradient,
        depth_gradient,
    )

SEQ = 512
OWN = 128
WIDTH = 768
ROWS = 8
GROUP = 4
PACK = 640
BLOCK = WIDTH // ROWS
CHUNK = BLOCK // GROUP
QBLOCK = 256
BF = jnp.bfloat16
F32 = jnp.float32
MESH = pl.DeviceIdType.MESH


def dot(a, b, ca=1, cb=0):
    return lax.dot_general(a, b, (((ca,), (cb,)), ((), ())), preferred_element_type=F32)


def lane_id(shape):
    return lax.broadcasted_iota(jnp.int32, shape, len(shape) - 1)


def row_id(shape):
    return lax.broadcasted_iota(jnp.int32, shape, len(shape) - 2)


def tiles_of(value):
    return [value[:, 128 * i : 128 * (i + 1)] for i in range(value.shape[1] // 128)]


def permute_chunks(tiles, picks):
    group = lax.div(lane_id(tiles[0].shape), jnp.int32(32))
    out = []
    for t in range(len(picks) // 4):
        total, rolled = jnp.zeros_like(tiles[0]), {}
        for j in range(4):
            pick = picks[4 * t + j]
            if pick is None:
                continue
            source, place = divmod(pick, 4)
            shift = (j - place) * 32 % 128
            if (source, shift) not in rolled:
                value = tiles[source]
                rolled[source, shift] = pltpu.roll(value, shift, 1) if shift else value
            total = jnp.where(group == j, rolled[source, shift], total)
        out.append(total)
    return out


def fold(tiles):
    half = (len(tiles) + 1) // 2
    low = [t[16:] for t in tiles]
    if len(low) % 2:
        low.append(jnp.zeros_like(low[0]))
    return [t[:16] for t in tiles] + [
        jnp.concatenate([low[i], low[half + i]], axis=0) for i in range(half)
    ]


def unfold(tiles, count):
    half = (count + 1) // 2
    rest = tiles[count:]
    low = [rest[i][:8] for i in range(half)] + [rest[i][8:] for i in range(half)]
    return [jnp.concatenate([tiles[i], low[i]], axis=0) for i in range(count)]


def qkv_chunk(block, head, half):
    return 24 * block + 2 * head + half


def qkv_picks(d):
    heads = [3 * d + i for i in range(3)]
    picks = []
    for block in range(2):
        for half in range(2):
            picks += [qkv_chunk(block, h, half) for h in heads]
            picks.append(qkv_chunk(2, heads[2], half) if block == 0 else None)
    return picks + [qkv_chunk(2, h, half) for h in heads[:2] for half in range(2)]


def up_picks(d):
    return [3 * (GROUP * r + d) + j for r in range(ROWS) for j in range(3)]


def inverse_picks(per_device, count, tiles_each):
    back = [None] * count
    for d, picks in enumerate(per_device):
        for place, pick in enumerate(picks):
            if pick is not None:
                back[pick] = 4 * tiles_each * d + place
    return back


QKV_BACK = inverse_picks([qkv_picks(d) for d in range(GROUP)], 72, 5)
UP_BACK = inverse_picks([up_picks(d) for d in range(GROUP)], 96, 6)


def tables():
    half = HD // 2
    freq = np.float32(10000.0) ** (-np.arange(half, dtype=np.float32) / np.float32(half))
    angle = (np.arange(SEQ, dtype=np.float32)[:, None] * freq[None, :]).astype(np.float32)
    angle = angle.astype(np.float64)
    cosine, sine = np.ones((SEQ, 128), np.float32), np.zeros((SEQ, 128), np.float32)
    cosine[:, :96] = np.tile(np.cos(angle), (1, 3))
    sine[:, :96] = np.tile(np.sin(angle), (1, 3))
    return cosine, sine


def standardize(value):
    center = value - jnp.mean(value, axis=-1, keepdims=True)
    spread = jnp.mean(center * center, axis=-1, keepdims=True)
    scale = lax.rsqrt(spread + 1e-05)
    return center * scale, scale


def norm_back(grad, gain, normal, scale):
    part = grad * (1.0 + gain)
    inner = jnp.mean(part, axis=-1, keepdims=True)
    along = jnp.mean(part * normal, axis=-1, keepdims=True)
    return scale * (part - inner - normal * along)


def sublane_sum(value):
    return jnp.sum(value.reshape(value.shape[0] // 8, 8, value.shape[1]), axis=0)


SCRATCH = dict(
    x_all=((GROUP, OWN, WIDTH), BF),
    c_all=((GROUP, OWN, WIDTH), BF),
    qp_s=((GROUP, 16, 1024), BF),
    qp_l=((GROUP, 16, 1024), BF),
    up_s=((GROUP, 16, 1152), BF),
    up_l=((GROUP, 16, 1152), BF),
    tmp=((BLOCK, WIDTH), F32),
    w_qkv=((WIDTH, PACK), BF),
    w_up=((WIDTH, WIDTH), BF),
    w_down=((WIDTH, WIDTH), BF),
    wo_l=((GROUP, ROWS, 16, 1152), BF),
    w_out=((WIDTH, WIDTH), BF),
    w_own=((384, WIDTH), BF),
    norms=((8, WIDTH), F32),
    normal=((SEQ, WIDTH), F32),
    h1=((SEQ, WIDTH), BF),
    qv=((SEQ, 256), BF),
    kk=((SEQ, 256), BF),
    v01=((SEQ, 128), BF),
    probs=((3, SEQ, SEQ), F32),
    o_l=((GROUP, 2, 384, 128), BF),
    ob=((SEQ, WIDTH), BF),
    y=((SEQ, WIDTH), F32),
    h2=((SEQ, WIDTH), BF),
    slope=((SEQ, WIDTH), F32),
    act=((SEQ, WIDTH), BF),
    dm=((SEQ, WIDTH), BF),
    g_down=((WIDTH, WIDTH), F32),
    g_up=((WIDTH, WIDTH), F32),
    g_out=((WIDTH, WIDTH), F32),
    g_qkv=((WIDTH, PACK), F32),
    du=((SEQ, WIDTH), BF),
    part=((SEQ, WIDTH), F32),
    dy=((OWN, WIDTH), F32),
    dyb=((GROUP, OWN, WIDTH), BF),
    dob=((SEQ, 384), BF),
    dq=((SEQ, 256), F32),
    dk=((SEQ, 256), F32),
    dv=((SEQ, 384), F32),
    dqkv=((SEQ, PACK), BF),
    terms=((8, WIDTH), F32),
    terms2=((8, WIDTH), F32),
    t0=((8, WIDTH), F32),
    t1=((8, WIDTH), F32),
    tz=((4, 8, WIDTH), F32),
    td=((4, 8, WIDTH), F32),
    a_qkv=((GROUP, CHUNK, PACK), F32),
    a_up=((GROUP, CHUNK, WIDTH), F32),
)
for _name, _rows, _cols in (
    ("down", BLOCK, WIDTH),
    ("up", BLOCK, WIDTH),
    ("out", 16, 1152),
    ("qkv", BLOCK, PACK),
):
    SCRATCH["xs_" + _name] = ((4, _rows, _cols), BF)
    SCRATCH["xl_" + _name] = ((4, _rows, _cols), BF)
    SCRATCH["zs_" + _name] = ((3, _rows, _cols), BF)
    SCRATCH["zl_" + _name] = ((3, _rows, _cols), BF)
    SCRATCH["f_" + _name] = ((_rows, _cols), F32)
for _name in ("mix", "mid", "in"):
    SCRATCH["s1_" + _name] = ((2, OWN, WIDTH), BF)
    SCRATCH["l1_" + _name] = ((2, OWN, WIDTH), BF)
    SCRATCH["s2_" + _name] = ((OWN, WIDTH), BF)
    SCRATCH["l2_" + _name] = ((OWN, WIDTH), BF)
N_SEMS = 160
N_IN = 12
N_OUT = 9


class Names:
    pass


def fused_kernel(*refs):
    (x_in, hist, cot, mask, wq, wo, wu, wd, nrm, dw, cosine, sine) = refs[:N_IN]
    (out_o, ig_o, hg_o, gq_o, go_o, gu_o, gd_o, ng_o, dg_o) = refs[N_IN : N_IN + N_OUT]
    s = Names()
    for name, ref in zip(SCRATCH, refs[N_IN + N_OUT :]):
        setattr(s, name, ref)
    send_sems, recv_sems = refs[-2:]

    r, d = lax.axis_index("rows"), lax.axis_index("depth")
    z, x = lax.div(r, 2), lax.rem(r, 2)
    yy, c = lax.div(d, 2), lax.rem(d, 2)
    other_x, other_c, other_y = 1 - x, 1 - c, 1 - yy
    x_dev = (2 * z + other_x, d)
    z_of = [lax.rem(z + k, 4) for k in range(4)]
    z_dev = [(2 * zk + x, d) for zk in z_of]
    core_d, y_d, far_d = 2 * yy + other_c, 2 * other_y + c, 2 * other_y + other_c
    core_dev, y_dev, far_dev = (r, core_d), (r, y_d), (r, far_d)
    mates = ((core_d, core_dev), (y_d, y_dev), (far_d, far_dev))
    counter = [0]
    sent = []

    def copy_to(src, dst, device):
        index = counter[0]
        counter[0] += 1
        copy = pltpu.make_async_remote_copy(
            src_ref=src,
            dst_ref=dst,
            send_sem=send_sems.at[index],
            recv_sem=recv_sems.at[index],
            device_id=device,
            device_id_type=MESH,
        )
        copy.start()
        sent.append(copy)
        return copy

    def rows_at(ref, index, size):
        return ref.at[pl.ds(pl.multiple_of(index * size, size), size)]

    def by_rows(count, step, body):
        def one(i, carry):
            body(pl.ds(pl.multiple_of(i * step, step), step))
            return carry

        lax.fori_loop(0, count // step, one, 0)

    barrier = pltpu.get_barrier_semaphore()
    for device in (x_dev, *z_dev[1:], core_dev, y_dev, far_dev):
        pl.semaphore_signal(barrier, inc=1, device_id=device, device_id_type=MESH)
    pl.semaphore_wait(barrier, 7)

    class Gather:
        def __init__(self, piece):
            self.piece = piece

        def send(self):
            mine = self.piece(r)
            self.along_z = [copy_to(mine, mine, z_dev[k]) for k in (1, 2, 3)]
            self.along_x = [copy_to(mine, mine, x_dev)]

        def forward(self):
            for k in (1, 2, 3):
                self.along_z[k - 1].wait_recv()
                piece = self.piece(2 * z_of[4 - k] + x)
                self.along_x.append(copy_to(piece, piece, x_dev))

        def finish(self):
            for copy in self.along_x:
                copy.wait_recv()

    class GroupGather:
        def __init__(self, slab):
            self.slab = slab

        def send(self):
            mine = self.slab(d)
            self.to_core = copy_to(mine, mine, core_dev)
            self.to_y = copy_to(mine, mine, y_dev)

        def relay(self):
            self.to_y.wait_recv()
            slab = self.slab(y_d)
            self.on = copy_to(slab, slab, core_dev)

        def finish(self):
            self.to_core.wait_recv()
            self.on.wait_recv()

    class RowSum:
        def __init__(self, name, block, step):
            self.xs, self.xl, self.zs, self.zl, self.total = (
                getattr(s, p + name) for p in ("xs_", "xl_", "zs_", "zl_", "f_")
            )
            self.block, self.step = block, step
            self.count = self.total.shape[0]

        def send(self):
            self.along_x = []
            for k in (2, 1, 3, 0):
                zk = z_of[k]

                def stage(at):
                    self.xs[zk, at, :] = self.block(2 * zk + other_x, at).astype(BF)

                by_rows(self.count, self.step, stage)
                self.along_x.append(copy_to(self.xs.at[zk], self.xl.at[zk], x_dev))

        def middle(self):
            self.along_z = {}
            for place, k in enumerate((2, 1, 3)):
                self.along_x[place].wait_recv()
                zk = z_of[k]

                def stage(at):
                    value = self.block(2 * zk + x, at) + self.xl[zk, at, :].astype(F32)
                    self.zs[k - 1, at, :] = value.astype(BF)

                by_rows(self.count, self.step, stage)
                self.along_z[k] = copy_to(self.zs.at[k - 1], self.zl.at[k - 1], z_dev[k])

        def finish(self):
            self.along_x[3].wait_recv()
            for k in (1, 2, 3):
                self.along_z[k].wait_recv()

            def stage(at):
                value = self.block(r, at) + self.xl[z, at, :].astype(F32)
                for k in range(3):
                    value = value + self.zl[k, at, :].astype(F32)
                self.total[at, :] = value

            by_rows(self.count, self.step, stage)

    class GroupSum:
        def __init__(self, name, source):
            self.s1, self.l1, self.s2, self.l2 = (
                getattr(s, p + name) for p in ("s1_", "l1_", "s2_", "l2_")
            )
            self.source = source

        def block(self, index, at):
            return self.source[pl.ds(pl.multiple_of(index * OWN + at.start, at.size), at.size), :]

        def send(self):
            self.first = []
            for j, yj in enumerate((other_y, yy)):

                def stage(at):
                    self.s1[j, at, :] = self.block(2 * yj + other_c, at).astype(BF)

                by_rows(OWN, 32, stage)
                self.first.append(copy_to(self.s1.at[j], self.l1.at[j], core_dev))

        def middle(self):
            self.first[0].wait_recv()

            def stage(at):
                value = self.block(2 * other_y + c, at) + self.l1[0, at, :].astype(F32)
                self.s2[at, :] = value.astype(BF)

            by_rows(OWN, 32, stage)
            self.second = copy_to(self.s2, self.l2, y_dev)

        def wait(self):
            self.first[1].wait_recv()
            self.second.wait_recv()

        def value(self, at):
            return (
                self.block(d, at)
                + self.l1[1, at, :].astype(F32)
                + self.l2[at, :].astype(F32)
            )

    out_gather = Gather(lambda i: s.wo_l.at[d, i])
    for t, tile in enumerate(fold(tiles_of(wo[...].astype(F32)))):
        s.wo_l[d, r, :, 128 * t : 128 * (t + 1)] = tile.astype(BF)
    out_gather.send()

    lane = lane_id((CHUNK, 128))
    eye = row_id((CHUNK, CHUNK)) == lane_id((CHUNK, CHUNK))
    extra = jnp.zeros((CHUNK, 128), F32)
    for k in range(4):
        column = jnp.sum(jnp.where(eye, nrm[k : k + 1, :], 0.0), axis=1, keepdims=True)
        high = column.astype(BF).astype(F32)
        extra = jnp.where(lane == 96 + k, high, extra)
        extra = jnp.where(lane == 100 + k, column - high, extra)
    mask_row = mask[...].astype(F32)
    ones = jnp.sum(mask_row, axis=1, keepdims=True)
    extra = jnp.where((lane == 104) & (row_id((CHUNK, 128)) == 0), ones, extra)

    wq_tiles = tiles_of(wq[...].astype(F32))
    for k in range(GROUP):
        tiles = permute_chunks(wq_tiles, qkv_picks(k))
        tiles[2] = tiles[2] + extra
        for t, tile in enumerate(fold(tiles)):
            s.qp_s[k, :, 128 * t : 128 * (t + 1)] = tile.astype(BF)
    qp_copies = [copy_to(s.qp_s.at[m], s.qp_l.at[d], device) for m, device in mates]
    s.qp_l[d] = s.qp_s[d]

    s.x_all[d] = x_in[...]
    x_gather = GroupGather(lambda i: s.x_all.at[i])
    x_gather.send()

    wu_tiles = tiles_of(wu[...].astype(F32))
    for k in range(GROUP):
        for t, tile in enumerate(fold(permute_chunks(wu_tiles, up_picks(k)))):
            s.up_s[k, :, 128 * t : 128 * (t + 1)] = tile.astype(BF)
    up_copies = [copy_to(s.up_s.at[m], s.up_l.at[d], device) for m, device in mates]
    s.up_l[d] = s.up_s[d]

    diagonal = jnp.where(
        row_id((OWN, OWN)) == lane_id((OWN, OWN)), jnp.broadcast_to(mask_row, (OWN, OWN)), 0.0
    )
    s.c_all[d] = dot(diagonal.astype(BF), cot[...]).astype(BF)
    c_gather = GroupGather(lambda i: s.c_all.at[i])
    c_gather.send()

    rows_at(s.w_down, r, BLOCK)[...] = wd[...]

    def assemble(landing, count, target):
        for k in range(GROUP):
            tiles = [t.astype(F32) for t in tiles_of(landing[k])]
            for t, tile in enumerate(unfold(tiles, count)):
                s.tmp[CHUNK * k : CHUNK * (k + 1), 128 * t : 128 * (t + 1)] = tile
        rows_at(target, r, BLOCK)[...] = s.tmp[:, : 128 * count].astype(BF)

    for copy in qp_copies:
        copy.wait_recv()
    assemble(s.qp_l, 5, s.w_qkv)
    qkv_gather = Gather(lambda i: rows_at(s.w_qkv, i, BLOCK))
    qkv_gather.send()
    for copy in up_copies:
        copy.wait_recv()
    assemble(s.up_l, 6, s.w_up)
    up_gather = Gather(lambda i: rows_at(s.w_up, i, BLOCK))
    up_gather.send()
    down_gather = Gather(lambda i: rows_at(s.w_down, i, BLOCK))
    down_gather.send()

    x_gather.relay()
    c_gather.relay()
    out_gather.forward()
    x_gather.finish()

    for i in range(GROUP):

        def normalize(at, i=i):
            normal, _ = standardize(s.x_all[i, at, :].astype(F32))
            s.normal[pl.ds(pl.multiple_of(OWN * i + at.start, at.size), at.size), :] = normal

        by_rows(OWN, 64, normalize)
    qkv_gather.forward()
    out_gather.finish()
    slab_gather = GroupGather(lambda i: s.wo_l.at[i])
    slab_gather.send()
    qkv_gather.finish()

    lane = lane_id((8, 128))
    row = row_id((8, 128))
    pick = jnp.where((lane == 96 + row) | (lane == 100 + row), 1.0, 0.0)
    pick = jnp.where(row < 4, pick, jnp.where((row == 4) & (lane == 104), 1.0, 0.0))
    s.norms[...] = dot(pick.astype(BF), s.w_qkv[:, 256:384], 1, 1)
    total = jnp.sum(s.norms[4:5, :], axis=1, keepdims=True)
    loss_scale = (SEQ * ROWS) / total
    own_weight = dw[d]
    last_weight = dw[GROUP]

    def first_norm(at):
        value = s.normal[at, :] * (1.0 + s.norms[0:1, :]) + s.norms[1:2, :]
        s.h1[at, :] = value.astype(BF)

    by_rows(SEQ, 64, first_norm)

    def project(at):
        value = dot(s.h1[at, :], s.w_qkv[...])
        co, si = cosine[at, :], sine[at, :]
        for left, target in ((0, s.qv), (256, s.kk)):
            a, b = value[:, left : left + 128], value[:, left + 128 : left + 256]
            target[at, :128] = (a * co - b * si).astype(BF)
            target[at, 128:] = (b * co + a * si).astype(BF)
        s.v01[at, :] = value[:, 512:].astype(BF)

    by_rows(SEQ, 256, project)
    slab_gather.relay()
    c_gather.finish()

    s.terms[...] = jnp.zeros((8, WIDTH), F32)
    for i in range(GROUP):

        def loss_rows(at, i=i):
            here = pl.ds(pl.multiple_of(OWN * i + at.start, at.size), at.size)
            grad = s.c_all[i, at, :].astype(F32) * loss_scale
            s.dm[here, :] = (last_weight * grad).astype(BF)
            hg_o[here, :] = (own_weight * grad).astype(BF)
            s.terms[...] += sublane_sum(grad * hist[here, :].astype(F32))

        by_rows(OWN, 32, loss_rows)
    up_gather.forward()

    lane2 = lax.div(lax.rem(lane_id((1, 256)), 128), jnp.int32(32))
    head_mask = [jnp.where(lane2 == h, 1.0, 0.0).astype(BF) for h in range(3)]
    tail_mask = jnp.where(lane2 == 3, 1.0, 0.0).astype(BF)
    half_id = lax.div(lane_id((1, 128)), jnp.int32(64))
    half_mask = [jnp.where(half_id == h, 1.0, 0.0).astype(BF) for h in range(2)]
    root = HD**-0.5
    o_gathers = []
    for b in range(2):
        rows = slice(QBLOCK * b, QBLOCK * (b + 1))
        keys = QBLOCK * (b + 1)
        query = s.qv[rows, :]
        allowed = row_id((QBLOCK, keys)) + QBLOCK * b >= lane_id((QBLOCK, keys))
        first = jnp.zeros((QBLOCK, 128), F32)
        third = None
        for h in range(3):
            scores = dot(query * head_mask[h], s.kk[:keys, :], 1, 1) * root
            scores = jnp.where(allowed, scores, -1e30)
            raised = jnp.exp(scores - jnp.max(scores, axis=1, keepdims=True))
            probs = raised * (1.0 / jnp.sum(raised, axis=1, keepdims=True))
            s.probs[h, rows, :keys] = probs
            if h < 2:
                first = first + dot(probs.astype(BF), s.v01[:keys, :] * half_mask[h])
            else:
                third = dot(probs.astype(BF), s.qv[:keys, :])
        s.o_l[d, b, :QBLOCK, :] = first.astype(BF)
        lane = lane_id((QBLOCK, 128))
        third = jnp.where(
            lane < 32, pltpu.roll(third[:, :128], 32, 1), pltpu.roll(third[:, 128:], 64, 1)
        )
        lane = lane_id((OWN, 128))
        third = jnp.where(lane < 64, third[:OWN], pltpu.roll(third[OWN:], 64, 1))
        s.o_l[d, b, QBLOCK:, :] = third.astype(BF)
        o_gathers.append(GroupGather(lambda i, b=b: s.o_l.at[i, b]))
        o_gathers[b].send()
        if b == 0:
            slab_gather.finish()
            for k in range(GROUP):
                for i in range(ROWS):
                    tiles = [t.astype(F32) for t in tiles_of(s.wo_l[k, i])]
                    at = CHUNK * (GROUP * i + k)
                    for t, tile in enumerate(unfold(tiles, 6)):
                        s.g_out[at : at + CHUNK, 128 * t : 128 * (t + 1)] = tile
    down_gather.forward()

    def out_place(head):
        k, h = divmod(head, 3)
        return 128 * k + 64 * h if h < 2 else 512 + 64 * k

    for head in range(HEADS):
        at = out_place(head)
        s.w_out[at : at + 64, :] = s.g_out[64 * head : 64 * head + 64, :].astype(BF)
    s.w_own[...] = jnp.zeros((384, WIDTH), BF)
    third_rows = rows_at(s.w_out.at[pl.ds(512, 256)], d, 64)
    s.w_own[96:128, :] = third_rows[:32, :]
    s.w_own[224:256, :] = third_rows[32:, :]
    s.w_own[256:, :] = rows_at(s.w_out.at[pl.ds(0, 512)], d, 128)[...]

    for b in range(2):
        o_gathers[b].relay()
        o_gathers[b].finish()
        rows = slice(QBLOCK * b, QBLOCK * (b + 1))
        thirds = []
        for k in range(GROUP):
            s.ob[rows, 128 * k : 128 * (k + 1)] = s.o_l[k, b, :QBLOCK, :]
            thirds.append(s.o_l[k, b, QBLOCK:, :].astype(F32))
        lane = lane_id((OWN, 128))
        for p in range(2):
            even, odd = thirds[2 * p], thirds[2 * p + 1]
            top = jnp.where(lane < 64, even, pltpu.roll(odd, 64, 1))
            low = jnp.where(lane < 64, pltpu.roll(even, 64, 1), odd)
            cols = slice(512 + 128 * p, 640 + 128 * p)
            s.ob[QBLOCK * b : QBLOCK * b + OWN, cols] = top.astype(BF)
            s.ob[QBLOCK * b + OWN : QBLOCK * (b + 1), cols] = low.astype(BF)
        s.y[rows, :] = dot(s.ob[rows, :], s.w_out[...])
        for i in (2 * b, 2 * b + 1):

            def second_norm(at, i=i):
                here = pl.ds(pl.multiple_of(OWN * i + at.start, at.size), at.size)
                value = s.y[here, :] + s.x_all[i, at, :].astype(F32)
                s.y[here, :] = value
                normal, _ = standardize(value)
                value = normal * (1.0 + s.norms[2:3, :]) + s.norms[3:4, :]
                s.h2[here, :] = value.astype(BF)

            by_rows(OWN, 64, second_norm)

    up_gather.finish()

    def widen(at):
        s.part[at, :] = dot(s.h2[at, :], s.w_up[...])

    by_rows(SEQ, 256, widen)

    def gate(at):
        u = s.part[at, :]
        rate = 0.7978845608028654
        bend = jnp.tanh(rate * (u + 0.044715 * u * u * u))
        s.act[at, :] = (0.5 * u * (1.0 + bend)).astype(BF)
        inner = rate * (1.0 + 3 * 0.044715 * u * u)
        s.slope[at, :] = 0.5 * (1.0 + bend) + 0.5 * u * (1.0 - bend * bend) * inner

    by_rows(SEQ, 32, gate)

    def block_of(ref):
        def block(index, at):
            return ref[pl.ds(pl.multiple_of(index * BLOCK + at.start, at.size), at.size), :]

        return block

    for i in range(3):
        cols = slice(QBLOCK * i, QBLOCK * (i + 1))
        s.g_down[cols, :] = dot(s.act[:, cols], s.dm[...], 0, 0)
    down_sum = RowSum("down", block_of(s.g_down), 16)
    down_sum.send()

    down_gather.finish()

    def narrow(at):
        value = dot(s.dm[at, :], s.w_down[...], 1, 1)
        s.du[at, :] = (value * s.slope[at, :]).astype(BF)

    by_rows(SEQ, 256, narrow)

    def second_back(at):
        s.part[at, :] = dot(s.du[at, :], s.w_up[...], 1, 1)

    by_rows(SEQ, 256, second_back)
    mid_sum = GroupSum("mid", s.part)
    mid_sum.send()
    down_sum.middle()

    for i in range(3):
        cols = slice(QBLOCK * i, QBLOCK * (i + 1))
        s.g_up[cols, :] = dot(s.h2[:, cols], s.du[...], 0, 0)
    up_sum = RowSum("up", block_of(s.g_up), 16)
    up_sum.send()
    mid_sum.middle()
    mid_sum.wait()

    s.terms2[...] = jnp.zeros((8, WIDTH), F32)
    s.t0[...] = jnp.zeros((8, WIDTH), F32)

    def second_norm_back(at):
        here = pl.ds(pl.multiple_of(OWN * d + at.start, at.size), at.size)
        grad = mid_sum.value(at)
        value = s.y[here, :]
        normal, scale = standardize(value)
        loss = s.c_all[d, at, :].astype(F32) * loss_scale
        back = last_weight * loss + norm_back(grad, s.norms[2:3, :], normal, scale)
        s.dy[at, :] = back
        s.dyb[d, at, :] = back.astype(BF)
        s.t0[2:3, :] += jnp.sum(grad * normal, axis=0, keepdims=True)
        s.t0[3:4, :] += jnp.sum(grad, axis=0, keepdims=True)
        s.terms2[...] += sublane_sum(loss * value)

    by_rows(OWN, 32, second_norm_back)
    dy_gather = GroupGather(lambda i: s.dyb.at[i])
    dy_gather.send()

    def block_out(at):
        value = dot(s.act[at, :], s.w_down[...])
        s.part[at, :] = value

    by_rows(SEQ, 256, block_out)
    for i in range(GROUP):

        def mix(at, i=i):
            here = pl.ds(pl.multiple_of(OWN * i + at.start, at.size), at.size)
            value = s.part[here, :]
            loss = s.c_all[i, at, :].astype(F32) * loss_scale
            s.terms2[...] += sublane_sum(loss * value)
            s.part[here, :] = own_weight * hist[here, :].astype(F32) + last_weight * value

        by_rows(OWN, 32, mix)
    mix_sum = GroupSum("mix", s.part)
    mix_sum.send()
    up_sum.middle()
    dy_gather.relay()
    mix_sum.middle()
    dy_gather.finish()

    by_group = s.dyb[...].reshape(SEQ, WIDTH)

    s.dob[...] = dot(by_group, s.w_own[...], 1, 1).astype(BF)
    for p in range(3):
        cols = slice(QBLOCK * p, QBLOCK * (p + 1))
        value = dot(s.ob[:, cols], by_group, 0, 0)
        for i in range(4):
            place = QBLOCK * p + 64 * i
            for head in range(HEADS):
                if out_place(head) == place:
                    s.g_out[64 * head : 64 * head + 64, :] = value[64 * i : 64 * i + 64]

    def out_block(index, at):
        start = pl.multiple_of((GROUP * index + d) * CHUNK, 8)
        tiles = tiles_of(s.g_out[pl.ds(start, CHUNK), :])
        return jnp.concatenate(fold(tiles), axis=1)

    out_sum = RowSum("out", out_block, 16)
    out_sum.send()
    mix_sum.wait()

    def write_out(at):
        here = pl.ds(pl.multiple_of(OWN * d + at.start, at.size), at.size)
        out_o[at, :] = (mix_sum.value(at) + last_weight * s.y[here, :]).astype(BF)

    by_rows(OWN, 32, write_out)

    for b in range(2):
        rows = slice(QBLOCK * b, QBLOCK * (b + 1))
        keys = QBLOCK * (b + 1)
        query = s.qv[rows, :]
        dq = jnp.zeros((QBLOCK, 256), F32)
        for h in range(3):
            probs = s.probs[h, rows, :keys]
            if h < 2:
                grad = s.dob[rows, 256:] * half_mask[h]
                dp = dot(grad, s.v01[:keys, :], 1, 1)
            else:
                grad = s.dob[rows, :256]
                dp = dot(grad, s.qv[:keys, :], 1, 1)
            delta = jnp.sum(dp * probs, axis=1, keepdims=True)
            ds = (probs * (dp - delta)).astype(BF)
            dq = dq + dot(ds, s.kk[:keys, :] * head_mask[h])
            dk = dot(ds, query * head_mask[h], 0, 0) * root
            dv = dot(probs.astype(BF), grad, 0, 0)
            cols = slice(256, 384) if h < 2 else slice(0, 256)
            if b == 0:
                old, new = slice(0, QBLOCK), None
            else:
                old, new = slice(0, QBLOCK), slice(QBLOCK, SEQ)
            if h == 0 and b == 0:
                s.dk[old, :] = dk[:QBLOCK]
            else:
                s.dk[old, :] += dk[:QBLOCK]
            if b == 0 and h != 1:
                s.dv[old, cols] = dv[:QBLOCK]
            else:
                s.dv[old, cols] += dv[:QBLOCK]
            if new is not None:
                if h == 0:
                    s.dk[new, :] = dk[QBLOCK:]
                else:
                    s.dk[new, :] += dk[QBLOCK:]
                if h != 1:
                    s.dv[new, cols] = dv[QBLOCK:]
                else:
                    s.dv[new, cols] += dv[QBLOCK:]
        s.dq[rows, :] = dq * root

    def turn_back(at):
        co, si = cosine[at, :], sine[at, :]
        for left, source in ((0, s.dq), (256, s.dk)):
            a, b = source[at, :128], source[at, 128:]
            first, second = a * co + b * si, b * co - a * si
            if left == 0:
                first, second = first + s.dv[at, :128], second + s.dv[at, 128:256]
            s.dqkv[at, left : left + 128] = first.astype(BF)
            s.dqkv[at, left + 128 : left + 256] = second.astype(BF)
        s.dqkv[at, 512:] = s.dv[at, 256:].astype(BF)

    by_rows(SEQ, 64, turn_back)
    for i in range(3):
        cols = slice(QBLOCK * i, QBLOCK * (i + 1))
        s.g_qkv[cols, :] = dot(s.h1[:, cols], s.dqkv[...], 0, 0)
    qkv_sum = RowSum("qkv", block_of(s.g_qkv), 16)
    qkv_sum.send()

    def first_back(at):
        s.part[at, :] = dot(s.dqkv[at, :], s.w_qkv[...], 1, 1)

    by_rows(SEQ, 256, first_back)
    in_sum = GroupSum("in", s.part)
    in_sum.send()
    out_sum.middle()
    in_sum.middle()

    def spread(total, landing):
        copies = [
            copy_to(total.at[pl.ds(pl.multiple_of(CHUNK * m, CHUNK), CHUNK)], landing.at[d], device)
            for m, device in mates
        ]
        landing[d] = total[pl.ds(pl.multiple_of(CHUNK * d, CHUNK), CHUNK), :]
        return copies

    down_sum.finish()
    gd_o[...] = s.f_down[...]
    up_sum.finish()
    up_spread = spread(s.f_up, s.a_up)
    qkv_sum.middle()
    in_sum.wait()

    def first_norm_back(at):
        grad = in_sum.value(at)
        normal, scale = standardize(x_in[at, :].astype(F32))
        back = norm_back(grad, s.norms[0:1, :], normal, scale)
        ig_o[at, :] = (s.dy[at, :] + back).astype(BF)
        s.t0[0:1, :] += jnp.sum(grad * normal, axis=0, keepdims=True)
        s.t0[1:2, :] += jnp.sum(grad, axis=0, keepdims=True)

    by_rows(OWN, 32, first_norm_back)

    lane = lane_id((1, WIDTH))
    own_term = jnp.sum(jnp.sum(s.terms[...], axis=0, keepdims=True), axis=1, keepdims=True)
    last_term = jnp.sum(jnp.sum(s.terms2[...], axis=0, keepdims=True), axis=1, keepdims=True)
    s.t0[4:5, :] = jnp.where(lane == d, own_term, jnp.where(lane == GROUP, last_term, 0.0))
    small = copy_to(s.t0, s.t1, x_dev)
    out_sum.finish()
    for t, tile in enumerate(unfold(tiles_of(s.f_out[...]), 6)):
        go_o[:, 128 * t : 128 * (t + 1)] = tile
    small.wait_recv()
    s.tz[z] = s.t0[...] + s.t1[...]
    small_z = [copy_to(s.tz.at[z], s.tz.at[z], z_dev[k]) for k in (1, 2, 3)]
    for copy in up_spread:
        copy.wait_recv()
    tiles = [t for k in range(GROUP) for t in tiles_of(s.a_up[k])]
    for t, tile in enumerate(permute_chunks(tiles, UP_BACK)):
        gu_o[:, 128 * t : 128 * (t + 1)] = tile
    for copy in small_z:
        copy.wait_recv()
    s.td[d] = (s.tz[0] + s.tz[1]) + (s.tz[2] + s.tz[3])
    small_d = [copy_to(s.td.at[d], s.td.at[d], device) for m, device in mates]

    qkv_sum.finish()
    qkv_spread = spread(s.f_qkv, s.a_qkv)
    for copy in small_d:
        copy.wait_recv()
    value = (s.td[0] + s.td[1]) + (s.td[2] + s.td[3])
    dg_o[...] = value[:, :128]
    choose = row_id((WIDTH, 128)) == lane_id((WIDTH, 128)) + CHUNK * (GROUP * r + d)
    ng_o[...] = lax.dot_general(
        value,
        jnp.where(choose, 1.0, 0.0),
        (((1,), (0,)), ((), ())),
        preferred_element_type=F32,
        precision=lax.Precision.HIGHEST,
    )
    for copy in qkv_spread:
        copy.wait_recv()
    tiles = [t for k in range(GROUP) for t in tiles_of(s.a_qkv[k])]
    for t, tile in enumerate(permute_chunks(tiles, QKV_BACK)):
        gq_o[:, 128 * t : 128 * (t + 1)] = tile
    for copy in sent:
        copy.wait_send()


def fused(
    block_input,
    history,
    cotangent,
    token_mask,
    qkv_weight,
    out_weight,
    up_weight,
    down_weight,
    norm_params,
    depth_weights,
):
    cosine, sine = tables()
    vmem = pl.BlockSpec(memory_space=pltpu.VMEM)
    smem = pl.BlockSpec(memory_space=pltpu.SMEM)
    shape = jax.ShapeDtypeStruct
    outs = pl.pallas_call(
        fused_kernel,
        out_shape=(
            shape((OWN, WIDTH), BF),
            shape((OWN, WIDTH), BF),
            shape((SEQ, WIDTH), BF),
            shape((CHUNK, 3 * WIDTH), F32),
            shape((CHUNK, WIDTH), F32),
            shape((CHUNK, 4 * WIDTH), F32),
            shape((BLOCK, WIDTH), F32),
            shape((8, 128), F32),
            shape((8, 128), F32),
        ),
        in_specs=[vmem] * 9 + [smem] + [vmem] * 2,
        out_specs=[vmem] * 9,
        scratch_shapes=[pltpu.VMEM(dims, kind) for dims, kind in SCRATCH.values()]
        + [pltpu.SemaphoreType.DMA((N_SEMS,))] * 2,
        compiler_params=pltpu.CompilerParams(
            collective_id=0, has_side_effects=True, vmem_limit_bytes=62 * 2**20
        ),
        cost_estimate=pl.CostEstimate(flops=12 * 10**9, bytes_accessed=4 * 10**6, transcendentals=10**6),
    )(
        block_input,
        history.reshape(SEQ, WIDTH),
        cotangent,
        token_mask.reshape(1, OWN),
        qkv_weight,
        out_weight,
        up_weight,
        down_weight,
        norm_params,
        depth_weights,
        jnp.asarray(cosine),
        jnp.asarray(sine),
    )
    out, input_grad, history_grad, g_qkv, g_out, g_up, g_down, g_norm, g_depth = outs
    return (
        out,
        input_grad,
        history_grad.reshape(1, SEQ, WIDTH),
        g_qkv,
        g_out,
        g_up,
        g_down,
        g_norm[:4, :CHUNK],
        g_depth[4, : GROUP + 1],
    )


def fits(mesh, block_input, history, up_weight):
    devices = ROWS * GROUP
    return (
        mesh.shape["rows"] == ROWS
        and mesh.shape["depth"] == GROUP
        and block_input.shape == (OWN * devices, WIDTH)
        and history.shape[0] == GROUP
        and up_weight.shape == (WIDTH, 4 * WIDTH)
    )


def solution(mesh):
    weights = P(("rows", "depth"), None)
    in_specs = (
        weights,
        P("depth", "rows", None),
        weights,
        P(("rows", "depth")),
        weights,
        weights,
        weights,
        weights,
        P(None, ("rows", "depth")),
        P(),
    )
    out_specs = (
        weights,
        weights,
        P("depth", "rows", None),
        weights,
        weights,
        weights,
        weights,
        P(None, ("rows", "depth")),
        P(),
    )

    def run(*args):
        body = fused if fits(mesh, args[0], args[1], args[6]) else local
        return jax.shard_map(
            body, mesh=mesh, in_specs=in_specs, out_specs=out_specs, check_vma=False
        )(*args)

    return run
```

```python
import functools

import jax
import jax.numpy as jnp
import numpy as np
from jax import lax
from jax.experimental import pallas as pl
from jax.experimental.pallas import tpu as pltpu
from jax.sharding import PartitionSpec as P

HEADS = 12
HD = 64


def norm_rows(value, gain, shift):
    center = value - jnp.mean(value, axis=-1, keepdims=True)
    spread = jnp.mean(center * center, axis=-1, keepdims=True)
    return center * lax.rsqrt(spread + 1e-05) * (1.0 + gain) + shift


def rotate(value, place, sign):
    half = value.shape[-1] // 2
    freq = 10000.0 ** (-jnp.arange(half, dtype=jnp.float32) / half)
    angle = place.astype(jnp.float32)[:, None] * freq[None, :]
    cosine = jnp.cos(angle)[:, None, :]
    sine = jnp.sin(angle)[:, None, :] * sign
    first = value[..., :half]
    second = value[..., half:]
    return jnp.concatenate(
        [first * cosine - second * sine, second * cosine + first * sine], axis=-1
    )


def block_scores(query, key_block, start, query_place, scale):
    block_len = key_block.shape[0]
    scores = (
        jnp.einsum("qhd,khd->hqk", query, key_block, preferred_element_type=jnp.float32) * scale
    )
    key_place = start + jnp.arange(block_len, dtype=jnp.int32)
    allowed = query_place[:, None] >= key_place[None, :]
    return (scores, allowed)


def local(
    block_input,
    history,
    cotangent,
    token_mask,
    qkv_weight,
    out_weight,
    up_weight,
    down_weight,
    norm_params,
    depth_weights,
):
    rows_tok, width = block_input.shape
    depth_count = lax.axis_size("depth")
    device_count = lax.axis_size("rows") * depth_count
    place_depth = lax.axis_index("depth")
    heads = HEADS
    head_size = HD
    scale = head_size ** (-0.5)
    seq_len = rows_tok * depth_count
    slot_count = history.shape[0]
    hist_total = slot_count * depth_count
    wide_qkv, wide_out, wide_up, wide_down, wide_norms = (
        lax.all_gather(qkv_weight, ("rows", "depth"), axis=0, tiled=True),
        lax.all_gather(out_weight, ("rows", "depth"), axis=0, tiled=True),
        lax.all_gather(up_weight, ("rows", "depth"), axis=0, tiled=True),
        lax.all_gather(down_weight, ("rows", "depth"), axis=0, tiled=True),
        lax.all_gather(
            norm_params.astype(jnp.bfloat16), ("rows", "depth"), axis=1, tiled=True
        ).astype(norm_params.dtype),
    )
    total = lax.psum(jnp.sum(token_mask), ("rows", "depth")).astype(jnp.float32)
    loss_scale = rows_tok * device_count / total
    float_input = block_input.astype(jnp.float32)
    place = place_depth * rows_tok + jnp.arange(rows_tok, dtype=jnp.int32)
    first = norm_rows(float_input, wide_norms[0], wide_norms[1]).astype(jnp.bfloat16)
    projected = jnp.dot(first, wide_qkv, preferred_element_type=jnp.float32)
    query = rotate(projected[:, :width].reshape(rows_tok, heads, head_size), place, 1.0).astype(
        jnp.bfloat16
    )
    keys = rotate(projected[:, width : 2 * width].reshape(rows_tok, heads, head_size), place, 1.0)
    keys = keys.astype(jnp.bfloat16).reshape(rows_tok, width)
    values = projected[:, 2 * width :].astype(jnp.bfloat16)
    all_keys, all_values = (
        lax.all_gather(keys, "depth", axis=0, tiled=True),
        lax.all_gather(values, "depth", axis=0, tiled=True),
    )
    block_len = min(512, seq_len)
    block_count = seq_len // block_len
    key_blocks = all_keys.reshape(block_count, block_len, heads, head_size)
    value_blocks = all_values.reshape(block_count, block_len, heads, head_size)
    starts = jnp.arange(block_count, dtype=jnp.int32) * block_len

    def peak_step(carry, item):
        peak, weight_sum = carry
        key_block, value_block, start = item
        scores, allowed = block_scores(query, key_block, start, place, scale)
        scores = jnp.where(allowed[None], scores, -1e30)
        new_peak = jnp.maximum(peak, jnp.max(scores, axis=-1))
        weight_sum = weight_sum * jnp.exp(peak - new_peak) + jnp.sum(
            jnp.exp(scores - new_peak[..., None]), axis=-1
        )
        return ((new_peak, weight_sum), None)

    start_carry = (
        jnp.full((heads, rows_tok), -1e30, jnp.float32),
        jnp.zeros((heads, rows_tok), jnp.float32),
    )
    (peak, weight_sum), _ = lax.scan(peak_step, start_carry, (key_blocks, value_blocks, starts))
    log_total = peak + jnp.log(weight_sum)

    def value_step(running, item):
        key_block, value_block, start = item
        scores, allowed = block_scores(query, key_block, start, place, scale)
        probs = jnp.where(allowed[None], jnp.exp(scores - log_total[..., None]), 0.0)
        running = running + jnp.einsum(
            "hqk,khd->qhd",
            probs.astype(jnp.bfloat16),
            value_block,
            preferred_element_type=jnp.float32,
        )
        return (running, None)

    running, _ = lax.scan(
        value_step,
        jnp.zeros((rows_tok, heads, head_size), jnp.float32),
        (key_blocks, value_blocks, starts),
    )
    mixed = running.reshape(rows_tok, width)
    mixed_low = mixed.astype(jnp.bfloat16)
    middle = float_input + jnp.dot(mixed_low, wide_out, preferred_element_type=jnp.float32)
    second = norm_rows(middle, wide_norms[2], wide_norms[3]).astype(jnp.bfloat16)
    upper = jnp.dot(second, wide_up, preferred_element_type=jnp.float32)
    active = jax.nn.gelu(upper).astype(jnp.bfloat16)
    block_out = middle + jnp.dot(active, wide_down, preferred_element_type=jnp.float32)
    own_alpha = lax.dynamic_slice_in_dim(depth_weights, place_depth * slot_count, slot_count)
    partial_mix = jnp.sum(own_alpha[:, None, None] * history.astype(jnp.float32), axis=0)
    mixture = lax.psum_scatter(
        partial_mix.astype(jnp.bfloat16), "depth", scatter_dimension=0, tiled=True
    ).astype(jnp.float32)
    output = (mixture + depth_weights[hist_total] * block_out).astype(jnp.bfloat16)
    grad_out = token_mask.astype(jnp.float32)[:, None] * cotangent.astype(jnp.float32) * loss_scale
    last_term = jnp.sum(grad_out * block_out)
    index_all = jnp.arange(hist_total + 1, dtype=jnp.int32)
    grad_rows = lax.all_gather(grad_out.astype(jnp.bfloat16), "depth", axis=0, tiled=True).astype(
        grad_out.dtype
    )
    history_grad = (own_alpha[:, None, None] * grad_rows[None]).astype(jnp.bfloat16)
    hist_terms = jnp.sum(history.astype(jnp.float32) * grad_rows[None], axis=(1, 2))
    own_index = place_depth * slot_count + jnp.arange(slot_count, dtype=jnp.int32)
    alpha_terms = jnp.sum(
        jnp.where(index_all[None, :] == own_index[:, None], hist_terms[:, None], 0.0), axis=0
    )
    alpha_terms = alpha_terms + jnp.where(index_all == hist_total, last_term, 0.0)
    depth_gradient = lax.psum(alpha_terms, ("rows", "depth"))
    wide_qkv, wide_out, wide_up, wide_down, wide_norms = (
        lax.all_gather(qkv_weight, ("rows", "depth"), axis=0, tiled=True),
        lax.all_gather(out_weight, ("rows", "depth"), axis=0, tiled=True),
        lax.all_gather(up_weight, ("rows", "depth"), axis=0, tiled=True),
        lax.all_gather(down_weight, ("rows", "depth"), axis=0, tiled=True),
        lax.all_gather(
            norm_params.astype(jnp.bfloat16), ("rows", "depth"), axis=1, tiled=True
        ).astype(norm_params.dtype),
    )
    block_grad = depth_weights[hist_total] * grad_out
    lower_grad = block_grad.astype(jnp.bfloat16)
    down_gradient = jnp.dot(active.T, lower_grad, preferred_element_type=jnp.float32)
    active_grad = jnp.dot(lower_grad, wide_down.T, preferred_element_type=jnp.float32)
    _, gelu_pull = jax.vjp(jax.nn.gelu, upper)
    upper_grad = gelu_pull(active_grad)[0].astype(jnp.bfloat16)
    up_gradient = jnp.dot(second.T, upper_grad, preferred_element_type=jnp.float32)
    second_grad = jnp.dot(upper_grad, wide_up.T, preferred_element_type=jnp.float32)
    _, norm_pull = jax.vjp(norm_rows, middle, wide_norms[2], wide_norms[3])
    middle_part, gain_two, shift_two = norm_pull(second_grad)
    middle_grad = block_grad + middle_part
    branch_grad = middle_grad.astype(jnp.bfloat16)
    out_gradient = jnp.dot(mixed_low.T, branch_grad, preferred_element_type=jnp.float32)
    mixed_grad = jnp.dot(branch_grad, wide_out.T, preferred_element_type=jnp.float32).astype(
        jnp.bfloat16
    )
    delta = jnp.sum(
        (mixed_grad.astype(jnp.float32) * mixed).reshape(rows_tok, heads, head_size), axis=-1
    ).T
    mixed_heads = mixed_grad.reshape(rows_tok, heads, head_size)

    def score_grads(
        query_rows, grad_rows, lse_rows, delta_rows, key_block, value_block, query_place, start
    ):
        scores, allowed = block_scores(query_rows, key_block, start, query_place, scale)
        probs = jnp.where(allowed[None], jnp.exp(scores - lse_rows[..., None]), 0.0)
        prob_grad = jnp.einsum(
            "qhd,khd->hqk", grad_rows, value_block, preferred_element_type=jnp.float32
        )
        score_grad = (probs * (prob_grad - delta_rows[..., None])).astype(jnp.bfloat16)
        return (probs, score_grad)

    def grad_step(query_total, item):
        key_block, value_block, start = item
        probs, score_grad = score_grads(
            query, mixed_heads, log_total, delta, key_block, value_block, place, start
        )
        query_total = (
            query_total
            + jnp.einsum("hqk,khd->qhd", score_grad, key_block, preferred_element_type=jnp.float32)
            * scale
        )
        key_part = (
            jnp.einsum("hqk,qhd->khd", score_grad, query, preferred_element_type=jnp.float32)
            * scale
        )
        value_part = jnp.einsum(
            "hqk,qhd->khd",
            probs.astype(jnp.bfloat16),
            mixed_heads,
            preferred_element_type=jnp.float32,
        )
        return (query_total, (key_part, value_part))

    query_total, (key_parts, value_parts) = lax.scan(
        grad_step,
        jnp.zeros((rows_tok, heads, head_size), jnp.float32),
        (key_blocks, value_blocks, starts),
    )
    key_sum, value_sum = (
        lax.psum_scatter(
            key_parts.reshape(seq_len, width).astype(jnp.bfloat16),
            "depth",
            scatter_dimension=0,
            tiled=True,
        ).astype(jnp.float32),
        lax.psum_scatter(
            value_parts.reshape(seq_len, width).astype(jnp.bfloat16),
            "depth",
            scatter_dimension=0,
            tiled=True,
        ).astype(jnp.float32),
    )
    query_grad = rotate(query_total, place, -1.0).reshape(rows_tok, width)
    key_grad = rotate(key_sum.reshape(rows_tok, heads, head_size), place, -1.0).reshape(
        rows_tok, width
    )
    projected_grad = jnp.concatenate([query_grad, key_grad, value_sum], axis=1).astype(jnp.bfloat16)
    qkv_gradient = jnp.dot(first.T, projected_grad, preferred_element_type=jnp.float32)
    first_grad = jnp.dot(projected_grad, wide_qkv.T, preferred_element_type=jnp.float32)
    _, first_pull = jax.vjp(norm_rows, float_input, wide_norms[0], wide_norms[1])
    input_part, gain_one, shift_one = first_pull(first_grad)
    input_grad = (middle_grad + input_part).astype(jnp.bfloat16)
    norms_full = jnp.stack([gain_one, shift_one, gain_two, shift_two])
    qkv_gradient, out_gradient, up_gradient, down_gradient, norm_gradient = (
        lax.psum_scatter(qkv_gradient, ("rows", "depth"), scatter_dimension=0, tiled=True),
        lax.psum_scatter(out_gradient, ("rows", "depth"), scatter_dimension=0, tiled=True),
        lax.psum_scatter(up_gradient, ("rows", "depth"), scatter_dimension=0, tiled=True),
        lax.psum_scatter(down_gradient, ("rows", "depth"), scatter_dimension=0, tiled=True),
        lax.psum_scatter(norms_full, ("rows", "depth"), scatter_dimension=1, tiled=True),
    )
    return (
        output,
        input_grad,
        history_grad,
        qkv_gradient,
        out_gradient,
        up_gradient,
        down_gradient,
        norm_gradient,
        depth_gradient,
    )

SEQ = 512
OWN = 128
WIDTH = 768
ROWS = 8
GROUP = 4
PACK = 640
BLOCK = WIDTH // ROWS
CHUNK = BLOCK // GROUP
QBLOCK = 256
BF = jnp.bfloat16
F32 = jnp.float32
MESH = pl.DeviceIdType.MESH


def dot(a, b, ca=1, cb=0):
    return lax.dot_general(a, b, (((ca,), (cb,)), ((), ())), preferred_element_type=F32)


def lane_id(shape):
    return lax.broadcasted_iota(jnp.int32, shape, len(shape) - 1)


def row_id(shape):
    return lax.broadcasted_iota(jnp.int32, shape, len(shape) - 2)


def tiles_of(value):
    return [value[:, 128 * i : 128 * (i + 1)] for i in range(value.shape[1] // 128)]


def permute_chunks(tiles, picks):
    group = lax.div(lane_id(tiles[0].shape), jnp.int32(32))
    out = []
    for t in range(len(picks) // 4):
        total, rolled = jnp.zeros_like(tiles[0]), {}
        for j in range(4):
            pick = picks[4 * t + j]
            if pick is None:
                continue
            source, place = divmod(pick, 4)
            shift = (j - place) * 32 % 128
            if (source, shift) not in rolled:
                value = tiles[source]
                rolled[source, shift] = pltpu.roll(value, shift, 1) if shift else value
            total = jnp.where(group == j, rolled[source, shift], total)
        out.append(total)
    return out


def fold(tiles):
    half = (len(tiles) + 1) // 2
    low = [t[16:] for t in tiles]
    if len(low) % 2:
        low.append(jnp.zeros_like(low[0]))
    return [t[:16] for t in tiles] + [
        jnp.concatenate([low[i], low[half + i]], axis=0) for i in range(half)
    ]


def unfold(tiles, count):
    half = (count + 1) // 2
    rest = tiles[count:]
    low = [rest[i][:8] for i in range(half)] + [rest[i][8:] for i in range(half)]
    return [jnp.concatenate([tiles[i], low[i]], axis=0) for i in range(count)]


def qkv_chunk(block, head, half):
    return 24 * block + 2 * head + half


def qkv_picks(d):
    heads = [3 * d + i for i in range(3)]
    picks = []
    for block in range(2):
        for half in range(2):
            picks += [qkv_chunk(block, h, half) for h in heads]
            picks.append(qkv_chunk(2, heads[2], half) if block == 0 else None)
    return picks + [qkv_chunk(2, h, half) for h in heads[:2] for half in range(2)]


def up_picks(d):
    return [3 * (GROUP * r + d) + j for r in range(ROWS) for j in range(3)]


def inverse_picks(per_device, count, tiles_each):
    back = [None] * count
    for d, picks in enumerate(per_device):
        for place, pick in enumerate(picks):
            if pick is not None:
                back[pick] = 4 * tiles_each * d + place
    return back


QKV_BACK = inverse_picks([qkv_picks(d) for d in range(GROUP)], 72, 5)
UP_BACK = inverse_picks([up_picks(d) for d in range(GROUP)], 96, 6)


def tables():
    half = HD // 2
    freq = np.float32(10000.0) ** (-np.arange(half, dtype=np.float32) / np.float32(half))
    angle = (np.arange(SEQ, dtype=np.float32)[:, None] * freq[None, :]).astype(np.float32)
    angle = angle.astype(np.float64)
    cosine, sine = np.ones((SEQ, 128), np.float32), np.zeros((SEQ, 128), np.float32)
    cosine[:, :96] = np.tile(np.cos(angle), (1, 3))
    sine[:, :96] = np.tile(np.sin(angle), (1, 3))
    return cosine, sine


def standardize(value):
    center = value - jnp.mean(value, axis=-1, keepdims=True)
    spread = jnp.mean(center * center, axis=-1, keepdims=True)
    scale = lax.rsqrt(spread + 1e-05)
    return center * scale, scale


def norm_back(grad, gain, normal, scale):
    part = grad * (1.0 + gain)
    inner = jnp.mean(part, axis=-1, keepdims=True)
    along = jnp.mean(part * normal, axis=-1, keepdims=True)
    return scale * (part - inner - normal * along)


def sublane_sum(value):
    return jnp.sum(value.reshape(value.shape[0] // 8, 8, value.shape[1]), axis=0)


SCRATCH = dict(
    x_all=((GROUP, OWN, WIDTH), BF),
    c_all=((GROUP, OWN, WIDTH), BF),
    qp_s=((GROUP, 16, 1024), BF),
    qp_l=((GROUP, 16, 1024), BF),
    up_s=((GROUP, 16, 1152), BF),
    up_l=((GROUP, 16, 1152), BF),
    tmp=((BLOCK, WIDTH), F32),
    w_qkv=((WIDTH, PACK), BF),
    w_up=((WIDTH, WIDTH), BF),
    w_down=((WIDTH, WIDTH), BF),
    wo_l=((GROUP, ROWS, 16, 1152), BF),
    w_out=((WIDTH, WIDTH), BF),
    w_own=((384, WIDTH), BF),
    norms=((8, WIDTH), F32),
    normal=((SEQ, WIDTH), F32),
    h1=((SEQ, WIDTH), BF),
    qv=((SEQ, 256), BF),
    kk=((SEQ, 256), BF),
    v01=((SEQ, 128), BF),
    probs=((3, SEQ, SEQ), F32),
    o_l=((GROUP, 2, 384, 128), BF),
    ob=((SEQ, WIDTH), BF),
    y=((SEQ, WIDTH), F32),
    h2=((SEQ, WIDTH), BF),
    slope=((SEQ, WIDTH), F32),
    act=((SEQ, WIDTH), BF),
    dm=((SEQ, WIDTH), BF),
    g_down=((WIDTH, WIDTH), F32),
    g_up=((WIDTH, WIDTH), F32),
    g_out=((WIDTH, WIDTH), F32),
    g_qkv=((WIDTH, PACK), F32),
    du=((SEQ, WIDTH), BF),
    part=((SEQ, WIDTH), F32),
    part2=((SEQ, WIDTH), F32),
    dy=((OWN, WIDTH), F32),
    dyb=((GROUP, OWN, WIDTH), BF),
    dob=((SEQ, 384), BF),
    dq=((SEQ, 256), F32),
    dk=((SEQ, 256), F32),
    dv=((SEQ, 384), F32),
    dqkv=((SEQ, PACK), BF),
    terms=((8, WIDTH), F32),
    terms2=((8, WIDTH), F32),
    t0=((8, WIDTH), F32),
    t1=((8, WIDTH), F32),
    tz=((4, 8, WIDTH), F32),
    td=((4, 8, WIDTH), F32),
    a_qkv=((GROUP, 16, 1024), BF),
    a_up=((GROUP, 16, 1152), BF),
    b_qkv=((GROUP, 16, 1024), BF),
    b_up=((GROUP, 16, 1152), BF),
    gain_sum=((8, WIDTH), F32),
    shift_sum=((8, WIDTH), F32),
)
for _name, _rows, _cols in (
    ("down", BLOCK, WIDTH),
    ("up", BLOCK, WIDTH),
    ("out", 16, 1152),
    ("qkv", BLOCK, PACK),
):
    SCRATCH["xs_" + _name] = ((4, _rows, _cols), BF)
    SCRATCH["xl_" + _name] = ((4, _rows, _cols), BF)
    SCRATCH["zs_" + _name] = ((2, _rows, _cols), BF)
    SCRATCH["zl_" + _name] = ((3, _rows, _cols), BF)
    SCRATCH["ns_" + _name] = ((2, _rows, _cols), BF)
    SCRATCH["nl_" + _name] = ((2, _rows, _cols), BF)
    SCRATCH["f_" + _name] = ((_rows, _cols), F32)
for _name in ("mix", "mid", "in"):
    SCRATCH["s1_" + _name] = ((2, OWN, WIDTH), BF)
    SCRATCH["l1_" + _name] = ((2, OWN, WIDTH), BF)
    SCRATCH["s2_" + _name] = ((OWN, WIDTH), BF)
    SCRATCH["l2_" + _name] = ((OWN, WIDTH), BF)
N_SEMS = 160
N_IN = 12
N_OUT = 9
VMEM_MIB = 60


class Names:
    pass


def fused_kernel(*refs):
    (x_in, hist, cot, mask, wq, wo, wu, wd, nrm, dw, cosine, sine) = refs[:N_IN]
    (out_o, ig_o, hg_o, gq_o, go_o, gu_o, gd_o, ng_o, dg_o) = refs[N_IN : N_IN + N_OUT]
    s = Names()
    for name, ref in zip(SCRATCH, refs[N_IN + N_OUT :]):
        setattr(s, name, ref)
    send_sems, recv_sems = refs[-2:]

    r, d = lax.axis_index("rows"), lax.axis_index("depth")
    z, x = lax.div(r, 2), lax.rem(r, 2)
    yy, c = lax.div(d, 2), lax.rem(d, 2)
    other_x, other_c, other_y = 1 - x, 1 - c, 1 - yy
    x_dev = (2 * z + other_x, d)
    z_two, z_mirror, z_near = lax.rem(z + 2, 4), 3 - z, z + 1 - 2 * lax.rem(z, 2)
    two_dev, mirror_dev, near_dev = ((2 * zk + x, d) for zk in (z_two, z_mirror, z_near))
    inside = lax.rem(z + 1, 4) >= 2
    core_d, y_d, far_d = 2 * yy + other_c, 2 * other_y + c, 2 * other_y + other_c
    core_dev, y_dev, far_dev = (r, core_d), (r, y_d), (r, far_d)
    mates = ((core_d, core_dev), (y_d, y_dev), (far_d, far_dev))
    counter = [0]
    sent = []
    sent_inside = []
    sent_outside = []

    def prepare(src, dst, device, arrival=None):
        index = counter[0]
        counter[0] += 1
        copy = pltpu.make_async_remote_copy(
            src_ref=src,
            dst_ref=dst,
            send_sem=send_sems.at[index],
            recv_sem=recv_sems.at[index if arrival is None else arrival],
            device_id=device,
            device_id_type=MESH,
        )
        return copy, index

    def copy_to(src, dst, device):
        copy, _ = prepare(src, dst, device)
        copy.start()
        sent.append(copy)
        return copy

    def rows_at(ref, index, size):
        return ref.at[pl.ds(pl.multiple_of(index * size, size), size)]

    def by_rows(count, step, body):
        def one(i, carry):
            body(pl.ds(pl.multiple_of(i * step, step), step))
            return carry

        lax.fori_loop(0, count // step, one, 0)

    barrier = pltpu.get_barrier_semaphore()
    for device in (x_dev, two_dev, mirror_dev, near_dev, core_dev, y_dev, far_dev):
        pl.semaphore_signal(barrier, inc=1, device_id=device, device_id_type=MESH)
    pl.semaphore_wait(barrier, 7)

    class Gather:
        def __init__(self, piece, cross=False):
            self.piece, self.cross = piece, cross
            self.along_x = []

        def send_two(self):
            mine = self.piece(r)
            self.two = copy_to(mine, mine, two_dev)

        def send_mirror(self):
            mine, passed = self.piece(r), self.piece(2 * z_two + x)
            self.mirror, index = prepare(mine, mine, mirror_dev)
            self.passing, _ = prepare(passed, passed, near_dev, index)
            sent_inside.extend([self.mirror, self.passing])
            pl.when(inside)(self.mirror.start)

        def send_near(self, where=None):
            if where is not False:
                mine = self.piece(r)
                self.near, _ = prepare(mine, mine, near_dev)
                sent.append(self.near)
            if where is None:
                self.near.start()
            else:
                pl.when(jnp.logical_not(inside) if where else inside)(self.near.start)

        def send_x(self, index=r):
            piece = self.piece(index)
            self.along_x.append(copy_to(piece, piece, x_dev))

        def forward_near(self):
            self.near.wait_recv()
            if not self.cross:
                self.send_x(2 * z_near + x)

        def forward_cross(self):
            self.along_x[0].wait_recv()
            piece = self.piece(2 * z + other_x)
            self.along_x[0] = copy_to(piece, piece, near_dev)

        def forward_two(self):
            self.two.wait_recv()
            pl.when(inside)(self.passing.start)
            self.send_x(2 * z_two + x)

        def forward_mirror(self):
            self.mirror.wait_recv()
            self.send_x(2 * z_mirror + x)

        def finish(self):
            for copy in self.along_x:
                copy.wait_recv()

    class GroupGather:
        def __init__(self, slab):
            self.slab = slab

        def send(self):
            mine = self.slab(d)
            self.to_core = copy_to(mine, mine, core_dev)
            self.to_y = copy_to(mine, mine, y_dev)

        def relay(self):
            self.to_y.wait_recv()
            slab = self.slab(y_d)
            self.on = copy_to(slab, slab, core_dev)

        def finish(self):
            self.to_core.wait_recv()
            self.on.wait_recv()

    class RowSum:
        def __init__(self, name, block, step, cross):
            self.xs, self.xl, self.zs, self.zl, self.ns, self.nl, self.total = (
                getattr(s, p + name) for p in ("xs_", "xl_", "zs_", "zl_", "ns_", "nl_", "f_")
            )
            self.block, self.step, self.cross = block, step, cross
            self.count = self.total.shape[0]
            self.along_x = {}

        def stage(self, target, index, *extras):
            def one(at):
                value = self.block(index, at)
                for ref in extras:
                    value = value + ref[at, :].astype(F32)
                target[at, :] = value.astype(BF)

            by_rows(self.count, self.step, one)

        def send_x(self, name, zk, *extras):
            self.stage(self.xs.at[zk], 2 * zk + other_x, *extras)
            self.along_x[name] = copy_to(self.xs.at[zk], self.xl.at[zk], x_dev)

        def send(self):
            self.send_x("mirror", z_mirror)
            if self.cross:
                self.stage(self.ns.at[0], 2 * z_near + other_x)
                self.crossing = copy_to(self.ns.at[0], self.nl.at[0], near_dev)
            self.send_x("two", z_two)
            if self.cross:
                self.stage(self.ns.at[1], 2 * z_near + x)
                self.near = copy_to(self.ns.at[1], self.nl.at[1], near_dev)
            else:
                self.send_x("near", z_near)
                self.send_x("own", z)

        def send_own(self):
            self.crossing.wait_recv()
            self.send_x("own", z, self.nl.at[0])

        def send_mirror(self):
            self.along_x["mirror"].wait_recv()
            self.stage(self.zs.at[0], 2 * z_mirror + x, self.xl.at[z_mirror])
            self.mirror, _ = prepare(self.zs.at[0], self.zl.at[0], mirror_dev)
            self.passing, _ = prepare(self.zs.at[0], self.zl.at[2], near_dev)
            sent_inside.append(self.mirror)
            sent_outside.append(self.passing)
            pl.when(inside)(self.mirror.start)
            pl.when(jnp.logical_not(inside))(self.passing.start)

        def send_two(self):
            self.along_x["two"].wait_recv()

            @pl.when(inside)
            def _():
                self.passing.wait_recv()
                self.stage(self.zs.at[1], 2 * z_two + x, self.xl.at[z_two], self.zl.at[2])

            @pl.when(jnp.logical_not(inside))
            def _():
                self.stage(self.zs.at[1], 2 * z_two + x, self.xl.at[z_two])

            self.two = copy_to(self.zs.at[1], self.zl.at[1], two_dev)

        def send_near(self):
            self.along_x["near"].wait_recv()
            self.stage(self.ns.at[1], 2 * z_near + x, self.xl.at[z_near])
            self.near = copy_to(self.ns.at[1], self.nl.at[1], near_dev)

        def finish(self):
            self.along_x["own"].wait_recv()
            self.two.wait_recv()
            self.near.wait_recv()

            def add(at):
                self.total[at, :] = (
                    self.block(r, at)
                    + self.xl[z, at, :].astype(F32)
                    + self.zl[1, at, :].astype(F32)
                    + self.nl[1, at, :].astype(F32)
                )

            by_rows(self.count, self.step, add)

            @pl.when(inside)
            def _():
                self.mirror.wait_recv()

                def add_mirror(at):
                    self.total[at, :] += self.zl[0, at, :].astype(F32)

                by_rows(self.count, self.step, add_mirror)

    class GroupSum:
        def __init__(self, name, source):
            self.s1, self.l1, self.s2, self.l2 = (
                getattr(s, p + name) for p in ("s1_", "l1_", "s2_", "l2_")
            )
            self.source = source

        def block(self, index, at):
            return self.source[pl.ds(pl.multiple_of(index * OWN + at.start, at.size), at.size), :]

        def send(self):
            self.first = []
            for j, yj in enumerate((other_y, yy)):

                def stage(at):
                    self.s1[j, at, :] = self.block(2 * yj + other_c, at).astype(BF)

                by_rows(OWN, 32, stage)
                self.first.append(copy_to(self.s1.at[j], self.l1.at[j], core_dev))

        def middle(self):
            self.first[0].wait_recv()

            def stage(at):
                value = self.block(2 * other_y + c, at) + self.l1[0, at, :].astype(F32)
                self.s2[at, :] = value.astype(BF)

            by_rows(OWN, 32, stage)
            self.second = copy_to(self.s2, self.l2, y_dev)

        def wait(self):
            self.first[1].wait_recv()
            self.second.wait_recv()

        def value(self, at):
            return (
                self.block(d, at)
                + self.l1[1, at, :].astype(F32)
                + self.l2[at, :].astype(F32)
            )

    out_gather = Gather(lambda i: s.wo_l.at[d, i])
    for t, tile in enumerate(fold(tiles_of(wo[...].astype(F32)))):
        s.wo_l[d, r, :, 128 * t : 128 * (t + 1)] = tile.astype(BF)
    out_gather.send_two()
    out_gather.send_mirror()
    out_gather.send_near()
    out_gather.send_x()

    lane = lane_id((CHUNK, 128))
    eye = row_id((CHUNK, CHUNK)) == lane_id((CHUNK, CHUNK))
    extra = jnp.zeros((CHUNK, 128), F32)
    for k in range(4):
        column = jnp.sum(jnp.where(eye, nrm[k : k + 1, :], 0.0), axis=1, keepdims=True)
        high = column.astype(BF).astype(F32)
        extra = jnp.where(lane == 96 + k, high, extra)
        extra = jnp.where(lane == 100 + k, column - high, extra)
    mask_row = mask[...].astype(F32)
    ones = jnp.sum(mask_row, axis=1, keepdims=True)
    extra = jnp.where((lane == 104) & (row_id((CHUNK, 128)) == 0), ones, extra)

    wq_tiles = tiles_of(wq[...].astype(F32))
    for k in range(GROUP):
        tiles = permute_chunks(wq_tiles, qkv_picks(k))
        tiles[2] = tiles[2] + extra
        for t, tile in enumerate(fold(tiles)):
            s.qp_s[k, :, 128 * t : 128 * (t + 1)] = tile.astype(BF)
    qp_copies = [copy_to(s.qp_s.at[m], s.qp_l.at[d], device) for m, device in mates]
    s.qp_l[d] = s.qp_s[d]

    wu_tiles = tiles_of(wu[...].astype(F32))
    for k in range(GROUP):
        for t, tile in enumerate(fold(permute_chunks(wu_tiles, up_picks(k)))):
            s.up_s[k, :, 128 * t : 128 * (t + 1)] = tile.astype(BF)
    up_copies = [copy_to(s.up_s.at[m], s.up_l.at[d], device) for m, device in mates]
    s.up_l[d] = s.up_s[d]

    rows_at(s.w_down, r, BLOCK)[...] = wd[...]
    downs = [
        Gather(lambda i, h=h: rows_at(s.w_down, 2 * i + h, BLOCK // 2), cross=True) for h in range(2)
    ]
    downs[0].send_two()
    downs[0].send_near(True)
    for half in downs:
        half.send_x()

    s.x_all[d] = x_in[...]
    x_gather = GroupGather(lambda i: s.x_all.at[i])
    x_gather.send()

    diagonal = jnp.where(
        row_id((OWN, OWN)) == lane_id((OWN, OWN)), jnp.broadcast_to(mask_row, (OWN, OWN)), 0.0
    )
    s.c_all[d] = dot(diagonal.astype(BF), cot[...]).astype(BF)
    c_gather = GroupGather(lambda i: s.c_all.at[i])
    c_gather.send()

    def assemble(landing, count, target):
        for k in range(GROUP):
            tiles = [t.astype(F32) for t in tiles_of(landing[k])]
            for t, tile in enumerate(unfold(tiles, count)):
                s.tmp[CHUNK * k : CHUNK * (k + 1), 128 * t : 128 * (t + 1)] = tile
        rows_at(target, r, BLOCK)[...] = s.tmp[:, : 128 * count].astype(BF)

    for copy in qp_copies:
        copy.wait_recv()
    assemble(s.qp_l, 5, s.w_qkv)
    halves = [Gather(lambda i, h=h: rows_at(s.w_qkv, 2 * i + h, BLOCK // 2)) for h in range(2)]
    for half in halves:
        half.send_two()
    for half in halves:
        half.send_near()
        half.send_x()
    for half in halves:
        half.send_mirror()
    out_gather.forward_two()
    out_gather.forward_near()
    for copy in up_copies:
        copy.wait_recv()
    assemble(s.up_l, 6, s.w_up)
    up_gather = Gather(lambda i: rows_at(s.w_up, i, BLOCK))
    up_gather.send_two()
    up_gather.send_near(True)
    up_gather.send_x()
    x_gather.relay()
    halves[0].forward_near()
    halves[0].forward_two()
    out_gather.forward_mirror()
    halves[1].forward_near()
    x_gather.finish()

    def normalize(i):
        def one(at):
            normal, _ = standardize(s.x_all[i, at, :].astype(F32))
            s.normal[pl.ds(pl.multiple_of(OWN * i + at.start, at.size), at.size), :] = normal

        by_rows(OWN, 64, one)

    normalize(0)
    halves[1].forward_two()
    up_gather.send_near(False)
    up_gather.send_mirror()
    downs[1].send_two()
    downs[1].send_near(True)
    normalize(1)
    halves[0].forward_mirror()
    normalize(2)
    normalize(3)
    out_gather.finish()
    slab_gather = GroupGather(lambda i: s.wo_l.at[i])
    slab_gather.send()
    halves[1].forward_mirror()
    c_gather.relay()
    for half in halves:
        half.finish()

    lane = lane_id((8, 128))
    row = row_id((8, 128))
    pick = jnp.where((lane == 96 + row) | (lane == 100 + row), 1.0, 0.0)
    pick = jnp.where(row < 4, pick, jnp.where((row == 4) & (lane == 104), 1.0, 0.0))
    s.norms[...] = dot(pick.astype(BF), s.w_qkv[:, 256:384], 1, 1)
    total = jnp.sum(s.norms[4:5, :], axis=1, keepdims=True)
    loss_scale = (SEQ * ROWS) / total
    own_weight = dw[d]
    last_weight = dw[GROUP]

    def first_norm(at):
        value = s.normal[at, :] * (1.0 + s.norms[0:1, :]) + s.norms[1:2, :]
        s.h1[at, :] = value.astype(BF)

    by_rows(SEQ, 64, first_norm)

    def project(at):
        value = dot(s.h1[at, :], s.w_qkv[...])
        co, si = cosine[at, :], sine[at, :]
        for left, target in ((0, s.qv), (256, s.kk)):
            a, b = value[:, left : left + 128], value[:, left + 128 : left + 256]
            target[at, :128] = (a * co - b * si).astype(BF)
            target[at, 128:] = (b * co + a * si).astype(BF)
        s.v01[at, :] = value[:, 512:].astype(BF)

    up_gather.forward_near()
    by_rows(SEQ, 256, project)

    lane2 = lax.div(lax.rem(lane_id((1, 256)), 128), jnp.int32(32))
    head_mask = [jnp.where(lane2 == h, 1.0, 0.0).astype(BF) for h in range(3)]
    tail_mask = jnp.where(lane2 == 3, 1.0, 0.0).astype(BF)
    half_id = lax.div(lane_id((1, 128)), jnp.int32(64))
    half_mask = [jnp.where(half_id == h, 1.0, 0.0).astype(BF) for h in range(2)]
    root = HD**-0.5
    o_gathers = [GroupGather(lambda i, b=b: s.o_l.at[i, b]) for b in range(2)]

    def attend(b):
        rows = slice(QBLOCK * b, QBLOCK * (b + 1))
        keys = QBLOCK * (b + 1)
        query = s.qv[rows, :]
        allowed = row_id((QBLOCK, keys)) + QBLOCK * b >= lane_id((QBLOCK, keys))
        first = jnp.zeros((QBLOCK, 128), F32)
        third = None
        for h in range(3):
            scores = dot(query * head_mask[h], s.kk[:keys, :], 1, 1) * root
            scores = jnp.where(allowed, scores, -1e30)
            raised = jnp.exp(scores - jnp.max(scores, axis=1, keepdims=True))
            probs = raised * (1.0 / jnp.sum(raised, axis=1, keepdims=True))
            s.probs[h, rows, :keys] = probs
            if h < 2:
                first = first + dot(probs.astype(BF), s.v01[:keys, :] * half_mask[h])
            else:
                third = dot(probs.astype(BF), s.qv[:keys, :])
            if b == 1 and h == 0:
                up_gather.forward_two()
                for half in downs:
                    half.send_near(False)
                    half.send_mirror()
            if b == 1 and h == 1:
                downs[0].forward_two()
        s.o_l[d, b, :QBLOCK, :] = first.astype(BF)
        lane = lane_id((QBLOCK, 128))
        third = jnp.where(
            lane < 32, pltpu.roll(third[:, :128], 32, 1), pltpu.roll(third[:, 128:], 64, 1)
        )
        lane = lane_id((OWN, 128))
        third = jnp.where(lane < 64, third[:OWN], pltpu.roll(third[OWN:], 64, 1))
        s.o_l[d, b, QBLOCK:, :] = third.astype(BF)
        o_gathers[b].send()

    attend(1)
    slab_gather.relay()
    attend(0)
    for half in downs:
        half.forward_cross()
    up_gather.forward_mirror()
    slab_gather.finish()
    for k in range(GROUP):
        for i in range(ROWS):
            tiles = [t.astype(F32) for t in tiles_of(s.wo_l[k, i])]
            at = CHUNK * (GROUP * i + k)
            for t, tile in enumerate(unfold(tiles, 6)):
                s.g_out[at : at + CHUNK, 128 * t : 128 * (t + 1)] = tile

    def out_place(head):
        k, h = divmod(head, 3)
        return 128 * k + 64 * h if h < 2 else 512 + 64 * k

    for head in range(HEADS):
        at = out_place(head)
        s.w_out[at : at + 64, :] = s.g_out[64 * head : 64 * head + 64, :].astype(BF)
    s.w_own[...] = jnp.zeros((384, WIDTH), BF)
    third_rows = rows_at(s.w_out.at[pl.ds(512, 256)], d, 64)
    s.w_own[96:128, :] = third_rows[:32, :]
    s.w_own[224:256, :] = third_rows[32:, :]
    s.w_own[256:, :] = rows_at(s.w_out.at[pl.ds(0, 512)], d, 128)[...]
    o_gathers[1].relay()
    c_gather.finish()

    s.terms[...] = jnp.zeros((8, WIDTH), F32)
    for i in range(GROUP):

        def loss_rows(at, i=i):
            here = pl.ds(pl.multiple_of(OWN * i + at.start, at.size), at.size)
            grad = s.c_all[i, at, :].astype(F32) * loss_scale
            s.dm[here, :] = (last_weight * grad).astype(BF)
            hg_o[here, :] = (own_weight * grad).astype(BF)
            s.terms[...] += sublane_sum(grad * hist[here, :].astype(F32))

        by_rows(OWN, 32, loss_rows)

    downs[1].forward_two()
    for b in (1, 0):
        if b == 0:
            o_gathers[0].relay()
            downs[0].forward_mirror()
        o_gathers[b].finish()
        rows = slice(QBLOCK * b, QBLOCK * (b + 1))
        thirds = []
        for k in range(GROUP):
            s.ob[rows, 128 * k : 128 * (k + 1)] = s.o_l[k, b, :QBLOCK, :]
            thirds.append(s.o_l[k, b, QBLOCK:, :].astype(F32))
        lane = lane_id((OWN, 128))
        for p in range(2):
            even, odd = thirds[2 * p], thirds[2 * p + 1]
            top = jnp.where(lane < 64, even, pltpu.roll(odd, 64, 1))
            low = jnp.where(lane < 64, pltpu.roll(even, 64, 1), odd)
            cols = slice(512 + 128 * p, 640 + 128 * p)
            s.ob[QBLOCK * b : QBLOCK * b + OWN, cols] = top.astype(BF)
            s.ob[QBLOCK * b + OWN : QBLOCK * (b + 1), cols] = low.astype(BF)
        s.y[rows, :] = dot(s.ob[rows, :], s.w_out[...])
        for i in (2 * b, 2 * b + 1):

            def second_norm(at, i=i):
                here = pl.ds(pl.multiple_of(OWN * i + at.start, at.size), at.size)
                value = s.y[here, :] + s.x_all[i, at, :].astype(F32)
                s.y[here, :] = value
                normal, _ = standardize(value)
                value = normal * (1.0 + s.norms[2:3, :]) + s.norms[3:4, :]
                s.h2[here, :] = value.astype(BF)

            by_rows(OWN, 64, second_norm)

    up_gather.finish()

    def widen(at):
        s.part[at, :] = dot(s.h2[at, :], s.w_up[...])

    by_rows(SEQ, 256, widen)

    rate = 0.7978845608028654

    def gate(at):
        u = s.part[at, :]
        bend = jnp.tanh(rate * (u + 0.044715 * u * u * u))
        s.act[at, :] = (0.5 * u * (1.0 + bend)).astype(BF)
        s.slope[at, :] = bend

    by_rows(SEQ, 32, gate)
    downs[1].forward_mirror()

    def gate_slope(at):
        u, bend = s.part[at, :], s.slope[at, :]
        inner = rate * (1.0 + 3 * 0.044715 * u * u)
        s.slope[at, :] = 0.5 * (1.0 + bend) + 0.5 * u * (1.0 - bend * bend) * inner

    def block_of(ref):
        def block(index, at):
            return ref[pl.ds(pl.multiple_of(index * BLOCK + at.start, at.size), at.size), :]

        return block

    for i in range(3):
        cols = slice(QBLOCK * i, QBLOCK * (i + 1))
        s.g_down[cols, :] = dot(s.act[:, cols], s.dm[...], 0, 0)
    down_sum = RowSum("down", block_of(s.g_down), 16, True)
    down_sum.send()
    by_rows(SEQ, 32, gate_slope)
    for half in downs:
        half.forward_near()
        half.finish()

    def narrow(at):
        value = dot(s.dm[at, :], s.w_down[...], 1, 1)
        s.du[at, :] = (value * s.slope[at, :]).astype(BF)

    by_rows(SEQ, 256, narrow)

    def second_back(at):
        s.part[at, :] = dot(s.du[at, :], s.w_up[...], 1, 1)

    by_rows(SEQ, 256, second_back)
    mid_sum = GroupSum("mid", s.part)
    mid_sum.send()

    for i in range(3):
        cols = slice(QBLOCK * i, QBLOCK * (i + 1))
        s.g_up[cols, :] = dot(s.h2[:, cols], s.du[...], 0, 0)
    up_sum = RowSum("up", block_of(s.g_up), 16, True)
    mid_sum.middle()
    up_sum.send()
    down_sum.send_own()

    def block_out(at):
        value = dot(s.act[at, :], s.w_down[...])
        s.part2[at, :] = value

    s.terms2[...] = jnp.zeros((8, WIDTH), F32)
    by_rows(SEQ, 256, block_out)
    for i in range(GROUP):

        def mix(at, i=i):
            here = pl.ds(pl.multiple_of(OWN * i + at.start, at.size), at.size)
            value = s.part2[here, :]
            loss = s.c_all[i, at, :].astype(F32) * loss_scale
            s.terms2[...] += sublane_sum(loss * value)
            s.part2[here, :] = own_weight * hist[here, :].astype(F32) + last_weight * value

        by_rows(OWN, 32, mix)
    mix_sum = GroupSum("mix", s.part2)
    mix_sum.send()
    mid_sum.wait()

    s.t0[...] = jnp.zeros((8, WIDTH), F32)

    def second_norm_back(at):
        here = pl.ds(pl.multiple_of(OWN * d + at.start, at.size), at.size)
        grad = mid_sum.value(at)
        value = s.y[here, :]
        normal, scale = standardize(value)
        loss = s.c_all[d, at, :].astype(F32) * loss_scale
        back = last_weight * loss + norm_back(grad, s.norms[2:3, :], normal, scale)
        s.dy[at, :] = back
        s.dyb[d, at, :] = back.astype(BF)
        s.t0[2:3, :] += jnp.sum(grad * normal, axis=0, keepdims=True)
        s.t0[3:4, :] += jnp.sum(grad, axis=0, keepdims=True)
        s.terms2[...] += sublane_sum(loss * value)

    by_rows(OWN, 32, second_norm_back)
    dy_gather = GroupGather(lambda i: s.dyb.at[i])
    dy_gather.send()

    mix_sum.middle()
    down_sum.send_mirror()
    up_sum.send_own()
    dy_gather.relay()
    down_sum.send_two()
    dy_gather.finish()

    by_group = s.dyb[...].reshape(SEQ, WIDTH)

    s.dob[...] = dot(by_group, s.w_own[...], 1, 1).astype(BF)
    for p in range(3):
        cols = slice(QBLOCK * p, QBLOCK * (p + 1))
        value = dot(s.ob[:, cols], by_group, 0, 0)
        for i in range(4):
            place = QBLOCK * p + 64 * i
            for head in range(HEADS):
                if out_place(head) == place:
                    s.g_out[64 * head : 64 * head + 64, :] = value[64 * i : 64 * i + 64]

    def out_block(index, at):
        start = pl.multiple_of((GROUP * index + d) * CHUNK, 8)
        tiles = tiles_of(s.g_out[pl.ds(start, CHUNK), :])
        return jnp.concatenate(fold(tiles), axis=1)

    out_sum = RowSum("out", out_block, 16, False)
    out_sum.send()
    mix_sum.wait()

    def write_out(at):
        here = pl.ds(pl.multiple_of(OWN * d + at.start, at.size), at.size)
        out_o[at, :] = (mix_sum.value(at) + last_weight * s.y[here, :]).astype(BF)

    by_rows(OWN, 32, write_out)
    up_sum.send_mirror()

    for b in range(2):
        rows = slice(QBLOCK * b, QBLOCK * (b + 1))
        keys = QBLOCK * (b + 1)
        query = s.qv[rows, :]
        dq = jnp.zeros((QBLOCK, 256), F32)
        for h in range(3):
            probs = s.probs[h, rows, :keys]
            if h < 2:
                grad = s.dob[rows, 256:] * half_mask[h]
                dp = dot(grad, s.v01[:keys, :], 1, 1)
            else:
                grad = s.dob[rows, :256]
                dp = dot(grad, s.qv[:keys, :], 1, 1)
            delta = jnp.sum(dp * probs, axis=1, keepdims=True)
            ds = (probs * (dp - delta)).astype(BF)
            dq = dq + dot(ds, s.kk[:keys, :] * head_mask[h])
            dk = dot(ds, query * head_mask[h], 0, 0) * root
            dv = dot(probs.astype(BF), grad, 0, 0)
            cols = slice(256, 384) if h < 2 else slice(0, 256)
            if b == 0:
                old, new = slice(0, QBLOCK), None
            else:
                old, new = slice(0, QBLOCK), slice(QBLOCK, SEQ)
            if h == 0 and b == 0:
                s.dk[old, :] = dk[:QBLOCK]
            else:
                s.dk[old, :] += dk[:QBLOCK]
            if b == 0 and h != 1:
                s.dv[old, cols] = dv[:QBLOCK]
            else:
                s.dv[old, cols] += dv[:QBLOCK]
            if new is not None:
                if h == 0:
                    s.dk[new, :] = dk[QBLOCK:]
                else:
                    s.dk[new, :] += dk[QBLOCK:]
                if h != 1:
                    s.dv[new, cols] = dv[QBLOCK:]
                else:
                    s.dv[new, cols] += dv[QBLOCK:]
        s.dq[rows, :] = dq * root

    def turn_back(at):
        co, si = cosine[at, :], sine[at, :]
        for left, source in ((0, s.dq), (256, s.dk)):
            a, b = source[at, :128], source[at, 128:]
            first, second = a * co + b * si, b * co - a * si
            if left == 0:
                first, second = first + s.dv[at, :128], second + s.dv[at, 128:256]
            s.dqkv[at, left : left + 128] = first.astype(BF)
            s.dqkv[at, left + 128 : left + 256] = second.astype(BF)
        s.dqkv[at, 512:] = s.dv[at, 256:].astype(BF)

    by_rows(SEQ, 64, turn_back)
    for i in range(3):
        cols = slice(QBLOCK * i, QBLOCK * (i + 1))
        s.g_qkv[cols, :] = dot(s.h1[:, cols], s.dqkv[...], 0, 0)
    qkv_sum = RowSum("qkv", block_of(s.g_qkv), 16, True)
    qkv_sum.send()

    def first_back(at):
        s.part[at, :] = dot(s.dqkv[at, :], s.w_qkv[...], 1, 1)

    by_rows(SEQ, 256, first_back)
    in_sum = GroupSum("in", s.part)
    in_sum.send()
    s.gain_sum[...] = jnp.zeros((8, WIDTH), F32)
    s.shift_sum[...] = jnp.zeros((8, WIDTH), F32)

    def first_norm_sums(at):
        grad = s.part[at, :]
        s.gain_sum[...] += sublane_sum(grad * s.normal[at, :])
        s.shift_sum[...] += sublane_sum(grad)

    by_rows(SEQ, 32, first_norm_sums)
    in_sum.middle()
    s.t0[0:1, :] = jnp.sum(s.gain_sum[...], axis=0, keepdims=True)
    s.t0[1:2, :] = jnp.sum(s.shift_sum[...], axis=0, keepdims=True)
    lane = lane_id((1, WIDTH))
    own_term = jnp.sum(jnp.sum(s.terms[...], axis=0, keepdims=True), axis=1, keepdims=True)
    last_term = jnp.sum(jnp.sum(s.terms2[...], axis=0, keepdims=True), axis=1, keepdims=True)
    s.t0[4:5, :] = jnp.where(lane == d, own_term, jnp.where(lane == GROUP, last_term, 0.0))
    small = copy_to(s.t0, s.t1, x_dev)
    up_sum.send_two()
    out_sum.send_mirror()
    qkv_sum.send_own()
    out_sum.send_near()
    out_sum.send_two()

    def spread(total, staged, landing):
        copies = []
        for m, device in mates:
            rows = total[pl.ds(pl.multiple_of(CHUNK * m, CHUNK), CHUNK), :]
            for t, tile in enumerate(fold(tiles_of(rows))):
                staged[m, :, 128 * t : 128 * (t + 1)] = tile.astype(BF)
            copies.append(copy_to(staged.at[m], landing.at[d], device))
        rows = total[pl.ds(pl.multiple_of(CHUNK * d, CHUNK), CHUNK), :]
        for t, tile in enumerate(fold(tiles_of(rows))):
            landing[d, :, 128 * t : 128 * (t + 1)] = tile.astype(BF)
        return copies

    def collect(copies, landing, count, back, target):
        for copy in copies:
            copy.wait_recv()
        tiles = []
        for k in range(GROUP):
            tiles += unfold([t.astype(F32) for t in tiles_of(landing[k])], count)
        for t, tile in enumerate(permute_chunks(tiles, back)):
            target[:, 128 * t : 128 * (t + 1)] = tile

    qkv_sum.send_mirror()
    small.wait_recv()
    s.tz[z] = s.t0[...] + s.t1[...]
    small_z = [
        copy_to(s.tz.at[z], s.tz.at[z], device) for device in (two_dev, mirror_dev, near_dev)
    ]
    qkv_sum.send_two()
    down_sum.finish()
    gd_o[...] = s.f_down[...]
    up_sum.finish()
    up_spread = spread(s.f_up, s.b_up, s.a_up)
    in_sum.wait()

    def first_norm_back(at):
        grad = in_sum.value(at)
        normal, scale = standardize(x_in[at, :].astype(F32))
        back = norm_back(grad, s.norms[0:1, :], normal, scale)
        ig_o[at, :] = (s.dy[at, :] + back).astype(BF)

    by_rows(OWN, 32, first_norm_back)
    for copy in small_z:
        copy.wait_recv()
    s.td[d] = (s.tz[0] + s.tz[1]) + (s.tz[2] + s.tz[3])
    small_d = [copy_to(s.td.at[d], s.td.at[d], device) for m, device in mates]
    out_sum.finish()
    for t, tile in enumerate(unfold(tiles_of(s.f_out[...]), 6)):
        go_o[:, 128 * t : 128 * (t + 1)] = tile
    collect(up_spread, s.a_up, 6, UP_BACK, gu_o)
    for copy in small_d:
        copy.wait_recv()
    value = (s.td[0] + s.td[1]) + (s.td[2] + s.td[3])
    dg_o[...] = value[:, :128]
    choose = row_id((WIDTH, 128)) == lane_id((WIDTH, 128)) + CHUNK * (GROUP * r + d)
    ng_o[...] = lax.dot_general(
        value,
        jnp.where(choose, 1.0, 0.0),
        (((1,), (0,)), ((), ())),
        preferred_element_type=F32,
        precision=lax.Precision.HIGHEST,
    )
    qkv_sum.finish()
    qkv_spread = spread(s.f_qkv, s.b_qkv, s.a_qkv)
    collect(qkv_spread, s.a_qkv, 5, QKV_BACK, gq_o)
    for copy in sent:
        copy.wait_send()

    @pl.when(inside)
    def _():
        for copy in sent_inside:
            copy.wait_send()

    @pl.when(jnp.logical_not(inside))
    def _():
        for copy in sent_outside:
            copy.wait_send()


def finish_kernel(*refs):
    count = N_OUT - 2
    ins, refs = refs[:count], refs[count:]
    (norm, depth), refs = refs[:2], refs[2:]
    outs, (norm_o, depth_o), refs = refs[:count], refs[count : count + 2], refs[count + 2 :]
    held, sems = refs[:-1], refs[-1]
    first = [pltpu.make_async_copy(a, b, sems.at[i]) for i, (a, b) in enumerate(zip(ins, held))]
    for copy in first:
        copy.start()
    norm_o[...] = norm[:4, :CHUNK]
    depth_o[...] = depth[4:5, : GROUP + 1]
    second = []
    for i, copy in enumerate(first):
        copy.wait()
        second.append(pltpu.make_async_copy(held[i], outs[i], sems.at[count + i]))
        second[i].start()
    for copy in second:
        copy.wait()


def fused(
    block_input,
    history,
    cotangent,
    token_mask,
    qkv_weight,
    out_weight,
    up_weight,
    down_weight,
    norm_params,
    depth_weights,
):
    cosine, sine = tables()
    vmem = pl.BlockSpec(memory_space=pltpu.VMEM)
    smem = pl.BlockSpec(memory_space=pltpu.SMEM)
    anywhere = pl.BlockSpec(memory_space=pl.ANY)
    shape = jax.ShapeDtypeStruct
    shapes = (
        shape((OWN, WIDTH), BF),
        shape((OWN, WIDTH), BF),
        shape((SEQ, WIDTH), BF),
        shape((CHUNK, 3 * WIDTH), F32),
        shape((CHUNK, WIDTH), F32),
        shape((CHUNK, 4 * WIDTH), F32),
        shape((BLOCK, WIDTH), F32),
        shape((8, 128), F32),
        shape((8, 128), F32),
    )
    outs = pl.pallas_call(
        fused_kernel,
        out_shape=shapes,
        in_specs=[vmem] * 9 + [smem] + [vmem] * 2,
        out_specs=[vmem] * 9,
        scratch_shapes=[pltpu.VMEM(dims, kind) for dims, kind in SCRATCH.values()]
        + [pltpu.SemaphoreType.DMA((N_SEMS,))] * 2,
        compiler_params=pltpu.CompilerParams(
            collective_id=0, has_side_effects=True, vmem_limit_bytes=VMEM_MIB * 2**20
        ),
        cost_estimate=pl.CostEstimate(flops=12 * 10**9, bytes_accessed=4 * 10**6, transcendentals=10**6),
    )(
        block_input,
        history.reshape(SEQ, WIDTH),
        cotangent,
        token_mask.reshape(1, OWN),
        qkv_weight,
        out_weight,
        up_weight,
        down_weight,
        norm_params,
        depth_weights,
        jnp.asarray(cosine),
        jnp.asarray(sine),
    )
    held = pl.pallas_call(
        finish_kernel,
        out_shape=shapes[:7] + (shape((4, CHUNK), F32), shape((1, GROUP + 1), F32)),
        in_specs=[anywhere] * 7 + [vmem] * 2,
        out_specs=[anywhere] * 7 + [vmem] * 2,
        scratch_shapes=[pltpu.VMEM(one.shape, one.dtype) for one in shapes[:7]]
        + [pltpu.SemaphoreType.DMA((14,))],
        compiler_params=pltpu.CompilerParams(vmem_limit_bytes=VMEM_MIB * 2**20),
    )(*outs)
    out, input_grad, history_grad, *grads, g_depth = held
    return (out, input_grad, history_grad.reshape(1, SEQ, WIDTH), *grads, g_depth.reshape(GROUP + 1))


def fits(mesh, block_input, history, up_weight):
    devices = ROWS * GROUP
    return (
        mesh.shape["rows"] == ROWS
        and mesh.shape["depth"] == GROUP
        and block_input.shape == (OWN * devices, WIDTH)
        and history.shape[0] == GROUP
        and up_weight.shape == (WIDTH, 4 * WIDTH)
    )


def solution(mesh):
    weights = P(("rows", "depth"), None)
    in_specs = (
        weights,
        P("depth", "rows", None),
        weights,
        P(("rows", "depth")),
        weights,
        weights,
        weights,
        weights,
        P(None, ("rows", "depth")),
        P(),
    )
    out_specs = (
        weights,
        weights,
        P("depth", "rows", None),
        weights,
        weights,
        weights,
        weights,
        P(None, ("rows", "depth")),
        P(),
    )

    def run(*args):
        body = fused if fits(mesh, args[0], args[1], args[6]) else local
        return jax.shard_map(
            body, mesh=mesh, in_specs=in_specs, out_specs=out_specs, check_vma=False
        )(*args)

    return run
```

```python
import functools

import jax
import jax.numpy as jnp
import numpy as np
from jax import lax
from jax.experimental import pallas as pl
from jax.experimental.pallas import tpu as pltpu
from jax.sharding import PartitionSpec as P

HEADS = 12
HD = 64


def norm_rows(value, gain, shift):
    center = value - jnp.mean(value, axis=-1, keepdims=True)
    spread = jnp.mean(center * center, axis=-1, keepdims=True)
    return center * lax.rsqrt(spread + 1e-05) * (1.0 + gain) + shift


def rotate(value, place, sign):
    half = value.shape[-1] // 2
    freq = 10000.0 ** (-jnp.arange(half, dtype=jnp.float32) / half)
    angle = place.astype(jnp.float32)[:, None] * freq[None, :]
    cosine = jnp.cos(angle)[:, None, :]
    sine = jnp.sin(angle)[:, None, :] * sign
    first = value[..., :half]
    second = value[..., half:]
    return jnp.concatenate(
        [first * cosine - second * sine, second * cosine + first * sine], axis=-1
    )


def block_scores(query, key_block, start, query_place, scale):
    block_len = key_block.shape[0]
    scores = (
        jnp.einsum("qhd,khd->hqk", query, key_block, preferred_element_type=jnp.float32) * scale
    )
    key_place = start + jnp.arange(block_len, dtype=jnp.int32)
    allowed = query_place[:, None] >= key_place[None, :]
    return (scores, allowed)


def local(
    block_input,
    history,
    cotangent,
    token_mask,
    qkv_weight,
    out_weight,
    up_weight,
    down_weight,
    norm_params,
    depth_weights,
):
    rows_tok, width = block_input.shape
    depth_count = lax.axis_size("depth")
    device_count = lax.axis_size("rows") * depth_count
    place_depth = lax.axis_index("depth")
    heads = HEADS
    head_size = HD
    scale = head_size ** (-0.5)
    seq_len = rows_tok * depth_count
    slot_count = history.shape[0]
    hist_total = slot_count * depth_count
    wide_qkv, wide_out, wide_up, wide_down, wide_norms = (
        lax.all_gather(qkv_weight, ("rows", "depth"), axis=0, tiled=True),
        lax.all_gather(out_weight, ("rows", "depth"), axis=0, tiled=True),
        lax.all_gather(up_weight, ("rows", "depth"), axis=0, tiled=True),
        lax.all_gather(down_weight, ("rows", "depth"), axis=0, tiled=True),
        lax.all_gather(
            norm_params.astype(jnp.bfloat16), ("rows", "depth"), axis=1, tiled=True
        ).astype(norm_params.dtype),
    )
    total = lax.psum(jnp.sum(token_mask), ("rows", "depth")).astype(jnp.float32)
    loss_scale = rows_tok * device_count / total
    float_input = block_input.astype(jnp.float32)
    place = place_depth * rows_tok + jnp.arange(rows_tok, dtype=jnp.int32)
    first = norm_rows(float_input, wide_norms[0], wide_norms[1]).astype(jnp.bfloat16)
    projected = jnp.dot(first, wide_qkv, preferred_element_type=jnp.float32)
    query = rotate(projected[:, :width].reshape(rows_tok, heads, head_size), place, 1.0).astype(
        jnp.bfloat16
    )
    keys = rotate(projected[:, width : 2 * width].reshape(rows_tok, heads, head_size), place, 1.0)
    keys = keys.astype(jnp.bfloat16).reshape(rows_tok, width)
    values = projected[:, 2 * width :].astype(jnp.bfloat16)
    all_keys, all_values = (
        lax.all_gather(keys, "depth", axis=0, tiled=True),
        lax.all_gather(values, "depth", axis=0, tiled=True),
    )
    block_len = min(512, seq_len)
    block_count = seq_len // block_len
    key_blocks = all_keys.reshape(block_count, block_len, heads, head_size)
    value_blocks = all_values.reshape(block_count, block_len, heads, head_size)
    starts = jnp.arange(block_count, dtype=jnp.int32) * block_len

    def peak_step(carry, item):
        peak, weight_sum = carry
        key_block, value_block, start = item
        scores, allowed = block_scores(query, key_block, start, place, scale)
        scores = jnp.where(allowed[None], scores, -1e30)
        new_peak = jnp.maximum(peak, jnp.max(scores, axis=-1))
        weight_sum = weight_sum * jnp.exp(peak - new_peak) + jnp.sum(
            jnp.exp(scores - new_peak[..., None]), axis=-1
        )
        return ((new_peak, weight_sum), None)

    start_carry = (
        jnp.full((heads, rows_tok), -1e30, jnp.float32),
        jnp.zeros((heads, rows_tok), jnp.float32),
    )
    (peak, weight_sum), _ = lax.scan(peak_step, start_carry, (key_blocks, value_blocks, starts))
    log_total = peak + jnp.log(weight_sum)

    def value_step(running, item):
        key_block, value_block, start = item
        scores, allowed = block_scores(query, key_block, start, place, scale)
        probs = jnp.where(allowed[None], jnp.exp(scores - log_total[..., None]), 0.0)
        running = running + jnp.einsum(
            "hqk,khd->qhd",
            probs.astype(jnp.bfloat16),
            value_block,
            preferred_element_type=jnp.float32,
        )
        return (running, None)

    running, _ = lax.scan(
        value_step,
        jnp.zeros((rows_tok, heads, head_size), jnp.float32),
        (key_blocks, value_blocks, starts),
    )
    mixed = running.reshape(rows_tok, width)
    mixed_low = mixed.astype(jnp.bfloat16)
    middle = float_input + jnp.dot(mixed_low, wide_out, preferred_element_type=jnp.float32)
    second = norm_rows(middle, wide_norms[2], wide_norms[3]).astype(jnp.bfloat16)
    upper = jnp.dot(second, wide_up, preferred_element_type=jnp.float32)
    active = jax.nn.gelu(upper).astype(jnp.bfloat16)
    block_out = middle + jnp.dot(active, wide_down, preferred_element_type=jnp.float32)
    own_alpha = lax.dynamic_slice_in_dim(depth_weights, place_depth * slot_count, slot_count)
    partial_mix = jnp.sum(own_alpha[:, None, None] * history.astype(jnp.float32), axis=0)
    mixture = lax.psum_scatter(
        partial_mix.astype(jnp.bfloat16), "depth", scatter_dimension=0, tiled=True
    ).astype(jnp.float32)
    output = (mixture + depth_weights[hist_total] * block_out).astype(jnp.bfloat16)
    grad_out = token_mask.astype(jnp.float32)[:, None] * cotangent.astype(jnp.float32) * loss_scale
    last_term = jnp.sum(grad_out * block_out)
    index_all = jnp.arange(hist_total + 1, dtype=jnp.int32)
    grad_rows = lax.all_gather(grad_out.astype(jnp.bfloat16), "depth", axis=0, tiled=True).astype(
        grad_out.dtype
    )
    history_grad = (own_alpha[:, None, None] * grad_rows[None]).astype(jnp.bfloat16)
    hist_terms = jnp.sum(history.astype(jnp.float32) * grad_rows[None], axis=(1, 2))
    own_index = place_depth * slot_count + jnp.arange(slot_count, dtype=jnp.int32)
    alpha_terms = jnp.sum(
        jnp.where(index_all[None, :] == own_index[:, None], hist_terms[:, None], 0.0), axis=0
    )
    alpha_terms = alpha_terms + jnp.where(index_all == hist_total, last_term, 0.0)
    depth_gradient = lax.psum(alpha_terms, ("rows", "depth"))
    wide_qkv, wide_out, wide_up, wide_down, wide_norms = (
        lax.all_gather(qkv_weight, ("rows", "depth"), axis=0, tiled=True),
        lax.all_gather(out_weight, ("rows", "depth"), axis=0, tiled=True),
        lax.all_gather(up_weight, ("rows", "depth"), axis=0, tiled=True),
        lax.all_gather(down_weight, ("rows", "depth"), axis=0, tiled=True),
        lax.all_gather(
            norm_params.astype(jnp.bfloat16), ("rows", "depth"), axis=1, tiled=True
        ).astype(norm_params.dtype),
    )
    block_grad = depth_weights[hist_total] * grad_out
    lower_grad = block_grad.astype(jnp.bfloat16)
    down_gradient = jnp.dot(active.T, lower_grad, preferred_element_type=jnp.float32)
    active_grad = jnp.dot(lower_grad, wide_down.T, preferred_element_type=jnp.float32)
    _, gelu_pull = jax.vjp(jax.nn.gelu, upper)
    upper_grad = gelu_pull(active_grad)[0].astype(jnp.bfloat16)
    up_gradient = jnp.dot(second.T, upper_grad, preferred_element_type=jnp.float32)
    second_grad = jnp.dot(upper_grad, wide_up.T, preferred_element_type=jnp.float32)
    _, norm_pull = jax.vjp(norm_rows, middle, wide_norms[2], wide_norms[3])
    middle_part, gain_two, shift_two = norm_pull(second_grad)
    middle_grad = block_grad + middle_part
    branch_grad = middle_grad.astype(jnp.bfloat16)
    out_gradient = jnp.dot(mixed_low.T, branch_grad, preferred_element_type=jnp.float32)
    mixed_grad = jnp.dot(branch_grad, wide_out.T, preferred_element_type=jnp.float32).astype(
        jnp.bfloat16
    )
    delta = jnp.sum(
        (mixed_grad.astype(jnp.float32) * mixed).reshape(rows_tok, heads, head_size), axis=-1
    ).T
    mixed_heads = mixed_grad.reshape(rows_tok, heads, head_size)

    def score_grads(
        query_rows, grad_rows, lse_rows, delta_rows, key_block, value_block, query_place, start
    ):
        scores, allowed = block_scores(query_rows, key_block, start, query_place, scale)
        probs = jnp.where(allowed[None], jnp.exp(scores - lse_rows[..., None]), 0.0)
        prob_grad = jnp.einsum(
            "qhd,khd->hqk", grad_rows, value_block, preferred_element_type=jnp.float32
        )
        score_grad = (probs * (prob_grad - delta_rows[..., None])).astype(jnp.bfloat16)
        return (probs, score_grad)

    def grad_step(query_total, item):
        key_block, value_block, start = item
        probs, score_grad = score_grads(
            query, mixed_heads, log_total, delta, key_block, value_block, place, start
        )
        query_total = (
            query_total
            + jnp.einsum("hqk,khd->qhd", score_grad, key_block, preferred_element_type=jnp.float32)
            * scale
        )
        key_part = (
            jnp.einsum("hqk,qhd->khd", score_grad, query, preferred_element_type=jnp.float32)
            * scale
        )
        value_part = jnp.einsum(
            "hqk,qhd->khd",
            probs.astype(jnp.bfloat16),
            mixed_heads,
            preferred_element_type=jnp.float32,
        )
        return (query_total, (key_part, value_part))

    query_total, (key_parts, value_parts) = lax.scan(
        grad_step,
        jnp.zeros((rows_tok, heads, head_size), jnp.float32),
        (key_blocks, value_blocks, starts),
    )
    key_sum, value_sum = (
        lax.psum_scatter(
            key_parts.reshape(seq_len, width).astype(jnp.bfloat16),
            "depth",
            scatter_dimension=0,
            tiled=True,
        ).astype(jnp.float32),
        lax.psum_scatter(
            value_parts.reshape(seq_len, width).astype(jnp.bfloat16),
            "depth",
            scatter_dimension=0,
            tiled=True,
        ).astype(jnp.float32),
    )
    query_grad = rotate(query_total, place, -1.0).reshape(rows_tok, width)
    key_grad = rotate(key_sum.reshape(rows_tok, heads, head_size), place, -1.0).reshape(
        rows_tok, width
    )
    projected_grad = jnp.concatenate([query_grad, key_grad, value_sum], axis=1).astype(jnp.bfloat16)
    qkv_gradient = jnp.dot(first.T, projected_grad, preferred_element_type=jnp.float32)
    first_grad = jnp.dot(projected_grad, wide_qkv.T, preferred_element_type=jnp.float32)
    _, first_pull = jax.vjp(norm_rows, float_input, wide_norms[0], wide_norms[1])
    input_part, gain_one, shift_one = first_pull(first_grad)
    input_grad = (middle_grad + input_part).astype(jnp.bfloat16)
    norms_full = jnp.stack([gain_one, shift_one, gain_two, shift_two])
    qkv_gradient, out_gradient, up_gradient, down_gradient, norm_gradient = (
        lax.psum_scatter(qkv_gradient, ("rows", "depth"), scatter_dimension=0, tiled=True),
        lax.psum_scatter(out_gradient, ("rows", "depth"), scatter_dimension=0, tiled=True),
        lax.psum_scatter(up_gradient, ("rows", "depth"), scatter_dimension=0, tiled=True),
        lax.psum_scatter(down_gradient, ("rows", "depth"), scatter_dimension=0, tiled=True),
        lax.psum_scatter(norms_full, ("rows", "depth"), scatter_dimension=1, tiled=True),
    )
    return (
        output,
        input_grad,
        history_grad,
        qkv_gradient,
        out_gradient,
        up_gradient,
        down_gradient,
        norm_gradient,
        depth_gradient,
    )

SEQ = 512
OWN = 128
WIDTH = 768
ROWS = 8
GROUP = 4
PACK = 640
BLOCK = WIDTH // ROWS
CHUNK = BLOCK // GROUP
QBLOCK = 256
BF = jnp.bfloat16
F32 = jnp.float32
MESH = pl.DeviceIdType.MESH


def dot(a, b, ca=1, cb=0):
    return lax.dot_general(a, b, (((ca,), (cb,)), ((), ())), preferred_element_type=F32)


def lane_id(shape):
    return lax.broadcasted_iota(jnp.int32, shape, len(shape) - 1)


def row_id(shape):
    return lax.broadcasted_iota(jnp.int32, shape, len(shape) - 2)


def tiles_of(value):
    return [value[:, 128 * i : 128 * (i + 1)] for i in range(value.shape[1] // 128)]


def permute_chunks(tiles, picks):
    group = lax.div(lane_id(tiles[0].shape), jnp.int32(32))
    out = []
    for t in range(len(picks) // 4):
        total, rolled = jnp.zeros_like(tiles[0]), {}
        for j in range(4):
            pick = picks[4 * t + j]
            if pick is None:
                continue
            source, place = divmod(pick, 4)
            shift = (j - place) * 32 % 128
            if (source, shift) not in rolled:
                value = tiles[source]
                rolled[source, shift] = pltpu.roll(value, shift, 1) if shift else value
            total = jnp.where(group == j, rolled[source, shift], total)
        out.append(total)
    return out


def fold(tiles):
    half = (len(tiles) + 1) // 2
    low = [t[16:] for t in tiles]
    if len(low) % 2:
        low.append(jnp.zeros_like(low[0]))
    return [t[:16] for t in tiles] + [
        jnp.concatenate([low[i], low[half + i]], axis=0) for i in range(half)
    ]


def unfold(tiles, count):
    half = (count + 1) // 2
    rest = tiles[count:]
    low = [rest[i][:8] for i in range(half)] + [rest[i][8:] for i in range(half)]
    return [jnp.concatenate([tiles[i], low[i]], axis=0) for i in range(count)]


def qkv_chunk(block, head, half):
    return 24 * block + 2 * head + half


def qkv_picks(d):
    heads = [3 * d + i for i in range(3)]
    picks = []
    for block in range(2):
        for half in range(2):
            picks += [qkv_chunk(block, h, half) for h in heads]
            picks.append(qkv_chunk(2, heads[2], half) if block == 0 else None)
    return picks + [qkv_chunk(2, h, half) for h in heads[:2] for half in range(2)]


def up_picks(d):
    return [3 * (GROUP * r + d) + j for r in range(ROWS) for j in range(3)]


def inverse_picks(per_device, count, tiles_each):
    back = [None] * count
    for d, picks in enumerate(per_device):
        for place, pick in enumerate(picks):
            if pick is not None:
                back[pick] = 4 * tiles_each * d + place
    return back


QKV_BACK = inverse_picks([qkv_picks(d) for d in range(GROUP)], 72, 5)
UP_BACK = inverse_picks([up_picks(d) for d in range(GROUP)], 96, 6)


def tables():
    half = HD // 2
    freq = np.float32(10000.0) ** (-np.arange(half, dtype=np.float32) / np.float32(half))
    angle = (np.arange(SEQ, dtype=np.float32)[:, None] * freq[None, :]).astype(np.float32)
    angle = angle.astype(np.float64)
    cosine, sine = np.ones((SEQ, 128), np.float32), np.zeros((SEQ, 128), np.float32)
    cosine[:, :96] = np.tile(np.cos(angle), (1, 3))
    sine[:, :96] = np.tile(np.sin(angle), (1, 3))
    return cosine, sine


def standardize(value):
    center = value - jnp.mean(value, axis=-1, keepdims=True)
    spread = jnp.mean(center * center, axis=-1, keepdims=True)
    scale = lax.rsqrt(spread + 1e-05)
    return center * scale, scale


def norm_back(grad, gain, normal, scale):
    part = grad * (1.0 + gain)
    inner = jnp.mean(part, axis=-1, keepdims=True)
    along = jnp.mean(part * normal, axis=-1, keepdims=True)
    return scale * (part - inner - normal * along)


def sublane_sum(value):
    return jnp.sum(value.reshape(value.shape[0] // 8, 8, value.shape[1]), axis=0)


SCRATCH = dict(
    hist=((SEQ, WIDTH), BF),
    cot=((OWN, WIDTH), BF),
    wq=((CHUNK, 3 * WIDTH), BF),
    wo=((CHUNK, WIDTH), BF),
    wu=((CHUNK, 4 * WIDTH), BF),
    cosine=((SEQ, 128), F32),
    sine=((SEQ, 128), F32),
    r_0=((OWN, WIDTH), BF),
    r_1=((OWN, WIDTH), BF),
    r_2=((SEQ, WIDTH), BF),
    r_3=((CHUNK, 3 * WIDTH), F32),
    r_4=((CHUNK, WIDTH), F32),
    r_5=((CHUNK, 4 * WIDTH), F32),
    r_6=((BLOCK, WIDTH), F32),
    x_all=((GROUP, OWN, WIDTH), BF),
    c_all=((GROUP, OWN, WIDTH), BF),
    qp_s=((GROUP, 16, 1024), BF),
    q_all=((ROWS, GROUP, 16, 1024), BF),
    up_s=((GROUP, 16, 1152), BF),
    up_l=((GROUP, 16, 1152), BF),
    tmp=((BLOCK, WIDTH), F32),
    w_qkv=((WIDTH, PACK), BF),
    w_up=((WIDTH, WIDTH), BF),
    w_down=((WIDTH, WIDTH), BF),
    wo_l=((GROUP, 2, ROWS // 2, 16, 1152), BF),
    w_out=((WIDTH, WIDTH), BF),
    w_own=((384, WIDTH), BF),
    norms=((8, WIDTH), F32),
    normal=((SEQ, WIDTH), F32),
    h1=((SEQ, WIDTH), BF),
    qv=((SEQ, 256), BF),
    kk=((SEQ, 256), BF),
    v01=((SEQ, 128), BF),
    probs=((3, SEQ, SEQ), F32),
    o_l=((GROUP, 2, 384, 128), BF),
    ob=((SEQ, WIDTH), BF),
    y=((SEQ, WIDTH), F32),
    h2=((SEQ, WIDTH), BF),
    slope=((SEQ, WIDTH), F32),
    act=((SEQ, WIDTH), BF),
    dm=((SEQ, WIDTH), BF),
    g_down=((WIDTH, WIDTH), F32),
    g_up=((WIDTH, WIDTH), F32),
    g_out=((WIDTH, WIDTH), F32),
    g_qkv=((WIDTH, PACK), F32),
    du=((SEQ, WIDTH), BF),
    part=((SEQ, WIDTH), F32),
    part2=((SEQ, WIDTH), F32),
    dy=((OWN, WIDTH), F32),
    dyb=((GROUP, OWN, WIDTH), BF),
    dob=((SEQ, 384), BF),
    dq=((SEQ, 256), F32),
    dk=((SEQ, 256), F32),
    dv=((SEQ, 384), F32),
    dqkv=((SEQ, PACK), BF),
    terms=((8, WIDTH), F32),
    terms2=((8, WIDTH), F32),
    t0=((8, WIDTH), F32),
    td=((4, 8, WIDTH), F32),
    ext=((ROWS, 16, 128), F32),
    u0=((8, 128), F32),
    u1=((8, 128), F32),
    uz=((4, 8, 128), F32),
    ud=((4, 8, 128), F32),
    fin=((4, GROUP, 16, 1024), BF),
    q_sum=((GROUP, 16, 1024), F32),
    a_up=((GROUP, 16, 1152), BF),
    f_down=((BLOCK, WIDTH), F32),
    f_up=((BLOCK, WIDTH), F32),
    f_out=((16, 1280), F32),
    b_up=((GROUP, 16, 1152), BF),
    gain_sum=((8, WIDTH), F32),
    shift_sum=((8, WIDTH), F32),
)
for _name, _rows, _cols in (
    ("down", BLOCK, WIDTH),
    ("up", BLOCK, WIDTH),
    ("out", 16, 1280),
):
    SCRATCH["xs_" + _name] = ((4, _rows, _cols), BF)
    SCRATCH["xl_" + _name] = ((4, _rows, _cols), BF)
    SCRATCH["zs_" + _name] = ((2, _rows, _cols), BF)
    SCRATCH["zl_" + _name] = ((3, _rows, _cols), BF)
    SCRATCH["ns_" + _name] = ((2, _rows, _cols), BF)
    SCRATCH["nl_" + _name] = ((2, _rows, _cols), BF)
for _h in range(2):
    for _name in ("xs", "xl"):
        SCRATCH[f"{_name}_qkv{_h}"] = ((4, BLOCK // 2, PACK), BF)
    for _name in ("cs", "cl", "zs", "zl"):
        SCRATCH[f"{_name}_qkv{_h}"] = ((BLOCK // 2, PACK), BF)
    SCRATCH[f"ps_qkv{_h}"] = ((4, 2, 16, 1024), BF)
for _name in ("mix", "mid", "in"):
    SCRATCH["s1_" + _name] = ((2, OWN, WIDTH), BF)
    SCRATCH["l1_" + _name] = ((2, OWN, WIDTH), BF)
    SCRATCH["s2_" + _name] = ((OWN, WIDTH), BF)
    SCRATCH["l2_" + _name] = ((OWN, WIDTH), BF)
N_SEMS = 224
N_IN = 12
N_OUT = 9
VMEM_MIB = 60


class Names:
    pass


def fused_kernel(*refs):
    (x_hbm, hist_hbm, cot_hbm, mask, wq_hbm, wo_hbm, wu_hbm, wd_hbm) = refs[:8]
    (nrm, dw, cosine_hbm, sine_hbm) = refs[8:N_IN]
    results, (ng_o, dg_o) = refs[N_IN : N_IN + N_OUT - 2], refs[N_IN + N_OUT - 2 : N_IN + N_OUT]
    s = Names()
    for name, ref in zip(SCRATCH, refs[N_IN + N_OUT :]):
        setattr(s, name, ref)
    send_sems, recv_sems, local_sems = refs[-3:]

    r, d = lax.axis_index("rows"), lax.axis_index("depth")
    z, x = lax.div(r, 2), lax.rem(r, 2)
    yy, c = lax.div(d, 2), lax.rem(d, 2)
    other_x, other_c, other_y = 1 - x, 1 - c, 1 - yy
    x_dev = (2 * z + other_x, d)
    z_two, z_mirror, z_near = lax.rem(z + 2, 4), 3 - z, z + 1 - 2 * lax.rem(z, 2)
    two_dev, mirror_dev, near_dev = ((2 * zk + x, d) for zk in (z_two, z_mirror, z_near))
    inside = lax.rem(z + 1, 4) >= 2
    outside = jnp.logical_not(inside)
    core_d, y_d, far_d = 2 * yy + other_c, 2 * other_y + c, 2 * other_y + other_c
    core_dev, y_dev, far_dev = (r, core_d), (r, y_d), (r, far_d)
    mates = ((core_d, core_dev), (y_d, y_dev), (far_d, far_dev))
    counter = [0]
    sent = []

    def prepare(src, dst, device, arrival=None):
        index = counter[0]
        counter[0] += 1
        copy = pltpu.make_async_remote_copy(
            src_ref=src,
            dst_ref=dst,
            send_sem=send_sems.at[index],
            recv_sem=recv_sems.at[index if arrival is None else arrival],
            device_id=device,
            device_id_type=MESH,
        )
        return copy, index

    def copy_to(src, dst, device):
        copy, _ = prepare(src, dst, device)
        start(copy)
        return copy

    def start(copy, condition=None):
        if condition is None:
            copy.start()
        else:
            pl.when(condition)(copy.start)
        sent.append((copy, condition))

    def reserve(count):
        counter[0] += count
        return counter[0] - count

    def rows_at(ref, index, size):
        return ref.at[pl.ds(pl.multiple_of(index * size, size), size)]

    def by_rows(count, step, body):
        def one(i, carry):
            body(pl.ds(pl.multiple_of(i * step, step), step))
            return carry

        lax.fori_loop(0, count // step, one, 0)

    hist, cot, wq, wo, wu, cosine, sine = s.hist, s.cot, s.wq, s.wo, s.wu, s.cosine, s.sine
    loads = {}
    for name, source, target in (
        ("wq", wq_hbm, wq),
        ("x", x_hbm, s.x_all.at[d]),
        ("wo", wo_hbm, wo),
        ("wu", wu_hbm, wu),
        ("wd", wd_hbm, rows_at(s.w_down, r, BLOCK)),
        ("cot", cot_hbm, cot),
        ("cosine", cosine_hbm, cosine),
        ("sine", sine_hbm, sine),
        ("hist", hist_hbm, hist),
    ):
        loads[name] = pltpu.make_async_copy(source, target, local_sems.at[len(loads)])
        loads[name].start()
    out_o, ig_o, hg_o, gq_o, go_o, gu_o, gd_o = (
        getattr(s, f"r_{i}") for i in range(N_OUT - 2)
    )
    stores = []

    def store(i):
        copy = pltpu.make_async_copy(
            getattr(s, f"r_{i}"), results[i], local_sems.at[len(loads) + i]
        )
        copy.start()
        stores.append(copy)

    barrier = pltpu.get_barrier_semaphore()
    partners = [x_dev, core_dev, y_dev, far_dev]
    partners += [
        (2 * zk + x, m) for zk in (z_two, z_mirror, z_near) for m in (d, core_d, y_d, far_d)
    ]
    for device in partners:
        pl.semaphore_signal(barrier, inc=1, device_id=device, device_id_type=MESH)
    pl.semaphore_wait(barrier, len(partners))

    class Gather:
        def __init__(self, piece, cross=False):
            self.piece, self.cross = piece, cross
            self.along_x = []

        def send_two(self):
            mine = self.piece(z, x)
            self.two = copy_to(mine, mine, two_dev)

        def send_mirror(self):
            mine, passed = self.piece(z, x), self.piece(z_two, x)
            self.mirror, index = prepare(mine, mine, mirror_dev)
            self.passing, _ = prepare(passed, passed, near_dev, index)
            start(self.mirror, inside)

        def send_near(self, where=None):
            if where is not False:
                mine = self.piece(z, x)
                self.near, _ = prepare(mine, mine, near_dev)
            start(self.near, None if where is None else outside if where else inside)

        def send_x(self, zk=z):
            piece = self.piece(zk, x)
            self.along_x.append(copy_to(piece, piece, x_dev))

        def arrive_near(self):
            self.near.wait_recv()

        def forward_near(self):
            self.arrive_near()
            if not self.cross:
                self.send_x(z_near)

        def forward_cross(self):
            self.along_x[0].wait_recv()
            piece = self.piece(z, other_x)
            self.along_x[0] = copy_to(piece, piece, near_dev)

        def pass_two(self):
            self.two.wait_recv()
            start(self.passing, inside)

        def forward_two(self):
            self.pass_two()
            self.send_x(z_two)

        def forward_mirror(self):
            self.mirror.wait_recv()
            self.send_x(z_mirror)

        def finish(self):
            for copy in self.along_x:
                copy.wait_recv()

    class GroupGather:
        def __init__(self, slab):
            self.slab = slab

        def send(self):
            mine = self.slab(d)
            self.to_core = copy_to(mine, mine, core_dev)
            self.to_y = copy_to(mine, mine, y_dev)

        def relay(self):
            self.to_y.wait_recv()
            slab = self.slab(y_d)
            self.on = copy_to(slab, slab, core_dev)

        def finish(self):
            self.to_core.wait_recv()
            self.on.wait_recv()

    class RowSum:
        def __init__(self, name, total, block, step, cross):
            self.xs, self.xl, self.zs, self.zl, self.ns, self.nl = (
                getattr(s, p + name) for p in ("xs_", "xl_", "zs_", "zl_", "ns_", "nl_")
            )
            self.total = total
            self.block, self.step, self.cross = block, step, cross
            self.count = self.total.shape[0]
            self.along_x = {}

        def stage(self, target, index, *extras):
            def one(at):
                value = self.block(index, at)
                for ref in extras:
                    value = value + ref[at, :].astype(F32)
                target[at, :] = value.astype(BF)

            by_rows(self.count, self.step, one)

        def send_x(self, name, zk, *extras):
            self.stage(self.xs.at[zk], 2 * zk + other_x, *extras)
            self.along_x[name] = copy_to(self.xs.at[zk], self.xl.at[zk], x_dev)

        def send(self):
            self.send_x("mirror", z_mirror)
            if self.cross:
                self.send_crossing()
            self.send_x("two", z_two)
            if not self.cross:
                self.send_x("near", z_near)
                self.send_x("own", z)

        def send_crossing(self):
            self.stage(self.ns.at[0], 2 * z_near + other_x)
            self.crossing = copy_to(self.ns.at[0], self.nl.at[0], near_dev)

        def send_own(self):
            self.crossing.wait_recv()
            self.send_x("own", z, self.nl.at[0])

        def send_mirror(self):
            self.along_x["mirror"].wait_recv()
            self.stage(self.zs.at[0], 2 * z_mirror + x, self.xl.at[z_mirror])
            self.mirror, _ = prepare(self.zs.at[0], self.zl.at[0], mirror_dev)
            self.passing, _ = prepare(self.zs.at[0], self.zl.at[2], near_dev)
            start(self.mirror, inside)
            start(self.passing, outside)

        def send_two(self):
            self.along_x["two"].wait_recv()

            @pl.when(inside)
            def _():
                self.passing.wait_recv()
                self.stage(self.zs.at[1], 2 * z_two + x, self.xl.at[z_two], self.zl.at[2])

            @pl.when(outside)
            def _():
                self.stage(self.zs.at[1], 2 * z_two + x, self.xl.at[z_two])

            self.two = copy_to(self.zs.at[1], self.zl.at[1], two_dev)

        def send_near(self):
            extras = ()
            if not self.cross:
                self.along_x["near"].wait_recv()
                extras = (self.xl.at[z_near],)
            self.stage(self.ns.at[1], 2 * z_near + x, *extras)
            self.near = copy_to(self.ns.at[1], self.nl.at[1], near_dev)

        def finish(self):
            self.along_x["own"].wait_recv()
            self.two.wait_recv()
            self.near.wait_recv()

            def add(at):
                self.total[at, :] = (
                    self.block(r, at)
                    + self.xl[z, at, :].astype(F32)
                    + self.zl[1, at, :].astype(F32)
                    + self.nl[1, at, :].astype(F32)
                )

            by_rows(self.count, self.step, add)

            @pl.when(inside)
            def _():
                self.mirror.wait_recv()

                def add_mirror(at):
                    self.total[at, :] += self.zl[0, at, :].astype(F32)

                by_rows(self.count, self.step, add_mirror)

    class SpreadSum:
        def __init__(self, half, arrivals):
            self.xs, self.xl, self.cs, self.cl, self.zs, self.zl, self.ps = (
                getattr(s, f"{p}_qkv{half}") for p in ("xs", "xl", "cs", "cl", "zs", "zl", "ps")
            )
            self.half, self.arrivals = half, arrivals
            self.along_x = {}

        def value(self, index, *extras):
            rows = BLOCK // 2
            start_row = pl.multiple_of((2 * index + self.half) * rows, rows)
            value = s.g_qkv[pl.ds(start_row, rows), :]
            for extra in extras:
                value = value + extra.astype(F32)
            return value

        def send_x(self, name, zk, *extras):
            self.xs[zk] = self.value(2 * zk + other_x, *extras).astype(BF)
            self.along_x[name] = copy_to(self.xs.at[zk], self.xl.at[zk], x_dev)

        def send_crossing(self):
            self.cs[...] = self.value(2 * z_near + other_x).astype(BF)
            self.crossing = copy_to(self.cs, self.cl, near_dev)

        def send_own(self):
            self.crossing.wait_recv()
            self.send_x("own", z, self.cl[...])

        def deliver(self, slot, zk, value, condition=None):
            for j in range(2):
                to = 2 * self.half + j
                for t, tile in enumerate(fold(tiles_of(value[CHUNK * j : CHUNK * (j + 1)]))):
                    self.ps[slot, j, :, 128 * t : 128 * (t + 1)] = tile.astype(BF)
                copy, _ = prepare(
                    self.ps.at[slot, j],
                    s.fin.at[slot, d],
                    (2 * zk + x, to),
                    self.arrivals + GROUP * slot + d,
                )
                if slot == 3:
                    start(copy, d != to)

                    @pl.when(d == to)
                    def _(j=j):
                        s.fin[slot, d] = self.ps[slot, j]
                else:
                    start(copy, condition)

        def send_mirror(self):
            self.along_x["mirror"].wait_recv()
            value = self.value(2 * z_mirror + x, self.xl[z_mirror])
            self.deliver(2, z_mirror, value, inside)
            self.zs[...] = value.astype(BF)
            self.passing, _ = prepare(self.zs, self.zl, near_dev)
            start(self.passing, outside)

        def send_two(self):
            self.along_x["two"].wait_recv()

            @pl.when(outside)
            def _():
                self.zl[...] = jnp.zeros((BLOCK // 2, PACK), BF)

            pl.when(inside)(self.passing.wait_recv)
            self.deliver(0, z_two, self.value(2 * z_two + x, self.xl[z_two], self.zl[...]))

        def send_near(self):
            self.deliver(1, z_near, self.value(2 * z_near + x))

        def keep_own(self):
            self.along_x["own"].wait_recv()
            self.deliver(3, z, self.value(r, self.xl[z]))

    class GroupSum:
        def __init__(self, name, source, parts=1):
            self.s1, self.l1, self.s2, self.l2 = (
                getattr(s, p + name) for p in ("s1_", "l1_", "s2_", "l2_")
            )
            self.source, self.parts, self.size = source, parts, OWN // parts
            self.first, self.second = {}, {}

        def block(self, index, at):
            return self.source[pl.ds(pl.multiple_of(index * OWN + at.start, at.size), at.size), :]

        def part(self, i):
            return pl.ds(self.size * i, self.size)

        def over(self, i, body):
            def shifted(at):
                body(pl.ds(pl.multiple_of(self.size * i + at.start, at.size), at.size))

            by_rows(self.size, 32, shifted)

        def send(self):
            for j, yj in enumerate((other_y, yy)):
                for i in range(self.parts):

                    def stage(at):
                        self.s1[j, at, :] = self.block(2 * yj + other_c, at).astype(BF)

                    self.over(i, stage)
                    self.first[j, i] = copy_to(
                        self.s1.at[j, self.part(i)], self.l1.at[j, self.part(i)], core_dev
                    )

        def middle(self):
            for i in range(self.parts):
                self.first[0, i].wait_recv()

                def stage(at):
                    value = self.block(2 * other_y + c, at) + self.l1[0, at, :].astype(F32)
                    self.s2[at, :] = value.astype(BF)

                self.over(i, stage)
                self.second[i] = copy_to(
                    self.s2.at[self.part(i)], self.l2.at[self.part(i)], y_dev
                )

        def wait(self, i=0):
            self.first[1, i].wait_recv()
            self.second[i].wait_recv()

        def value(self, at):
            return (
                self.block(d, at)
                + self.l1[1, at, :].astype(F32)
                + self.l2[at, :].astype(F32)
            )

    class PieceGather:
        def __init__(self):
            self.along_x = {}

        def fan(self, zk, mates_only=False, condition=None):
            copies = [None] if mates_only else []
            for m in (core_d, y_d, far_d) if mates_only else (d, core_d, y_d, far_d):
                copy, _ = prepare(s.qp_s.at[m], s.q_all.at[r, d], (2 * zk + x, m))
                start(copy, condition)
                copies.append(copy)
            return copies

        def slab(self, zk, xk, h):
            return s.q_all.at[2 * zk + xk, pl.ds(pl.multiple_of(2 * (other_y if h else yy), 2), 2)]

        def send(self):
            self.own = self.fan(z, mates_only=True)
            self.two = self.fan(z_two)
            self.near = self.fan(z_near)
            self.mirror = self.fan(z_mirror, condition=inside)
            self.passing = []
            for h in range(2):
                slab = self.slab(z_two, x, h)
                self.passing.append(prepare(slab, slab, near_dev)[0])

        def send_x(self, name, zk, h):
            slab = self.slab(zk, x, h)
            self.along_x[name, h] = copy_to(slab, slab, x_dev)

        def wait(self, copies, h):
            for copy in copies[2 * h : 2 * h + 2]:
                if copy is not None:
                    copy.wait_recv()

        def forward_own(self, h):
            self.wait(self.own, h)
            self.send_x("own", z, h)

        def forward_near(self, h):
            self.wait(self.near, h)
            self.send_x("near", z_near, h)

        def forward_two(self, h):
            self.wait(self.two, h)
            start(self.passing[h], inside)
            self.send_x("two", z_two, h)

        def forward_mirror(self, h):
            pl.when(inside)(lambda: self.wait(self.mirror, h))
            pl.when(outside)(self.passing[h].wait_recv)
            self.send_x("mirror", z_mirror, h)

        def finish(self, name):
            for h in range(2):
                self.along_x[name, h].wait_recv()

    def assemble(landing, count, target, row):
        for k in range(GROUP):
            tiles = [t.astype(F32) for t in tiles_of(landing[k])]
            for t, tile in enumerate(unfold(tiles, count)):
                s.tmp[CHUNK * k : CHUNK * (k + 1), 128 * t : 128 * (t + 1)] = tile
        rows_at(target, row, BLOCK)[...] = s.tmp[:, : 128 * count].astype(BF)

    def assemble_qkv(row):
        assemble(s.q_all.at[row], 5, s.w_qkv, row)

    lane = lane_id((CHUNK, 128))
    eye = row_id((CHUNK, CHUNK)) == lane_id((CHUNK, CHUNK))
    extra = jnp.zeros((CHUNK, 128), F32)
    for k in range(4):
        column = jnp.sum(jnp.where(eye, nrm[k : k + 1, :], 0.0), axis=1, keepdims=True)
        high = column.astype(BF).astype(F32)
        extra = jnp.where(lane == 96 + k, high, extra)
        extra = jnp.where(lane == 100 + k, column - high, extra)
    mask_row = mask[...].astype(F32)
    ones = jnp.sum(mask_row, axis=1, keepdims=True)
    extra = jnp.where((lane == 104) & (row_id((CHUNK, 128)) == 0), ones, extra)

    loads["wq"].wait()
    wq_tiles = tiles_of(wq[...].astype(F32))
    for k in range(GROUP):
        tiles = permute_chunks(wq_tiles, qkv_picks(k))
        tiles[2] = tiles[2] + extra
        for t, tile in enumerate(fold(tiles)):
            s.qp_s[k, :, 128 * t : 128 * (t + 1)] = tile.astype(BF)
    qkv_gather = PieceGather()
    qkv_gather.send()
    s.q_all[r, d] = s.qp_s[d]

    loads["wo"].wait()
    out_gather = Gather(lambda zk, xk: s.wo_l.at[d, xk, zk])
    for t, tile in enumerate(fold(tiles_of(wo[...].astype(F32)))):
        s.wo_l[d, x, z, :, 128 * t : 128 * (t + 1)] = tile.astype(BF)
    out_gather.send_two()
    out_gather.send_mirror()
    out_gather.send_near()
    out_gather.send_x()

    loads["wu"].wait()
    wu_tiles = tiles_of(wu[...].astype(F32))
    for k in range(GROUP):
        for t, tile in enumerate(fold(permute_chunks(wu_tiles, up_picks(k)))):
            s.up_s[k, :, 128 * t : 128 * (t + 1)] = tile.astype(BF)
    up_copies = [copy_to(s.up_s.at[m], s.up_l.at[d], device) for m, device in mates]
    s.up_l[d] = s.up_s[d]

    loads["x"].wait()
    x_gather = GroupGather(lambda i: s.x_all.at[i])
    x_gather.send()

    loads["wd"].wait()
    up_gather = Gather(lambda zk, xk: rows_at(s.w_up, 2 * zk + xk, BLOCK), cross=True)
    downs = [
        Gather(
            lambda zk, xk, h=h: rows_at(s.w_down, 2 * (2 * zk + xk) + h, BLOCK // 2), cross=h == 0
        )
        for h in range(2)
    ]
    diagonal = jnp.where(
        row_id((OWN, OWN)) == lane_id((OWN, OWN)), jnp.broadcast_to(mask_row, (OWN, OWN)), 0.0
    )
    loads["cot"].wait()
    s.c_all[d] = dot(diagonal.astype(BF), cot[...]).astype(BF)
    c_gather = GroupGather(lambda i: s.c_all.at[i])
    c_gather.send()

    def normalize(i):
        def one(at):
            normal, _ = standardize(s.x_all[i, at, :].astype(F32))
            s.normal[pl.ds(pl.multiple_of(OWN * i + at.start, at.size), at.size), :] = normal

        by_rows(OWN, 64, one)

    qkv_gather.forward_own(0)
    qkv_gather.forward_near(0)
    qkv_gather.forward_own(1)
    assemble_qkv(r)
    qkv_gather.forward_two(0)
    qkv_gather.forward_near(1)
    assemble_qkv(2 * z_near + x)
    qkv_gather.forward_two(1)
    out_gather.pass_two()
    assemble_qkv(2 * z_two + x)
    for copy in up_copies:
        copy.wait_recv()
    assemble(s.up_l, 6, s.w_up, r)
    up_gather.send_two()
    up_gather.send_near(True)
    qkv_gather.forward_mirror(0)
    x_gather.relay()
    qkv_gather.forward_mirror(1)
    up_gather.send_near(False)
    up_gather.send_mirror()
    for half in downs:
        half.send_two()
        half.send_near()
    out_gather.send_x(z_two)
    out_gather.forward_near()
    out_gather.forward_mirror()
    up_gather.send_x()
    for half in downs:
        half.send_x()
    columns = [GroupGather(lambda i, xk=xk: s.wo_l.at[i, xk]) for xk in (x, other_x)]
    columns[0].send()
    assemble_qkv(2 * z_mirror + x)
    x_gather.finish()
    for i in range(GROUP):
        normalize(i)
    for name, zk in (("own", z), ("near", z_near), ("two", z_two)):
        qkv_gather.finish(name)
        assemble_qkv(2 * zk + other_x)
    c_gather.relay()
    qkv_gather.finish("mirror")
    assemble_qkv(2 * z_mirror + other_x)

    lane = lane_id((8, 128))
    row = row_id((8, 128))
    pick = jnp.where((lane == 96 + row) | (lane == 100 + row), 1.0, 0.0)
    pick = jnp.where(row < 4, pick, jnp.where((row == 4) & (lane == 104), 1.0, 0.0))
    s.norms[...] = dot(pick.astype(BF), s.w_qkv[:, 256:384], 1, 1)
    total = jnp.sum(s.norms[4:5, :], axis=1, keepdims=True)
    loss_scale = (SEQ * ROWS) / total
    own_weight = dw[d]
    last_weight = dw[GROUP]

    def first_norm(at):
        value = s.normal[at, :] * (1.0 + s.norms[0:1, :]) + s.norms[1:2, :]
        s.h1[at, :] = value.astype(BF)

    by_rows(SEQ, 64, first_norm)

    def project(at):
        value = dot(s.h1[at, :], s.w_qkv[...])
        co, si = cosine[at, :], sine[at, :]
        for left, target in ((0, s.qv), (256, s.kk)):
            a, b = value[:, left : left + 128], value[:, left + 128 : left + 256]
            target[at, :128] = (a * co - b * si).astype(BF)
            target[at, 128:] = (b * co + a * si).astype(BF)
        s.v01[at, :] = value[:, 512:].astype(BF)

    loads["cosine"].wait()
    loads["sine"].wait()
    by_rows(SEQ, 256, project)

    lane2 = lax.div(lax.rem(lane_id((1, 256)), 128), jnp.int32(32))
    head_mask = [jnp.where(lane2 == h, 1.0, 0.0).astype(BF) for h in range(3)]
    tail_mask = jnp.where(lane2 == 3, 1.0, 0.0).astype(BF)
    half_id = lax.div(lane_id((1, 128)), jnp.int32(64))
    half_mask = [jnp.where(half_id == h, 1.0, 0.0).astype(BF) for h in range(2)]
    root = HD**-0.5
    o_gathers = [GroupGather(lambda i, b=b: s.o_l.at[i, b]) for b in range(2)]

    def attend(b):
        rows = slice(QBLOCK * b, QBLOCK * (b + 1))
        keys = QBLOCK * (b + 1)
        query = s.qv[rows, :]
        allowed = row_id((QBLOCK, keys)) + QBLOCK * b >= lane_id((QBLOCK, keys))
        first = jnp.zeros((QBLOCK, 128), F32)
        third = None
        for h in range(3):
            scores = dot(query * head_mask[h], s.kk[:keys, :], 1, 1) * root
            scores = jnp.where(allowed, scores, -1e30)
            raised = jnp.exp(scores - jnp.max(scores, axis=1, keepdims=True))
            probs = raised * (1.0 / jnp.sum(raised, axis=1, keepdims=True))
            s.probs[h, rows, :keys] = probs
            if h < 2:
                first = first + dot(probs.astype(BF), s.v01[:keys, :] * half_mask[h])
            else:
                third = dot(probs.astype(BF), s.qv[:keys, :])
            if b == 1 and h == 0:
                up_gather.forward_two()
                for half in downs:
                    half.send_mirror()
            if b == 1 and h == 1:
                out_gather.finish()
                columns[1].send()
        s.o_l[d, b, :QBLOCK, :] = first.astype(BF)
        lane = lane_id((QBLOCK, 128))
        third = jnp.where(
            lane < 32, pltpu.roll(third[:, :128], 32, 1), pltpu.roll(third[:, 128:], 64, 1)
        )
        lane = lane_id((OWN, 128))
        third = jnp.where(lane < 64, third[:OWN], pltpu.roll(third[OWN:], 64, 1))
        s.o_l[d, b, QBLOCK:, :] = third.astype(BF)
        o_gathers[b].send()

    attend(1)
    columns[0].relay()
    attend(0)
    up_gather.forward_cross()
    columns[1].relay()
    downs[1].forward_near()
    up_gather.forward_mirror()
    for column in columns:
        column.finish()
    for k in range(GROUP):
        for i in range(ROWS):
            tiles = [t.astype(F32) for t in tiles_of(s.wo_l[k, i % 2, i // 2])]
            at = CHUNK * (GROUP * i + k)
            for t, tile in enumerate(unfold(tiles, 6)):
                s.g_out[at : at + CHUNK, 128 * t : 128 * (t + 1)] = tile

    def out_place(head):
        k, h = divmod(head, 3)
        return 128 * k + 64 * h if h < 2 else 512 + 64 * k

    for head in range(HEADS):
        at = out_place(head)
        s.w_out[at : at + 64, :] = s.g_out[64 * head : 64 * head + 64, :].astype(BF)
    s.w_own[...] = jnp.zeros((384, WIDTH), BF)
    third_rows = rows_at(s.w_out.at[pl.ds(512, 256)], d, 64)
    s.w_own[96:128, :] = third_rows[:32, :]
    s.w_own[224:256, :] = third_rows[32:, :]
    s.w_own[256:, :] = rows_at(s.w_out.at[pl.ds(0, 512)], d, 128)[...]
    downs[0].forward_two()
    downs[0].forward_cross()
    o_gathers[1].relay()
    c_gather.finish()

    loads["hist"].wait()
    s.terms[...] = jnp.zeros((8, WIDTH), F32)
    for i in range(GROUP):

        def loss_rows(at, i=i):
            here = pl.ds(pl.multiple_of(OWN * i + at.start, at.size), at.size)
            grad = s.c_all[i, at, :].astype(F32) * loss_scale
            s.dm[here, :] = (last_weight * grad).astype(BF)
            hg_o[here, :] = (own_weight * grad).astype(BF)
            s.terms[...] += sublane_sum(grad * hist[here, :].astype(F32))

        by_rows(OWN, 32, loss_rows)

    store(2)
    downs[1].forward_two()
    for b in (1, 0):
        if b == 0:
            o_gathers[0].relay()
            downs[0].forward_mirror()
        o_gathers[b].finish()
        rows = slice(QBLOCK * b, QBLOCK * (b + 1))
        thirds = []
        for k in range(GROUP):
            s.ob[rows, 128 * k : 128 * (k + 1)] = s.o_l[k, b, :QBLOCK, :]
            thirds.append(s.o_l[k, b, QBLOCK:, :].astype(F32))
        lane = lane_id((OWN, 128))
        for p in range(2):
            even, odd = thirds[2 * p], thirds[2 * p + 1]
            top = jnp.where(lane < 64, even, pltpu.roll(odd, 64, 1))
            low = jnp.where(lane < 64, pltpu.roll(even, 64, 1), odd)
            cols = slice(512 + 128 * p, 640 + 128 * p)
            s.ob[QBLOCK * b : QBLOCK * b + OWN, cols] = top.astype(BF)
            s.ob[QBLOCK * b + OWN : QBLOCK * (b + 1), cols] = low.astype(BF)
        s.y[rows, :] = dot(s.ob[rows, :], s.w_out[...])
        for i in (2 * b, 2 * b + 1):

            def second_norm(at, i=i):
                here = pl.ds(pl.multiple_of(OWN * i + at.start, at.size), at.size)
                value = s.y[here, :] + s.x_all[i, at, :].astype(F32)
                s.y[here, :] = value
                normal, _ = standardize(value)
                value = normal * (1.0 + s.norms[2:3, :]) + s.norms[3:4, :]
                s.h2[here, :] = value.astype(BF)

            by_rows(OWN, 64, second_norm)

    up_gather.arrive_near()
    up_gather.finish()

    def widen(at):
        s.part[at, :] = dot(s.h2[at, :], s.w_up[...])

    by_rows(SEQ, 256, widen)

    rate = 0.7978845608028654

    def gate(at):
        u = s.part[at, :]
        bend = jnp.tanh(rate * (u + 0.044715 * u * u * u))
        s.act[at, :] = (0.5 * u * (1.0 + bend)).astype(BF)
        s.slope[at, :] = bend

    by_rows(SEQ, 32, gate)
    downs[1].forward_mirror()

    def gate_slope(at):
        u, bend = s.part[at, :], s.slope[at, :]
        inner = rate * (1.0 + 3 * 0.044715 * u * u)
        s.slope[at, :] = 0.5 * (1.0 + bend) + 0.5 * u * (1.0 - bend * bend) * inner

    def block_of(ref, shift=0):
        def block(index, at):
            start = pl.multiple_of(index * BLOCK + shift + at.start, at.size)
            return ref[pl.ds(start, at.size), :]

        return block

    for i in range(3):
        cols = slice(QBLOCK * i, QBLOCK * (i + 1))
        s.g_down[cols, :] = dot(s.act[:, cols], s.dm[...], 0, 0)
    down_sum = RowSum("down", s.f_down, block_of(s.g_down), 16, True)
    down_sum.send()
    by_rows(SEQ, 32, gate_slope)
    downs[0].arrive_near()
    for half in downs:
        half.finish()

    def narrow(at):
        value = dot(s.dm[at, :], s.w_down[...], 1, 1)
        s.du[at, :] = (value * s.slope[at, :]).astype(BF)

    by_rows(SEQ, 256, narrow)

    def second_back(at):
        s.part[at, :] = dot(s.du[at, :], s.w_up[...], 1, 1)

    by_rows(SEQ, 256, second_back)
    mid_sum = GroupSum("mid", s.part, 4)
    mid_sum.send()

    for i in range(3):
        cols = slice(QBLOCK * i, QBLOCK * (i + 1))
        s.g_up[cols, :] = dot(s.h2[:, cols], s.du[...], 0, 0)
    up_sum = RowSum("up", s.f_up, block_of(s.g_up), 16, True)
    mid_sum.middle()
    down_sum.send_mirror()
    up_sum.send()

    def block_out(at):
        value = dot(s.act[at, :], s.w_down[...])
        s.part2[at, :] = value

    s.terms2[...] = jnp.zeros((8, WIDTH), F32)
    by_rows(SEQ, 256, block_out)
    for i in range(GROUP):

        def mix(at, i=i):
            here = pl.ds(pl.multiple_of(OWN * i + at.start, at.size), at.size)
            value = s.part2[here, :]
            loss = s.c_all[i, at, :].astype(F32) * loss_scale
            s.terms2[...] += sublane_sum(loss * value)
            s.part2[here, :] = own_weight * hist[here, :].astype(F32) + last_weight * value

        by_rows(OWN, 32, mix)
    mix_sum = GroupSum("mix", s.part2)
    mix_sum.send()
    s.t0[...] = jnp.zeros((8, WIDTH), F32)

    def second_norm_back(at):
        here = pl.ds(pl.multiple_of(OWN * d + at.start, at.size), at.size)
        grad = mid_sum.value(at)
        value = s.y[here, :]
        normal, scale = standardize(value)
        loss = s.c_all[d, at, :].astype(F32) * loss_scale
        back = last_weight * loss + norm_back(grad, s.norms[2:3, :], normal, scale)
        s.dy[at, :] = back
        s.dyb[d, at, :] = back.astype(BF)
        s.t0[2:3, :] += jnp.sum(grad * normal, axis=0, keepdims=True)
        s.t0[3:4, :] += jnp.sum(grad, axis=0, keepdims=True)
        s.terms2[...] += sublane_sum(loss * value)

    dy_gathers = []
    for i in range(4):
        mid_sum.wait(i)
        mid_sum.over(i, second_norm_back)
        dy_gathers.append(GroupGather(lambda j, i=i: s.dyb.at[j, mid_sum.part(i)]))
        dy_gathers[i].send()

    down_sum.send_two()
    down_sum.send_own()
    mix_sum.middle()
    lane = lane_id((8, 128))
    own_term = jnp.sum(jnp.sum(s.terms[...], axis=0, keepdims=True), axis=1, keepdims=True)
    last_term = jnp.sum(jnp.sum(s.terms2[...], axis=0, keepdims=True), axis=1, keepdims=True)
    s.u0[...] = jnp.where(lane == d, own_term, jnp.where(lane == GROUP, last_term, 0.0))
    depth_x = copy_to(s.u0, s.u1, x_dev)
    for i, one in enumerate(dy_gathers):
        one.relay()
        if i == 0:
            up_sum.send_mirror()
    for one in dy_gathers:
        one.finish()
    up_sum.send_own()
    down_sum.send_near()

    by_group = s.dyb[...].reshape(SEQ, WIDTH)

    s.dob[...] = dot(by_group, s.w_own[...], 1, 1).astype(BF)
    for b in range(2):
        rows = slice(QBLOCK * b, QBLOCK * (b + 1))
        keys = QBLOCK * (b + 1)
        query = s.qv[rows, :]
        dq = jnp.zeros((QBLOCK, 256), F32)
        for h in range(3):
            probs = s.probs[h, rows, :keys]
            if h < 2:
                grad = s.dob[rows, 256:] * half_mask[h]
                dp = dot(grad, s.v01[:keys, :], 1, 1)
            else:
                grad = s.dob[rows, :256]
                dp = dot(grad, s.qv[:keys, :], 1, 1)
            delta = jnp.sum(dp * probs, axis=1, keepdims=True)
            ds = (probs * (dp - delta)).astype(BF)
            dq = dq + dot(ds, s.kk[:keys, :] * head_mask[h])
            dk = dot(ds, query * head_mask[h], 0, 0) * root
            dv = dot(probs.astype(BF), grad, 0, 0)
            cols = slice(256, 384) if h < 2 else slice(0, 256)
            if b == 0:
                old, new = slice(0, QBLOCK), None
            else:
                old, new = slice(0, QBLOCK), slice(QBLOCK, SEQ)
            if h == 0 and b == 0:
                s.dk[old, :] = dk[:QBLOCK]
            else:
                s.dk[old, :] += dk[:QBLOCK]
            if b == 0 and h != 1:
                s.dv[old, cols] = dv[:QBLOCK]
            else:
                s.dv[old, cols] += dv[:QBLOCK]
            if new is not None:
                if h == 0:
                    s.dk[new, :] = dk[QBLOCK:]
                else:
                    s.dk[new, :] += dk[QBLOCK:]
                if h != 1:
                    s.dv[new, cols] = dv[QBLOCK:]
                else:
                    s.dv[new, cols] += dv[QBLOCK:]
        s.dq[rows, :] = dq * root
        if b == 0:
            up_sum.send_two()
            up_sum.send_near()

    def turn_back(at):
        co, si = cosine[at, :], sine[at, :]
        for left, source in ((0, s.dq), (256, s.dk)):
            a, b = source[at, :128], source[at, 128:]
            first, second = a * co + b * si, b * co - a * si
            if left == 0:
                first, second = first + s.dv[at, :128], second + s.dv[at, 128:256]
            s.dqkv[at, left : left + 128] = first.astype(BF)
            s.dqkv[at, left + 128 : left + 256] = second.astype(BF)
        s.dqkv[at, 512:] = s.dv[at, 256:].astype(BF)

    by_rows(SEQ, 64, turn_back)
    for i in range(3):
        cols = slice(QBLOCK * i, QBLOCK * (i + 1))
        s.g_qkv[cols, :] = dot(s.h1[:, cols], s.dqkv[...], 0, 0)
    qkv_arrivals = reserve(16)
    sums = [SpreadSum(h, qkv_arrivals) for h in range(2)]
    for one in sums:
        one.send_x("mirror", z_mirror)
        one.send_crossing()
    for one in sums:
        one.send_x("two", z_two)
    depth_x.wait_recv()
    s.uz[z] = s.u0[...] + s.u1[...]
    depth_z = [
        copy_to(s.uz.at[z], s.uz.at[z], device) for device in (two_dev, mirror_dev, near_dev)
    ]

    def first_back(at):
        s.part[at, :] = dot(s.dqkv[at, :], s.w_qkv[...], 1, 1)

    by_rows(SEQ, 256, first_back)
    in_sum = GroupSum("in", s.part)
    in_sum.send()
    s.gain_sum[...] = jnp.zeros((8, WIDTH), F32)
    s.shift_sum[...] = jnp.zeros((8, WIDTH), F32)

    def first_norm_sums(at):
        grad = s.part[at, :]
        s.gain_sum[...] += sublane_sum(grad * s.normal[at, :])
        s.shift_sum[...] += sublane_sum(grad)

    by_rows(SEQ, 32, first_norm_sums)
    s.t0[0:1, :] = jnp.sum(s.gain_sum[...], axis=0, keepdims=True)
    s.t0[1:2, :] = jnp.sum(s.shift_sum[...], axis=0, keepdims=True)
    s.td[d] = s.t0[...]
    norm_copies = [copy_to(s.td.at[d], s.td.at[d], device) for m, device in mates]
    in_sum.middle()
    for p in range(3):
        cols = slice(QBLOCK * p, QBLOCK * (p + 1))
        value = dot(s.ob[:, cols], s.dyb[...].reshape(SEQ, WIDTH), 0, 0)
        for i in range(4):
            place = QBLOCK * p + 64 * i
            for head in range(HEADS):
                if out_place(head) == place:
                    s.g_out[64 * head : 64 * head + 64, :] = value[64 * i : 64 * i + 64]

    for one in sums:
        one.send_mirror()
    for copy in norm_copies:
        copy.wait_recv()
    value = (s.td[0] + s.td[1]) + (s.td[2] + s.td[3])
    value = pltpu.roll(value, lax.rem(WIDTH - CHUNK * d, WIDTH), 1)
    for i in range(ROWS):
        shift = (WIDTH - BLOCK * i) % WIDTH
        shifted = pltpu.roll(value, shift, 1) if shift else value
        s.ext[i] = jnp.concatenate([shifted[:, :128], jnp.zeros((8, 128), F32)], axis=0)

    def out_block(index, at):
        start_row = pl.multiple_of((GROUP * index + d) * CHUNK, 8)
        tiles = tiles_of(s.g_out[pl.ds(start_row, CHUNK), :])
        return jnp.concatenate(fold(tiles) + [s.ext[index]], axis=1)

    out_sum = RowSum("out", s.f_out, out_block, 16, False)
    out_sum.send()
    down_sum.finish()
    gd_o[...] = s.f_down[...]
    store(6)
    mix_sum.wait()

    def write_out(at):
        here = pl.ds(pl.multiple_of(OWN * d + at.start, at.size), at.size)
        out_o[at, :] = (mix_sum.value(at) + last_weight * s.y[here, :]).astype(BF)

    by_rows(OWN, 32, write_out)
    store(0)

    def spread(total, staged, landing):
        copies = []
        for m, device in mates:
            rows = total[pl.ds(pl.multiple_of(CHUNK * m, CHUNK), CHUNK), :]
            for t, tile in enumerate(fold(tiles_of(rows))):
                staged[m, :, 128 * t : 128 * (t + 1)] = tile.astype(BF)
            copies.append(copy_to(staged.at[m], landing.at[d], device))
        rows = total[pl.ds(pl.multiple_of(CHUNK * d, CHUNK), CHUNK), :]
        for t, tile in enumerate(fold(tiles_of(rows))):
            landing[d, :, 128 * t : 128 * (t + 1)] = tile.astype(BF)
        return copies

    def collect(copies, landing, count, back, target):
        for copy in copies:
            copy.wait_recv()
        tiles = []
        for k in range(GROUP):
            tiles += unfold([t.astype(F32) for t in tiles_of(landing[k])], count)
        for t, tile in enumerate(permute_chunks(tiles, back)):
            target[:, 128 * t : 128 * (t + 1)] = tile

    up_sum.finish()
    up_spread = spread(s.f_up, s.b_up, s.a_up)
    for one in sums:
        one.send_two()
    for one in sums:
        one.send_near()
    for one in sums:
        one.send_own()
    in_sum.wait()

    def first_norm_back(at):
        grad = in_sum.value(at)
        normal, scale = standardize(s.x_all[d, at, :].astype(F32))
        back = norm_back(grad, s.norms[0:1, :], normal, scale)
        ig_o[at, :] = (s.dy[at, :] + back).astype(BF)

    by_rows(OWN, 32, first_norm_back)
    store(1)
    out_sum.send_mirror()
    for copy in depth_z:
        copy.wait_recv()
    s.ud[d] = (s.uz[0] + s.uz[1]) + (s.uz[2] + s.uz[3])
    depth_d = [copy_to(s.ud.at[d], s.ud.at[d], device) for m, device in mates]
    out_sum.send_near()
    for one in sums:
        one.keep_own()
    collect(up_spread, s.a_up, 6, UP_BACK, gu_o)
    store(5)
    out_sum.send_two()
    for copy in depth_d:
        copy.wait_recv()
    dg_o[...] = (s.ud[0] + s.ud[1]) + (s.ud[2] + s.ud[3])

    def arrived(slot, k):
        return pltpu.make_async_remote_copy(
            src_ref=s.fin.at[slot, k],
            dst_ref=s.fin.at[slot, k],
            send_sem=send_sems.at[0],
            recv_sem=recv_sems.at[qkv_arrivals + GROUP * slot + k],
            device_id=x_dev,
            device_id_type=MESH,
        )

    for k in range(GROUP):
        pl.when(d != k)(arrived(3, k).wait_recv)
        arrived(1, k).wait_recv()
        arrived(0, k).wait_recv()
        s.q_sum[k] = (
            s.fin[3, k].astype(F32) + s.fin[1, k].astype(F32) + s.fin[0, k].astype(F32)
        )

    @pl.when(inside)
    def _():
        for k in range(GROUP):
            arrived(2, k).wait_recv()
            s.q_sum[k] += s.fin[2, k].astype(F32)

    tiles = []
    for k in range(GROUP):
        tiles += unfold(tiles_of(s.q_sum[k]), 5)
    for t, tile in enumerate(permute_chunks(tiles, QKV_BACK)):
        gq_o[:, 128 * t : 128 * (t + 1)] = tile
    store(3)
    out_sum.finish()
    for t, tile in enumerate(unfold(tiles_of(s.f_out[:, :1152]), 6)):
        go_o[:, 128 * t : 128 * (t + 1)] = tile
    ng_o[...] = s.f_out[:8, 1152:]
    store(4)
    for copy in stores:
        copy.wait()
    for copy, condition in sent:
        if condition is None:
            copy.wait_send()
        else:
            pl.when(condition)(copy.wait_send)


def finish_kernel(*refs):
    count = N_OUT - 2
    ins, refs = refs[:count], refs[count:]
    (norm, depth), refs = refs[:2], refs[2:]
    outs, (norm_o, depth_o), refs = refs[:count], refs[count : count + 2], refs[count + 2 :]
    held, sems = refs[:-1], refs[-1]
    first = [pltpu.make_async_copy(a, b, sems.at[i]) for i, (a, b) in enumerate(zip(ins, held))]
    for copy in first:
        copy.start()
    norm_o[...] = norm[:4, :CHUNK]
    depth_o[...] = depth[:1, : GROUP + 1]
    second = []
    for i, copy in enumerate(first):
        copy.wait()
        second.append(pltpu.make_async_copy(held[i], outs[i], sems.at[count + i]))
        second[i].start()
    for copy in second:
        copy.wait()


def fused(
    block_input,
    history,
    cotangent,
    token_mask,
    qkv_weight,
    out_weight,
    up_weight,
    down_weight,
    norm_params,
    depth_weights,
):
    cosine, sine = tables()
    vmem = pl.BlockSpec(memory_space=pltpu.VMEM)
    smem = pl.BlockSpec(memory_space=pltpu.SMEM)
    hbm = pl.BlockSpec(memory_space=pltpu.HBM)
    shape = jax.ShapeDtypeStruct
    shapes = (
        shape((OWN, WIDTH), BF),
        shape((OWN, WIDTH), BF),
        shape((SEQ, WIDTH), BF),
        shape((CHUNK, 3 * WIDTH), F32),
        shape((CHUNK, WIDTH), F32),
        shape((CHUNK, 4 * WIDTH), F32),
        shape((BLOCK, WIDTH), F32),
        shape((8, 128), F32),
        shape((8, 128), F32),
    )
    outs = pl.pallas_call(
        fused_kernel,
        out_shape=shapes,
        in_specs=[hbm] * 3 + [vmem] + [hbm] * 4 + [vmem, smem] + [hbm] * 2,
        out_specs=[hbm] * 7 + [vmem] * 2,
        scratch_shapes=[pltpu.VMEM(dims, kind) for dims, kind in SCRATCH.values()]
        + [pltpu.SemaphoreType.DMA((N_SEMS,))] * 2
        + [pltpu.SemaphoreType.DMA((16,))],
        compiler_params=pltpu.CompilerParams(
            collective_id=0, has_side_effects=True, vmem_limit_bytes=VMEM_MIB * 2**20
        ),
        cost_estimate=pl.CostEstimate(flops=12 * 10**9, bytes_accessed=4 * 10**6, transcendentals=10**6),
    )(
        block_input,
        history.reshape(SEQ, WIDTH),
        cotangent,
        token_mask.reshape(1, OWN),
        qkv_weight,
        out_weight,
        up_weight,
        down_weight,
        norm_params,
        depth_weights,
        jnp.asarray(cosine),
        jnp.asarray(sine),
    )
    held = pl.pallas_call(
        finish_kernel,
        out_shape=shapes[:7] + (shape((4, CHUNK), F32), shape((1, GROUP + 1), F32)),
        in_specs=[hbm] * 7 + [vmem] * 2,
        out_specs=[hbm] * 7 + [vmem] * 2,
        scratch_shapes=[pltpu.VMEM(one.shape, one.dtype) for one in shapes[:7]]
        + [pltpu.SemaphoreType.DMA((14,))],
        compiler_params=pltpu.CompilerParams(vmem_limit_bytes=VMEM_MIB * 2**20),
    )(*outs)
    out, input_grad, history_grad, *grads, g_depth = held
    return (out, input_grad, history_grad.reshape(1, SEQ, WIDTH), *grads, g_depth.reshape(GROUP + 1))


def fits(mesh, block_input, history, up_weight):
    devices = ROWS * GROUP
    return (
        mesh.shape["rows"] == ROWS
        and mesh.shape["depth"] == GROUP
        and block_input.shape == (OWN * devices, WIDTH)
        and history.shape[0] == GROUP
        and up_weight.shape == (WIDTH, 4 * WIDTH)
    )


def solution(mesh):
    weights = P(("rows", "depth"), None)
    in_specs = (
        weights,
        P("depth", "rows", None),
        weights,
        P(("rows", "depth")),
        weights,
        weights,
        weights,
        weights,
        P(None, ("rows", "depth")),
        P(),
    )
    out_specs = (
        weights,
        weights,
        P("depth", "rows", None),
        weights,
        weights,
        weights,
        weights,
        P(None, ("rows", "depth")),
        P(),
    )

    def run(*args):
        body = fused if fits(mesh, args[0], args[1], args[6]) else local
        return jax.shard_map(
            body, mesh=mesh, in_specs=in_specs, out_specs=out_specs, check_vma=False
        )(*args)

    return run
```

```python
import functools

import jax
import jax.numpy as jnp
import numpy as np
from jax import lax
from jax.experimental import pallas as pl
from jax.experimental.pallas import tpu as pltpu
from jax.sharding import PartitionSpec as P

HEADS = 12
HD = 64


def norm_rows(value, gain, shift):
    center = value - jnp.mean(value, axis=-1, keepdims=True)
    spread = jnp.mean(center * center, axis=-1, keepdims=True)
    return center * lax.rsqrt(spread + 1e-05) * (1.0 + gain) + shift


def rotate(value, place, sign):
    half = value.shape[-1] // 2
    freq = 10000.0 ** (-jnp.arange(half, dtype=jnp.float32) / half)
    angle = place.astype(jnp.float32)[:, None] * freq[None, :]
    cosine = jnp.cos(angle)[:, None, :]
    sine = jnp.sin(angle)[:, None, :] * sign
    first = value[..., :half]
    second = value[..., half:]
    return jnp.concatenate(
        [first * cosine - second * sine, second * cosine + first * sine], axis=-1
    )


def block_scores(query, key_block, start, query_place, scale):
    block_len = key_block.shape[0]
    scores = (
        jnp.einsum("qhd,khd->hqk", query, key_block, preferred_element_type=jnp.float32) * scale
    )
    key_place = start + jnp.arange(block_len, dtype=jnp.int32)
    allowed = query_place[:, None] >= key_place[None, :]
    return (scores, allowed)


def local(
    block_input,
    history,
    cotangent,
    token_mask,
    qkv_weight,
    out_weight,
    up_weight,
    down_weight,
    norm_params,
    depth_weights,
):
    rows_tok, width = block_input.shape
    depth_count = lax.axis_size("depth")
    device_count = lax.axis_size("rows") * depth_count
    place_depth = lax.axis_index("depth")
    heads = HEADS
    head_size = HD
    scale = head_size ** (-0.5)
    seq_len = rows_tok * depth_count
    slot_count = history.shape[0]
    hist_total = slot_count * depth_count
    wide_qkv, wide_out, wide_up, wide_down, wide_norms = (
        lax.all_gather(qkv_weight, ("rows", "depth"), axis=0, tiled=True),
        lax.all_gather(out_weight, ("rows", "depth"), axis=0, tiled=True),
        lax.all_gather(up_weight, ("rows", "depth"), axis=0, tiled=True),
        lax.all_gather(down_weight, ("rows", "depth"), axis=0, tiled=True),
        lax.all_gather(
            norm_params.astype(jnp.bfloat16), ("rows", "depth"), axis=1, tiled=True
        ).astype(norm_params.dtype),
    )
    total = lax.psum(jnp.sum(token_mask), ("rows", "depth")).astype(jnp.float32)
    loss_scale = rows_tok * device_count / total
    float_input = block_input.astype(jnp.float32)
    place = place_depth * rows_tok + jnp.arange(rows_tok, dtype=jnp.int32)
    first = norm_rows(float_input, wide_norms[0], wide_norms[1]).astype(jnp.bfloat16)
    projected = jnp.dot(first, wide_qkv, preferred_element_type=jnp.float32)
    query = rotate(projected[:, :width].reshape(rows_tok, heads, head_size), place, 1.0).astype(
        jnp.bfloat16
    )
    keys = rotate(projected[:, width : 2 * width].reshape(rows_tok, heads, head_size), place, 1.0)
    keys = keys.astype(jnp.bfloat16).reshape(rows_tok, width)
    values = projected[:, 2 * width :].astype(jnp.bfloat16)
    all_keys, all_values = (
        lax.all_gather(keys, "depth", axis=0, tiled=True),
        lax.all_gather(values, "depth", axis=0, tiled=True),
    )
    block_len = min(512, seq_len)
    block_count = seq_len // block_len
    key_blocks = all_keys.reshape(block_count, block_len, heads, head_size)
    value_blocks = all_values.reshape(block_count, block_len, heads, head_size)
    starts = jnp.arange(block_count, dtype=jnp.int32) * block_len

    def peak_step(carry, item):
        peak, weight_sum = carry
        key_block, value_block, start = item
        scores, allowed = block_scores(query, key_block, start, place, scale)
        scores = jnp.where(allowed[None], scores, -1e30)
        new_peak = jnp.maximum(peak, jnp.max(scores, axis=-1))
        weight_sum = weight_sum * jnp.exp(peak - new_peak) + jnp.sum(
            jnp.exp(scores - new_peak[..., None]), axis=-1
        )
        return ((new_peak, weight_sum), None)

    start_carry = (
        jnp.full((heads, rows_tok), -1e30, jnp.float32),
        jnp.zeros((heads, rows_tok), jnp.float32),
    )
    (peak, weight_sum), _ = lax.scan(peak_step, start_carry, (key_blocks, value_blocks, starts))
    log_total = peak + jnp.log(weight_sum)

    def value_step(running, item):
        key_block, value_block, start = item
        scores, allowed = block_scores(query, key_block, start, place, scale)
        probs = jnp.where(allowed[None], jnp.exp(scores - log_total[..., None]), 0.0)
        running = running + jnp.einsum(
            "hqk,khd->qhd",
            probs.astype(jnp.bfloat16),
            value_block,
            preferred_element_type=jnp.float32,
        )
        return (running, None)

    running, _ = lax.scan(
        value_step,
        jnp.zeros((rows_tok, heads, head_size), jnp.float32),
        (key_blocks, value_blocks, starts),
    )
    mixed = running.reshape(rows_tok, width)
    mixed_low = mixed.astype(jnp.bfloat16)
    middle = float_input + jnp.dot(mixed_low, wide_out, preferred_element_type=jnp.float32)
    second = norm_rows(middle, wide_norms[2], wide_norms[3]).astype(jnp.bfloat16)
    upper = jnp.dot(second, wide_up, preferred_element_type=jnp.float32)
    active = jax.nn.gelu(upper).astype(jnp.bfloat16)
    block_out = middle + jnp.dot(active, wide_down, preferred_element_type=jnp.float32)
    own_alpha = lax.dynamic_slice_in_dim(depth_weights, place_depth * slot_count, slot_count)
    partial_mix = jnp.sum(own_alpha[:, None, None] * history.astype(jnp.float32), axis=0)
    mixture = lax.psum_scatter(
        partial_mix.astype(jnp.bfloat16), "depth", scatter_dimension=0, tiled=True
    ).astype(jnp.float32)
    output = (mixture + depth_weights[hist_total] * block_out).astype(jnp.bfloat16)
    grad_out = token_mask.astype(jnp.float32)[:, None] * cotangent.astype(jnp.float32) * loss_scale
    last_term = jnp.sum(grad_out * block_out)
    index_all = jnp.arange(hist_total + 1, dtype=jnp.int32)
    grad_rows = lax.all_gather(grad_out.astype(jnp.bfloat16), "depth", axis=0, tiled=True).astype(
        grad_out.dtype
    )
    history_grad = (own_alpha[:, None, None] * grad_rows[None]).astype(jnp.bfloat16)
    hist_terms = jnp.sum(history.astype(jnp.float32) * grad_rows[None], axis=(1, 2))
    own_index = place_depth * slot_count + jnp.arange(slot_count, dtype=jnp.int32)
    alpha_terms = jnp.sum(
        jnp.where(index_all[None, :] == own_index[:, None], hist_terms[:, None], 0.0), axis=0
    )
    alpha_terms = alpha_terms + jnp.where(index_all == hist_total, last_term, 0.0)
    depth_gradient = lax.psum(alpha_terms, ("rows", "depth"))
    wide_qkv, wide_out, wide_up, wide_down, wide_norms = (
        lax.all_gather(qkv_weight, ("rows", "depth"), axis=0, tiled=True),
        lax.all_gather(out_weight, ("rows", "depth"), axis=0, tiled=True),
        lax.all_gather(up_weight, ("rows", "depth"), axis=0, tiled=True),
        lax.all_gather(down_weight, ("rows", "depth"), axis=0, tiled=True),
        lax.all_gather(
            norm_params.astype(jnp.bfloat16), ("rows", "depth"), axis=1, tiled=True
        ).astype(norm_params.dtype),
    )
    block_grad = depth_weights[hist_total] * grad_out
    lower_grad = block_grad.astype(jnp.bfloat16)
    down_gradient = jnp.dot(active.T, lower_grad, preferred_element_type=jnp.float32)
    active_grad = jnp.dot(lower_grad, wide_down.T, preferred_element_type=jnp.float32)
    _, gelu_pull = jax.vjp(jax.nn.gelu, upper)
    upper_grad = gelu_pull(active_grad)[0].astype(jnp.bfloat16)
    up_gradient = jnp.dot(second.T, upper_grad, preferred_element_type=jnp.float32)
    second_grad = jnp.dot(upper_grad, wide_up.T, preferred_element_type=jnp.float32)
    _, norm_pull = jax.vjp(norm_rows, middle, wide_norms[2], wide_norms[3])
    middle_part, gain_two, shift_two = norm_pull(second_grad)
    middle_grad = block_grad + middle_part
    branch_grad = middle_grad.astype(jnp.bfloat16)
    out_gradient = jnp.dot(mixed_low.T, branch_grad, preferred_element_type=jnp.float32)
    mixed_grad = jnp.dot(branch_grad, wide_out.T, preferred_element_type=jnp.float32).astype(
        jnp.bfloat16
    )
    delta = jnp.sum(
        (mixed_grad.astype(jnp.float32) * mixed).reshape(rows_tok, heads, head_size), axis=-1
    ).T
    mixed_heads = mixed_grad.reshape(rows_tok, heads, head_size)

    def score_grads(
        query_rows, grad_rows, lse_rows, delta_rows, key_block, value_block, query_place, start
    ):
        scores, allowed = block_scores(query_rows, key_block, start, query_place, scale)
        probs = jnp.where(allowed[None], jnp.exp(scores - lse_rows[..., None]), 0.0)
        prob_grad = jnp.einsum(
            "qhd,khd->hqk", grad_rows, value_block, preferred_element_type=jnp.float32
        )
        score_grad = (probs * (prob_grad - delta_rows[..., None])).astype(jnp.bfloat16)
        return (probs, score_grad)

    def grad_step(query_total, item):
        key_block, value_block, start = item
        probs, score_grad = score_grads(
            query, mixed_heads, log_total, delta, key_block, value_block, place, start
        )
        query_total = (
            query_total
            + jnp.einsum("hqk,khd->qhd", score_grad, key_block, preferred_element_type=jnp.float32)
            * scale
        )
        key_part = (
            jnp.einsum("hqk,qhd->khd", score_grad, query, preferred_element_type=jnp.float32)
            * scale
        )
        value_part = jnp.einsum(
            "hqk,qhd->khd",
            probs.astype(jnp.bfloat16),
            mixed_heads,
            preferred_element_type=jnp.float32,
        )
        return (query_total, (key_part, value_part))

    query_total, (key_parts, value_parts) = lax.scan(
        grad_step,
        jnp.zeros((rows_tok, heads, head_size), jnp.float32),
        (key_blocks, value_blocks, starts),
    )
    key_sum, value_sum = (
        lax.psum_scatter(
            key_parts.reshape(seq_len, width).astype(jnp.bfloat16),
            "depth",
            scatter_dimension=0,
            tiled=True,
        ).astype(jnp.float32),
        lax.psum_scatter(
            value_parts.reshape(seq_len, width).astype(jnp.bfloat16),
            "depth",
            scatter_dimension=0,
            tiled=True,
        ).astype(jnp.float32),
    )
    query_grad = rotate(query_total, place, -1.0).reshape(rows_tok, width)
    key_grad = rotate(key_sum.reshape(rows_tok, heads, head_size), place, -1.0).reshape(
        rows_tok, width
    )
    projected_grad = jnp.concatenate([query_grad, key_grad, value_sum], axis=1).astype(jnp.bfloat16)
    qkv_gradient = jnp.dot(first.T, projected_grad, preferred_element_type=jnp.float32)
    first_grad = jnp.dot(projected_grad, wide_qkv.T, preferred_element_type=jnp.float32)
    _, first_pull = jax.vjp(norm_rows, float_input, wide_norms[0], wide_norms[1])
    input_part, gain_one, shift_one = first_pull(first_grad)
    input_grad = (middle_grad + input_part).astype(jnp.bfloat16)
    norms_full = jnp.stack([gain_one, shift_one, gain_two, shift_two])
    qkv_gradient, out_gradient, up_gradient, down_gradient, norm_gradient = (
        lax.psum_scatter(qkv_gradient, ("rows", "depth"), scatter_dimension=0, tiled=True),
        lax.psum_scatter(out_gradient, ("rows", "depth"), scatter_dimension=0, tiled=True),
        lax.psum_scatter(up_gradient, ("rows", "depth"), scatter_dimension=0, tiled=True),
        lax.psum_scatter(down_gradient, ("rows", "depth"), scatter_dimension=0, tiled=True),
        lax.psum_scatter(norms_full, ("rows", "depth"), scatter_dimension=1, tiled=True),
    )
    return (
        output,
        input_grad,
        history_grad,
        qkv_gradient,
        out_gradient,
        up_gradient,
        down_gradient,
        norm_gradient,
        depth_gradient,
    )

SEQ = 512
OWN = 128
WIDTH = 768
ROWS = 8
GROUP = 4
PACK = 640
BLOCK = WIDTH // ROWS
CHUNK = BLOCK // GROUP
QBLOCK = 256
BF = jnp.bfloat16
F32 = jnp.float32
MESH = pl.DeviceIdType.MESH


def dot(a, b, ca=1, cb=0):
    return lax.dot_general(a, b, (((ca,), (cb,)), ((), ())), preferred_element_type=F32)


def lane_id(shape):
    return lax.broadcasted_iota(jnp.int32, shape, len(shape) - 1)


def row_id(shape):
    return lax.broadcasted_iota(jnp.int32, shape, len(shape) - 2)


def tiles_of(value):
    return [value[:, 128 * i : 128 * (i + 1)] for i in range(value.shape[1] // 128)]


def permute_chunks(tiles, picks):
    group = lax.div(lane_id(tiles[0].shape), jnp.int32(32))
    out = []
    for t in range(len(picks) // 4):
        total, rolled = jnp.zeros_like(tiles[0]), {}
        for j in range(4):
            pick = picks[4 * t + j]
            if pick is None:
                continue
            source, place = divmod(pick, 4)
            shift = (j - place) * 32 % 128
            if (source, shift) not in rolled:
                value = tiles[source]
                rolled[source, shift] = pltpu.roll(value, shift, 1) if shift else value
            total = jnp.where(group == j, rolled[source, shift], total)
        out.append(total)
    return out


def fold(tiles):
    half = (len(tiles) + 1) // 2
    low = [t[16:] for t in tiles]
    if len(low) % 2:
        low.append(jnp.zeros_like(low[0]))
    return [t[:16] for t in tiles] + [
        jnp.concatenate([low[i], low[half + i]], axis=0) for i in range(half)
    ]


def unfold(tiles, count):
    half = (count + 1) // 2
    rest = tiles[count:]
    low = [rest[i][:8] for i in range(half)] + [rest[i][8:] for i in range(half)]
    return [jnp.concatenate([tiles[i], low[i]], axis=0) for i in range(count)]


def qkv_chunk(block, head, half):
    return 24 * block + 2 * head + half


def qkv_picks(d):
    heads = [3 * d + i for i in range(3)]
    picks = []
    for block in range(2):
        for half in range(2):
            picks += [qkv_chunk(block, h, half) for h in heads]
            picks.append(qkv_chunk(2, heads[2], half) if block == 0 else None)
    return picks + [qkv_chunk(2, h, half) for h in heads[:2] for half in range(2)]


def up_picks(d):
    return [3 * (GROUP * r + d) + j for r in range(ROWS) for j in range(3)]


def inverse_picks(per_device, count, tiles_each):
    back = [None] * count
    for d, picks in enumerate(per_device):
        for place, pick in enumerate(picks):
            if pick is not None:
                back[pick] = 4 * tiles_each * d + place
    return back


QKV_BACK = inverse_picks([qkv_picks(d) for d in range(GROUP)], 72, 5)
UP_BACK = inverse_picks([up_picks(d) for d in range(GROUP)], 96, 6)


def tables():
    half = HD // 2
    freq = np.float32(10000.0) ** (-np.arange(half, dtype=np.float32) / np.float32(half))
    angle = (np.arange(SEQ, dtype=np.float32)[:, None] * freq[None, :]).astype(np.float32)
    angle = angle.astype(np.float64)
    cosine, sine = np.ones((SEQ, 128), np.float32), np.zeros((SEQ, 128), np.float32)
    cosine[:, :96] = np.tile(np.cos(angle), (1, 3))
    sine[:, :96] = np.tile(np.sin(angle), (1, 3))
    return cosine, sine


def standardize(value):
    center = value - jnp.mean(value, axis=-1, keepdims=True)
    spread = jnp.mean(center * center, axis=-1, keepdims=True)
    scale = lax.rsqrt(spread + 1e-05)
    return center * scale, scale


def norm_back(grad, gain, normal, scale):
    part = grad * (1.0 + gain)
    inner = jnp.mean(part, axis=-1, keepdims=True)
    along = jnp.mean(part * normal, axis=-1, keepdims=True)
    return scale * (part - inner - normal * along)


def sublane_sum(value):
    return jnp.sum(value.reshape(value.shape[0] // 8, 8, value.shape[1]), axis=0)


SCRATCH = dict(
    hist=((SEQ, WIDTH), BF),
    cot=((OWN, WIDTH), BF),
    wq=((CHUNK, 3 * WIDTH), BF),
    wo=((CHUNK, WIDTH), BF),
    wu=((CHUNK, 4 * WIDTH), BF),
    cosine=((SEQ, 128), F32),
    sine=((SEQ, 128), F32),
    r_0=((OWN, WIDTH), BF),
    r_1=((OWN, WIDTH), BF),
    r_2=((SEQ, WIDTH), BF),
    r_3=((CHUNK, 3 * WIDTH), F32),
    r_4=((CHUNK, WIDTH), F32),
    r_5=((CHUNK, 4 * WIDTH), F32),
    r_6=((BLOCK, WIDTH), F32),
    x_all=((GROUP, OWN, WIDTH), BF),
    c_all=((GROUP, OWN, WIDTH), BF),
    qp_s=((GROUP, 16, 1024), BF),
    q_all=((ROWS * GROUP, 16, 1024), BF),
    up_s=((GROUP, 16, 1152), BF),
    up_l=((GROUP, 16, 1152), BF),
    tmp=((BLOCK, WIDTH), F32),
    w_qkv=((WIDTH, PACK), BF),
    w_up=((WIDTH, WIDTH), BF),
    w_down=((WIDTH, WIDTH), BF),
    wo_l=((GROUP, 2, ROWS // 2, 16, 1152), BF),
    w_out=((WIDTH, WIDTH), BF),
    w_own=((384, WIDTH), BF),
    norms=((8, WIDTH), F32),
    normal=((SEQ, WIDTH), F32),
    h1=((SEQ, WIDTH), BF),
    qv=((SEQ, 256), BF),
    kk=((SEQ, 256), BF),
    v01=((SEQ, 128), BF),
    v_all=((SEQ, 384), BF),
    k_heads=((3, SEQ, 256), BF),
    probs=((3, SEQ, SEQ), F32),
    o_l=((GROUP, 2, 384, 128), BF),
    ob=((SEQ, WIDTH), BF),
    y=((SEQ, WIDTH), F32),
    h2=((SEQ, WIDTH), BF),
    slope=((SEQ, WIDTH), F32),
    act=((SEQ, WIDTH), BF),
    dm=((SEQ, WIDTH), BF),
    g_down=((WIDTH, WIDTH), F32),
    g_up=((WIDTH, WIDTH), F32),
    g_out=((WIDTH, WIDTH), F32),
    g_qkv=((WIDTH, PACK), F32),
    du=((SEQ, WIDTH), BF),
    part=((SEQ, WIDTH), F32),
    part2=((SEQ, WIDTH), F32),
    dy=((OWN, WIDTH), F32),
    dyb=((GROUP, OWN, WIDTH), BF),
    dq=((SEQ, 256), F32),
    dk=((SEQ, 256), F32),
    dv=((SEQ, 384), F32),
    dqkv=((SEQ, PACK), BF),
    terms=((8, WIDTH), F32),
    terms2=((8, WIDTH), F32),
    t0=((8, WIDTH), F32),
    td=((4, 8, WIDTH), F32),
    ext=((ROWS, 16, 128), F32),
    u0=((8, 128), F32),
    u1=((8, 128), F32),
    uzd=((8, 8, 128), F32),
    fin=((16, 16, 1024), BF),
    ps=((16, 16, 1024), BF),
    q_sum=((GROUP, 16, 1024), F32),
    a_up=((GROUP, 16, 1152), BF),
    f_down=((BLOCK, WIDTH), F32),
    f_up=((BLOCK, WIDTH), F32),
    f_out=((16, 1280), F32),
    b_up=((GROUP, 16, 1152), BF),
    gain_sum=((8, WIDTH), F32),
    shift_sum=((8, WIDTH), F32),
)
for _name, _rows, _cols in (
    ("down", BLOCK, WIDTH),
    ("up", BLOCK, WIDTH),
    ("out", 16, 1280),
):
    SCRATCH["st_" + _name] = ((8, _rows, _cols), BF)
    SCRATCH["xl_" + _name] = ((4, _rows, _cols), BF)
    SCRATCH["zl_" + _name] = ((3, _rows, _cols), BF)
    SCRATCH["nl_" + _name] = ((2, _rows, _cols), BF)
for _h in range(2):
    SCRATCH[f"st_qkv{_h}"] = ((6, BLOCK // 2, PACK), BF)
    SCRATCH[f"xl_qkv{_h}"] = ((4, BLOCK // 2, PACK), BF)
    for _name in ("cl", "zl"):
        SCRATCH[f"{_name}_qkv{_h}"] = ((BLOCK // 2, PACK), BF)
for _name in ("mix", "mid", "in"):
    SCRATCH["gs_" + _name] = ((3, OWN, WIDTH), BF)
    SCRATCH["l1_" + _name] = ((2, OWN, WIDTH), BF)
    SCRATCH["l2_" + _name] = ((OWN, WIDTH), BF)
N_SENDS = 36
N_ARRIVALS = 116
N_IN = 12
N_OUT = 9
VMEM_MIB = 60


class Names:
    pass


def fused_kernel(*refs):
    (x_hbm, hist_hbm, cot_hbm, mask, wq_hbm, wo_hbm, wu_hbm, wd_hbm) = refs[:8]
    (nrm, dw, cosine_hbm, sine_hbm) = refs[8:N_IN]
    results, (ng_o, dg_o) = refs[N_IN : N_IN + N_OUT - 2], refs[N_IN + N_OUT - 2 : N_IN + N_OUT]
    s = Names()
    for name, ref in zip(SCRATCH, refs[N_IN + N_OUT :]):
        setattr(s, name, ref)
    send_sems, recv_sems, local_sems = refs[-3:]

    r, d = lax.axis_index("rows"), lax.axis_index("depth")
    z, x = lax.div(r, 2), lax.rem(r, 2)
    yy, c = lax.div(d, 2), lax.rem(d, 2)
    other_x, other_c, other_y = 1 - x, 1 - c, 1 - yy
    x_dev = (2 * z + other_x, d)
    z_two, z_mirror, z_near = lax.rem(z + 2, 4), 3 - z, z + 1 - 2 * lax.rem(z, 2)
    two_dev, mirror_dev, near_dev = ((2 * zk + x, d) for zk in (z_two, z_mirror, z_near))
    inside = lax.rem(z + 1, 4) >= 2
    outside = jnp.logical_not(inside)
    core_d, y_d, far_d = 2 * yy + other_c, 2 * other_y + c, 2 * other_y + other_c
    core_dev, y_dev, far_dev = (r, core_d), (r, y_d), (r, far_d)
    mates = ((core_d, core_dev), (y_d, y_dev), (far_d, far_dev))
    used = {"send": 0, "arrival": 0}
    send_groups = []

    def arrivals(count=1):
        used["arrival"] += count
        return used["arrival"] - count

    def sends(view, condition=None):
        used["send"] += 1
        send_groups.append((used["send"] - 1, view, condition))
        return used["send"] - 1

    def prepare(src, dst, device, arrival, group):
        return pltpu.make_async_remote_copy(
            src_ref=src,
            dst_ref=dst,
            send_sem=send_sems.at[group],
            recv_sem=recv_sems.at[arrival],
            device_id=device,
            device_id_type=MESH,
        )

    def copy_to(src, dst, device, arrival, group, condition=None):
        copy = prepare(src, dst, device, arrival, group)
        if condition is None:
            copy.start()
        else:
            pl.when(condition)(copy.start)

    def arrive(view, arrival):
        prepare(view, view, x_dev, arrival, 0).wait_recv()

    def rows_at(ref, index, size):
        return ref.at[pl.ds(pl.multiple_of(index * size, size), size)]

    def by_rows(count, step, body):
        def one(i, carry):
            body(pl.ds(pl.multiple_of(i * step, step), step))
            return carry

        lax.fori_loop(0, count // step, one, 0)

    hist, cot, wq, wo, wu, cosine, sine = s.hist, s.cot, s.wq, s.wo, s.wu, s.cosine, s.sine
    loads = {}
    for name, source, target in (
        ("wq", wq_hbm, wq),
        ("x", x_hbm, s.x_all.at[d]),
        ("wo", wo_hbm, wo),
        ("wu", wu_hbm, wu),
        ("wd", wd_hbm, rows_at(s.w_down, r, BLOCK)),
        ("cot", cot_hbm, cot),
        ("cosine", cosine_hbm, cosine),
        ("sine", sine_hbm, sine),
        ("hist", hist_hbm, hist),
    ):
        loads[name] = pltpu.make_async_copy(source, target, local_sems.at[len(loads)])
        loads[name].start()
    out_o, ig_o, hg_o, gq_o, go_o, gu_o, gd_o = (
        getattr(s, f"r_{i}") for i in range(N_OUT - 2)
    )
    stores = []

    def store(i):
        copy = pltpu.make_async_copy(
            getattr(s, f"r_{i}"), results[i], local_sems.at[len(loads) + i]
        )
        copy.start()
        stores.append(copy)

    barrier = pltpu.get_barrier_semaphore()
    partners = [x_dev, core_dev, y_dev, far_dev]
    partners += [
        (2 * zk + x, m) for zk in (z_two, z_mirror, z_near) for m in (d, core_d, y_d, far_d)
    ]
    for device in partners:
        pl.semaphore_signal(barrier, inc=1, device_id=device, device_id_type=MESH)
    pl.semaphore_wait(barrier, len(partners))

    class Gather:
        def __init__(self, piece, pieces, cross=False):
            self.piece, self.pieces, self.cross = piece, pieces, cross
            self.group, self.inner = sends(pieces(6)), sends(pieces(2), inside)
            self.two, self.near, self.mirror, self.along_x = (arrivals() for _ in range(4))
            self.own_x = arrivals() if cross else self.along_x

        def copy(self, zk, xk, device, arrival, inner=False, condition=None):
            piece = self.piece(zk, xk)
            group = self.inner if inner else self.group
            copy_to(piece, piece, device, arrival, group, condition)

        def send_two(self):
            self.copy(z, x, two_dev, self.two)

        def send_mirror(self):
            self.copy(z, x, mirror_dev, self.mirror, True, inside)

        def send_near(self, where=None):
            condition = None if where is None else outside if where else inside
            self.copy(z, x, near_dev, self.near, condition=condition)

        def send_x(self, zk=z):
            self.copy(zk, x, x_dev, self.along_x)

        def send_own_x(self):
            self.copy(z, x, x_dev, self.own_x)

        def arrive_near(self):
            arrive(self.piece(z_near, x), self.near)

        def forward_near(self):
            self.arrive_near()
            if not self.cross:
                self.send_x(z_near)

        def forward_cross(self):
            arrive(self.piece(z, other_x), self.own_x)
            self.copy(z, other_x, near_dev, self.along_x)

        def pass_two(self):
            arrive(self.piece(z_two, x), self.two)
            self.copy(z_two, x, near_dev, self.mirror, True, inside)

        def forward_two(self):
            self.pass_two()
            self.send_x(z_two)

        def forward_mirror(self):
            arrive(self.piece(z_mirror, x), self.mirror)
            self.send_x(z_mirror)

        def finish(self):
            arrive(self.pieces(3 if self.cross else 4), self.along_x)

    class GroupGather:
        def __init__(self, slab, slabs, group=None):
            self.slab, self.slabs = slab, slabs
            self.group = sends(slabs(3)) if group is None else group
            self.from_y, self.others = arrivals(), arrivals()

        def send(self):
            mine = self.slab(d)
            copy_to(mine, mine, core_dev, self.others, self.group)
            copy_to(mine, mine, y_dev, self.from_y, self.group)

        def relay(self):
            slab = self.slab(y_d)
            arrive(slab, self.from_y)
            copy_to(slab, slab, core_dev, self.others, self.group)

        def finish(self):
            arrive(self.slabs(2), self.others)

    class RowSum:
        def __init__(self, name, total, block, step, cross):
            staged = getattr(s, "st_" + name)
            self.xs, self.zs, self.ns = (
                [staged.at[i + j] for j in range(n)] for i, n in ((0, 4), (4, 2), (6, 2))
            )
            self.xs = staged.at[pl.ds(0, 4)]
            self.xl, self.zl, self.nl = (getattr(s, p + name) for p in ("xl_", "zl_", "nl_"))
            self.total = total
            self.block, self.step, self.cross = block, step, cross
            self.count = self.total.shape[0]
            self.group = sends(staged.at[pl.ds(0, 7)])
            self.along_x = {k: arrivals() for k in ("mirror", "two", "own")}
            if not cross:
                self.along_x["near"] = arrivals()
            self.crossing, self.near, self.two, self.mirror, self.passing = (
                arrivals() for _ in range(5)
            )

        def stage(self, target, index, *extras):
            def one(at):
                value = self.block(index, at)
                for ref in extras:
                    value = value + ref[at, :].astype(F32)
                target[at, :] = value.astype(BF)

            by_rows(self.count, self.step, one)

        def send_x(self, name, zk, *extras):
            self.stage(self.xs.at[zk], 2 * zk + other_x, *extras)
            copy_to(self.xs.at[zk], self.xl.at[zk], x_dev, self.along_x[name], self.group)

        def arrive_x(self, name, zk):
            arrive(self.xl.at[zk], self.along_x[name])

        def send(self, early_near=False):
            self.send_x("mirror", z_mirror)
            if self.cross:
                self.send_crossing()
            self.send_x("two", z_two)
            if self.cross and early_near:
                self.send_near()
            if not self.cross:
                self.send_x("near", z_near)
                self.send_x("own", z)

        def send_crossing(self):
            self.stage(self.ns[0], 2 * z_near + other_x)
            copy_to(self.ns[0], self.nl.at[0], near_dev, self.crossing, self.group)

        def send_own(self):
            arrive(self.nl.at[0], self.crossing)
            self.send_x("own", z, self.nl.at[0])

        def send_mirror(self):
            self.arrive_x("mirror", z_mirror)
            self.stage(self.zs[0], 2 * z_mirror + x, self.xl.at[z_mirror])
            copy_to(self.zs[0], self.zl.at[0], mirror_dev, self.mirror, self.group, inside)
            copy_to(self.zs[0], self.zl.at[2], near_dev, self.passing, self.group, outside)

        def send_two(self):
            self.arrive_x("two", z_two)

            @pl.when(inside)
            def _():
                arrive(self.zl.at[2], self.passing)
                self.stage(self.zs[1], 2 * z_two + x, self.xl.at[z_two], self.zl.at[2])

            @pl.when(outside)
            def _():
                self.stage(self.zs[1], 2 * z_two + x, self.xl.at[z_two])

            copy_to(self.zs[1], self.zl.at[1], two_dev, self.two, self.group)

        def send_near(self):
            extras = ()
            if not self.cross:
                self.arrive_x("near", z_near)
                extras = (self.xl.at[z_near],)
            self.stage(self.ns[1], 2 * z_near + x, *extras)
            copy_to(self.ns[1], self.nl.at[1], near_dev, self.near, self.group)

        def finish(self):
            self.arrive_x("own", z)
            arrive(self.zl.at[1], self.two)
            arrive(self.nl.at[1], self.near)

            def add(at):
                self.total[at, :] = (
                    self.block(r, at)
                    + self.xl[z, at, :].astype(F32)
                    + self.zl[1, at, :].astype(F32)
                    + self.nl[1, at, :].astype(F32)
                )

            by_rows(self.count, self.step, add)

            @pl.when(inside)
            def _():
                arrive(self.zl.at[0], self.mirror)

                def add_mirror(at):
                    self.total[at, :] += self.zl[0, at, :].astype(F32)

                by_rows(self.count, self.step, add_mirror)

    class SpreadSum:
        def __init__(self, half, shared):
            staged = getattr(s, f"st_qkv{half}")
            self.xs, self.cs, self.zs = staged.at[pl.ds(0, 4)], staged.at[4], staged.at[5]
            self.xl, self.cl, self.zl = (getattr(s, f"{p}_qkv{half}") for p in ("xl", "cl", "zl"))
            self.half = half
            self.group = sends(staged.at[pl.ds(0, 4)])
            self.inner, self.outer, self.last, self.final, self.final_mirror = shared
            self.along_x = {k: arrivals() for k in ("mirror", "two", "own")}
            self.crossing, self.passing = arrivals(), arrivals()

        def value(self, index, *extras):
            rows = BLOCK // 2
            start_row = pl.multiple_of((2 * index + self.half) * rows, rows)
            value = s.g_qkv[pl.ds(start_row, rows), :]
            for extra in extras:
                value = value + extra.astype(F32)
            return value

        def send_x(self, name, zk, *extras):
            self.xs[zk] = self.value(2 * zk + other_x, *extras).astype(BF)
            copy_to(self.xs.at[zk], self.xl.at[zk], x_dev, self.along_x[name], self.group)

        def arrive_x(self, name, zk):
            arrive(self.xl.at[zk], self.along_x[name])

        def send_crossing(self):
            self.cs[...] = self.value(2 * z_near + other_x).astype(BF)
            copy_to(self.cs, self.cl, near_dev, self.crossing, self.group)

        def send_own(self):
            arrive(self.cl, self.crossing)
            self.send_x("own", z, self.cl[...])

        def deliver(self, slot, zk, value):
            for j in range(2):
                to = 2 * self.half + j
                at = 8 * self.half + 2 * slot + j
                for t, tile in enumerate(fold(tiles_of(value[CHUNK * j : CHUNK * (j + 1)]))):
                    s.ps[at, :, 128 * t : 128 * (t + 1)] = tile.astype(BF)
                copy_to(
                    s.ps.at[at],
                    s.fin.at[GROUP * slot + d],
                    (2 * zk + x, to),
                    self.final_mirror if slot == 2 else self.final,
                    self.inner if slot == 2 else self.last,
                    inside if slot == 2 else d != to if slot == 3 else None,
                )
                if slot == 3:

                    @pl.when(d == to)
                    def _(at=at):
                        s.fin[GROUP * slot + d] = s.ps[at]

        def send_mirror(self):
            self.arrive_x("mirror", z_mirror)
            value = self.value(2 * z_mirror + x, self.xl[z_mirror])
            self.deliver(2, z_mirror, value)
            self.zs[...] = value.astype(BF)
            copy_to(self.zs, self.zl, near_dev, self.passing, self.outer, outside)

        def send_two(self):
            self.arrive_x("two", z_two)

            @pl.when(outside)
            def _():
                self.zl[...] = jnp.zeros((BLOCK // 2, PACK), BF)

            pl.when(inside)(lambda: arrive(self.zl, self.passing))
            self.deliver(0, z_two, self.value(2 * z_two + x, self.xl[z_two], self.zl[...]))

        def send_near(self):
            self.deliver(1, z_near, self.value(2 * z_near + x))

        def keep_own(self):
            self.arrive_x("own", z)
            self.deliver(3, z, self.value(r, self.xl[z]))

    class GroupSum:
        def __init__(self, name, source, parts=1):
            staged = getattr(s, "gs_" + name)
            self.s1, self.s2 = staged.at[pl.ds(0, 2)], staged.at[2]
            self.l1, self.l2 = (getattr(s, p + name) for p in ("l1_", "l2_"))
            self.source, self.parts, self.size = source, parts, OWN // parts
            self.group = sends(staged)
            self.first, self.second = arrivals(parts), arrivals(parts)
            self.kept = arrivals()

        def block(self, index, at):
            return self.source[pl.ds(pl.multiple_of(index * OWN + at.start, at.size), at.size), :]

        def part(self, i):
            return pl.ds(self.size * i, self.size)

        def over(self, i, body):
            def shifted(at):
                body(pl.ds(pl.multiple_of(self.size * i + at.start, at.size), at.size))

            by_rows(self.size, 32, shifted)

        def send(self, i=0):
            for j, yj in enumerate((other_y, yy)):

                def stage(at):
                    self.s1[j, at, :] = self.block(2 * yj + other_c, at).astype(BF)

                self.over(i, stage)
                copy_to(
                    self.s1.at[j, self.part(i)],
                    self.l1.at[j, self.part(i)],
                    core_dev,
                    self.kept if j else self.first + i,
                    self.group,
                )

        def middle(self, i=0):
            arrive(self.l1.at[0, self.part(i)], self.first + i)

            def stage(at):
                value = self.block(2 * other_y + c, at) + self.l1[0, at, :].astype(F32)
                self.s2[at, :] = value.astype(BF)

            self.over(i, stage)
            copy_to(
                self.s2.at[self.part(i)],
                self.l2.at[self.part(i)],
                y_dev,
                self.second + i,
                self.group,
            )

        def wait(self, i=0):
            if i == 0:
                arrive(self.l1.at[1], self.kept)
            arrive(self.l2.at[self.part(i)], self.second + i)

        def value(self, at):
            return (
                self.block(d, at)
                + self.l1[1, at, :].astype(F32)
                + self.l2[at, :].astype(F32)
            )

    class PieceGather:
        def __init__(self):
            self.group = sends(s.q_all.at[pl.ds(0, 27)])
            self.inner = sends(s.q_all.at[pl.ds(0, 8)], inside)
            self.own, self.two, self.near, self.mirror = (arrivals(2) for _ in range(4))
            self.along_x = {k: arrivals() for k in ("own", "near", "two", "mirror")}

        def fan(self, zk, arrival, group, condition=None):
            for i, m in enumerate((d, core_d, y_d, far_d)):
                if i == 0 and zk is z:
                    continue
                copy_to(
                    s.qp_s.at[m],
                    s.q_all.at[GROUP * r + d],
                    (2 * zk + x, m),
                    arrival + i // 2,
                    group,
                    condition,
                )

        def slab(self, zk, xk, h):
            first = GROUP * (2 * zk + xk) + 2 * (other_y if h else yy)
            return s.q_all.at[pl.ds(pl.multiple_of(first, 2), 2)]

        def send(self):
            self.fan(z, self.own, self.group)
            self.fan(z_two, self.two, self.group)
            self.fan(z_near, self.near, self.group)
            self.fan(z_mirror, self.mirror, self.inner, inside)

        def send_x(self, name, zk, h):
            slab = self.slab(zk, x, h)
            copy_to(slab, slab, x_dev, self.along_x[name], self.group)

        def forward_own(self, h):
            if h:
                arrive(self.slab(z, x, h), self.own + h)
            else:
                arrive(s.q_all.at[GROUP * r + core_d], self.own)
            self.send_x("own", z, h)

        def forward_near(self, h):
            arrive(self.slab(z_near, x, h), self.near + h)
            self.send_x("near", z_near, h)

        def forward_two(self, h):
            slab = self.slab(z_two, x, h)
            arrive(slab, self.two + h)
            copy_to(slab, slab, near_dev, self.mirror + h, self.inner, inside)
            self.send_x("two", z_two, h)

        def forward_mirror(self, h):
            arrive(self.slab(z_mirror, x, h), self.mirror + h)
            self.send_x("mirror", z_mirror, h)

        def finish(self, name, zk):
            first = pl.multiple_of(GROUP * (2 * zk + other_x), GROUP)
            arrive(s.q_all.at[pl.ds(first, GROUP)], self.along_x[name])

    def assemble(landing, count, target, row):
        for k in range(GROUP):
            landed = landing[k][...] if isinstance(landing, list) else landing[k]
            tiles = [t.astype(F32) for t in tiles_of(landed)]
            for t, tile in enumerate(unfold(tiles, count)):
                s.tmp[CHUNK * k : CHUNK * (k + 1), 128 * t : 128 * (t + 1)] = tile
        rows_at(target, row, BLOCK)[...] = s.tmp[:, : 128 * count].astype(BF)

    def assemble_qkv(row):
        assemble([s.q_all.at[GROUP * row + k] for k in range(GROUP)], 5, s.w_qkv, row)

    lane = lane_id((CHUNK, 128))
    eye = row_id((CHUNK, CHUNK)) == lane_id((CHUNK, CHUNK))
    extra = jnp.zeros((CHUNK, 128), F32)
    for k in range(4):
        column = jnp.sum(jnp.where(eye, nrm[k : k + 1, :], 0.0), axis=1, keepdims=True)
        high = column.astype(BF).astype(F32)
        extra = jnp.where(lane == 96 + k, high, extra)
        extra = jnp.where(lane == 100 + k, column - high, extra)
    mask_row = mask[...].astype(F32)
    ones = jnp.sum(mask_row, axis=1, keepdims=True)
    extra = jnp.where((lane == 104) & (row_id((CHUNK, 128)) == 0), ones, extra)

    loads["wq"].wait()
    wq_tiles = tiles_of(wq[...].astype(F32))
    for k in range(GROUP):
        tiles = permute_chunks(wq_tiles, qkv_picks(k))
        tiles[2] = tiles[2] + extra
        for t, tile in enumerate(fold(tiles)):
            s.qp_s[k, :, 128 * t : 128 * (t + 1)] = tile.astype(BF)
    qkv_gather = PieceGather()
    qkv_gather.send()
    s.q_all[GROUP * r + d] = s.qp_s[d]

    loads["wo"].wait()
    out_gather = Gather(
        lambda zk, xk: s.wo_l.at[d, xk, zk],
        lambda n: s.wo_l.at[0, 0, pl.ds(0, n)] if n <= 4 else s.wo_l.at[0, :, pl.ds(0, n // 2)],
    )
    for t, tile in enumerate(fold(tiles_of(wo[...].astype(F32)))):
        s.wo_l[d, x, z, :, 128 * t : 128 * (t + 1)] = tile.astype(BF)
    out_gather.send_two()
    out_gather.send_mirror()
    out_gather.send_near()
    out_gather.send_own_x()

    loads["wu"].wait()
    wu_tiles = tiles_of(wu[...].astype(F32))
    for k in range(GROUP):
        for t, tile in enumerate(fold(permute_chunks(wu_tiles, up_picks(k)))):
            s.up_s[k, :, 128 * t : 128 * (t + 1)] = tile.astype(BF)
    up_arrival, up_group = arrivals(), sends(s.up_s.at[pl.ds(0, 3)])
    for m, device in mates:
        copy_to(s.up_s.at[m], s.up_l.at[d], device, up_arrival, up_group)
    s.up_l[d] = s.up_s[d]

    loads["x"].wait()
    x_gather = GroupGather(lambda i: s.x_all.at[i], lambda n: s.x_all.at[pl.ds(0, n)])
    x_gather.send()

    loads["wd"].wait()
    up_gather = Gather(
        lambda zk, xk: rows_at(s.w_up, 2 * zk + xk, BLOCK),
        lambda n: s.w_up.at[pl.ds(0, n * BLOCK)],
        cross=True,
    )
    downs = [
        Gather(
            lambda zk, xk, h=h: rows_at(s.w_down, 2 * (2 * zk + xk) + h, BLOCK // 2),
            lambda n: s.w_down.at[pl.ds(0, n * BLOCK // 2)],
            cross=h == 0,
        )
        for h in range(2)
    ]
    diagonal = jnp.where(
        row_id((OWN, OWN)) == lane_id((OWN, OWN)), jnp.broadcast_to(mask_row, (OWN, OWN)), 0.0
    )
    loads["cot"].wait()
    s.c_all[d] = dot(diagonal.astype(BF), cot[...]).astype(BF)
    c_gather = GroupGather(lambda i: s.c_all.at[i], lambda n: s.c_all.at[pl.ds(0, n)])
    c_gather.send()

    def normalize(i):
        def one(at):
            normal, _ = standardize(s.x_all[i, at, :].astype(F32))
            s.normal[pl.ds(pl.multiple_of(OWN * i + at.start, at.size), at.size), :] = normal

        by_rows(OWN, 64, one)

    for half in downs:
        half.send_own_x()
    qkv_gather.forward_own(0)
    qkv_gather.forward_own(1)
    qkv_gather.forward_near(0)
    assemble_qkv(r)
    qkv_gather.forward_two(0)
    qkv_gather.forward_near(1)
    assemble_qkv(2 * z_near + x)
    qkv_gather.forward_two(1)
    out_gather.pass_two()
    assemble_qkv(2 * z_two + x)
    arrive(s.up_l.at[pl.ds(0, 3)], up_arrival)
    assemble(s.up_l, 6, s.w_up, r)
    up_gather.send_two()
    up_gather.send_near(True)
    qkv_gather.forward_mirror(0)
    x_gather.relay()
    qkv_gather.forward_mirror(1)
    up_gather.send_near(False)
    up_gather.send_mirror()
    for half in downs:
        half.send_two()
        half.send_near()
    out_gather.send_x(z_two)
    out_gather.forward_near()
    out_gather.forward_mirror()
    up_gather.send_own_x()
    columns = [
        GroupGather(lambda i, xk=xk: s.wo_l.at[i, xk], lambda n: s.wo_l.at[pl.ds(0, n), 0])
        for xk in (x, other_x)
    ]
    columns[0].send()
    assemble_qkv(2 * z_mirror + x)
    x_gather.finish()
    for i in range(GROUP):
        normalize(i)
    for name, zk in (("own", z), ("near", z_near), ("two", z_two)):
        qkv_gather.finish(name, zk)
        assemble_qkv(2 * zk + other_x)
    c_gather.relay()
    qkv_gather.finish("mirror", z_mirror)
    assemble_qkv(2 * z_mirror + other_x)

    lane = lane_id((8, 128))
    row = row_id((8, 128))
    pick = jnp.where((lane == 96 + row) | (lane == 100 + row), 1.0, 0.0)
    pick = jnp.where(row < 4, pick, jnp.where((row == 4) & (lane == 104), 1.0, 0.0))
    s.norms[...] = dot(pick.astype(BF), s.w_qkv[:, 256:384], 1, 1)
    total = jnp.sum(s.norms[4:5, :], axis=1, keepdims=True)
    loss_scale = (SEQ * ROWS) / total
    own_weight = dw[d]
    last_weight = dw[GROUP]

    def first_norm(at):
        value = s.normal[at, :] * (1.0 + s.norms[0:1, :]) + s.norms[1:2, :]
        s.h1[at, :] = value.astype(BF)

    by_rows(SEQ, 64, first_norm)

    def project(at):
        value = dot(s.h1[at, :], s.w_qkv[...])
        co, si = cosine[at, :], sine[at, :]
        for left, target in ((0, s.qv), (256, s.kk)):
            a, b = value[:, left : left + 128], value[:, left + 128 : left + 256]
            target[at, :128] = (a * co - b * si).astype(BF)
            target[at, 128:] = (b * co + a * si).astype(BF)
        s.v01[at, :] = value[:, 512:].astype(BF)

    loads["cosine"].wait()
    loads["sine"].wait()
    by_rows(SEQ, 256, project)

    lane2 = lax.div(lax.rem(lane_id((1, 256)), 128), jnp.int32(32))
    head_mask = [jnp.where(lane2 == h, 1.0, 0.0).astype(BF) for h in range(3)]
    tail_mask = jnp.where(lane2 == 3, 1.0, 0.0).astype(BF)
    half_id = lax.div(lane_id((1, 128)), jnp.int32(64))
    half_mask = [jnp.where(half_id == h, 1.0, 0.0).astype(BF) for h in range(2)]
    root = HD**-0.5
    o_gathers = [
        GroupGather(lambda i, b=b: s.o_l.at[i, b], lambda n: s.o_l.at[pl.ds(0, n), 0])
        for b in range(2)
    ]

    def attend(b):
        rows = slice(QBLOCK * b, QBLOCK * (b + 1))
        keys = QBLOCK * (b + 1)
        query = s.qv[rows, :]
        allowed = row_id((QBLOCK, keys)) + QBLOCK * b >= lane_id((QBLOCK, keys))
        first = jnp.zeros((QBLOCK, 128), F32)
        third = None
        for h in range(3):
            scores = dot(query * head_mask[h], s.kk[:keys, :], 1, 1) * root
            scores = jnp.where(allowed, scores, -1e30)
            raised = jnp.exp(scores - jnp.max(scores, axis=1, keepdims=True))
            probs = raised * (1.0 / jnp.sum(raised, axis=1, keepdims=True))
            s.probs[h, rows, :keys] = probs
            if h < 2:
                first = first + dot(probs.astype(BF), s.v01[:keys, :] * half_mask[h])
            else:
                third = dot(probs.astype(BF), s.qv[:keys, :])
            if b == 1 and h == 0:
                up_gather.forward_two()
                for half in downs:
                    half.send_mirror()
            if b == 1 and h == 1:
                out_gather.finish()
                columns[1].send()
        s.o_l[d, b, :QBLOCK, :] = first.astype(BF)
        lane = lane_id((QBLOCK, 128))
        third = jnp.where(
            lane < 32, pltpu.roll(third[:, :128], 32, 1), pltpu.roll(third[:, 128:], 64, 1)
        )
        lane = lane_id((OWN, 128))
        third = jnp.where(lane < 64, third[:OWN], pltpu.roll(third[OWN:], 64, 1))
        s.o_l[d, b, QBLOCK:, :] = third.astype(BF)
        o_gathers[b].send()

    attend(1)
    columns[0].relay()
    attend(0)
    for h in range(3):
        s.probs[h, :QBLOCK, QBLOCK:] = jnp.zeros((QBLOCK, QBLOCK), F32)
        s.k_heads[h] = s.kk[...] * head_mask[h]
    s.v_all[:, :256] = s.qv[...]
    s.v_all[:, 256:] = s.v01[...]
    up_gather.forward_cross()
    columns[1].relay()
    downs[1].forward_near()
    up_gather.forward_mirror()
    for column in columns:
        column.finish()
    for k in range(GROUP):
        for i in range(ROWS):
            tiles = [t.astype(F32) for t in tiles_of(s.wo_l[k, i % 2, i // 2])]
            at = CHUNK * (GROUP * i + k)
            for t, tile in enumerate(unfold(tiles, 6)):
                s.g_out[at : at + CHUNK, 128 * t : 128 * (t + 1)] = tile

    def out_place(head):
        k, h = divmod(head, 3)
        return 128 * k + 64 * h if h < 2 else 512 + 64 * k

    for head in range(HEADS):
        at = out_place(head)
        s.w_out[at : at + 64, :] = s.g_out[64 * head : 64 * head + 64, :].astype(BF)
    s.w_own[...] = jnp.zeros((384, WIDTH), BF)
    third_rows = rows_at(s.w_out.at[pl.ds(512, 256)], d, 64)
    s.w_own[96:128, :] = third_rows[:32, :]
    s.w_own[224:256, :] = third_rows[32:, :]
    s.w_own[256:, :] = rows_at(s.w_out.at[pl.ds(0, 512)], d, 128)[...]
    downs[0].forward_two()
    downs[0].forward_cross()
    o_gathers[1].relay()
    c_gather.finish()

    loads["hist"].wait()
    s.terms[...] = jnp.zeros((8, WIDTH), F32)
    for i in range(GROUP):

        def loss_rows(at, i=i):
            here = pl.ds(pl.multiple_of(OWN * i + at.start, at.size), at.size)
            grad = s.c_all[i, at, :].astype(F32) * loss_scale
            s.dm[here, :] = (last_weight * grad).astype(BF)
            hg_o[here, :] = (own_weight * grad).astype(BF)
            s.terms[...] += sublane_sum(grad * hist[here, :].astype(F32))

        by_rows(OWN, 32, loss_rows)

    store(2)
    downs[1].forward_two()
    for b in (1, 0):
        if b == 0:
            o_gathers[0].relay()
            downs[0].forward_mirror()
        o_gathers[b].finish()
        rows = slice(QBLOCK * b, QBLOCK * (b + 1))
        thirds = []
        for k in range(GROUP):
            s.ob[rows, 128 * k : 128 * (k + 1)] = s.o_l[k, b, :QBLOCK, :]
            thirds.append(s.o_l[k, b, QBLOCK:, :].astype(F32))
        lane = lane_id((OWN, 128))
        for p in range(2):
            even, odd = thirds[2 * p], thirds[2 * p + 1]
            top = jnp.where(lane < 64, even, pltpu.roll(odd, 64, 1))
            low = jnp.where(lane < 64, pltpu.roll(even, 64, 1), odd)
            cols = slice(512 + 128 * p, 640 + 128 * p)
            s.ob[QBLOCK * b : QBLOCK * b + OWN, cols] = top.astype(BF)
            s.ob[QBLOCK * b + OWN : QBLOCK * (b + 1), cols] = low.astype(BF)
        s.y[rows, :] = dot(s.ob[rows, :], s.w_out[...])
        for i in (2 * b, 2 * b + 1):

            def second_norm(at, i=i):
                here = pl.ds(pl.multiple_of(OWN * i + at.start, at.size), at.size)
                value = s.y[here, :] + s.x_all[i, at, :].astype(F32)
                s.y[here, :] = value
                normal, _ = standardize(value)
                value = normal * (1.0 + s.norms[2:3, :]) + s.norms[3:4, :]
                s.h2[here, :] = value.astype(BF)

            by_rows(OWN, 64, second_norm)

    downs[1].forward_mirror()
    up_gather.arrive_near()
    up_gather.finish()

    def widen(at):
        s.part[at, :] = dot(s.h2[at, :], s.w_up[...])

    by_rows(SEQ, 256, widen)

    rate = 0.7978845608028654

    def gate(at):
        u = s.part[at, :]
        bend = jnp.tanh(rate * (u + 0.044715 * u * u * u))
        s.act[at, :] = (0.5 * u * (1.0 + bend)).astype(BF)
        s.slope[at, :] = bend

    by_rows(SEQ, 32, gate)

    def gate_slope(at):
        u, bend = s.part[at, :], s.slope[at, :]
        inner = rate * (1.0 + 3 * 0.044715 * u * u)
        s.slope[at, :] = 0.5 * (1.0 + bend) + 0.5 * u * (1.0 - bend * bend) * inner

    def block_of(ref, shift=0):
        def block(index, at):
            start = pl.multiple_of(index * BLOCK + shift + at.start, at.size)
            return ref[pl.ds(start, at.size), :]

        return block

    for i in range(3):
        cols = slice(QBLOCK * i, QBLOCK * (i + 1))
        s.g_down[cols, :] = dot(s.act[:, cols], s.dm[...], 0, 0)
    down_sum = RowSum("down", s.f_down, block_of(s.g_down), 16, True)
    down_sum.send(early_near=True)
    by_rows(SEQ, 32, gate_slope)
    downs[0].arrive_near()
    for half in downs:
        half.finish()

    mid_sum = GroupSum("mid", s.part, 4)

    def quarter(ref, i):
        return jnp.concatenate(
            [ref[OWN * j + 32 * i : OWN * j + 32 * (i + 1), :] for j in range(GROUP)], axis=0
        )

    def put_quarter(ref, i, value):
        for j in range(GROUP):
            ref[OWN * j + 32 * i : OWN * j + 32 * (i + 1), :] = value[32 * j : 32 * (j + 1)]

    for i in range(4):
        value = dot(quarter(s.dm, i), s.w_down[...], 1, 1)
        value = (value * quarter(s.slope, i)).astype(BF)
        put_quarter(s.du, i, value)
        put_quarter(s.part, i, dot(value, s.w_up[...], 1, 1))
        mid_sum.send(i)
        if i >= 1:
            mid_sum.middle(i - 1)

    down_sum.send_mirror()
    mid_sum.middle(3)
    down_sum.send_own()

    def up_part(i):
        cols = slice(QBLOCK * i, QBLOCK * (i + 1))
        s.g_up[cols, :] = dot(s.h2[:, cols], s.du[...], 0, 0)

    up_part(0)
    s.terms2[...] = jnp.zeros((8, WIDTH), F32)
    s.t0[...] = jnp.zeros((8, WIDTH), F32)

    def second_norm_back(at):
        here = pl.ds(pl.multiple_of(OWN * d + at.start, at.size), at.size)
        grad = mid_sum.value(at)
        value = s.y[here, :]
        normal, scale = standardize(value)
        loss = s.c_all[d, at, :].astype(F32) * loss_scale
        back = last_weight * loss + norm_back(grad, s.norms[2:3, :], normal, scale)
        s.dy[at, :] = back
        s.dyb[d, at, :] = back.astype(BF)
        s.t0[2:3, :] += jnp.sum(grad * normal, axis=0, keepdims=True)
        s.t0[3:4, :] += jnp.sum(grad, axis=0, keepdims=True)
        s.terms2[...] += sublane_sum(loss * value)

    up_sum = RowSum("up", s.f_up, block_of(s.g_up), 16, True)
    dy_gathers = []
    dy_group = sends(s.dyb.at[pl.ds(0, 3)])
    for i in range(4):
        mid_sum.wait(i)
        mid_sum.over(i, second_norm_back)
        dy_gathers.append(
            GroupGather(
                lambda j, i=i: s.dyb.at[j, mid_sum.part(i)],
                lambda n: s.dyb.at[pl.ds(0, n), mid_sum.part(0)],
                dy_group,
            )
        )
        dy_gathers[i].send()
        if i < 2:
            up_part(i + 1)
        if i == 2:
            up_sum.send(early_near=True)

    def block_out(at):
        value = dot(s.act[at, :], s.w_down[...])
        s.part2[at, :] = value

    by_rows(SEQ, 256, block_out)
    def mix_quarter(i):
        def mix(at):
            here = pl.ds(pl.multiple_of(OWN * i + at.start, at.size), at.size)
            value = s.part2[here, :]
            loss = s.c_all[i, at, :].astype(F32) * loss_scale
            s.terms2[...] += sublane_sum(loss * value)
            s.part2[here, :] = own_weight * hist[here, :].astype(F32) + last_weight * value

        by_rows(OWN, 32, mix)

    dy_gathers[0].relay()
    mix_quarter(0)
    mix_quarter(1)
    dy_gathers[1].relay()
    mix_quarter(2)
    mix_quarter(3)
    mix_sum = GroupSum("mix", s.part2)
    mix_sum.send()
    lane = lane_id((8, 128))
    own_term = jnp.sum(jnp.sum(s.terms[...], axis=0, keepdims=True), axis=1, keepdims=True)
    last_term = jnp.sum(jnp.sum(s.terms2[...], axis=0, keepdims=True), axis=1, keepdims=True)
    s.u0[...] = jnp.where(lane == d, own_term, jnp.where(lane == GROUP, last_term, 0.0))
    depth_x, depth_z, depth_d = (arrivals() for _ in range(3))
    depth_group = sends(s.uzd.at[pl.ds(0, 7)])
    copy_to(s.u0, s.u1, x_dev, depth_x, depth_group)
    down_sum.send_two()

    lane = lane_id((1, 384))
    head_lanes = [jnp.where(lax.div(lane, jnp.int32(64)) == 4 + h, 1.0, 0.0) for h in range(2)]
    head_lanes = [m.astype(BF) for m in head_lanes + [jnp.where(lane < 256, 1.0, 0.0)]]
    for i in range(4):
        dy_gathers[i].finish()
        rows = s.dyb[:, 32 * i : 32 * (i + 1), :].reshape(OWN, WIDTH)
        grad = dot(rows, s.w_own[...], 1, 1).astype(BF)
        grad = jnp.concatenate([grad * m for m in head_lanes], axis=0)
        probs = jnp.concatenate([quarter(s.probs.at[h], i) for h in range(3)], axis=0)
        dp = dot(grad, s.v_all[...], 1, 1)
        delta = jnp.sum(dp * probs, axis=1, keepdims=True)
        ds = (probs * (dp - delta)).astype(BF)
        query = quarter(s.qv, i)
        query = jnp.concatenate([query * m for m in head_mask], axis=0)
        dk = dot(ds, query, 0, 0) * root
        dv = dot(probs.astype(BF), grad, 0, 0)
        if i == 0:
            s.dk[...] = dk
            s.dv[...] = dv
        else:
            s.dk[...] += dk
            s.dv[...] += dv
        dq = sum(dot(ds[OWN * h : OWN * (h + 1)], s.k_heads[h]) for h in range(3))
        put_quarter(s.dq, i, dq * root)
        if i < 2:
            dy_gathers[i + 2].relay()
        if i == 1:
            mix_sum.middle()
        if i == 2:
            up_sum.send_mirror()
            up_sum.send_own()

    def turn_back(at):
        co, si = cosine[at, :], sine[at, :]
        for left, source in ((0, s.dq), (256, s.dk)):
            a, b = source[at, :128], source[at, 128:]
            first, second = a * co + b * si, b * co - a * si
            if left == 0:
                first, second = first + s.dv[at, :128], second + s.dv[at, 128:256]
            s.dqkv[at, left : left + 128] = first.astype(BF)
            s.dqkv[at, left + 128 : left + 256] = second.astype(BF)
        s.dqkv[at, 512:] = s.dv[at, 256:].astype(BF)

    by_rows(SEQ, 64, turn_back)
    for i in range(3):
        cols = slice(QBLOCK * i, QBLOCK * (i + 1))
        s.g_qkv[cols, :] = dot(s.h1[:, cols], s.dqkv[...], 0, 0)
    shared = (
        sends(s.fin.at[pl.ds(0, 4)], inside),
        sends(s.st_qkv0.at[pl.ds(0, 2)], outside),
        sends(s.fin.at[pl.ds(0, 11)]),
        arrivals(),
        arrivals(),
    )
    sums = [SpreadSum(h, shared) for h in range(2)]
    for one in sums:
        one.send_x("mirror", z_mirror)
        one.send_crossing()
    for one in sums:
        one.send_x("two", z_two)
    arrive(s.u1, depth_x)
    s.uzd[z] = s.u0[...] + s.u1[...]
    for device in (two_dev, mirror_dev, near_dev):
        copy_to(s.uzd.at[z], s.uzd.at[z], device, depth_z, depth_group)

    def first_back(at):
        s.part[at, :] = dot(s.dqkv[at, :], s.w_qkv[...], 1, 1)

    by_rows(SEQ, 256, first_back)
    in_sum = GroupSum("in", s.part)
    in_sum.send()
    s.gain_sum[...] = jnp.zeros((8, WIDTH), F32)
    s.shift_sum[...] = jnp.zeros((8, WIDTH), F32)

    def first_norm_sums(at):
        grad = s.part[at, :]
        s.gain_sum[...] += sublane_sum(grad * s.normal[at, :])
        s.shift_sum[...] += sublane_sum(grad)

    by_rows(SEQ, 32, first_norm_sums)
    s.t0[0:1, :] = jnp.sum(s.gain_sum[...], axis=0, keepdims=True)
    s.t0[1:2, :] = jnp.sum(s.shift_sum[...], axis=0, keepdims=True)
    s.td[d] = s.t0[...]
    norm_arrival, norm_group = arrivals(), sends(s.td.at[pl.ds(0, 3)])
    for m, device in mates:
        copy_to(s.td.at[d], s.td.at[d], device, norm_arrival, norm_group)
    in_sum.middle()
    for p in range(3):
        cols = slice(QBLOCK * p, QBLOCK * (p + 1))
        value = dot(s.ob[:, cols], s.dyb[...].reshape(SEQ, WIDTH), 0, 0)
        for i in range(4):
            place = QBLOCK * p + 64 * i
            for head in range(HEADS):
                if out_place(head) == place:
                    s.g_out[64 * head : 64 * head + 64, :] = value[64 * i : 64 * i + 64]

    up_sum.send_two()
    for one in sums:
        one.send_mirror()
    arrive(s.td.at[pl.ds(0, 3)], norm_arrival)
    value = (s.td[0] + s.td[1]) + (s.td[2] + s.td[3])
    value = pltpu.roll(value, lax.rem(WIDTH - CHUNK * d, WIDTH), 1)
    for i in range(ROWS):
        shift = (WIDTH - BLOCK * i) % WIDTH
        shifted = pltpu.roll(value, shift, 1) if shift else value
        s.ext[i] = jnp.concatenate([shifted[:, :128], jnp.zeros((8, 128), F32)], axis=0)

    def out_block(index, at):
        start_row = pl.multiple_of((GROUP * index + d) * CHUNK, 8)
        tiles = tiles_of(s.g_out[pl.ds(start_row, CHUNK), :])
        return jnp.concatenate(fold(tiles) + [s.ext[index]], axis=1)

    out_sum = RowSum("out", s.f_out, out_block, 16, False)
    out_sum.send()
    for one in sums:
        one.send_own()

    down_sum.finish()
    gd_o[...] = s.f_down[...]
    store(6)
    def spread(total, staged, landing):
        arrival, group = arrivals(), sends(staged.at[pl.ds(0, 3)])
        for m, device in mates:
            rows = total[pl.ds(pl.multiple_of(CHUNK * m, CHUNK), CHUNK), :]
            for t, tile in enumerate(fold(tiles_of(rows))):
                staged[m, :, 128 * t : 128 * (t + 1)] = tile.astype(BF)
            copy_to(staged.at[m], landing.at[d], device, arrival, group)
        rows = total[pl.ds(pl.multiple_of(CHUNK * d, CHUNK), CHUNK), :]
        for t, tile in enumerate(fold(tiles_of(rows))):
            landing[d, :, 128 * t : 128 * (t + 1)] = tile.astype(BF)
        return arrival

    def collect(arrival, landing, count, back, target):
        arrive(landing.at[pl.ds(0, 3)], arrival)
        tiles = []
        for k in range(GROUP):
            tiles += unfold([t.astype(F32) for t in tiles_of(landing[k])], count)
        for t, tile in enumerate(permute_chunks(tiles, back)):
            target[:, 128 * t : 128 * (t + 1)] = tile

    mix_sum.wait()

    def write_out(at):
        here = pl.ds(pl.multiple_of(OWN * d + at.start, at.size), at.size)
        out_o[at, :] = (mix_sum.value(at) + last_weight * s.y[here, :]).astype(BF)

    by_rows(OWN, 32, write_out)
    store(0)

    in_sum.wait()
    out_sum.send_mirror()

    def first_norm_back(at):
        grad = in_sum.value(at)
        normal, scale = standardize(s.x_all[d, at, :].astype(F32))
        back = norm_back(grad, s.norms[0:1, :], normal, scale)
        ig_o[at, :] = (s.dy[at, :] + back).astype(BF)

    by_rows(OWN, 32, first_norm_back)
    store(1)
    for one in sums:
        one.send_two()
    for one in sums:
        one.send_near()
    arrive(s.uzd.at[pl.ds(0, 3)], depth_z)
    s.uzd[4 + d] = (s.uzd[0] + s.uzd[1]) + (s.uzd[2] + s.uzd[3])
    for m, device in mates:
        copy_to(s.uzd.at[4 + d], s.uzd.at[4 + d], device, depth_d, depth_group)
    out_sum.send_near()
    for one in sums:
        one.keep_own()
    up_sum.finish()
    up_spread = spread(s.f_up, s.b_up, s.a_up)
    out_sum.send_two()
    collect(up_spread, s.a_up, 6, UP_BACK, gu_o)
    store(5)
    arrive(s.uzd.at[pl.ds(0, 3)], depth_d)
    dg_o[...] = (s.uzd[4] + s.uzd[5]) + (s.uzd[6] + s.uzd[7])

    arrive(s.fin.at[pl.ds(0, 11)], shared[3])
    for k in range(GROUP):
        s.q_sum[k] = (
            s.fin[12 + k].astype(F32) + s.fin[4 + k].astype(F32) + s.fin[k].astype(F32)
        )

    @pl.when(inside)
    def _():
        arrive(s.fin.at[pl.ds(0, 4)], shared[4])
        for k in range(GROUP):
            s.q_sum[k] += s.fin[8 + k].astype(F32)

    tiles = []
    for k in range(GROUP):
        tiles += unfold(tiles_of(s.q_sum[k]), 5)
    for t, tile in enumerate(permute_chunks(tiles, QKV_BACK)):
        gq_o[:, 128 * t : 128 * (t + 1)] = tile
    store(3)
    out_sum.finish()
    for t, tile in enumerate(unfold(tiles_of(s.f_out[:, :1152]), 6)):
        go_o[:, 128 * t : 128 * (t + 1)] = tile
    ng_o[...] = s.f_out[:8, 1152:]
    store(4)
    for copy in stores:
        copy.wait()
    for group, view, condition in send_groups:
        wait = prepare(view, view, x_dev, 0, group).wait_send
        if condition is None:
            wait()
        else:
            pl.when(condition)(wait)
    assert used["send"] <= N_SENDS and used["arrival"] <= N_ARRIVALS, used


def finish_kernel(*refs):
    count = N_OUT - 2
    ins, refs = refs[:count], refs[count:]
    (norm, depth), refs = refs[:2], refs[2:]
    outs, (norm_o, depth_o), refs = refs[:count], refs[count : count + 2], refs[count + 2 :]
    held, sems = refs[:-1], refs[-1]
    first = [pltpu.make_async_copy(a, b, sems.at[i]) for i, (a, b) in enumerate(zip(ins, held))]
    for copy in first:
        copy.start()
    norm_o[...] = norm[:4, :CHUNK]
    depth_o[...] = depth[:1, : GROUP + 1]
    second = []
    for i, copy in enumerate(first):
        copy.wait()
        second.append(pltpu.make_async_copy(held[i], outs[i], sems.at[count + i]))
        second[i].start()
    for copy in second:
        copy.wait()


def fused(
    block_input,
    history,
    cotangent,
    token_mask,
    qkv_weight,
    out_weight,
    up_weight,
    down_weight,
    norm_params,
    depth_weights,
):
    cosine, sine = tables()
    vmem = pl.BlockSpec(memory_space=pltpu.VMEM)
    smem = pl.BlockSpec(memory_space=pltpu.SMEM)
    hbm = pl.BlockSpec(memory_space=pltpu.HBM)
    shape = jax.ShapeDtypeStruct
    shapes = (
        shape((OWN, WIDTH), BF),
        shape((OWN, WIDTH), BF),
        shape((SEQ, WIDTH), BF),
        shape((CHUNK, 3 * WIDTH), F32),
        shape((CHUNK, WIDTH), F32),
        shape((CHUNK, 4 * WIDTH), F32),
        shape((BLOCK, WIDTH), F32),
        shape((8, 128), F32),
        shape((8, 128), F32),
    )
    outs = pl.pallas_call(
        fused_kernel,
        out_shape=shapes,
        in_specs=[hbm] * 3 + [vmem] + [hbm] * 4 + [vmem, smem] + [hbm] * 2,
        out_specs=[hbm] * 7 + [vmem] * 2,
        scratch_shapes=[pltpu.VMEM(dims, kind) for dims, kind in SCRATCH.values()]
        + [pltpu.SemaphoreType.DMA((n,)) for n in (N_SENDS, N_ARRIVALS, 16)],
        compiler_params=pltpu.CompilerParams(
            collective_id=0, has_side_effects=True, vmem_limit_bytes=VMEM_MIB * 2**20
        ),
        cost_estimate=pl.CostEstimate(flops=12 * 10**9, bytes_accessed=4 * 10**6, transcendentals=10**6),
    )(
        block_input,
        history.reshape(SEQ, WIDTH),
        cotangent,
        token_mask.reshape(1, OWN),
        qkv_weight,
        out_weight,
        up_weight,
        down_weight,
        norm_params,
        depth_weights,
        jnp.asarray(cosine),
        jnp.asarray(sine),
    )
    held = pl.pallas_call(
        finish_kernel,
        out_shape=shapes[:7] + (shape((4, CHUNK), F32), shape((1, GROUP + 1), F32)),
        in_specs=[hbm] * 7 + [vmem] * 2,
        out_specs=[hbm] * 7 + [vmem] * 2,
        scratch_shapes=[pltpu.VMEM(one.shape, one.dtype) for one in shapes[:7]]
        + [pltpu.SemaphoreType.DMA((14,))],
        compiler_params=pltpu.CompilerParams(vmem_limit_bytes=VMEM_MIB * 2**20),
    )(*outs)
    out, input_grad, history_grad, *grads, g_depth = held
    return (out, input_grad, history_grad.reshape(1, SEQ, WIDTH), *grads, g_depth.reshape(GROUP + 1))


def fits(mesh, block_input, history, up_weight):
    devices = ROWS * GROUP
    return (
        mesh.shape["rows"] == ROWS
        and mesh.shape["depth"] == GROUP
        and block_input.shape == (OWN * devices, WIDTH)
        and history.shape[0] == GROUP
        and up_weight.shape == (WIDTH, 4 * WIDTH)
    )


def solution(mesh):
    weights = P(("rows", "depth"), None)
    in_specs = (
        weights,
        P("depth", "rows", None),
        weights,
        P(("rows", "depth")),
        weights,
        weights,
        weights,
        weights,
        P(None, ("rows", "depth")),
        P(),
    )
    out_specs = (
        weights,
        weights,
        P("depth", "rows", None),
        weights,
        weights,
        weights,
        weights,
        P(None, ("rows", "depth")),
        P(),
    )

    def run(*args):
        body = fused if fits(mesh, args[0], args[1], args[6]) else local
        return jax.shard_map(
            body, mesh=mesh, in_specs=in_specs, out_specs=out_specs, check_vma=False
        )(*args)

    return run
```

```python
import functools

import jax
import jax.numpy as jnp
import numpy as np
from jax import lax
from jax.experimental import pallas as pl
from jax.experimental.pallas import tpu as pltpu
from jax.sharding import PartitionSpec as P

HEADS = 12
HD = 64


def norm_rows(value, gain, shift):
    center = value - jnp.mean(value, axis=-1, keepdims=True)
    spread = jnp.mean(center * center, axis=-1, keepdims=True)
    return center * lax.rsqrt(spread + 1e-05) * (1.0 + gain) + shift


def rotate(value, place, sign):
    half = value.shape[-1] // 2
    freq = 10000.0 ** (-jnp.arange(half, dtype=jnp.float32) / half)
    angle = place.astype(jnp.float32)[:, None] * freq[None, :]
    cosine = jnp.cos(angle)[:, None, :]
    sine = jnp.sin(angle)[:, None, :] * sign
    first = value[..., :half]
    second = value[..., half:]
    return jnp.concatenate(
        [first * cosine - second * sine, second * cosine + first * sine], axis=-1
    )


def block_scores(query, key_block, start, query_place, scale):
    block_len = key_block.shape[0]
    scores = (
        jnp.einsum("qhd,khd->hqk", query, key_block, preferred_element_type=jnp.float32) * scale
    )
    key_place = start + jnp.arange(block_len, dtype=jnp.int32)
    allowed = query_place[:, None] >= key_place[None, :]
    return (scores, allowed)


def local(
    block_input,
    history,
    cotangent,
    token_mask,
    qkv_weight,
    out_weight,
    up_weight,
    down_weight,
    norm_params,
    depth_weights,
):
    rows_tok, width = block_input.shape
    depth_count = lax.axis_size("depth")
    device_count = lax.axis_size("rows") * depth_count
    place_depth = lax.axis_index("depth")
    heads = HEADS
    head_size = HD
    scale = head_size ** (-0.5)
    seq_len = rows_tok * depth_count
    slot_count = history.shape[0]
    hist_total = slot_count * depth_count
    wide_qkv, wide_out, wide_up, wide_down, wide_norms = (
        lax.all_gather(qkv_weight, ("rows", "depth"), axis=0, tiled=True),
        lax.all_gather(out_weight, ("rows", "depth"), axis=0, tiled=True),
        lax.all_gather(up_weight, ("rows", "depth"), axis=0, tiled=True),
        lax.all_gather(down_weight, ("rows", "depth"), axis=0, tiled=True),
        lax.all_gather(
            norm_params.astype(jnp.bfloat16), ("rows", "depth"), axis=1, tiled=True
        ).astype(norm_params.dtype),
    )
    total = lax.psum(jnp.sum(token_mask), ("rows", "depth")).astype(jnp.float32)
    loss_scale = rows_tok * device_count / total
    float_input = block_input.astype(jnp.float32)
    place = place_depth * rows_tok + jnp.arange(rows_tok, dtype=jnp.int32)
    first = norm_rows(float_input, wide_norms[0], wide_norms[1]).astype(jnp.bfloat16)
    projected = jnp.dot(first, wide_qkv, preferred_element_type=jnp.float32)
    query = rotate(projected[:, :width].reshape(rows_tok, heads, head_size), place, 1.0).astype(
        jnp.bfloat16
    )
    keys = rotate(projected[:, width : 2 * width].reshape(rows_tok, heads, head_size), place, 1.0)
    keys = keys.astype(jnp.bfloat16).reshape(rows_tok, width)
    values = projected[:, 2 * width :].astype(jnp.bfloat16)
    all_keys, all_values = (
        lax.all_gather(keys, "depth", axis=0, tiled=True),
        lax.all_gather(values, "depth", axis=0, tiled=True),
    )
    block_len = min(512, seq_len)
    block_count = seq_len // block_len
    key_blocks = all_keys.reshape(block_count, block_len, heads, head_size)
    value_blocks = all_values.reshape(block_count, block_len, heads, head_size)
    starts = jnp.arange(block_count, dtype=jnp.int32) * block_len

    def peak_step(carry, item):
        peak, weight_sum = carry
        key_block, value_block, start = item
        scores, allowed = block_scores(query, key_block, start, place, scale)
        scores = jnp.where(allowed[None], scores, -1e30)
        new_peak = jnp.maximum(peak, jnp.max(scores, axis=-1))
        weight_sum = weight_sum * jnp.exp(peak - new_peak) + jnp.sum(
            jnp.exp(scores - new_peak[..., None]), axis=-1
        )
        return ((new_peak, weight_sum), None)

    start_carry = (
        jnp.full((heads, rows_tok), -1e30, jnp.float32),
        jnp.zeros((heads, rows_tok), jnp.float32),
    )
    (peak, weight_sum), _ = lax.scan(peak_step, start_carry, (key_blocks, value_blocks, starts))
    log_total = peak + jnp.log(weight_sum)

    def value_step(running, item):
        key_block, value_block, start = item
        scores, allowed = block_scores(query, key_block, start, place, scale)
        probs = jnp.where(allowed[None], jnp.exp(scores - log_total[..., None]), 0.0)
        running = running + jnp.einsum(
            "hqk,khd->qhd",
            probs.astype(jnp.bfloat16),
            value_block,
            preferred_element_type=jnp.float32,
        )
        return (running, None)

    running, _ = lax.scan(
        value_step,
        jnp.zeros((rows_tok, heads, head_size), jnp.float32),
        (key_blocks, value_blocks, starts),
    )
    mixed = running.reshape(rows_tok, width)
    mixed_low = mixed.astype(jnp.bfloat16)
    middle = float_input + jnp.dot(mixed_low, wide_out, preferred_element_type=jnp.float32)
    second = norm_rows(middle, wide_norms[2], wide_norms[3]).astype(jnp.bfloat16)
    upper = jnp.dot(second, wide_up, preferred_element_type=jnp.float32)
    active = jax.nn.gelu(upper).astype(jnp.bfloat16)
    block_out = middle + jnp.dot(active, wide_down, preferred_element_type=jnp.float32)
    own_alpha = lax.dynamic_slice_in_dim(depth_weights, place_depth * slot_count, slot_count)
    partial_mix = jnp.sum(own_alpha[:, None, None] * history.astype(jnp.float32), axis=0)
    mixture = lax.psum_scatter(
        partial_mix.astype(jnp.bfloat16), "depth", scatter_dimension=0, tiled=True
    ).astype(jnp.float32)
    output = (mixture + depth_weights[hist_total] * block_out).astype(jnp.bfloat16)
    grad_out = token_mask.astype(jnp.float32)[:, None] * cotangent.astype(jnp.float32) * loss_scale
    last_term = jnp.sum(grad_out * block_out)
    index_all = jnp.arange(hist_total + 1, dtype=jnp.int32)
    grad_rows = lax.all_gather(grad_out.astype(jnp.bfloat16), "depth", axis=0, tiled=True).astype(
        grad_out.dtype
    )
    history_grad = (own_alpha[:, None, None] * grad_rows[None]).astype(jnp.bfloat16)
    hist_terms = jnp.sum(history.astype(jnp.float32) * grad_rows[None], axis=(1, 2))
    own_index = place_depth * slot_count + jnp.arange(slot_count, dtype=jnp.int32)
    alpha_terms = jnp.sum(
        jnp.where(index_all[None, :] == own_index[:, None], hist_terms[:, None], 0.0), axis=0
    )
    alpha_terms = alpha_terms + jnp.where(index_all == hist_total, last_term, 0.0)
    depth_gradient = lax.psum(alpha_terms, ("rows", "depth"))
    wide_qkv, wide_out, wide_up, wide_down, wide_norms = (
        lax.all_gather(qkv_weight, ("rows", "depth"), axis=0, tiled=True),
        lax.all_gather(out_weight, ("rows", "depth"), axis=0, tiled=True),
        lax.all_gather(up_weight, ("rows", "depth"), axis=0, tiled=True),
        lax.all_gather(down_weight, ("rows", "depth"), axis=0, tiled=True),
        lax.all_gather(
            norm_params.astype(jnp.bfloat16), ("rows", "depth"), axis=1, tiled=True
        ).astype(norm_params.dtype),
    )
    block_grad = depth_weights[hist_total] * grad_out
    lower_grad = block_grad.astype(jnp.bfloat16)
    down_gradient = jnp.dot(active.T, lower_grad, preferred_element_type=jnp.float32)
    active_grad = jnp.dot(lower_grad, wide_down.T, preferred_element_type=jnp.float32)
    _, gelu_pull = jax.vjp(jax.nn.gelu, upper)
    upper_grad = gelu_pull(active_grad)[0].astype(jnp.bfloat16)
    up_gradient = jnp.dot(second.T, upper_grad, preferred_element_type=jnp.float32)
    second_grad = jnp.dot(upper_grad, wide_up.T, preferred_element_type=jnp.float32)
    _, norm_pull = jax.vjp(norm_rows, middle, wide_norms[2], wide_norms[3])
    middle_part, gain_two, shift_two = norm_pull(second_grad)
    middle_grad = block_grad + middle_part
    branch_grad = middle_grad.astype(jnp.bfloat16)
    out_gradient = jnp.dot(mixed_low.T, branch_grad, preferred_element_type=jnp.float32)
    mixed_grad = jnp.dot(branch_grad, wide_out.T, preferred_element_type=jnp.float32).astype(
        jnp.bfloat16
    )
    delta = jnp.sum(
        (mixed_grad.astype(jnp.float32) * mixed).reshape(rows_tok, heads, head_size), axis=-1
    ).T
    mixed_heads = mixed_grad.reshape(rows_tok, heads, head_size)

    def score_grads(
        query_rows, grad_rows, lse_rows, delta_rows, key_block, value_block, query_place, start
    ):
        scores, allowed = block_scores(query_rows, key_block, start, query_place, scale)
        probs = jnp.where(allowed[None], jnp.exp(scores - lse_rows[..., None]), 0.0)
        prob_grad = jnp.einsum(
            "qhd,khd->hqk", grad_rows, value_block, preferred_element_type=jnp.float32
        )
        score_grad = (probs * (prob_grad - delta_rows[..., None])).astype(jnp.bfloat16)
        return (probs, score_grad)

    def grad_step(query_total, item):
        key_block, value_block, start = item
        probs, score_grad = score_grads(
            query, mixed_heads, log_total, delta, key_block, value_block, place, start
        )
        query_total = (
            query_total
            + jnp.einsum("hqk,khd->qhd", score_grad, key_block, preferred_element_type=jnp.float32)
            * scale
        )
        key_part = (
            jnp.einsum("hqk,qhd->khd", score_grad, query, preferred_element_type=jnp.float32)
            * scale
        )
        value_part = jnp.einsum(
            "hqk,qhd->khd",
            probs.astype(jnp.bfloat16),
            mixed_heads,
            preferred_element_type=jnp.float32,
        )
        return (query_total, (key_part, value_part))

    query_total, (key_parts, value_parts) = lax.scan(
        grad_step,
        jnp.zeros((rows_tok, heads, head_size), jnp.float32),
        (key_blocks, value_blocks, starts),
    )
    key_sum, value_sum = (
        lax.psum_scatter(
            key_parts.reshape(seq_len, width).astype(jnp.bfloat16),
            "depth",
            scatter_dimension=0,
            tiled=True,
        ).astype(jnp.float32),
        lax.psum_scatter(
            value_parts.reshape(seq_len, width).astype(jnp.bfloat16),
            "depth",
            scatter_dimension=0,
            tiled=True,
        ).astype(jnp.float32),
    )
    query_grad = rotate(query_total, place, -1.0).reshape(rows_tok, width)
    key_grad = rotate(key_sum.reshape(rows_tok, heads, head_size), place, -1.0).reshape(
        rows_tok, width
    )
    projected_grad = jnp.concatenate([query_grad, key_grad, value_sum], axis=1).astype(jnp.bfloat16)
    qkv_gradient = jnp.dot(first.T, projected_grad, preferred_element_type=jnp.float32)
    first_grad = jnp.dot(projected_grad, wide_qkv.T, preferred_element_type=jnp.float32)
    _, first_pull = jax.vjp(norm_rows, float_input, wide_norms[0], wide_norms[1])
    input_part, gain_one, shift_one = first_pull(first_grad)
    input_grad = (middle_grad + input_part).astype(jnp.bfloat16)
    norms_full = jnp.stack([gain_one, shift_one, gain_two, shift_two])
    qkv_gradient, out_gradient, up_gradient, down_gradient, norm_gradient = (
        lax.psum_scatter(qkv_gradient, ("rows", "depth"), scatter_dimension=0, tiled=True),
        lax.psum_scatter(out_gradient, ("rows", "depth"), scatter_dimension=0, tiled=True),
        lax.psum_scatter(up_gradient, ("rows", "depth"), scatter_dimension=0, tiled=True),
        lax.psum_scatter(down_gradient, ("rows", "depth"), scatter_dimension=0, tiled=True),
        lax.psum_scatter(norms_full, ("rows", "depth"), scatter_dimension=1, tiled=True),
    )
    return (
        output,
        input_grad,
        history_grad,
        qkv_gradient,
        out_gradient,
        up_gradient,
        down_gradient,
        norm_gradient,
        depth_gradient,
    )

SEQ = 512
OWN = 128
WIDTH = 768
ROWS = 8
GROUP = 4
PACK = 640
BLOCK = WIDTH // ROWS
CHUNK = BLOCK // GROUP
QBLOCK = 256
BF = jnp.bfloat16
F32 = jnp.float32
MESH = pl.DeviceIdType.MESH


def dot(a, b, ca=1, cb=0):
    return lax.dot_general(a, b, (((ca,), (cb,)), ((), ())), preferred_element_type=F32)


def lane_id(shape):
    return lax.broadcasted_iota(jnp.int32, shape, len(shape) - 1)


def row_id(shape):
    return lax.broadcasted_iota(jnp.int32, shape, len(shape) - 2)


def tiles_of(value):
    return [value[:, 128 * i : 128 * (i + 1)] for i in range(value.shape[1] // 128)]


def permute_chunks(tiles, picks):
    group = lax.div(lane_id(tiles[0].shape), jnp.int32(32))
    out = []
    for t in range(len(picks) // 4):
        total, rolled = jnp.zeros_like(tiles[0]), {}
        for j in range(4):
            pick = picks[4 * t + j]
            if pick is None:
                continue
            source, place = divmod(pick, 4)
            shift = (j - place) * 32 % 128
            if (source, shift) not in rolled:
                value = tiles[source]
                rolled[source, shift] = pltpu.roll(value, shift, 1) if shift else value
            total = jnp.where(group == j, rolled[source, shift], total)
        out.append(total)
    return out


def fold(tiles):
    half = (len(tiles) + 1) // 2
    low = [t[16:] for t in tiles]
    if len(low) % 2:
        low.append(jnp.zeros_like(low[0]))
    return [t[:16] for t in tiles] + [
        jnp.concatenate([low[i], low[half + i]], axis=0) for i in range(half)
    ]


def unfold(tiles, count):
    half = (count + 1) // 2
    rest = tiles[count:]
    low = [rest[i][:8] for i in range(half)] + [rest[i][8:] for i in range(half)]
    return [jnp.concatenate([tiles[i], low[i]], axis=0) for i in range(count)]


def qkv_chunk(block, head, half):
    return 24 * block + 2 * head + half


def qkv_picks(d):
    heads = [3 * d + i for i in range(3)]
    picks = []
    for block in range(2):
        for half in range(2):
            picks += [qkv_chunk(block, h, half) for h in heads]
            picks.append(qkv_chunk(2, heads[2], half) if block == 0 else None)
    return picks + [qkv_chunk(2, h, half) for h in heads[:2] for half in range(2)]


def up_picks(d):
    return [3 * (GROUP * r + d) + j for r in range(ROWS) for j in range(3)]


def inverse_picks(per_device, count, tiles_each):
    back = [None] * count
    for d, picks in enumerate(per_device):
        for place, pick in enumerate(picks):
            if pick is not None:
                back[pick] = 4 * tiles_each * d + place
    return back


QKV_BACK = inverse_picks([qkv_picks(d) for d in range(GROUP)], 72, 5)
UP_BACK = inverse_picks([up_picks(d) for d in range(GROUP)], 96, 6)


def tables():
    half = HD // 2
    freq = np.float32(10000.0) ** (-np.arange(half, dtype=np.float32) / np.float32(half))
    angle = (np.arange(SEQ, dtype=np.float32)[:, None] * freq[None, :]).astype(np.float32)
    angle = angle.astype(np.float64)
    cosine, sine = np.ones((SEQ, 128), np.float32), np.zeros((SEQ, 128), np.float32)
    cosine[:, :96] = np.tile(np.cos(angle), (1, 3))
    sine[:, :96] = np.tile(np.sin(angle), (1, 3))
    return cosine, sine


def standardize(value):
    center = value - jnp.mean(value, axis=-1, keepdims=True)
    spread = jnp.mean(center * center, axis=-1, keepdims=True)
    scale = lax.rsqrt(spread + 1e-05)
    return center * scale, scale


def norm_back(grad, gain, normal, scale):
    part = grad * (1.0 + gain)
    inner = jnp.mean(part, axis=-1, keepdims=True)
    along = jnp.mean(part * normal, axis=-1, keepdims=True)
    return scale * (part - inner - normal * along)


def sublane_sum(value):
    return jnp.sum(value.reshape(value.shape[0] // 8, 8, value.shape[1]), axis=0)


SCRATCH = dict(
    hist=((SEQ, WIDTH), BF),
    cot=((OWN, WIDTH), BF),
    wq=((CHUNK, 3 * WIDTH), BF),
    wo=((CHUNK, WIDTH), BF),
    wu=((CHUNK, 4 * WIDTH), BF),
    cosine=((SEQ, 128), F32),
    sine=((SEQ, 128), F32),
    x_all=((GROUP, OWN, WIDTH), BF),
    c_all=((GROUP, OWN, WIDTH), BF),
    qp_s=((GROUP, 16, 1024), BF),
    q_all=((ROWS * GROUP, 16, 1024), BF),
    up_s=((GROUP, 16, 1152), BF),
    up_l=((GROUP, 16, 1152), BF),
    tmp=((BLOCK, WIDTH), F32),
    w_qkv=((WIDTH, PACK), BF),
    w_up=((WIDTH, WIDTH), BF),
    w_down=((WIDTH, WIDTH), BF),
    wo_l=((GROUP, 2, ROWS // 2, 16, 1152), BF),
    w_out=((WIDTH, WIDTH), BF),
    w_own=((384, WIDTH), BF),
    norms=((8, WIDTH), F32),
    normal=((SEQ, WIDTH), F32),
    h1=((SEQ, WIDTH), BF),
    qv=((SEQ, 256), BF),
    kk=((SEQ, 256), BF),
    v01=((SEQ, 128), BF),
    v_all=((SEQ, 384), BF),
    k_heads=((3, SEQ, 256), BF),
    probs=((3, SEQ, SEQ), F32),
    o_l=((GROUP, 2, 384, 128), BF),
    ob=((SEQ, WIDTH), BF),
    y=((SEQ, WIDTH), F32),
    h2=((SEQ, WIDTH), BF),
    slope=((SEQ, WIDTH), F32),
    act=((SEQ, WIDTH), BF),
    dm=((SEQ, WIDTH), BF),
    g_down=((WIDTH, WIDTH), F32),
    g_up=((WIDTH, WIDTH), F32),
    g_out=((WIDTH, WIDTH), F32),
    g_qkv=((WIDTH, PACK), F32),
    du=((SEQ, WIDTH), BF),
    part=((SEQ, WIDTH), F32),
    part2=((SEQ, WIDTH), F32),
    dy=((OWN, WIDTH), F32),
    dyb=((GROUP, OWN, WIDTH), BF),
    dq=((SEQ, 256), F32),
    dk=((SEQ, 256), F32),
    dv=((SEQ, 384), F32),
    dqkv=((SEQ, PACK), BF),
    terms=((8, WIDTH), F32),
    terms2=((8, WIDTH), F32),
    t0=((8, WIDTH), F32),
    td=((4, 8, WIDTH), F32),
    ext=((ROWS, 16, 128), F32),
    u0=((8, 128), F32),
    u1=((8, 128), F32),
    uzd=((8, 8, 128), F32),
    fin=((16, 16, 1024), BF),
    ps=((16, 16, 1024), BF),
    q_sum=((GROUP, 16, 1024), F32),
    a_up=((GROUP, 16, 1152), BF),
    f_down=((BLOCK, WIDTH), F32),
    f_up=((BLOCK, WIDTH), F32),
    f_out=((16, 1280), F32),
    b_up=((GROUP, 16, 1152), BF),
    gain_sum=((8, WIDTH), F32),
    shift_sum=((8, WIDTH), F32),
)
for _name, _rows, _cols in (
    ("down", BLOCK, WIDTH),
    ("up", BLOCK, WIDTH),
    ("out", 16, 1280),
):
    SCRATCH["st_" + _name] = ((8, _rows, _cols), BF)
    SCRATCH["xl_" + _name] = ((4, _rows, _cols), BF)
    SCRATCH["zl_" + _name] = ((3, _rows, _cols), BF)
    SCRATCH["nl_" + _name] = ((2, _rows, _cols), BF)
for _h in range(2):
    SCRATCH[f"st_qkv{_h}"] = ((6, BLOCK // 2, PACK), BF)
    SCRATCH[f"xl_qkv{_h}"] = ((4, BLOCK // 2, PACK), BF)
    for _name in ("cl", "zl"):
        SCRATCH[f"{_name}_qkv{_h}"] = ((BLOCK // 2, PACK), BF)
for _name in ("mix", "mid", "in"):
    SCRATCH["gs_" + _name] = ((3, OWN, WIDTH), BF)
    SCRATCH["l1_" + _name] = ((2, OWN, WIDTH), BF)
    SCRATCH["l2_" + _name] = ((OWN, WIDTH), BF)
N_SENDS = 36
N_ARRIVALS = 116
N_IN = 12
N_OUT = 9
VMEM_MIB = 60


class Names:
    pass


def fused_kernel(*refs):
    (x_hbm, hist_hbm, cot_hbm, mask, wq_hbm, wo_hbm, wu_hbm, wd_hbm) = refs[:8]
    (nrm, dw, cosine_hbm, sine_hbm) = refs[8:N_IN]
    results, (ng_o, dg_o) = refs[N_IN : N_IN + N_OUT - 2], refs[N_IN + N_OUT - 2 : N_IN + N_OUT]
    s = Names()
    for name, ref in zip(SCRATCH, refs[N_IN + N_OUT :]):
        setattr(s, name, ref)
    send_sems, recv_sems, local_sems = refs[-3:]

    r, d = lax.axis_index("rows"), lax.axis_index("depth")
    z, x = lax.div(r, 2), lax.rem(r, 2)
    yy, c = lax.div(d, 2), lax.rem(d, 2)
    other_x, other_c, other_y = 1 - x, 1 - c, 1 - yy
    x_dev = (2 * z + other_x, d)
    z_two, z_mirror, z_near = lax.rem(z + 2, 4), 3 - z, z + 1 - 2 * lax.rem(z, 2)
    two_dev, mirror_dev, near_dev = ((2 * zk + x, d) for zk in (z_two, z_mirror, z_near))
    inside = lax.rem(z + 1, 4) >= 2
    outside = jnp.logical_not(inside)
    core_d, y_d, far_d = 2 * yy + other_c, 2 * other_y + c, 2 * other_y + other_c
    core_dev, y_dev, far_dev = (r, core_d), (r, y_d), (r, far_d)
    mates = ((core_d, core_dev), (y_d, y_dev), (far_d, far_dev))
    used = {"send": 0, "arrival": 0}
    send_groups = []

    def arrivals(count=1):
        used["arrival"] += count
        return used["arrival"] - count

    def sends(view, condition=None):
        used["send"] += 1
        send_groups.append((used["send"] - 1, view, condition))
        return used["send"] - 1

    def prepare(src, dst, device, arrival, group):
        return pltpu.make_async_remote_copy(
            src_ref=src,
            dst_ref=dst,
            send_sem=send_sems.at[group],
            recv_sem=recv_sems.at[arrival],
            device_id=device,
            device_id_type=MESH,
        )

    def copy_to(src, dst, device, arrival, group, condition=None):
        copy = prepare(src, dst, device, arrival, group)
        if condition is None:
            copy.start()
        else:
            pl.when(condition)(copy.start)

    def arrive(view, arrival):
        prepare(view, view, x_dev, arrival, 0).wait_recv()

    def rows_at(ref, index, size):
        return ref.at[pl.ds(pl.multiple_of(index * size, size), size)]

    def by_rows(count, step, body):
        def one(i, carry):
            body(pl.ds(pl.multiple_of(i * step, step), step))
            return carry

        lax.fori_loop(0, count // step, one, 0)

    barrier = pltpu.get_barrier_semaphore()
    partners = [x_dev, core_dev, y_dev, far_dev]
    partners += [
        (2 * zk + x, m) for zk in (z_two, z_mirror, z_near) for m in (d, core_d, y_d, far_d)
    ]
    for device in partners:
        pl.semaphore_signal(barrier, inc=1, device_id=device, device_id_type=MESH)

    hist, cot, wq, wo, wu, cosine, sine = s.hist, s.cot, s.wq, s.wo, s.wu, s.cosine, s.sine
    loads = {}
    for name, source, target in (
        ("wq", wq_hbm, wq),
        ("x", x_hbm, s.x_all.at[d]),
        ("wo", wo_hbm, wo),
        ("wu", wu_hbm, wu),
        ("wd", wd_hbm, rows_at(s.w_down, r, BLOCK)),
        ("cot", cot_hbm, cot),
        ("cosine", cosine_hbm, cosine),
        ("sine", sine_hbm, sine),
        ("hist", hist_hbm, hist),
    ):
        loads[name] = pltpu.make_async_copy(source, target, local_sems.at[len(loads)])
        loads[name].start()
    out_o, ig_o, hg_o, gq_o, go_o, gu_o, gd_o = results


    class Gather:
        def __init__(self, piece, pieces, cross=False):
            self.piece, self.pieces, self.cross = piece, pieces, cross
            self.group, self.inner = sends(pieces(6)), sends(pieces(2), inside)
            self.two, self.near, self.mirror, self.along_x = (arrivals() for _ in range(4))
            self.own_x = arrivals() if cross else self.along_x

        def copy(self, zk, xk, device, arrival, inner=False, condition=None):
            piece = self.piece(zk, xk)
            group = self.inner if inner else self.group
            copy_to(piece, piece, device, arrival, group, condition)

        def send_two(self):
            self.copy(z, x, two_dev, self.two)

        def send_mirror(self):
            self.copy(z, x, mirror_dev, self.mirror, True, inside)

        def send_near(self, where=None):
            condition = None if where is None else outside if where else inside
            self.copy(z, x, near_dev, self.near, condition=condition)

        def send_x(self, zk=z):
            self.copy(zk, x, x_dev, self.along_x)

        def send_own_x(self):
            self.copy(z, x, x_dev, self.own_x)

        def arrive_near(self):
            arrive(self.piece(z_near, x), self.near)

        def forward_near(self):
            self.arrive_near()
            if not self.cross:
                self.send_x(z_near)

        def forward_cross(self):
            arrive(self.piece(z, other_x), self.own_x)
            self.copy(z, other_x, near_dev, self.along_x)

        def pass_two(self):
            arrive(self.piece(z_two, x), self.two)
            self.copy(z_two, x, near_dev, self.mirror, True, inside)

        def forward_two(self):
            self.pass_two()
            self.send_x(z_two)

        def forward_mirror(self):
            arrive(self.piece(z_mirror, x), self.mirror)
            self.send_x(z_mirror)

        def finish(self):
            arrive(self.pieces(3 if self.cross else 4), self.along_x)

    class GroupGather:
        def __init__(self, slab, slabs, group=None):
            self.slab, self.slabs = slab, slabs
            self.group = sends(slabs(3)) if group is None else group
            self.from_y, self.others = arrivals(), arrivals()

        def send(self):
            mine = self.slab(d)
            copy_to(mine, mine, core_dev, self.others, self.group)
            copy_to(mine, mine, y_dev, self.from_y, self.group)

        def relay(self):
            slab = self.slab(y_d)
            arrive(slab, self.from_y)
            copy_to(slab, slab, core_dev, self.others, self.group)

        def finish(self):
            arrive(self.slabs(2), self.others)

    class RowSum:
        def __init__(self, name, total, block, step, cross):
            staged = getattr(s, "st_" + name)
            self.xs, self.zs, self.ns = (
                [staged.at[i + j] for j in range(n)] for i, n in ((0, 4), (4, 2), (6, 2))
            )
            self.xs = staged.at[pl.ds(0, 4)]
            self.xl, self.zl, self.nl = (getattr(s, p + name) for p in ("xl_", "zl_", "nl_"))
            self.total = total
            self.block, self.step, self.cross = block, step, cross
            self.count = self.total.shape[0]
            self.group = sends(staged.at[pl.ds(0, 7)])
            self.along_x = {k: arrivals() for k in ("mirror", "two", "own")}
            if not cross:
                self.along_x["near"] = arrivals()
            self.crossing, self.near, self.two, self.mirror, self.passing = (
                arrivals() for _ in range(5)
            )

        def stage(self, target, index, *extras):
            def one(at):
                value = self.block(index, at)
                for ref in extras:
                    value = value + ref[at, :].astype(F32)
                target[at, :] = value.astype(BF)

            by_rows(self.count, self.step, one)

        def send_x(self, name, zk, *extras):
            self.stage(self.xs.at[zk], 2 * zk + other_x, *extras)
            copy_to(self.xs.at[zk], self.xl.at[zk], x_dev, self.along_x[name], self.group)

        def arrive_x(self, name, zk):
            arrive(self.xl.at[zk], self.along_x[name])

        def send(self, early_near=False):
            self.send_x("mirror", z_mirror)
            if self.cross:
                self.send_crossing()
            self.send_x("two", z_two)
            if self.cross and early_near:
                self.send_near()
            if not self.cross:
                self.send_x("near", z_near)
                self.send_x("own", z)

        def send_crossing(self):
            self.stage(self.ns[0], 2 * z_near + other_x)
            copy_to(self.ns[0], self.nl.at[0], near_dev, self.crossing, self.group)

        def send_own(self):
            arrive(self.nl.at[0], self.crossing)
            self.send_x("own", z, self.nl.at[0])

        def send_mirror(self):
            self.arrive_x("mirror", z_mirror)
            self.stage(self.zs[0], 2 * z_mirror + x, self.xl.at[z_mirror])
            copy_to(self.zs[0], self.zl.at[0], mirror_dev, self.mirror, self.group, inside)
            copy_to(self.zs[0], self.zl.at[2], near_dev, self.passing, self.group, outside)

        def send_two_outside(self):
            @pl.when(outside)
            def _():
                self.arrive_x("two", z_two)
                self.stage(self.zs[1], 2 * z_two + x, self.xl.at[z_two])
                copy_to(self.zs[1], self.zl.at[1], two_dev, self.two, self.group)

        def send_two_inside(self):
            @pl.when(inside)
            def _():
                self.arrive_x("two", z_two)
                arrive(self.zl.at[2], self.passing)
                self.stage(self.zs[1], 2 * z_two + x, self.xl.at[z_two], self.zl.at[2])
                copy_to(self.zs[1], self.zl.at[1], two_dev, self.two, self.group)

        def send_near(self):
            extras = ()
            if not self.cross:
                self.arrive_x("near", z_near)
                extras = (self.xl.at[z_near],)
            self.stage(self.ns[1], 2 * z_near + x, *extras)
            copy_to(self.ns[1], self.nl.at[1], near_dev, self.near, self.group)

        def finish(self):
            self.arrive_x("own", z)
            arrive(self.zl.at[1], self.two)
            arrive(self.nl.at[1], self.near)

            def add(at):
                self.total[at, :] = (
                    self.block(r, at)
                    + self.xl[z, at, :].astype(F32)
                    + self.zl[1, at, :].astype(F32)
                    + self.nl[1, at, :].astype(F32)
                )

            by_rows(self.count, self.step, add)

            @pl.when(inside)
            def _():
                arrive(self.zl.at[0], self.mirror)

                def add_mirror(at):
                    self.total[at, :] += self.zl[0, at, :].astype(F32)

                by_rows(self.count, self.step, add_mirror)

    class SpreadSum:
        def __init__(self, half, shared):
            staged = getattr(s, f"st_qkv{half}")
            self.xs, self.cs, self.zs = staged.at[pl.ds(0, 4)], staged.at[4], staged.at[5]
            self.xl, self.cl, self.zl = (getattr(s, f"{p}_qkv{half}") for p in ("xl", "cl", "zl"))
            self.half = half
            self.group = sends(staged.at[pl.ds(0, 4)])
            self.inner, self.outer, self.last, self.final, self.final_mirror = shared
            self.along_x = {k: arrivals() for k in ("mirror", "two", "near", "own")}
            self.crossing, self.passing = arrivals(), arrivals()

        def value(self, index, *extras):
            rows = BLOCK // 2
            start_row = pl.multiple_of((2 * index + self.half) * rows, rows)
            value = s.g_qkv[pl.ds(start_row, rows), :]
            for extra in extras:
                value = value + extra.astype(F32)
            return value

        def send_x(self, name, zk, *extras):
            self.xs[zk] = self.value(2 * zk + other_x, *extras).astype(BF)
            copy_to(self.xs.at[zk], self.xl.at[zk], x_dev, self.along_x[name], self.group)

        def arrive_x(self, name, zk):
            arrive(self.xl.at[zk], self.along_x[name])

        def send_crossing(self):
            @pl.when(inside)
            def _():
                self.cs[...] = self.value(2 * z_near + other_x).astype(BF)
                copy_to(self.cs, self.cl, near_dev, self.crossing, self.group)

        def send_third(self):
            pl.when(inside)(lambda: self.send_x("own", z))
            pl.when(outside)(lambda: self.send_x("near", z_near))

        def send_own_outside(self):
            @pl.when(outside)
            def _():
                arrive(self.cl, self.crossing)
                self.send_x("own", z, self.cl[...])

        def deliver(self, slot, zk, value):
            for j in range(2):
                to = 2 * self.half + j
                at = 8 * self.half + 2 * slot + j
                for t, tile in enumerate(fold(tiles_of(value[CHUNK * j : CHUNK * (j + 1)]))):
                    s.ps[at, :, 128 * t : 128 * (t + 1)] = tile.astype(BF)
                copy_to(
                    s.ps.at[at],
                    s.fin.at[GROUP * slot + d],
                    (2 * zk + x, to),
                    self.final_mirror if slot == 2 else self.final,
                    self.inner if slot == 2 else self.last,
                    inside if slot == 2 else d != to if slot == 3 else None,
                )
                if slot == 3:

                    @pl.when(d == to)
                    def _(at=at):
                        s.fin[GROUP * slot + d] = s.ps[at]

        def send_mirror(self):
            self.arrive_x("mirror", z_mirror)
            value = self.value(2 * z_mirror + x, self.xl[z_mirror])
            self.deliver(2, z_mirror, value)
            self.zs[...] = value.astype(BF)
            copy_to(self.zs, self.zl, near_dev, self.passing, self.outer, outside)

        def send_two(self):
            self.arrive_x("two", z_two)

            @pl.when(outside)
            def _():
                self.zl[...] = jnp.zeros((BLOCK // 2, PACK), BF)

            pl.when(inside)(lambda: arrive(self.zl, self.passing))
            self.deliver(0, z_two, self.value(2 * z_two + x, self.xl[z_two], self.zl[...]))

        def send_near(self):
            pl.when(inside)(lambda: self.deliver(1, z_near, self.value(2 * z_near + x)))

            @pl.when(outside)
            def _():
                self.arrive_x("near", z_near)
                self.deliver(1, z_near, self.value(2 * z_near + x, self.xl[z_near]))

        def keep_own(self):
            self.arrive_x("own", z)
            self.deliver(3, z, self.value(r, self.xl[z]))

    class GroupSum:
        def __init__(self, name, source, parts=1):
            staged = getattr(s, "gs_" + name)
            self.s1, self.s2 = staged.at[pl.ds(0, 2)], staged.at[2]
            self.l1, self.l2 = (getattr(s, p + name) for p in ("l1_", "l2_"))
            self.source, self.parts, self.size = source, parts, OWN // parts
            self.group = sends(staged)
            self.first, self.second = arrivals(parts), arrivals(parts)
            self.kept = arrivals()

        def block(self, index, at):
            return self.source[pl.ds(pl.multiple_of(index * OWN + at.start, at.size), at.size), :]

        def part(self, i):
            return pl.ds(self.size * i, self.size)

        def over(self, i, body):
            def shifted(at):
                body(pl.ds(pl.multiple_of(self.size * i + at.start, at.size), at.size))

            by_rows(self.size, 32, shifted)

        def send(self, i=0):
            for j, yj in enumerate((other_y, yy)):

                def stage(at):
                    self.s1[j, at, :] = self.block(2 * yj + other_c, at).astype(BF)

                self.over(i, stage)
                copy_to(
                    self.s1.at[j, self.part(i)],
                    self.l1.at[j, self.part(i)],
                    core_dev,
                    self.kept if j else self.first + i,
                    self.group,
                )

        def middle(self, i=0):
            arrive(self.l1.at[0, self.part(i)], self.first + i)

            def stage(at):
                value = self.block(2 * other_y + c, at) + self.l1[0, at, :].astype(F32)
                self.s2[at, :] = value.astype(BF)

            self.over(i, stage)
            copy_to(
                self.s2.at[self.part(i)],
                self.l2.at[self.part(i)],
                y_dev,
                self.second + i,
                self.group,
            )

        def wait(self, i=0):
            if i == 0:
                arrive(self.l1.at[1], self.kept)
            arrive(self.l2.at[self.part(i)], self.second + i)

        def value(self, at):
            return (
                self.block(d, at)
                + self.l1[1, at, :].astype(F32)
                + self.l2[at, :].astype(F32)
            )

    class PieceGather:
        def __init__(self):
            self.group = sends(s.q_all.at[pl.ds(0, 27)])
            self.inner = sends(s.q_all.at[pl.ds(0, 8)], inside)
            self.own, self.two, self.near, self.mirror = (arrivals(2) for _ in range(4))
            self.along_x = {k: arrivals() for k in ("own", "near", "two", "mirror")}

        def fan(self, zk, arrival, group, condition=None):
            for i, m in enumerate((d, core_d, y_d, far_d)):
                if i == 0 and zk is z:
                    continue
                copy_to(
                    s.qp_s.at[m],
                    s.q_all.at[GROUP * r + d],
                    (2 * zk + x, m),
                    arrival + i // 2,
                    group,
                    condition,
                )

        def slab(self, zk, xk, h):
            first = GROUP * (2 * zk + xk) + 2 * (other_y if h else yy)
            return s.q_all.at[pl.ds(pl.multiple_of(first, 2), 2)]

        def send(self):
            self.fan(z, self.own, self.group)
            self.fan(z_two, self.two, self.group)
            self.fan(z_near, self.near, self.group)
            self.fan(z_mirror, self.mirror, self.inner, inside)

        def send_x(self, name, zk, h):
            slab = self.slab(zk, x, h)
            copy_to(slab, slab, x_dev, self.along_x[name], self.group)

        def forward_own(self, h):
            if h:
                arrive(self.slab(z, x, h), self.own + h)
            else:
                arrive(s.q_all.at[GROUP * r + core_d], self.own)
            self.send_x("own", z, h)

        def forward_near(self, h):
            arrive(self.slab(z_near, x, h), self.near + h)
            self.send_x("near", z_near, h)

        def forward_two(self, h):
            slab = self.slab(z_two, x, h)
            arrive(slab, self.two + h)
            copy_to(slab, slab, near_dev, self.mirror + h, self.inner, inside)
            self.send_x("two", z_two, h)

        def forward_mirror(self, h):
            arrive(self.slab(z_mirror, x, h), self.mirror + h)
            self.send_x("mirror", z_mirror, h)

        def finish(self, name, zk):
            first = pl.multiple_of(GROUP * (2 * zk + other_x), GROUP)
            arrive(s.q_all.at[pl.ds(first, GROUP)], self.along_x[name])

    def assemble(landing, count, target, row):
        for k in range(GROUP):
            landed = landing[k][...] if isinstance(landing, list) else landing[k]
            tiles = [t.astype(F32) for t in tiles_of(landed)]
            for t, tile in enumerate(unfold(tiles, count)):
                s.tmp[CHUNK * k : CHUNK * (k + 1), 128 * t : 128 * (t + 1)] = tile
        rows_at(target, row, BLOCK)[...] = s.tmp[:, : 128 * count].astype(BF)

    def assemble_qkv(row):
        assemble([s.q_all.at[GROUP * row + k] for k in range(GROUP)], 5, s.w_qkv, row)

    lane = lane_id((CHUNK, 128))
    eye = row_id((CHUNK, CHUNK)) == lane_id((CHUNK, CHUNK))
    extra = jnp.zeros((CHUNK, 128), F32)
    for k in range(4):
        column = jnp.sum(jnp.where(eye, nrm[k : k + 1, :], 0.0), axis=1, keepdims=True)
        high = column.astype(BF).astype(F32)
        extra = jnp.where(lane == 96 + k, high, extra)
        extra = jnp.where(lane == 100 + k, column - high, extra)
    mask_row = mask[...].astype(F32)
    ones = jnp.sum(mask_row, axis=1, keepdims=True)
    extra = jnp.where((lane == 104) & (row_id((CHUNK, 128)) == 0), ones, extra)

    loads["wq"].wait()
    wq_tiles = tiles_of(wq[...].astype(F32))
    for k in range(GROUP):
        tiles = permute_chunks(wq_tiles, qkv_picks(k))
        tiles[2] = tiles[2] + extra
        for t, tile in enumerate(fold(tiles)):
            s.qp_s[k, :, 128 * t : 128 * (t + 1)] = tile.astype(BF)
    s.q_all[GROUP * r + d] = s.qp_s[d]
    loads["wo"].wait()
    for t, tile in enumerate(fold(tiles_of(wo[...].astype(F32)))):
        s.wo_l[d, x, z, :, 128 * t : 128 * (t + 1)] = tile.astype(BF)
    loads["wu"].wait()
    wu_tiles = tiles_of(wu[...].astype(F32))
    for k in range(GROUP):
        for t, tile in enumerate(fold(permute_chunks(wu_tiles, up_picks(k)))):
            s.up_s[k, :, 128 * t : 128 * (t + 1)] = tile.astype(BF)
    s.up_l[d] = s.up_s[d]
    diagonal = jnp.where(
        row_id((OWN, OWN)) == lane_id((OWN, OWN)), jnp.broadcast_to(mask_row, (OWN, OWN)), 0.0
    )
    loads["cot"].wait()
    s.c_all[d] = dot(diagonal.astype(BF), cot[...]).astype(BF)
    loads["x"].wait()
    loads["wd"].wait()
    pl.semaphore_wait(barrier, len(partners))

    qkv_gather = PieceGather()
    qkv_gather.send()
    out_gather = Gather(
        lambda zk, xk: s.wo_l.at[d, xk, zk],
        lambda n: s.wo_l.at[0, 0, pl.ds(0, n)] if n <= 4 else s.wo_l.at[0, :, pl.ds(0, n // 2)],
    )
    out_gather.send_two()
    out_gather.send_mirror()
    out_gather.send_near()
    out_gather.send_own_x()
    up_arrival, up_group = arrivals(), sends(s.up_s.at[pl.ds(0, 3)])
    for m, device in mates:
        copy_to(s.up_s.at[m], s.up_l.at[d], device, up_arrival, up_group)
    x_gather = GroupGather(lambda i: s.x_all.at[i], lambda n: s.x_all.at[pl.ds(0, n)])
    x_gather.send()
    up_gather = Gather(
        lambda zk, xk: rows_at(s.w_up, 2 * zk + xk, BLOCK),
        lambda n: s.w_up.at[pl.ds(0, n * BLOCK)],
        cross=True,
    )
    downs = [
        Gather(
            lambda zk, xk, h=h: rows_at(s.w_down, 2 * (2 * zk + xk) + h, BLOCK // 2),
            lambda n: s.w_down.at[pl.ds(0, n * BLOCK // 2)],
            cross=h == 0,
        )
        for h in range(2)
    ]
    c_gather = GroupGather(lambda i: s.c_all.at[i], lambda n: s.c_all.at[pl.ds(0, n)])
    c_gather.send()

    def normalize(i):
        def one(at):
            normal, _ = standardize(s.x_all[i, at, :].astype(F32))
            s.normal[pl.ds(pl.multiple_of(OWN * i + at.start, at.size), at.size), :] = normal

        by_rows(OWN, 64, one)

    for half in downs:
        half.send_own_x()
    qkv_gather.forward_own(0)
    qkv_gather.forward_own(1)
    qkv_gather.forward_near(0)
    assemble_qkv(r)
    qkv_gather.forward_two(0)
    qkv_gather.forward_near(1)
    assemble_qkv(2 * z_near + x)
    qkv_gather.forward_two(1)
    out_gather.pass_two()
    assemble_qkv(2 * z_two + x)
    arrive(s.up_l.at[pl.ds(0, 3)], up_arrival)
    assemble(s.up_l, 6, s.w_up, r)
    up_gather.send_two()
    up_gather.send_near(True)
    qkv_gather.forward_mirror(0)
    x_gather.relay()
    qkv_gather.forward_mirror(1)
    up_gather.send_near(False)
    up_gather.send_mirror()
    for half in downs:
        half.send_two()
        half.send_near()
    out_gather.send_x(z_two)
    out_gather.forward_near()
    out_gather.forward_mirror()
    up_gather.send_own_x()
    columns = [
        GroupGather(lambda i, xk=xk: s.wo_l.at[i, xk], lambda n: s.wo_l.at[pl.ds(0, n), 0])
        for xk in (x, other_x)
    ]
    columns[0].send()
    assemble_qkv(2 * z_mirror + x)
    x_gather.finish()
    for i in range(GROUP):
        normalize(i)
    for name, zk in (("own", z), ("near", z_near), ("two", z_two)):
        qkv_gather.finish(name, zk)
        assemble_qkv(2 * zk + other_x)
    c_gather.relay()
    qkv_gather.finish("mirror", z_mirror)
    assemble_qkv(2 * z_mirror + other_x)

    lane = lane_id((8, 128))
    row = row_id((8, 128))
    pick = jnp.where((lane == 96 + row) | (lane == 100 + row), 1.0, 0.0)
    pick = jnp.where(row < 4, pick, jnp.where((row == 4) & (lane == 104), 1.0, 0.0))
    s.norms[...] = dot(pick.astype(BF), s.w_qkv[:, 256:384], 1, 1)
    total = jnp.sum(s.norms[4:5, :], axis=1, keepdims=True)
    loss_scale = (SEQ * ROWS) / total
    own_weight = dw[d]
    last_weight = dw[GROUP]

    def first_norm(at):
        value = s.normal[at, :] * (1.0 + s.norms[0:1, :]) + s.norms[1:2, :]
        s.h1[at, :] = value.astype(BF)

    by_rows(SEQ, 64, first_norm)

    def project(at):
        value = dot(s.h1[at, :], s.w_qkv[...])
        co, si = cosine[at, :], sine[at, :]
        for left, target in ((0, s.qv), (256, s.kk)):
            a, b = value[:, left : left + 128], value[:, left + 128 : left + 256]
            target[at, :128] = (a * co - b * si).astype(BF)
            target[at, 128:] = (b * co + a * si).astype(BF)
        s.v01[at, :] = value[:, 512:].astype(BF)

    loads["cosine"].wait()
    loads["sine"].wait()
    by_rows(SEQ, 256, project)

    lane2 = lax.div(lax.rem(lane_id((1, 256)), 128), jnp.int32(32))
    head_mask = [jnp.where(lane2 == h, 1.0, 0.0).astype(BF) for h in range(3)]
    tail_mask = jnp.where(lane2 == 3, 1.0, 0.0).astype(BF)
    half_id = lax.div(lane_id((1, 128)), jnp.int32(64))
    half_mask = [jnp.where(half_id == h, 1.0, 0.0).astype(BF) for h in range(2)]
    root = HD**-0.5
    o_gathers = [
        GroupGather(lambda i, b=b: s.o_l.at[i, b], lambda n: s.o_l.at[pl.ds(0, n), 0])
        for b in range(2)
    ]

    def attend(b):
        rows = slice(QBLOCK * b, QBLOCK * (b + 1))
        keys = QBLOCK * (b + 1)
        query = s.qv[rows, :]
        allowed = row_id((QBLOCK, keys)) + QBLOCK * b >= lane_id((QBLOCK, keys))
        first = jnp.zeros((QBLOCK, 128), F32)
        third = None
        for h in range(3):
            scores = dot(query * head_mask[h], s.kk[:keys, :], 1, 1) * root
            scores = jnp.where(allowed, scores, -1e30)
            raised = jnp.exp(scores - jnp.max(scores, axis=1, keepdims=True))
            probs = raised * (1.0 / jnp.sum(raised, axis=1, keepdims=True))
            s.probs[h, rows, :keys] = probs
            if h < 2:
                first = first + dot(probs.astype(BF), s.v01[:keys, :] * half_mask[h])
            else:
                third = dot(probs.astype(BF), s.qv[:keys, :])
            if b == 1 and h == 0:
                up_gather.forward_two()
                for half in downs:
                    half.send_mirror()
            if b == 1 and h == 1:
                out_gather.finish()
                columns[1].send()
        s.o_l[d, b, :QBLOCK, :] = first.astype(BF)
        lane = lane_id((QBLOCK, 128))
        third = jnp.where(
            lane < 32, pltpu.roll(third[:, :128], 32, 1), pltpu.roll(third[:, 128:], 64, 1)
        )
        lane = lane_id((OWN, 128))
        third = jnp.where(lane < 64, third[:OWN], pltpu.roll(third[OWN:], 64, 1))
        s.o_l[d, b, QBLOCK:, :] = third.astype(BF)
        o_gathers[b].send()

    attend(1)
    columns[0].relay()
    attend(0)
    for h in range(3):
        s.probs[h, :QBLOCK, QBLOCK:] = jnp.zeros((QBLOCK, QBLOCK), F32)
        s.k_heads[h] = s.kk[...] * head_mask[h]
    s.v_all[:, :256] = s.qv[...]
    s.v_all[:, 256:] = s.v01[...]
    up_gather.forward_cross()
    columns[1].relay()
    downs[1].forward_near()
    up_gather.forward_mirror()
    for column in columns:
        column.finish()
    for k in range(GROUP):
        for i in range(ROWS):
            tiles = [t.astype(F32) for t in tiles_of(s.wo_l[k, i % 2, i // 2])]
            at = CHUNK * (GROUP * i + k)
            for t, tile in enumerate(unfold(tiles, 6)):
                s.g_out[at : at + CHUNK, 128 * t : 128 * (t + 1)] = tile

    def out_place(head):
        k, h = divmod(head, 3)
        return 128 * k + 64 * h if h < 2 else 512 + 64 * k

    for head in range(HEADS):
        at = out_place(head)
        s.w_out[at : at + 64, :] = s.g_out[64 * head : 64 * head + 64, :].astype(BF)
    s.w_own[...] = jnp.zeros((384, WIDTH), BF)
    third_rows = rows_at(s.w_out.at[pl.ds(512, 256)], d, 64)
    s.w_own[96:128, :] = third_rows[:32, :]
    s.w_own[224:256, :] = third_rows[32:, :]
    s.w_own[256:, :] = rows_at(s.w_out.at[pl.ds(0, 512)], d, 128)[...]
    downs[0].forward_two()
    downs[0].forward_cross()
    o_gathers[1].relay()
    c_gather.finish()

    loads["hist"].wait()
    s.terms[...] = jnp.zeros((8, WIDTH), F32)
    for i in range(GROUP):

        def loss_rows(at, i=i):
            here = pl.ds(pl.multiple_of(OWN * i + at.start, at.size), at.size)
            grad = s.c_all[i, at, :].astype(F32) * loss_scale
            s.dm[here, :] = (last_weight * grad).astype(BF)
            hg_o[here, :] = (own_weight * grad).astype(BF)
            s.terms[...] += sublane_sum(grad * hist[here, :].astype(F32))

        by_rows(OWN, 32, loss_rows)

    downs[1].forward_two()
    for b in (1, 0):
        if b == 0:
            o_gathers[0].relay()
            downs[0].forward_mirror()
        o_gathers[b].finish()
        rows = slice(QBLOCK * b, QBLOCK * (b + 1))
        thirds = []
        for k in range(GROUP):
            s.ob[rows, 128 * k : 128 * (k + 1)] = s.o_l[k, b, :QBLOCK, :]
            thirds.append(s.o_l[k, b, QBLOCK:, :].astype(F32))
        lane = lane_id((OWN, 128))
        for p in range(2):
            even, odd = thirds[2 * p], thirds[2 * p + 1]
            top = jnp.where(lane < 64, even, pltpu.roll(odd, 64, 1))
            low = jnp.where(lane < 64, pltpu.roll(even, 64, 1), odd)
            cols = slice(512 + 128 * p, 640 + 128 * p)
            s.ob[QBLOCK * b : QBLOCK * b + OWN, cols] = top.astype(BF)
            s.ob[QBLOCK * b + OWN : QBLOCK * (b + 1), cols] = low.astype(BF)
        s.y[rows, :] = dot(s.ob[rows, :], s.w_out[...])
        for i in (2 * b, 2 * b + 1):

            def second_norm(at, i=i):
                here = pl.ds(pl.multiple_of(OWN * i + at.start, at.size), at.size)
                value = s.y[here, :] + s.x_all[i, at, :].astype(F32)
                s.y[here, :] = value
                normal, _ = standardize(value)
                value = normal * (1.0 + s.norms[2:3, :]) + s.norms[3:4, :]
                s.h2[here, :] = value.astype(BF)

            by_rows(OWN, 64, second_norm)

    downs[1].forward_mirror()
    up_gather.arrive_near()
    up_gather.finish()

    def widen(at):
        s.part[at, :] = dot(s.h2[at, :], s.w_up[...])

    by_rows(SEQ, 256, widen)

    rate = 0.7978845608028654

    def gate(at):
        u = s.part[at, :]
        bend = jnp.tanh(rate * (u + 0.044715 * u * u * u))
        s.act[at, :] = (0.5 * u * (1.0 + bend)).astype(BF)
        s.slope[at, :] = bend

    by_rows(SEQ, 32, gate)

    def gate_slope(at):
        u, bend = s.part[at, :], s.slope[at, :]
        inner = rate * (1.0 + 3 * 0.044715 * u * u)
        s.slope[at, :] = 0.5 * (1.0 + bend) + 0.5 * u * (1.0 - bend * bend) * inner

    def block_of(ref, shift=0):
        def block(index, at):
            start = pl.multiple_of(index * BLOCK + shift + at.start, at.size)
            return ref[pl.ds(start, at.size), :]

        return block

    for i in range(3):
        cols = slice(QBLOCK * i, QBLOCK * (i + 1))
        s.g_down[cols, :] = dot(s.act[:, cols], s.dm[...], 0, 0)
    down_sum = RowSum("down", s.f_down, block_of(s.g_down), 16, True)
    down_sum.send(early_near=True)
    by_rows(SEQ, 32, gate_slope)
    downs[0].arrive_near()
    for half in downs:
        half.finish()

    mid_sum = GroupSum("mid", s.part, 4)

    def quarter(ref, i):
        return jnp.concatenate(
            [ref[OWN * j + 32 * i : OWN * j + 32 * (i + 1), :] for j in range(GROUP)], axis=0
        )

    def put_quarter(ref, i, value):
        for j in range(GROUP):
            ref[OWN * j + 32 * i : OWN * j + 32 * (i + 1), :] = value[32 * j : 32 * (j + 1)]

    for i in range(4):
        value = dot(quarter(s.dm, i), s.w_down[...], 1, 1)
        value = (value * quarter(s.slope, i)).astype(BF)
        put_quarter(s.du, i, value)
        put_quarter(s.part, i, dot(value, s.w_up[...], 1, 1))
        mid_sum.send(i)
        if i >= 1:
            mid_sum.middle(i - 1)

    down_sum.send_mirror()
    mid_sum.middle(3)
    down_sum.send_own()

    def up_part(i):
        cols = slice(QBLOCK * i, QBLOCK * (i + 1))
        s.g_up[cols, :] = dot(s.h2[:, cols], s.du[...], 0, 0)

    up_part(0)
    s.terms2[...] = jnp.zeros((8, WIDTH), F32)
    s.t0[...] = jnp.zeros((8, WIDTH), F32)

    def second_norm_back(at):
        here = pl.ds(pl.multiple_of(OWN * d + at.start, at.size), at.size)
        grad = mid_sum.value(at)
        value = s.y[here, :]
        normal, scale = standardize(value)
        loss = s.c_all[d, at, :].astype(F32) * loss_scale
        back = last_weight * loss + norm_back(grad, s.norms[2:3, :], normal, scale)
        s.dy[at, :] = back
        s.dyb[d, at, :] = back.astype(BF)
        s.t0[2:3, :] += jnp.sum(grad * normal, axis=0, keepdims=True)
        s.t0[3:4, :] += jnp.sum(grad, axis=0, keepdims=True)
        s.terms2[...] += sublane_sum(loss * value)

    up_sum = RowSum("up", s.f_up, block_of(s.g_up), 16, True)
    dy_gathers = []
    dy_group = sends(s.dyb.at[pl.ds(0, 3)])
    for i in range(4):
        mid_sum.wait(i)
        mid_sum.over(i, second_norm_back)
        dy_gathers.append(
            GroupGather(
                lambda j, i=i: s.dyb.at[j, mid_sum.part(i)],
                lambda n: s.dyb.at[pl.ds(0, n), mid_sum.part(0)],
                dy_group,
            )
        )
        dy_gathers[i].send()
        if i < 2:
            up_part(i + 1)
        if i == 2:
            up_sum.send()

    def block_out(at):
        value = dot(s.act[at, :], s.w_down[...])
        s.part2[at, :] = value

    by_rows(SEQ, 256, block_out)
    def mix_quarter(i):
        def mix(at):
            here = pl.ds(pl.multiple_of(OWN * i + at.start, at.size), at.size)
            value = s.part2[here, :]
            loss = s.c_all[i, at, :].astype(F32) * loss_scale
            s.terms2[...] += sublane_sum(loss * value)
            s.part2[here, :] = own_weight * hist[here, :].astype(F32) + last_weight * value

        by_rows(OWN, 32, mix)

    down_sum.send_two_outside()
    dy_gathers[0].relay()
    mix_quarter(0)
    mix_quarter(1)
    dy_gathers[1].relay()
    mix_quarter(2)
    mix_quarter(3)
    mix_sum = GroupSum("mix", s.part2)
    mix_sum.send()
    lane = lane_id((8, 128))
    own_term = jnp.sum(jnp.sum(s.terms[...], axis=0, keepdims=True), axis=1, keepdims=True)
    last_term = jnp.sum(jnp.sum(s.terms2[...], axis=0, keepdims=True), axis=1, keepdims=True)
    s.u0[...] = jnp.where(lane == d, own_term, jnp.where(lane == GROUP, last_term, 0.0))
    depth_x, depth_z, depth_d = (arrivals() for _ in range(3))
    depth_group = sends(s.uzd.at[pl.ds(0, 7)])
    copy_to(s.u0, s.u1, x_dev, depth_x, depth_group)
    down_sum.send_two_inside()

    lane = lane_id((1, 384))
    head_lanes = [jnp.where(lax.div(lane, jnp.int32(64)) == 4 + h, 1.0, 0.0) for h in range(2)]
    head_lanes = [m.astype(BF) for m in head_lanes + [jnp.where(lane < 256, 1.0, 0.0)]]
    for i in range(4):
        dy_gathers[i].finish()
        rows = s.dyb[:, 32 * i : 32 * (i + 1), :].reshape(OWN, WIDTH)
        grad = dot(rows, s.w_own[...], 1, 1).astype(BF)
        grad = jnp.concatenate([grad * m for m in head_lanes], axis=0)
        probs = jnp.concatenate([quarter(s.probs.at[h], i) for h in range(3)], axis=0)
        dp = dot(grad, s.v_all[...], 1, 1)
        delta = jnp.sum(dp * probs, axis=1, keepdims=True)
        ds = (probs * (dp - delta)).astype(BF)
        query = quarter(s.qv, i)
        query = jnp.concatenate([query * m for m in head_mask], axis=0)
        dk = dot(ds, query, 0, 0) * root
        dv = dot(probs.astype(BF), grad, 0, 0)
        if i == 0:
            s.dk[...] = dk
            s.dv[...] = dv
        else:
            s.dk[...] += dk
            s.dv[...] += dv
        dq = sum(dot(ds[OWN * h : OWN * (h + 1)], s.k_heads[h]) for h in range(3))
        put_quarter(s.dq, i, dq * root)
        if i < 2:
            dy_gathers[i + 2].relay()
        if i == 1:
            up_sum.send_mirror()
            mix_sum.middle()
        if i == 2:
            up_sum.send_own()
            up_sum.send_near()

    def turn_back(at):
        co, si = cosine[at, :], sine[at, :]
        for left, source in ((0, s.dq), (256, s.dk)):
            a, b = source[at, :128], source[at, 128:]
            first, second = a * co + b * si, b * co - a * si
            if left == 0:
                first, second = first + s.dv[at, :128], second + s.dv[at, 128:256]
            s.dqkv[at, left : left + 128] = first.astype(BF)
            s.dqkv[at, left + 128 : left + 256] = second.astype(BF)
        s.dqkv[at, 512:] = s.dv[at, 256:].astype(BF)

    by_rows(SEQ, 64, turn_back)
    up_sum.send_two_outside()
    for i in range(3):
        cols = slice(QBLOCK * i, QBLOCK * (i + 1))
        s.g_qkv[cols, :] = dot(s.h1[:, cols], s.dqkv[...], 0, 0)
    shared = (
        sends(s.fin.at[pl.ds(0, 4)], inside),
        sends(s.st_qkv0.at[pl.ds(0, 2)], outside),
        sends(s.fin.at[pl.ds(0, 11)]),
        arrivals(),
        arrivals(),
    )
    sums = [SpreadSum(h, shared) for h in range(2)]
    for one in sums:
        one.send_x("mirror", z_mirror)
        one.send_crossing()
    for one in sums:
        one.send_x("two", z_two)
    for one in sums:
        one.send_third()
    arrive(s.u1, depth_x)
    s.uzd[z] = s.u0[...] + s.u1[...]
    for device in (two_dev, mirror_dev, near_dev):
        copy_to(s.uzd.at[z], s.uzd.at[z], device, depth_z, depth_group)

    def first_back(at):
        s.part[at, :] = dot(s.dqkv[at, :], s.w_qkv[...], 1, 1)

    by_rows(SEQ, 256, first_back)
    in_sum = GroupSum("in", s.part)
    in_sum.send()
    up_sum.send_two_inside()
    s.gain_sum[...] = jnp.zeros((8, WIDTH), F32)
    s.shift_sum[...] = jnp.zeros((8, WIDTH), F32)

    def first_norm_sums(at):
        grad = s.part[at, :]
        s.gain_sum[...] += sublane_sum(grad * s.normal[at, :])
        s.shift_sum[...] += sublane_sum(grad)

    by_rows(SEQ, 32, first_norm_sums)
    s.t0[0:1, :] = jnp.sum(s.gain_sum[...], axis=0, keepdims=True)
    s.t0[1:2, :] = jnp.sum(s.shift_sum[...], axis=0, keepdims=True)
    s.td[d] = s.t0[...]
    norm_arrival, norm_group = arrivals(), sends(s.td.at[pl.ds(0, 3)])
    for m, device in mates:
        copy_to(s.td.at[d], s.td.at[d], device, norm_arrival, norm_group)
    in_sum.middle()
    for p in range(3):
        cols = slice(QBLOCK * p, QBLOCK * (p + 1))
        value = dot(s.ob[:, cols], s.dyb[...].reshape(SEQ, WIDTH), 0, 0)
        for i in range(4):
            place = QBLOCK * p + 64 * i
            for head in range(HEADS):
                if out_place(head) == place:
                    s.g_out[64 * head : 64 * head + 64, :] = value[64 * i : 64 * i + 64]

    for one in sums:
        one.send_mirror()
    arrive(s.td.at[pl.ds(0, 3)], norm_arrival)
    value = (s.td[0] + s.td[1]) + (s.td[2] + s.td[3])
    value = pltpu.roll(value, lax.rem(WIDTH - CHUNK * d, WIDTH), 1)
    for i in range(ROWS):
        shift = (WIDTH - BLOCK * i) % WIDTH
        shifted = pltpu.roll(value, shift, 1) if shift else value
        s.ext[i] = jnp.concatenate([shifted[:, :128], jnp.zeros((8, 128), F32)], axis=0)

    def out_block(index, at):
        start_row = pl.multiple_of((GROUP * index + d) * CHUNK, 8)
        tiles = tiles_of(s.g_out[pl.ds(start_row, CHUNK), :])
        return jnp.concatenate(fold(tiles) + [s.ext[index]], axis=1)

    out_sum = RowSum("out", s.f_out, out_block, 16, False)
    out_sum.send_x("mirror", z_mirror)
    out_sum.send_x("two", z_two)
    for one in sums:
        one.send_own_outside()
    out_sum.send_x("near", z_near)
    out_sum.send_x("own", z)

    down_sum.finish()
    gd_o[...] = s.f_down[...]
    def spread(total, staged, landing):
        arrival, group = arrivals(), sends(staged.at[pl.ds(0, 3)])
        for m, device in mates:
            rows = total[pl.ds(pl.multiple_of(CHUNK * m, CHUNK), CHUNK), :]
            for t, tile in enumerate(fold(tiles_of(rows))):
                staged[m, :, 128 * t : 128 * (t + 1)] = tile.astype(BF)
            copy_to(staged.at[m], landing.at[d], device, arrival, group)
        rows = total[pl.ds(pl.multiple_of(CHUNK * d, CHUNK), CHUNK), :]
        for t, tile in enumerate(fold(tiles_of(rows))):
            landing[d, :, 128 * t : 128 * (t + 1)] = tile.astype(BF)
        return arrival

    def collect(arrival, landing, count, back, target):
        arrive(landing.at[pl.ds(0, 3)], arrival)
        tiles = []
        for k in range(GROUP):
            tiles += unfold([t.astype(F32) for t in tiles_of(landing[k])], count)
        for t, tile in enumerate(permute_chunks(tiles, back)):
            target[:, 128 * t : 128 * (t + 1)] = tile

    mix_sum.wait()

    def write_out(at):
        here = pl.ds(pl.multiple_of(OWN * d + at.start, at.size), at.size)
        out_o[at, :] = (mix_sum.value(at) + last_weight * s.y[here, :]).astype(BF)

    by_rows(OWN, 32, write_out)

    for one in sums:
        one.send_two()
    out_sum.send_mirror()
    in_sum.wait()

    def first_norm_back(at):
        grad = in_sum.value(at)
        normal, scale = standardize(s.x_all[d, at, :].astype(F32))
        back = norm_back(grad, s.norms[0:1, :], normal, scale)
        ig_o[at, :] = (s.dy[at, :] + back).astype(BF)

    by_rows(OWN, 32, first_norm_back)
    for one in sums:
        one.send_near()
    up_sum.finish()
    up_spread = spread(s.f_up, s.b_up, s.a_up)
    arrive(s.uzd.at[pl.ds(0, 3)], depth_z)
    s.uzd[4 + d] = (s.uzd[0] + s.uzd[1]) + (s.uzd[2] + s.uzd[3])
    for m, device in mates:
        copy_to(s.uzd.at[4 + d], s.uzd.at[4 + d], device, depth_d, depth_group)
    for one in sums:
        one.keep_own()
    out_sum.send_two_outside()
    out_sum.send_two_inside()
    out_sum.send_near()
    arrive(s.uzd.at[pl.ds(0, 3)], depth_d)
    dg_o[...] = (s.uzd[4] + s.uzd[5]) + (s.uzd[6] + s.uzd[7])

    arrive(s.fin.at[pl.ds(0, 11)], shared[3])
    for k in range(GROUP):
        s.q_sum[k] = (
            s.fin[12 + k].astype(F32) + s.fin[4 + k].astype(F32) + s.fin[k].astype(F32)
        )

    @pl.when(inside)
    def _():
        arrive(s.fin.at[pl.ds(0, 4)], shared[4])
        for k in range(GROUP):
            s.q_sum[k] += s.fin[8 + k].astype(F32)

    tiles = []
    for k in range(GROUP):
        tiles += unfold(tiles_of(s.q_sum[k]), 5)
    for t, tile in enumerate(permute_chunks(tiles, QKV_BACK)):
        gq_o[:, 128 * t : 128 * (t + 1)] = tile
    collect(up_spread, s.a_up, 6, UP_BACK, gu_o)
    out_sum.finish()
    for t, tile in enumerate(unfold(tiles_of(s.f_out[:, :1152]), 6)):
        go_o[:, 128 * t : 128 * (t + 1)] = tile
    ng_o[...] = s.f_out[:8, 1152:]
    for group, view, condition in send_groups:
        wait = prepare(view, view, x_dev, 0, group).wait_send
        if condition is None:
            wait()
        else:
            pl.when(condition)(wait)
    assert used["send"] <= N_SENDS and used["arrival"] <= N_ARRIVALS, used


def finish_kernel(*refs):
    count = N_OUT - 2
    ins, refs = refs[:count], refs[count:]
    (norm, depth), refs = refs[:2], refs[2:]
    outs, (norm_o, depth_o), sems = refs[:count], refs[count : count + 2], refs[-1]
    copies = [pltpu.make_async_copy(a, b, sems.at[i]) for i, (a, b) in enumerate(zip(ins, outs))]
    for copy in copies:
        copy.start()
    norm_o[...] = norm[:4, :CHUNK]
    depth_o[...] = depth[:1, : GROUP + 1]
    for copy in copies:
        copy.wait()


def fused(
    block_input,
    history,
    cotangent,
    token_mask,
    qkv_weight,
    out_weight,
    up_weight,
    down_weight,
    norm_params,
    depth_weights,
):
    cosine, sine = tables()
    vmem = pl.BlockSpec(memory_space=pltpu.VMEM)
    smem = pl.BlockSpec(memory_space=pltpu.SMEM)
    hbm = pl.BlockSpec(memory_space=pltpu.HBM)
    shape = jax.ShapeDtypeStruct
    shapes = (
        shape((OWN, WIDTH), BF),
        shape((OWN, WIDTH), BF),
        shape((SEQ, WIDTH), BF),
        shape((CHUNK, 3 * WIDTH), F32),
        shape((CHUNK, WIDTH), F32),
        shape((CHUNK, 4 * WIDTH), F32),
        shape((BLOCK, WIDTH), F32),
        shape((8, 128), F32),
        shape((8, 128), F32),
    )
    outs = pl.pallas_call(
        fused_kernel,
        out_shape=tuple(pltpu.VMEM(one.shape, one.dtype) for one in shapes),
        in_specs=[hbm] * 3 + [vmem] + [hbm] * 4 + [vmem, smem] + [hbm] * 2,
        out_specs=[vmem] * 9,
        scratch_shapes=[pltpu.VMEM(dims, kind) for dims, kind in SCRATCH.values()]
        + [pltpu.SemaphoreType.DMA((n,)) for n in (N_SENDS, N_ARRIVALS, 9)],
        compiler_params=pltpu.CompilerParams(
            collective_id=0, has_side_effects=True, vmem_limit_bytes=VMEM_MIB * 2**20
        ),
        cost_estimate=pl.CostEstimate(flops=12 * 10**9, bytes_accessed=4 * 10**6, transcendentals=10**6),
    )(
        block_input,
        history.reshape(SEQ, WIDTH),
        cotangent,
        token_mask.reshape(1, OWN),
        qkv_weight,
        out_weight,
        up_weight,
        down_weight,
        norm_params,
        depth_weights,
        jnp.asarray(cosine),
        jnp.asarray(sine),
    )
    held = pl.pallas_call(
        finish_kernel,
        out_shape=shapes[:7] + (shape((4, CHUNK), F32), shape((1, GROUP + 1), F32)),
        in_specs=[vmem] * 9,
        out_specs=[hbm] * 7 + [vmem] * 2,
        scratch_shapes=[pltpu.SemaphoreType.DMA((7,))],
        compiler_params=pltpu.CompilerParams(vmem_limit_bytes=4 * 2**20),
    )(*outs)
    out, input_grad, history_grad, *grads, g_depth = held
    return (out, input_grad, history_grad.reshape(1, SEQ, WIDTH), *grads, g_depth.reshape(GROUP + 1))


def fits(mesh, block_input, history, up_weight):
    devices = ROWS * GROUP
    return (
        mesh.shape["rows"] == ROWS
        and mesh.shape["depth"] == GROUP
        and block_input.shape == (OWN * devices, WIDTH)
        and history.shape[0] == GROUP
        and up_weight.shape == (WIDTH, 4 * WIDTH)
    )


def solution(mesh):
    weights = P(("rows", "depth"), None)
    in_specs = (
        weights,
        P("depth", "rows", None),
        weights,
        P(("rows", "depth")),
        weights,
        weights,
        weights,
        weights,
        P(None, ("rows", "depth")),
        P(),
    )
    out_specs = (
        weights,
        weights,
        P("depth", "rows", None),
        weights,
        weights,
        weights,
        weights,
        P(None, ("rows", "depth")),
        P(),
    )

    def run(*args):
        body = fused if fits(mesh, args[0], args[1], args[6]) else local
        return jax.shard_map(
            body, mesh=mesh, in_specs=in_specs, out_specs=out_specs, check_vma=False
        )(*args)

    return run
```

```python
import functools

import jax
import jax.numpy as jnp
import numpy as np
from jax import lax
from jax.experimental import pallas as pl
from jax.experimental.pallas import tpu as pltpu
from jax.sharding import PartitionSpec as P

HEADS = 12
HD = 64


def norm_rows(value, gain, shift):
    center = value - jnp.mean(value, axis=-1, keepdims=True)
    spread = jnp.mean(center * center, axis=-1, keepdims=True)
    return center * lax.rsqrt(spread + 1e-05) * (1.0 + gain) + shift


def rotate(value, place, sign):
    half = value.shape[-1] // 2
    freq = 10000.0 ** (-jnp.arange(half, dtype=jnp.float32) / half)
    angle = place.astype(jnp.float32)[:, None] * freq[None, :]
    cosine = jnp.cos(angle)[:, None, :]
    sine = jnp.sin(angle)[:, None, :] * sign
    first = value[..., :half]
    second = value[..., half:]
    return jnp.concatenate(
        [first * cosine - second * sine, second * cosine + first * sine], axis=-1
    )


def block_scores(query, key_block, start, query_place, scale):
    block_len = key_block.shape[0]
    scores = (
        jnp.einsum("qhd,khd->hqk", query, key_block, preferred_element_type=jnp.float32) * scale
    )
    key_place = start + jnp.arange(block_len, dtype=jnp.int32)
    allowed = query_place[:, None] >= key_place[None, :]
    return (scores, allowed)


def local(
    block_input,
    history,
    cotangent,
    token_mask,
    qkv_weight,
    out_weight,
    up_weight,
    down_weight,
    norm_params,
    depth_weights,
):
    rows_tok, width = block_input.shape
    depth_count = lax.axis_size("depth")
    device_count = lax.axis_size("rows") * depth_count
    place_depth = lax.axis_index("depth")
    heads = HEADS
    head_size = HD
    scale = head_size ** (-0.5)
    seq_len = rows_tok * depth_count
    slot_count = history.shape[0]
    hist_total = slot_count * depth_count
    wide_qkv, wide_out, wide_up, wide_down, wide_norms = (
        lax.all_gather(qkv_weight, ("rows", "depth"), axis=0, tiled=True),
        lax.all_gather(out_weight, ("rows", "depth"), axis=0, tiled=True),
        lax.all_gather(up_weight, ("rows", "depth"), axis=0, tiled=True),
        lax.all_gather(down_weight, ("rows", "depth"), axis=0, tiled=True),
        lax.all_gather(
            norm_params.astype(jnp.bfloat16), ("rows", "depth"), axis=1, tiled=True
        ).astype(norm_params.dtype),
    )
    total = lax.psum(jnp.sum(token_mask), ("rows", "depth")).astype(jnp.float32)
    loss_scale = rows_tok * device_count / total
    float_input = block_input.astype(jnp.float32)
    place = place_depth * rows_tok + jnp.arange(rows_tok, dtype=jnp.int32)
    first = norm_rows(float_input, wide_norms[0], wide_norms[1]).astype(jnp.bfloat16)
    projected = jnp.dot(first, wide_qkv, preferred_element_type=jnp.float32)
    query = rotate(projected[:, :width].reshape(rows_tok, heads, head_size), place, 1.0).astype(
        jnp.bfloat16
    )
    keys = rotate(projected[:, width : 2 * width].reshape(rows_tok, heads, head_size), place, 1.0)
    keys = keys.astype(jnp.bfloat16).reshape(rows_tok, width)
    values = projected[:, 2 * width :].astype(jnp.bfloat16)
    all_keys, all_values = (
        lax.all_gather(keys, "depth", axis=0, tiled=True),
        lax.all_gather(values, "depth", axis=0, tiled=True),
    )
    block_len = min(512, seq_len)
    block_count = seq_len // block_len
    key_blocks = all_keys.reshape(block_count, block_len, heads, head_size)
    value_blocks = all_values.reshape(block_count, block_len, heads, head_size)
    starts = jnp.arange(block_count, dtype=jnp.int32) * block_len

    def peak_step(carry, item):
        peak, weight_sum = carry
        key_block, value_block, start = item
        scores, allowed = block_scores(query, key_block, start, place, scale)
        scores = jnp.where(allowed[None], scores, -1e30)
        new_peak = jnp.maximum(peak, jnp.max(scores, axis=-1))
        weight_sum = weight_sum * jnp.exp(peak - new_peak) + jnp.sum(
            jnp.exp(scores - new_peak[..., None]), axis=-1
        )
        return ((new_peak, weight_sum), None)

    start_carry = (
        jnp.full((heads, rows_tok), -1e30, jnp.float32),
        jnp.zeros((heads, rows_tok), jnp.float32),
    )
    (peak, weight_sum), _ = lax.scan(peak_step, start_carry, (key_blocks, value_blocks, starts))
    log_total = peak + jnp.log(weight_sum)

    def value_step(running, item):
        key_block, value_block, start = item
        scores, allowed = block_scores(query, key_block, start, place, scale)
        probs = jnp.where(allowed[None], jnp.exp(scores - log_total[..., None]), 0.0)
        running = running + jnp.einsum(
            "hqk,khd->qhd",
            probs.astype(jnp.bfloat16),
            value_block,
            preferred_element_type=jnp.float32,
        )
        return (running, None)

    running, _ = lax.scan(
        value_step,
        jnp.zeros((rows_tok, heads, head_size), jnp.float32),
        (key_blocks, value_blocks, starts),
    )
    mixed = running.reshape(rows_tok, width)
    mixed_low = mixed.astype(jnp.bfloat16)
    middle = float_input + jnp.dot(mixed_low, wide_out, preferred_element_type=jnp.float32)
    second = norm_rows(middle, wide_norms[2], wide_norms[3]).astype(jnp.bfloat16)
    upper = jnp.dot(second, wide_up, preferred_element_type=jnp.float32)
    active = jax.nn.gelu(upper).astype(jnp.bfloat16)
    block_out = middle + jnp.dot(active, wide_down, preferred_element_type=jnp.float32)
    own_alpha = lax.dynamic_slice_in_dim(depth_weights, place_depth * slot_count, slot_count)
    partial_mix = jnp.sum(own_alpha[:, None, None] * history.astype(jnp.float32), axis=0)
    mixture = lax.psum_scatter(
        partial_mix.astype(jnp.bfloat16), "depth", scatter_dimension=0, tiled=True
    ).astype(jnp.float32)
    output = (mixture + depth_weights[hist_total] * block_out).astype(jnp.bfloat16)
    grad_out = token_mask.astype(jnp.float32)[:, None] * cotangent.astype(jnp.float32) * loss_scale
    last_term = jnp.sum(grad_out * block_out)
    index_all = jnp.arange(hist_total + 1, dtype=jnp.int32)
    grad_rows = lax.all_gather(grad_out.astype(jnp.bfloat16), "depth", axis=0, tiled=True).astype(
        grad_out.dtype
    )
    history_grad = (own_alpha[:, None, None] * grad_rows[None]).astype(jnp.bfloat16)
    hist_terms = jnp.sum(history.astype(jnp.float32) * grad_rows[None], axis=(1, 2))
    own_index = place_depth * slot_count + jnp.arange(slot_count, dtype=jnp.int32)
    alpha_terms = jnp.sum(
        jnp.where(index_all[None, :] == own_index[:, None], hist_terms[:, None], 0.0), axis=0
    )
    alpha_terms = alpha_terms + jnp.where(index_all == hist_total, last_term, 0.0)
    depth_gradient = lax.psum(alpha_terms, ("rows", "depth"))
    wide_qkv, wide_out, wide_up, wide_down, wide_norms = (
        lax.all_gather(qkv_weight, ("rows", "depth"), axis=0, tiled=True),
        lax.all_gather(out_weight, ("rows", "depth"), axis=0, tiled=True),
        lax.all_gather(up_weight, ("rows", "depth"), axis=0, tiled=True),
        lax.all_gather(down_weight, ("rows", "depth"), axis=0, tiled=True),
        lax.all_gather(
            norm_params.astype(jnp.bfloat16), ("rows", "depth"), axis=1, tiled=True
        ).astype(norm_params.dtype),
    )
    block_grad = depth_weights[hist_total] * grad_out
    lower_grad = block_grad.astype(jnp.bfloat16)
    down_gradient = jnp.dot(active.T, lower_grad, preferred_element_type=jnp.float32)
    active_grad = jnp.dot(lower_grad, wide_down.T, preferred_element_type=jnp.float32)
    _, gelu_pull = jax.vjp(jax.nn.gelu, upper)
    upper_grad = gelu_pull(active_grad)[0].astype(jnp.bfloat16)
    up_gradient = jnp.dot(second.T, upper_grad, preferred_element_type=jnp.float32)
    second_grad = jnp.dot(upper_grad, wide_up.T, preferred_element_type=jnp.float32)
    _, norm_pull = jax.vjp(norm_rows, middle, wide_norms[2], wide_norms[3])
    middle_part, gain_two, shift_two = norm_pull(second_grad)
    middle_grad = block_grad + middle_part
    branch_grad = middle_grad.astype(jnp.bfloat16)
    out_gradient = jnp.dot(mixed_low.T, branch_grad, preferred_element_type=jnp.float32)
    mixed_grad = jnp.dot(branch_grad, wide_out.T, preferred_element_type=jnp.float32).astype(
        jnp.bfloat16
    )
    delta = jnp.sum(
        (mixed_grad.astype(jnp.float32) * mixed).reshape(rows_tok, heads, head_size), axis=-1
    ).T
    mixed_heads = mixed_grad.reshape(rows_tok, heads, head_size)

    def score_grads(
        query_rows, grad_rows, lse_rows, delta_rows, key_block, value_block, query_place, start
    ):
        scores, allowed = block_scores(query_rows, key_block, start, query_place, scale)
        probs = jnp.where(allowed[None], jnp.exp(scores - lse_rows[..., None]), 0.0)
        prob_grad = jnp.einsum(
            "qhd,khd->hqk", grad_rows, value_block, preferred_element_type=jnp.float32
        )
        score_grad = (probs * (prob_grad - delta_rows[..., None])).astype(jnp.bfloat16)
        return (probs, score_grad)

    def grad_step(query_total, item):
        key_block, value_block, start = item
        probs, score_grad = score_grads(
            query, mixed_heads, log_total, delta, key_block, value_block, place, start
        )
        query_total = (
            query_total
            + jnp.einsum("hqk,khd->qhd", score_grad, key_block, preferred_element_type=jnp.float32)
            * scale
        )
        key_part = (
            jnp.einsum("hqk,qhd->khd", score_grad, query, preferred_element_type=jnp.float32)
            * scale
        )
        value_part = jnp.einsum(
            "hqk,qhd->khd",
            probs.astype(jnp.bfloat16),
            mixed_heads,
            preferred_element_type=jnp.float32,
        )
        return (query_total, (key_part, value_part))

    query_total, (key_parts, value_parts) = lax.scan(
        grad_step,
        jnp.zeros((rows_tok, heads, head_size), jnp.float32),
        (key_blocks, value_blocks, starts),
    )
    key_sum, value_sum = (
        lax.psum_scatter(
            key_parts.reshape(seq_len, width).astype(jnp.bfloat16),
            "depth",
            scatter_dimension=0,
            tiled=True,
        ).astype(jnp.float32),
        lax.psum_scatter(
            value_parts.reshape(seq_len, width).astype(jnp.bfloat16),
            "depth",
            scatter_dimension=0,
            tiled=True,
        ).astype(jnp.float32),
    )
    query_grad = rotate(query_total, place, -1.0).reshape(rows_tok, width)
    key_grad = rotate(key_sum.reshape(rows_tok, heads, head_size), place, -1.0).reshape(
        rows_tok, width
    )
    projected_grad = jnp.concatenate([query_grad, key_grad, value_sum], axis=1).astype(jnp.bfloat16)
    qkv_gradient = jnp.dot(first.T, projected_grad, preferred_element_type=jnp.float32)
    first_grad = jnp.dot(projected_grad, wide_qkv.T, preferred_element_type=jnp.float32)
    _, first_pull = jax.vjp(norm_rows, float_input, wide_norms[0], wide_norms[1])
    input_part, gain_one, shift_one = first_pull(first_grad)
    input_grad = (middle_grad + input_part).astype(jnp.bfloat16)
    norms_full = jnp.stack([gain_one, shift_one, gain_two, shift_two])
    qkv_gradient, out_gradient, up_gradient, down_gradient, norm_gradient = (
        lax.psum_scatter(qkv_gradient, ("rows", "depth"), scatter_dimension=0, tiled=True),
        lax.psum_scatter(out_gradient, ("rows", "depth"), scatter_dimension=0, tiled=True),
        lax.psum_scatter(up_gradient, ("rows", "depth"), scatter_dimension=0, tiled=True),
        lax.psum_scatter(down_gradient, ("rows", "depth"), scatter_dimension=0, tiled=True),
        lax.psum_scatter(norms_full, ("rows", "depth"), scatter_dimension=1, tiled=True),
    )
    return (
        output,
        input_grad,
        history_grad,
        qkv_gradient,
        out_gradient,
        up_gradient,
        down_gradient,
        norm_gradient,
        depth_gradient,
    )

SEQ = 512
OWN = 128
WIDTH = 768
ROWS = 8
GROUP = 4
PACK = 640
BLOCK = WIDTH // ROWS
CHUNK = BLOCK // GROUP
QBLOCK = 256
BF = jnp.bfloat16
F32 = jnp.float32
MESH = pl.DeviceIdType.MESH


def dot(a, b, ca=1, cb=0):
    return lax.dot_general(a, b, (((ca,), (cb,)), ((), ())), preferred_element_type=F32)


def lane_id(shape):
    return lax.broadcasted_iota(jnp.int32, shape, len(shape) - 1)


def row_id(shape):
    return lax.broadcasted_iota(jnp.int32, shape, len(shape) - 2)


def tiles_of(value):
    return [value[:, 128 * i : 128 * (i + 1)] for i in range(value.shape[1] // 128)]


def permute_chunks(tiles, picks):
    group = lax.div(lane_id(tiles[0].shape), jnp.int32(32))
    out = []
    for t in range(len(picks) // 4):
        total, rolled = jnp.zeros_like(tiles[0]), {}
        for j in range(4):
            pick = picks[4 * t + j]
            if pick is None:
                continue
            source, place = divmod(pick, 4)
            shift = (j - place) * 32 % 128
            if (source, shift) not in rolled:
                value = tiles[source]
                rolled[source, shift] = pltpu.roll(value, shift, 1) if shift else value
            total = jnp.where(group == j, rolled[source, shift], total)
        out.append(total)
    return out


def fold(tiles):
    half = (len(tiles) + 1) // 2
    low = [t[16:] for t in tiles]
    if len(low) % 2:
        low.append(jnp.zeros_like(low[0]))
    return [t[:16] for t in tiles] + [
        jnp.concatenate([low[i], low[half + i]], axis=0) for i in range(half)
    ]


def unfold(tiles, count):
    half = (count + 1) // 2
    rest = tiles[count:]
    low = [rest[i][:8] for i in range(half)] + [rest[i][8:] for i in range(half)]
    return [jnp.concatenate([tiles[i], low[i]], axis=0) for i in range(count)]


def fold_qkv(tiles):
    t0, t1, t2, t3, t4 = tiles
    lane, lane8, lane16 = (lane_id((n, 128)) for n in (CHUNK, 8, 16))
    turned = pltpu.roll(t3, 96, 1)
    keys = jnp.where(lane < 96, t2, turned)
    extra = jnp.where(
        lane8 < 80,
        pltpu.roll(t2[:8], 96, 1),
        jnp.where(lane8 < 96, pltpu.roll(t2[8:16], 112, 1), t2[16:]),
    )
    right = jnp.concatenate([pltpu.roll(turned[16:], 64, 1), extra], axis=0)
    shared = jnp.where(lane16 < 64, turned[:16], right)
    return [t0[:16], t1[:16], t4[:16], keys[:16], shared] + [
        jnp.concatenate([a[16:], b[16:]], axis=0) for a, b in ((t0, t1), (t4, keys))
    ]


def unfold_qkv(tiles):
    u0, u1, u4, u3, shared, low01, low43 = tiles
    lane = lane_id((CHUNK, 128))
    t0 = jnp.concatenate([u0, low01[:8]], axis=0)
    t1 = jnp.concatenate([u1, low01[8:]], axis=0)
    t4 = jnp.concatenate([u4, low43[:8]], axis=0)
    keys = jnp.concatenate([u3, low43[8:]], axis=0)
    turned = jnp.concatenate([shared, pltpu.roll(shared[:8], 64, 1)], axis=0)
    t3 = jnp.where(lane < 32, pltpu.roll(keys, 32, 1), pltpu.roll(turned, 32, 1))
    t3 = jnp.where(lane < 96, t3, 0.0)
    extra = shared[8:]
    extra = jnp.concatenate([pltpu.roll(extra, 32, 1), pltpu.roll(extra, 16, 1), extra], axis=0)
    t2 = jnp.where(lane < 96, keys, jnp.where(lane < 112, extra, 0.0))
    return [t0, t1, t2, t3, t4]


def qkv_chunk(block, head, half):
    return 24 * block + 2 * head + half


def qkv_picks(d):
    heads = [3 * d + i for i in range(3)]
    picks = []
    for block in range(2):
        for half in range(2):
            picks += [qkv_chunk(block, h, half) for h in heads]
            picks.append(qkv_chunk(2, heads[2], half) if block == 0 else None)
    return picks + [qkv_chunk(2, h, half) for h in heads[:2] for half in range(2)]


def up_picks(d):
    return [3 * (GROUP * r + d) + j for r in range(ROWS) for j in range(3)]


def inverse_picks(per_device, count, tiles_each):
    back = [None] * count
    for d, picks in enumerate(per_device):
        for place, pick in enumerate(picks):
            if pick is not None:
                back[pick] = 4 * tiles_each * d + place
    return back


QKV_BACK = inverse_picks([qkv_picks(d) for d in range(GROUP)], 72, 5)
UP_BACK = inverse_picks([up_picks(d) for d in range(GROUP)], 96, 6)


def tables():
    half = HD // 2
    freq = np.float32(10000.0) ** (-np.arange(half, dtype=np.float32) / np.float32(half))
    angle = (np.arange(SEQ, dtype=np.float32)[:, None] * freq[None, :]).astype(np.float32)
    angle = angle.astype(np.float64)
    cosine, sine = np.ones((SEQ, 128), np.float32), np.zeros((SEQ, 128), np.float32)
    cosine[:, :96] = np.tile(np.cos(angle), (1, 3))
    sine[:, :96] = np.tile(np.sin(angle), (1, 3))
    return cosine, sine


def standardize(value):
    center = value - jnp.mean(value, axis=-1, keepdims=True)
    spread = jnp.mean(center * center, axis=-1, keepdims=True)
    scale = lax.rsqrt(spread + 1e-05)
    return center * scale, scale


def norm_back(grad, gain, normal, scale):
    part = grad * (1.0 + gain)
    inner = jnp.mean(part, axis=-1, keepdims=True)
    along = jnp.mean(part * normal, axis=-1, keepdims=True)
    return scale * (part - inner - normal * along)


def sublane_sum(value):
    return jnp.sum(value.reshape(value.shape[0] // 8, 8, value.shape[1]), axis=0)


SCRATCH = dict(
    hist=((SEQ, WIDTH), BF),
    cot=((OWN, WIDTH), BF),
    wq=((CHUNK, 3 * WIDTH), BF),
    wo=((CHUNK, WIDTH), BF),
    wu=((CHUNK, 4 * WIDTH), BF),
    cosine=((SEQ, 128), F32),
    sine=((SEQ, 128), F32),
    x_all=((GROUP, OWN, WIDTH), BF),
    c_all=((GROUP, OWN, WIDTH), BF),
    qp_s=((GROUP, 16, 896), BF),
    q_all=((ROWS * GROUP, 16, 896), BF),
    up_s=((GROUP, 16, 1152), BF),
    up_l=((GROUP, 16, 1152), BF),
    tmp=((BLOCK, WIDTH), F32),
    w_qkv=((WIDTH, PACK), BF),
    w_up=((WIDTH, WIDTH), BF),
    w_down=((WIDTH, WIDTH), BF),
    wo_l=((GROUP, 2, ROWS // 2, 16, 1152), BF),
    w_out=((WIDTH, WIDTH), BF),
    w_own=((384, WIDTH), BF),
    norms=((8, WIDTH), F32),
    normal=((SEQ, WIDTH), F32),
    h1=((SEQ, WIDTH), BF),
    qv=((SEQ, 256), BF),
    kk=((SEQ, 256), BF),
    v01=((SEQ, 128), BF),
    v_all=((SEQ, 384), BF),
    probs=((3, SEQ, SEQ), F32),
    o_l=((GROUP, 2, 384, 128), BF),
    ob=((SEQ, WIDTH), BF),
    y=((SEQ, WIDTH), F32),
    h2=((SEQ, WIDTH), BF),
    slope=((SEQ, WIDTH), F32),
    act=((SEQ, WIDTH), BF),
    dm=((SEQ, WIDTH), BF),
    g_down=((WIDTH, WIDTH), F32),
    g_up=((WIDTH, WIDTH), F32),
    g_out=((WIDTH, WIDTH), F32),
    g_qkv=((WIDTH, PACK), F32),
    du=((SEQ, WIDTH), BF),
    part=((SEQ, WIDTH), F32),
    part2=((SEQ, WIDTH), F32),
    dy=((OWN, WIDTH), F32),
    dyb=((GROUP, OWN, WIDTH), BF),
    dq=((SEQ, 256), F32),
    dk=((SEQ, 256), F32),
    dv=((SEQ, 384), F32),
    dqkv=((SEQ, PACK), BF),
    terms=((8, WIDTH), F32),
    terms2=((8, WIDTH), F32),
    t0=((8, WIDTH), F32),
    td=((4, 8, WIDTH), F32),
    ext=((ROWS, 16, 128), F32),
    u0=((8, 128), F32),
    u1=((8, 128), F32),
    uzd=((8, 8, 128), F32),
    fin=((16, 16, 896), BF),
    ps=((16, 16, 896), BF),
    q_sum=((GROUP, 16, 896), F32),
    a_up=((GROUP, 16, 1152), BF),
    f_down=((BLOCK, WIDTH), F32),
    f_up=((BLOCK, WIDTH), F32),
    f_out=((16, 1280), F32),
    b_up=((GROUP, 16, 1152), BF),
    gain_sum=((8, WIDTH), F32),
    shift_sum=((8, WIDTH), F32),
)
for _name, _rows, _cols in (
    ("down", BLOCK, WIDTH),
    ("up", BLOCK, WIDTH),
    ("out", 16, 1280),
):
    SCRATCH["st_" + _name] = ((8, _rows, _cols), BF)
    SCRATCH["xl_" + _name] = ((4, _rows, _cols), BF)
    SCRATCH["zl_" + _name] = ((3, _rows, _cols), BF)
    SCRATCH["nl_" + _name] = ((2, _rows, _cols), BF)
for _h in range(2):
    SCRATCH[f"st_qkv{_h}"] = ((6, BLOCK // 2, PACK), BF)
    SCRATCH[f"xl_qkv{_h}"] = ((4, BLOCK // 2, PACK), BF)
    for _name in ("cl", "zl"):
        SCRATCH[f"{_name}_qkv{_h}"] = ((BLOCK // 2, PACK), BF)
for _name in ("mix", "mid", "in"):
    SCRATCH["gs_" + _name] = ((3, OWN, WIDTH), BF)
    SCRATCH["l1_" + _name] = ((2, OWN, WIDTH), BF)
    SCRATCH["l2_" + _name] = ((OWN, WIDTH), BF)
N_SENDS = 36
N_ARRIVALS = 116
N_IN = 12
N_OUT = 9
VMEM_MIB = 60


class Names:
    pass


def fused_kernel(*refs):
    (x_hbm, hist_hbm, cot_hbm, mask, wq_hbm, wo_hbm, wu_hbm, wd_hbm) = refs[:8]
    (nrm, dw, cosine_hbm, sine_hbm) = refs[8:N_IN]
    results, (ng_o, dg_o) = refs[N_IN : N_IN + N_OUT - 2], refs[N_IN + N_OUT - 2 : N_IN + N_OUT]
    s = Names()
    for name, ref in zip(SCRATCH, refs[N_IN + N_OUT :]):
        setattr(s, name, ref)
    send_sems, recv_sems, local_sems = refs[-3:]

    r, d = lax.axis_index("rows"), lax.axis_index("depth")
    z, x = lax.div(r, 2), lax.rem(r, 2)
    yy, c = lax.div(d, 2), lax.rem(d, 2)
    other_x, other_c, other_y = 1 - x, 1 - c, 1 - yy
    x_dev = (2 * z + other_x, d)
    z_two, z_mirror, z_near = lax.rem(z + 2, 4), 3 - z, z + 1 - 2 * lax.rem(z, 2)
    two_dev, mirror_dev, near_dev = ((2 * zk + x, d) for zk in (z_two, z_mirror, z_near))
    inside = lax.rem(z + 1, 4) >= 2
    outside = jnp.logical_not(inside)
    core_d, y_d, far_d = 2 * yy + other_c, 2 * other_y + c, 2 * other_y + other_c
    core_dev, y_dev, far_dev = (r, core_d), (r, y_d), (r, far_d)
    mates = ((core_d, core_dev), (y_d, y_dev), (far_d, far_dev))
    used = {"send": 0, "arrival": 0}
    send_groups = []

    def arrivals(count=1):
        used["arrival"] += count
        return used["arrival"] - count

    def sends(view, condition=None):
        used["send"] += 1
        send_groups.append((used["send"] - 1, view, condition))
        return used["send"] - 1

    def prepare(src, dst, device, arrival, group):
        return pltpu.make_async_remote_copy(
            src_ref=src,
            dst_ref=dst,
            send_sem=send_sems.at[group],
            recv_sem=recv_sems.at[arrival],
            device_id=device,
            device_id_type=MESH,
        )

    def copy_to(src, dst, device, arrival, group, condition=None):
        copy = prepare(src, dst, device, arrival, group)
        if condition is None:
            copy.start()
        else:
            pl.when(condition)(copy.start)

    def arrive(view, arrival):
        prepare(view, view, x_dev, arrival, 0).wait_recv()

    def rows_at(ref, index, size):
        return ref.at[pl.ds(pl.multiple_of(index * size, size), size)]

    def by_rows(count, step, body):
        def one(i, carry):
            body(pl.ds(pl.multiple_of(i * step, step), step))
            return carry

        lax.fori_loop(0, count // step, one, 0)

    barrier = pltpu.get_barrier_semaphore()
    partners = [x_dev, core_dev, y_dev, far_dev]
    partners += [
        (2 * zk + x, m) for zk in (z_two, z_mirror, z_near) for m in (d, core_d, y_d, far_d)
    ]
    for device in partners:
        pl.semaphore_signal(barrier, inc=1, device_id=device, device_id_type=MESH)

    hist, cot, wq, wo, wu, cosine, sine = s.hist, s.cot, s.wq, s.wo, s.wu, s.cosine, s.sine
    loads = {}
    for name, source, target in (
        ("wq", wq_hbm, wq),
        ("x", x_hbm, s.x_all.at[d]),
        ("wo", wo_hbm, wo),
        ("wu", wu_hbm, wu),
        ("wd", wd_hbm, rows_at(s.w_down, r, BLOCK)),
        ("cot", cot_hbm, cot),
        ("cosine", cosine_hbm, cosine),
        ("sine", sine_hbm, sine),
        ("hist", hist_hbm, hist),
    ):
        loads[name] = pltpu.make_async_copy(source, target, local_sems.at[len(loads)])
        loads[name].start()
    out_o, ig_o, hg_o, gq_o, go_o, gu_o, gd_o = results


    class Gather:
        def __init__(self, piece, pieces, cross=False):
            self.piece, self.pieces, self.cross = piece, pieces, cross
            self.group, self.inner = sends(pieces(6)), sends(pieces(2), inside)
            self.two, self.near, self.mirror, self.along_x = (arrivals() for _ in range(4))
            self.own_x = arrivals() if cross else self.along_x

        def copy(self, zk, xk, device, arrival, inner=False, condition=None):
            piece = self.piece(zk, xk)
            group = self.inner if inner else self.group
            copy_to(piece, piece, device, arrival, group, condition)

        def send_two(self):
            self.copy(z, x, two_dev, self.two)

        def send_mirror(self):
            self.copy(z, x, mirror_dev, self.mirror, True, inside)

        def send_near(self, where=None):
            condition = None if where is None else outside if where else inside
            self.copy(z, x, near_dev, self.near, condition=condition)

        def send_x(self, zk=z):
            self.copy(zk, x, x_dev, self.along_x)

        def send_own_x(self):
            self.copy(z, x, x_dev, self.own_x)

        def arrive_near(self):
            arrive(self.piece(z_near, x), self.near)

        def forward_near(self):
            self.arrive_near()
            if not self.cross:
                self.send_x(z_near)

        def forward_cross(self):
            arrive(self.piece(z, other_x), self.own_x)
            self.copy(z, other_x, near_dev, self.along_x)

        def pass_two(self):
            arrive(self.piece(z_two, x), self.two)
            self.copy(z_two, x, near_dev, self.mirror, True, inside)

        def forward_two(self):
            self.pass_two()
            self.send_x(z_two)

        def forward_mirror(self):
            arrive(self.piece(z_mirror, x), self.mirror)
            self.send_x(z_mirror)

        def finish(self):
            arrive(self.pieces(3 if self.cross else 4), self.along_x)

    class GroupGather:
        def __init__(self, slab, slabs, group=None):
            self.slab, self.slabs = slab, slabs
            self.group = sends(slabs(3)) if group is None else group
            self.from_y, self.others = arrivals(), arrivals()

        def send(self):
            mine = self.slab(d)
            copy_to(mine, mine, core_dev, self.others, self.group)
            copy_to(mine, mine, y_dev, self.from_y, self.group)

        def relay(self):
            slab = self.slab(y_d)
            arrive(slab, self.from_y)
            copy_to(slab, slab, core_dev, self.others, self.group)

        def finish(self):
            arrive(self.slabs(2), self.others)

    class RowSum:
        def __init__(self, name, total, block, step, cross):
            staged = getattr(s, "st_" + name)
            self.xs, self.zs, self.ns = (
                [staged.at[i + j] for j in range(n)] for i, n in ((0, 4), (4, 2), (6, 2))
            )
            self.xs = staged.at[pl.ds(0, 4)]
            self.xl, self.zl, self.nl = (getattr(s, p + name) for p in ("xl_", "zl_", "nl_"))
            self.total = total
            self.block, self.step, self.cross = block, step, cross
            self.count = self.total.shape[0]
            self.group = sends(staged.at[pl.ds(0, 7)])
            self.along_x = {k: arrivals() for k in ("mirror", "two", "own")}
            if not cross:
                self.along_x["near"] = arrivals()
            self.crossing, self.near, self.two, self.mirror, self.passing = (
                arrivals() for _ in range(5)
            )

        def stage(self, target, index, *extras):
            def one(at):
                value = self.block(index, at)
                for ref in extras:
                    value = value + ref[at, :].astype(F32)
                target[at, :] = value.astype(BF)

            by_rows(self.count, self.step, one)

        def send_x(self, name, zk, *extras):
            self.stage(self.xs.at[zk], 2 * zk + other_x, *extras)
            copy_to(self.xs.at[zk], self.xl.at[zk], x_dev, self.along_x[name], self.group)

        def arrive_x(self, name, zk):
            arrive(self.xl.at[zk], self.along_x[name])

        def send(self, early_near=False):
            self.send_x("mirror", z_mirror)
            if self.cross:
                self.send_crossing()
            self.send_x("two", z_two)
            if self.cross and early_near:
                self.send_near()
            if not self.cross:
                self.send_x("near", z_near)
                self.send_x("own", z)

        def send_crossing(self):
            self.stage(self.ns[0], 2 * z_near + other_x)
            copy_to(self.ns[0], self.nl.at[0], near_dev, self.crossing, self.group)

        def send_own(self):
            arrive(self.nl.at[0], self.crossing)
            self.send_x("own", z, self.nl.at[0])

        def send_mirror(self):
            self.arrive_x("mirror", z_mirror)
            self.stage(self.zs[0], 2 * z_mirror + x, self.xl.at[z_mirror])
            copy_to(self.zs[0], self.zl.at[0], mirror_dev, self.mirror, self.group, inside)
            copy_to(self.zs[0], self.zl.at[2], near_dev, self.passing, self.group, outside)

        def send_two_outside(self):
            @pl.when(outside)
            def _():
                self.arrive_x("two", z_two)
                self.stage(self.zs[1], 2 * z_two + x, self.xl.at[z_two])
                copy_to(self.zs[1], self.zl.at[1], two_dev, self.two, self.group)

        def send_two_inside(self):
            @pl.when(inside)
            def _():
                self.arrive_x("two", z_two)
                arrive(self.zl.at[2], self.passing)
                self.stage(self.zs[1], 2 * z_two + x, self.xl.at[z_two], self.zl.at[2])
                copy_to(self.zs[1], self.zl.at[1], two_dev, self.two, self.group)

        def send_near(self):
            extras = ()
            if not self.cross:
                self.arrive_x("near", z_near)
                extras = (self.xl.at[z_near],)
            self.stage(self.ns[1], 2 * z_near + x, *extras)
            copy_to(self.ns[1], self.nl.at[1], near_dev, self.near, self.group)

        def finish(self):
            self.arrive_x("own", z)
            arrive(self.zl.at[1], self.two)
            arrive(self.nl.at[1], self.near)

            def add(at):
                self.total[at, :] = (
                    self.block(r, at)
                    + self.xl[z, at, :].astype(F32)
                    + self.zl[1, at, :].astype(F32)
                    + self.nl[1, at, :].astype(F32)
                )

            by_rows(self.count, self.step, add)

            @pl.when(inside)
            def _():
                arrive(self.zl.at[0], self.mirror)

                def add_mirror(at):
                    self.total[at, :] += self.zl[0, at, :].astype(F32)

                by_rows(self.count, self.step, add_mirror)

    class SpreadSum:
        def __init__(self, half, shared):
            staged = getattr(s, f"st_qkv{half}")
            self.xs, self.cs, self.zs = staged.at[pl.ds(0, 4)], staged.at[4], staged.at[5]
            self.xl, self.cl, self.zl = (getattr(s, f"{p}_qkv{half}") for p in ("xl", "cl", "zl"))
            self.half = half
            self.group = sends(staged.at[pl.ds(0, 4)])
            self.inner, self.outer, self.last, self.final, self.final_mirror = shared
            self.along_x = {k: arrivals() for k in ("mirror", "two", "near", "own")}
            self.crossing, self.passing = arrivals(), arrivals()

        def value(self, index, *extras):
            rows = BLOCK // 2
            start_row = pl.multiple_of((2 * index + self.half) * rows, rows)
            value = s.g_qkv[pl.ds(start_row, rows), :]
            for extra in extras:
                value = value + extra.astype(F32)
            return value

        def send_x(self, name, zk, *extras):
            self.xs[zk] = self.value(2 * zk + other_x, *extras).astype(BF)
            copy_to(self.xs.at[zk], self.xl.at[zk], x_dev, self.along_x[name], self.group)

        def arrive_x(self, name, zk):
            arrive(self.xl.at[zk], self.along_x[name])

        def send_crossing(self):
            @pl.when(inside)
            def _():
                self.cs[...] = self.value(2 * z_near + other_x).astype(BF)
                copy_to(self.cs, self.cl, near_dev, self.crossing, self.group)

        def send_third(self):
            pl.when(inside)(lambda: self.send_x("own", z))
            pl.when(outside)(lambda: self.send_x("near", z_near))

        def send_own_outside(self):
            @pl.when(outside)
            def _():
                arrive(self.cl, self.crossing)
                self.send_x("own", z, self.cl[...])

        def deliver(self, slot, zk, value):
            for j in range(2):
                to = 2 * self.half + j
                at = 8 * self.half + 2 * slot + j
                for t, tile in enumerate(fold_qkv(tiles_of(value[CHUNK * j : CHUNK * (j + 1)]))):
                    s.ps[at, :, 128 * t : 128 * (t + 1)] = tile.astype(BF)
                copy_to(
                    s.ps.at[at],
                    s.fin.at[GROUP * slot + d],
                    (2 * zk + x, to),
                    self.final_mirror if slot == 2 else self.final,
                    self.inner if slot == 2 else self.last,
                    inside if slot == 2 else d != to if slot == 3 else None,
                )
                if slot == 3:

                    @pl.when(d == to)
                    def _(at=at):
                        s.fin[GROUP * slot + d] = s.ps[at]

        def send_mirror(self):
            self.arrive_x("mirror", z_mirror)
            value = self.value(2 * z_mirror + x, self.xl[z_mirror])
            self.deliver(2, z_mirror, value)
            self.zs[...] = value.astype(BF)
            copy_to(self.zs, self.zl, near_dev, self.passing, self.outer, outside)

        def send_two(self):
            self.arrive_x("two", z_two)

            @pl.when(outside)
            def _():
                self.zl[...] = jnp.zeros((BLOCK // 2, PACK), BF)

            pl.when(inside)(lambda: arrive(self.zl, self.passing))
            self.deliver(0, z_two, self.value(2 * z_two + x, self.xl[z_two], self.zl[...]))

        def send_near(self):
            pl.when(inside)(lambda: self.deliver(1, z_near, self.value(2 * z_near + x)))

            @pl.when(outside)
            def _():
                self.arrive_x("near", z_near)
                self.deliver(1, z_near, self.value(2 * z_near + x, self.xl[z_near]))

        def keep_own(self):
            self.arrive_x("own", z)
            self.deliver(3, z, self.value(r, self.xl[z]))

    class GroupSum:
        def __init__(self, name, source, parts=1):
            staged = getattr(s, "gs_" + name)
            self.s1, self.s2 = staged.at[pl.ds(0, 2)], staged.at[2]
            self.l1, self.l2 = (getattr(s, p + name) for p in ("l1_", "l2_"))
            self.source, self.parts, self.size = source, parts, OWN // parts
            self.group = sends(staged)
            self.first, self.second = arrivals(parts), arrivals(parts)
            self.kept = arrivals()

        def block(self, index, at):
            return self.source[pl.ds(pl.multiple_of(index * OWN + at.start, at.size), at.size), :]

        def part(self, i):
            return pl.ds(self.size * i, self.size)

        def over(self, i, body):
            def shifted(at):
                body(pl.ds(pl.multiple_of(self.size * i + at.start, at.size), at.size))

            by_rows(self.size, 32, shifted)

        def send(self, i=0):
            for j, yj in enumerate((other_y, yy)):

                def stage(at):
                    self.s1[j, at, :] = self.block(2 * yj + other_c, at).astype(BF)

                self.over(i, stage)
                copy_to(
                    self.s1.at[j, self.part(i)],
                    self.l1.at[j, self.part(i)],
                    core_dev,
                    self.kept if j else self.first + i,
                    self.group,
                )

        def middle(self, i=0):
            arrive(self.l1.at[0, self.part(i)], self.first + i)

            def stage(at):
                value = self.block(2 * other_y + c, at) + self.l1[0, at, :].astype(F32)
                self.s2[at, :] = value.astype(BF)

            self.over(i, stage)
            copy_to(
                self.s2.at[self.part(i)],
                self.l2.at[self.part(i)],
                y_dev,
                self.second + i,
                self.group,
            )

        def wait(self, i=0):
            if i == 0:
                arrive(self.l1.at[1], self.kept)
            arrive(self.l2.at[self.part(i)], self.second + i)

        def value(self, at):
            return (
                self.block(d, at)
                + self.l1[1, at, :].astype(F32)
                + self.l2[at, :].astype(F32)
            )

    class PieceGather:
        def __init__(self):
            self.group = sends(s.q_all.at[pl.ds(0, 27)])
            self.inner = sends(s.q_all.at[pl.ds(0, 8)], inside)
            self.own, self.two, self.near, self.mirror = (arrivals(2) for _ in range(4))
            self.along_x = {k: arrivals() for k in ("own", "near", "two", "mirror")}

        def fan(self, zk, arrival, group, condition=None):
            for i, m in enumerate((d, core_d, y_d, far_d)):
                if i == 0 and zk is z:
                    continue
                copy_to(
                    s.qp_s.at[m],
                    s.q_all.at[GROUP * r + d],
                    (2 * zk + x, m),
                    arrival + i // 2,
                    group,
                    condition,
                )

        def slab(self, zk, xk, h):
            first = GROUP * (2 * zk + xk) + 2 * (other_y if h else yy)
            return s.q_all.at[pl.ds(pl.multiple_of(first, 2), 2)]

        def send(self):
            self.fan(z, self.own, self.group)
            self.fan(z_two, self.two, self.group)
            self.fan(z_near, self.near, self.group)
            self.fan(z_mirror, self.mirror, self.inner, inside)

        def send_x(self, name, zk, h):
            slab = self.slab(zk, x, h)
            copy_to(slab, slab, x_dev, self.along_x[name], self.group)

        def forward_own(self, h):
            if h:
                arrive(self.slab(z, x, h), self.own + h)
            else:
                arrive(s.q_all.at[GROUP * r + core_d], self.own)
            self.send_x("own", z, h)

        def forward_near(self, h):
            arrive(self.slab(z_near, x, h), self.near + h)
            self.send_x("near", z_near, h)

        def forward_two(self, h):
            slab = self.slab(z_two, x, h)
            arrive(slab, self.two + h)
            copy_to(slab, slab, near_dev, self.mirror + h, self.inner, inside)
            self.send_x("two", z_two, h)

        def forward_mirror(self, h):
            arrive(self.slab(z_mirror, x, h), self.mirror + h)
            self.send_x("mirror", z_mirror, h)

        def finish(self, name, zk):
            first = pl.multiple_of(GROUP * (2 * zk + other_x), GROUP)
            arrive(s.q_all.at[pl.ds(first, GROUP)], self.along_x[name])

    def assemble(landing, count, target, row):
        for k in range(GROUP):
            landed = landing[k][...] if isinstance(landing, list) else landing[k]
            tiles = [t.astype(F32) for t in tiles_of(landed)]
            for t, tile in enumerate(unfold_qkv(tiles) if count == 5 else unfold(tiles, count)):
                s.tmp[CHUNK * k : CHUNK * (k + 1), 128 * t : 128 * (t + 1)] = tile
        rows_at(target, row, BLOCK)[...] = s.tmp[:, : 128 * count].astype(BF)

    def assemble_qkv(row):
        assemble([s.q_all.at[GROUP * row + k] for k in range(GROUP)], 5, s.w_qkv, row)

    lane = lane_id((CHUNK, 128))
    eye = row_id((CHUNK, CHUNK)) == lane_id((CHUNK, CHUNK))
    extra = jnp.zeros((CHUNK, 128), F32)
    for k in range(4):
        column = jnp.sum(jnp.where(eye, nrm[k : k + 1, :], 0.0), axis=1, keepdims=True)
        high = column.astype(BF).astype(F32)
        extra = jnp.where(lane == 96 + k, high, extra)
        extra = jnp.where(lane == 100 + k, column - high, extra)
    mask_row = mask[...].astype(F32)
    ones = jnp.sum(mask_row, axis=1, keepdims=True)
    extra = jnp.where((lane == 104) & (row_id((CHUNK, 128)) == 0), ones, extra)

    loads["wq"].wait()
    wq_tiles = tiles_of(wq[...].astype(F32))
    for k in range(GROUP):
        tiles = permute_chunks(wq_tiles, qkv_picks(k))
        tiles[2] = tiles[2] + extra
        for t, tile in enumerate(fold_qkv(tiles)):
            s.qp_s[k, :, 128 * t : 128 * (t + 1)] = tile.astype(BF)
    s.q_all[GROUP * r + d] = s.qp_s[d]
    loads["wo"].wait()
    for t, tile in enumerate(fold(tiles_of(wo[...].astype(F32)))):
        s.wo_l[d, x, z, :, 128 * t : 128 * (t + 1)] = tile.astype(BF)
    loads["wu"].wait()
    wu_tiles = tiles_of(wu[...].astype(F32))
    for k in range(GROUP):
        for t, tile in enumerate(fold(permute_chunks(wu_tiles, up_picks(k)))):
            s.up_s[k, :, 128 * t : 128 * (t + 1)] = tile.astype(BF)
    s.up_l[d] = s.up_s[d]
    diagonal = jnp.where(
        row_id((OWN, OWN)) == lane_id((OWN, OWN)), jnp.broadcast_to(mask_row, (OWN, OWN)), 0.0
    )
    loads["cot"].wait()
    s.c_all[d] = dot(diagonal.astype(BF), cot[...]).astype(BF)
    loads["x"].wait()
    loads["wd"].wait()
    pl.semaphore_wait(barrier, len(partners))

    qkv_gather = PieceGather()
    qkv_gather.send()
    out_gather = Gather(
        lambda zk, xk: s.wo_l.at[d, xk, zk],
        lambda n: s.wo_l.at[0, 0, pl.ds(0, n)] if n <= 4 else s.wo_l.at[0, :, pl.ds(0, n // 2)],
    )
    out_gather.send_two()
    out_gather.send_mirror()
    out_gather.send_near()
    out_gather.send_own_x()
    up_arrival, up_group = arrivals(), sends(s.up_s.at[pl.ds(0, 3)])
    for m, device in mates:
        copy_to(s.up_s.at[m], s.up_l.at[d], device, up_arrival, up_group)
    x_gather = GroupGather(lambda i: s.x_all.at[i], lambda n: s.x_all.at[pl.ds(0, n)])
    x_gather.send()
    up_gather = Gather(
        lambda zk, xk: rows_at(s.w_up, 2 * zk + xk, BLOCK),
        lambda n: s.w_up.at[pl.ds(0, n * BLOCK)],
        cross=True,
    )
    downs = [
        Gather(
            lambda zk, xk, h=h: rows_at(s.w_down, 2 * (2 * zk + xk) + h, BLOCK // 2),
            lambda n: s.w_down.at[pl.ds(0, n * BLOCK // 2)],
            cross=h == 0,
        )
        for h in range(2)
    ]
    c_gather = GroupGather(lambda i: s.c_all.at[i], lambda n: s.c_all.at[pl.ds(0, n)])
    c_gather.send()

    def normalize(i):
        def one(at):
            normal, _ = standardize(s.x_all[i, at, :].astype(F32))
            s.normal[pl.ds(pl.multiple_of(OWN * i + at.start, at.size), at.size), :] = normal

        by_rows(OWN, 64, one)

    for half in downs:
        half.send_own_x()
    qkv_gather.forward_own(0)
    qkv_gather.forward_own(1)
    qkv_gather.forward_near(0)
    assemble_qkv(r)
    qkv_gather.forward_two(0)
    qkv_gather.forward_near(1)
    assemble_qkv(2 * z_near + x)
    qkv_gather.forward_two(1)
    out_gather.pass_two()
    assemble_qkv(2 * z_two + x)
    arrive(s.up_l.at[pl.ds(0, 3)], up_arrival)
    assemble(s.up_l, 6, s.w_up, r)
    up_gather.send_two()
    up_gather.send_near(True)
    qkv_gather.forward_mirror(0)
    x_gather.relay()
    qkv_gather.forward_mirror(1)
    up_gather.send_near(False)
    up_gather.send_mirror()
    for half in downs:
        half.send_two()
        half.send_near()
    out_gather.send_x(z_two)
    out_gather.forward_near()
    out_gather.forward_mirror()
    up_gather.send_own_x()
    columns = [
        GroupGather(lambda i, xk=xk: s.wo_l.at[i, xk], lambda n: s.wo_l.at[pl.ds(0, n), 0])
        for xk in (x, other_x)
    ]
    columns[0].send()
    assemble_qkv(2 * z_mirror + x)
    x_gather.finish()
    for i in range(GROUP):
        normalize(i)
    for name, zk in (("own", z), ("near", z_near), ("two", z_two)):
        qkv_gather.finish(name, zk)
        assemble_qkv(2 * zk + other_x)
    c_gather.relay()
    qkv_gather.finish("mirror", z_mirror)
    assemble_qkv(2 * z_mirror + other_x)

    lane = lane_id((8, 128))
    row = row_id((8, 128))
    pick = jnp.where((lane == 96 + row) | (lane == 100 + row), 1.0, 0.0)
    pick = jnp.where(row < 4, pick, jnp.where((row == 4) & (lane == 104), 1.0, 0.0))
    s.norms[...] = dot(pick.astype(BF), s.w_qkv[:, 256:384], 1, 1)
    total = jnp.sum(s.norms[4:5, :], axis=1, keepdims=True)
    loss_scale = (SEQ * ROWS) / total
    own_weight = dw[d]
    last_weight = dw[GROUP]

    def first_norm(at):
        value = s.normal[at, :] * (1.0 + s.norms[0:1, :]) + s.norms[1:2, :]
        s.h1[at, :] = value.astype(BF)

    by_rows(SEQ, 64, first_norm)

    def project(at):
        value = dot(s.h1[at, :], s.w_qkv[...])
        co, si = cosine[at, :], sine[at, :]
        for left, target in ((0, s.qv), (256, s.kk)):
            a, b = value[:, left : left + 128], value[:, left + 128 : left + 256]
            target[at, :128] = (a * co - b * si).astype(BF)
            target[at, 128:] = (b * co + a * si).astype(BF)
        s.v01[at, :] = value[:, 512:].astype(BF)

    loads["cosine"].wait()
    loads["sine"].wait()
    by_rows(SEQ, 256, project)

    lane2 = lax.div(lax.rem(lane_id((1, 256)), 128), jnp.int32(32))
    head_mask = [jnp.where(lane2 == h, 1.0, 0.0).astype(BF) for h in range(3)]
    tail_mask = jnp.where(lane2 == 3, 1.0, 0.0).astype(BF)
    half_id = lax.div(lane_id((1, 128)), jnp.int32(64))
    half_mask = [jnp.where(half_id == h, 1.0, 0.0).astype(BF) for h in range(2)]
    root = HD**-0.5
    o_gathers = [
        GroupGather(lambda i, b=b: s.o_l.at[i, b], lambda n: s.o_l.at[pl.ds(0, n), 0])
        for b in range(2)
    ]

    def attend(b):
        rows = slice(QBLOCK * b, QBLOCK * (b + 1))
        keys = QBLOCK * (b + 1)
        query = s.qv[rows, :]
        allowed = row_id((QBLOCK, keys)) + QBLOCK * b >= lane_id((QBLOCK, keys))
        first = jnp.zeros((QBLOCK, 128), F32)
        third = None
        for h in range(3):
            scores = dot(query * head_mask[h], s.kk[:keys, :], 1, 1) * root
            scores = jnp.where(allowed, scores, -1e30)
            raised = jnp.exp(scores - jnp.max(scores, axis=1, keepdims=True))
            probs = raised * (1.0 / jnp.sum(raised, axis=1, keepdims=True))
            s.probs[h, rows, :keys] = probs
            if h < 2:
                first = first + dot(probs.astype(BF), s.v01[:keys, :] * half_mask[h])
            else:
                third = dot(probs.astype(BF), s.qv[:keys, :])
            if b == 1 and h == 0:
                up_gather.forward_two()
                for half in downs:
                    half.send_mirror()
            if b == 1 and h == 1:
                out_gather.finish()
                columns[1].send()
        s.o_l[d, b, :QBLOCK, :] = first.astype(BF)
        lane = lane_id((QBLOCK, 128))
        third = jnp.where(
            lane < 32, pltpu.roll(third[:, :128], 32, 1), pltpu.roll(third[:, 128:], 64, 1)
        )
        lane = lane_id((OWN, 128))
        third = jnp.where(lane < 64, third[:OWN], pltpu.roll(third[OWN:], 64, 1))
        s.o_l[d, b, QBLOCK:, :] = third.astype(BF)
        o_gathers[b].send()

    attend(1)
    columns[0].relay()
    attend(0)
    for h in range(3):
        s.probs[h, :QBLOCK, QBLOCK:] = jnp.zeros((QBLOCK, QBLOCK), F32)
    s.v_all[:, :256] = s.qv[...]
    s.v_all[:, 256:] = s.v01[...]
    up_gather.forward_cross()
    columns[1].relay()
    downs[1].forward_near()
    up_gather.forward_mirror()
    for column in columns:
        column.finish()
    for k in range(GROUP):
        for i in range(ROWS):
            tiles = [t.astype(F32) for t in tiles_of(s.wo_l[k, i % 2, i // 2])]
            at = CHUNK * (GROUP * i + k)
            for t, tile in enumerate(unfold(tiles, 6)):
                s.g_out[at : at + CHUNK, 128 * t : 128 * (t + 1)] = tile

    def out_place(head):
        k, h = divmod(head, 3)
        return 128 * k + 64 * h if h < 2 else 512 + 64 * k

    for head in range(HEADS):
        at = out_place(head)
        s.w_out[at : at + 64, :] = s.g_out[64 * head : 64 * head + 64, :].astype(BF)
    s.w_own[...] = jnp.zeros((384, WIDTH), BF)
    third_rows = rows_at(s.w_out.at[pl.ds(512, 256)], d, 64)
    s.w_own[96:128, :] = third_rows[:32, :]
    s.w_own[224:256, :] = third_rows[32:, :]
    s.w_own[256:, :] = rows_at(s.w_out.at[pl.ds(0, 512)], d, 128)[...]
    downs[0].forward_two()
    downs[0].forward_cross()
    o_gathers[1].relay()
    c_gather.finish()

    loads["hist"].wait()
    s.terms[...] = jnp.zeros((8, WIDTH), F32)
    for i in range(GROUP):

        def loss_rows(at, i=i):
            here = pl.ds(pl.multiple_of(OWN * i + at.start, at.size), at.size)
            grad = s.c_all[i, at, :].astype(F32) * loss_scale
            s.dm[here, :] = (last_weight * grad).astype(BF)
            hg_o[here, :] = (own_weight * grad).astype(BF)
            s.terms[...] += sublane_sum(grad * hist[here, :].astype(F32))

        by_rows(OWN, 32, loss_rows)

    downs[1].forward_two()
    for b in (1, 0):
        if b == 0:
            o_gathers[0].relay()
            downs[0].forward_mirror()
        o_gathers[b].finish()
        rows = slice(QBLOCK * b, QBLOCK * (b + 1))
        thirds = []
        for k in range(GROUP):
            s.ob[rows, 128 * k : 128 * (k + 1)] = s.o_l[k, b, :QBLOCK, :]
            thirds.append(s.o_l[k, b, QBLOCK:, :].astype(F32))
        lane = lane_id((OWN, 128))
        for p in range(2):
            even, odd = thirds[2 * p], thirds[2 * p + 1]
            top = jnp.where(lane < 64, even, pltpu.roll(odd, 64, 1))
            low = jnp.where(lane < 64, pltpu.roll(even, 64, 1), odd)
            cols = slice(512 + 128 * p, 640 + 128 * p)
            s.ob[QBLOCK * b : QBLOCK * b + OWN, cols] = top.astype(BF)
            s.ob[QBLOCK * b + OWN : QBLOCK * (b + 1), cols] = low.astype(BF)
        s.y[rows, :] = dot(s.ob[rows, :], s.w_out[...])
        for i in (2 * b, 2 * b + 1):

            def second_norm(at, i=i):
                here = pl.ds(pl.multiple_of(OWN * i + at.start, at.size), at.size)
                value = s.y[here, :] + s.x_all[i, at, :].astype(F32)
                s.y[here, :] = value
                normal, _ = standardize(value)
                value = normal * (1.0 + s.norms[2:3, :]) + s.norms[3:4, :]
                s.h2[here, :] = value.astype(BF)

            by_rows(OWN, 64, second_norm)

    downs[1].forward_mirror()
    up_gather.arrive_near()
    up_gather.finish()

    def widen(at):
        s.part[at, :] = dot(s.h2[at, :], s.w_up[...])

    by_rows(SEQ, 256, widen)

    rate = 0.7978845608028654

    def gate(at):
        u = s.part[at, :]
        bend = jnp.tanh(rate * (u + 0.044715 * u * u * u))
        s.act[at, :] = (0.5 * u * (1.0 + bend)).astype(BF)
        s.slope[at, :] = bend

    by_rows(SEQ, 32, gate)

    def gate_slope(at):
        u, bend = s.part[at, :], s.slope[at, :]
        inner = rate * (1.0 + 3 * 0.044715 * u * u)
        s.slope[at, :] = 0.5 * (1.0 + bend) + 0.5 * u * (1.0 - bend * bend) * inner

    def block_of(ref, shift=0):
        def block(index, at):
            start = pl.multiple_of(index * BLOCK + shift + at.start, at.size)
            return ref[pl.ds(start, at.size), :]

        return block

    for i in range(3):
        cols = slice(QBLOCK * i, QBLOCK * (i + 1))
        s.g_down[cols, :] = dot(s.act[:, cols], s.dm[...], 0, 0)
    down_sum = RowSum("down", s.f_down, block_of(s.g_down), 16, True)
    down_sum.send(early_near=True)
    by_rows(SEQ, 32, gate_slope)
    downs[0].arrive_near()
    for half in downs:
        half.finish()

    mid_sum = GroupSum("mid", s.part, 4)

    def quarter(ref, i, size=32):
        return jnp.concatenate(
            [ref[OWN * j + 32 * i : OWN * j + 32 * i + size, :] for j in range(GROUP)], axis=0
        )

    def put_quarter(ref, i, value, size=32):
        for j in range(GROUP):
            ref[OWN * j + 32 * i : OWN * j + 32 * i + size, :] = value[size * j : size * (j + 1)]

    for i in (0, 2):
        value = dot(quarter(s.dm, i, 64), s.w_down[...], 1, 1)
        value = (value * quarter(s.slope, i, 64)).astype(BF)
        put_quarter(s.du, i, value, 64)
        put_quarter(s.part, i, dot(value, s.w_up[...], 1, 1), 64)
        mid_sum.send(i)
        mid_sum.send(i + 1)
    for i in range(3):
        mid_sum.middle(i)
    down_sum.send_mirror()
    mid_sum.middle(3)
    down_sum.send_own()

    def up_part(i):
        cols = slice(QBLOCK * i, QBLOCK * (i + 1))
        s.g_up[cols, :] = dot(s.h2[:, cols], s.du[...], 0, 0)

    up_part(0)
    s.terms2[...] = jnp.zeros((8, WIDTH), F32)
    s.t0[...] = jnp.zeros((8, WIDTH), F32)

    def second_norm_back(at):
        here = pl.ds(pl.multiple_of(OWN * d + at.start, at.size), at.size)
        grad = mid_sum.value(at)
        value = s.y[here, :]
        normal, scale = standardize(value)
        loss = s.c_all[d, at, :].astype(F32) * loss_scale
        back = last_weight * loss + norm_back(grad, s.norms[2:3, :], normal, scale)
        s.dy[at, :] = back
        s.dyb[d, at, :] = back.astype(BF)
        s.t0[2:3, :] += jnp.sum(grad * normal, axis=0, keepdims=True)
        s.t0[3:4, :] += jnp.sum(grad, axis=0, keepdims=True)
        s.terms2[...] += sublane_sum(loss * value)

    up_sum = RowSum("up", s.f_up, block_of(s.g_up), 16, True)
    dy_gathers = []
    dy_group = sends(s.dyb.at[pl.ds(0, 3)])
    for i in range(4):
        mid_sum.wait(i)
        mid_sum.over(i, second_norm_back)
        dy_gathers.append(
            GroupGather(
                lambda j, i=i: s.dyb.at[j, mid_sum.part(i)],
                lambda n: s.dyb.at[pl.ds(0, n), mid_sum.part(0)],
                dy_group,
            )
        )
        dy_gathers[i].send()
        if i < 2:
            up_part(i + 1)
        if i == 2:
            up_sum.send()

    def block_out(at):
        value = dot(s.act[at, :], s.w_down[...])
        s.part2[at, :] = value

    by_rows(SEQ, 256, block_out)
    def mix_quarter(i):
        def mix(at):
            here = pl.ds(pl.multiple_of(OWN * i + at.start, at.size), at.size)
            value = s.part2[here, :]
            loss = s.c_all[i, at, :].astype(F32) * loss_scale
            s.terms2[...] += sublane_sum(loss * value)
            s.part2[here, :] = own_weight * hist[here, :].astype(F32) + last_weight * value

        by_rows(OWN, 32, mix)

    down_sum.send_two_outside()
    dy_gathers[0].relay()
    mix_quarter(0)
    mix_quarter(1)
    dy_gathers[1].relay()
    mix_quarter(2)
    mix_quarter(3)
    mix_sum = GroupSum("mix", s.part2)
    mix_sum.send()
    lane = lane_id((8, 128))
    own_term = jnp.sum(jnp.sum(s.terms[...], axis=0, keepdims=True), axis=1, keepdims=True)
    last_term = jnp.sum(jnp.sum(s.terms2[...], axis=0, keepdims=True), axis=1, keepdims=True)
    s.u0[...] = jnp.where(lane == d, own_term, jnp.where(lane == GROUP, last_term, 0.0))
    depth_x, depth_z, depth_d = (arrivals() for _ in range(3))
    depth_group = sends(s.uzd.at[pl.ds(0, 7)])
    copy_to(s.u0, s.u1, x_dev, depth_x, depth_group)
    down_sum.send_two_inside()

    lane = lane_id((1, 384))
    head_lanes = [jnp.where(lax.div(lane, jnp.int32(64)) == 4 + h, 1.0, 0.0) for h in range(2)]
    head_scale = [jnp.where(lane2 == h, root, 0.0) for h in range(3)]
    head_lanes = [m.astype(BF) for m in head_lanes + [jnp.where(lane < 256, 1.0, 0.0)]]
    for i in range(4):
        dy_gathers[i].finish()
        rows = s.dyb[:, 32 * i : 32 * (i + 1), :].reshape(OWN, WIDTH)
        grad = dot(rows, s.w_own[...], 1, 1).astype(BF)
        grad = jnp.concatenate([grad * m for m in head_lanes], axis=0)
        probs = jnp.concatenate([quarter(s.probs.at[h], i) for h in range(3)], axis=0)
        dp = dot(grad, s.v_all[...], 1, 1)
        delta = jnp.sum(dp * probs, axis=1, keepdims=True)
        ds = (probs * (dp - delta)).astype(BF)
        query = quarter(s.qv, i)
        query = jnp.concatenate([query * m for m in head_mask], axis=0)
        dk = dot(ds, query, 0, 0) * root
        dv = dot(probs.astype(BF), grad, 0, 0)
        if i == 0:
            s.dk[...] = dk
            s.dv[...] = dv
        else:
            s.dk[...] += dk
            s.dv[...] += dv
        dq = dot(ds, s.kk[...])
        dq = sum(dq[OWN * h : OWN * (h + 1)] * head_scale[h] for h in range(3))
        put_quarter(s.dq, i, dq)
        if i < 2:
            dy_gathers[i + 2].relay()
        if i == 1:
            up_sum.send_mirror()
            up_sum.send_own()
            mix_sum.middle()
        if i == 2:
            up_sum.send_near()

    def turn_back(at):
        co, si = cosine[at, :], sine[at, :]
        for left, source in ((0, s.dq), (256, s.dk)):
            a, b = source[at, :128], source[at, 128:]
            first, second = a * co + b * si, b * co - a * si
            if left == 0:
                first, second = first + s.dv[at, :128], second + s.dv[at, 128:256]
            s.dqkv[at, left : left + 128] = first.astype(BF)
            s.dqkv[at, left + 128 : left + 256] = second.astype(BF)
        s.dqkv[at, 512:] = s.dv[at, 256:].astype(BF)

    by_rows(SEQ, 64, turn_back)
    up_sum.send_two_outside()
    for i in range(3):
        cols = slice(QBLOCK * i, QBLOCK * (i + 1))
        s.g_qkv[cols, :] = dot(s.h1[:, cols], s.dqkv[...], 0, 0)
    shared = (
        sends(s.fin.at[pl.ds(0, 4)], inside),
        sends(s.st_qkv0.at[pl.ds(0, 2)], outside),
        sends(s.fin.at[pl.ds(0, 11)]),
        arrivals(),
        arrivals(),
    )
    sums = [SpreadSum(h, shared) for h in range(2)]
    for one in sums:
        one.send_x("mirror", z_mirror)
        one.send_crossing()
    for one in sums:
        one.send_x("two", z_two)
    for one in sums:
        one.send_third()
    arrive(s.u1, depth_x)
    s.uzd[z] = s.u0[...] + s.u1[...]
    for device in (two_dev, mirror_dev, near_dev):
        copy_to(s.uzd.at[z], s.uzd.at[z], device, depth_z, depth_group)

    def first_back(at):
        s.part[at, :] = dot(s.dqkv[at, :], s.w_qkv[...], 1, 1)

    by_rows(SEQ, 256, first_back)
    in_sum = GroupSum("in", s.part)
    in_sum.send()
    up_sum.send_two_inside()
    s.gain_sum[...] = jnp.zeros((8, WIDTH), F32)
    s.shift_sum[...] = jnp.zeros((8, WIDTH), F32)

    def first_norm_sums(at):
        grad = s.part[at, :]
        s.gain_sum[...] += sublane_sum(grad * s.normal[at, :])
        s.shift_sum[...] += sublane_sum(grad)

    by_rows(SEQ, 32, first_norm_sums)
    s.t0[0:1, :] = jnp.sum(s.gain_sum[...], axis=0, keepdims=True)
    s.t0[1:2, :] = jnp.sum(s.shift_sum[...], axis=0, keepdims=True)
    s.td[d] = s.t0[...]
    norm_arrival, norm_group = arrivals(), sends(s.td.at[pl.ds(0, 3)])
    for m, device in mates:
        copy_to(s.td.at[d], s.td.at[d], device, norm_arrival, norm_group)
    in_sum.middle()
    for p in range(3):
        cols = slice(QBLOCK * p, QBLOCK * (p + 1))
        value = dot(s.ob[:, cols], s.dyb[...].reshape(SEQ, WIDTH), 0, 0)
        for i in range(4):
            place = QBLOCK * p + 64 * i
            for head in range(HEADS):
                if out_place(head) == place:
                    s.g_out[64 * head : 64 * head + 64, :] = value[64 * i : 64 * i + 64]

    for one in sums:
        one.send_mirror()
    arrive(s.td.at[pl.ds(0, 3)], norm_arrival)
    value = (s.td[0] + s.td[1]) + (s.td[2] + s.td[3])
    value = pltpu.roll(value, lax.rem(WIDTH - CHUNK * d, WIDTH), 1)
    for i in range(ROWS):
        shift = (WIDTH - BLOCK * i) % WIDTH
        shifted = pltpu.roll(value, shift, 1) if shift else value
        s.ext[i] = jnp.concatenate([shifted[:, :128], jnp.zeros((8, 128), F32)], axis=0)

    def out_block(index, at):
        start_row = pl.multiple_of((GROUP * index + d) * CHUNK, 8)
        tiles = tiles_of(s.g_out[pl.ds(start_row, CHUNK), :])
        return jnp.concatenate(fold(tiles) + [s.ext[index]], axis=1)

    out_sum = RowSum("out", s.f_out, out_block, 16, False)
    out_sum.send_x("mirror", z_mirror)
    out_sum.send_x("two", z_two)
    for one in sums:
        one.send_own_outside()
    out_sum.send_x("near", z_near)
    out_sum.send_x("own", z)

    down_sum.finish()
    gd_o[...] = s.f_down[...]
    def spread(total, staged, landing):
        arrival, group = arrivals(), sends(staged.at[pl.ds(0, 3)])
        for m, device in mates:
            rows = total[pl.ds(pl.multiple_of(CHUNK * m, CHUNK), CHUNK), :]
            for t, tile in enumerate(fold(tiles_of(rows))):
                staged[m, :, 128 * t : 128 * (t + 1)] = tile.astype(BF)
            copy_to(staged.at[m], landing.at[d], device, arrival, group)
        rows = total[pl.ds(pl.multiple_of(CHUNK * d, CHUNK), CHUNK), :]
        for t, tile in enumerate(fold(tiles_of(rows))):
            landing[d, :, 128 * t : 128 * (t + 1)] = tile.astype(BF)
        return arrival

    def collect(arrival, landing, count, back, target):
        arrive(landing.at[pl.ds(0, 3)], arrival)
        tiles = []
        for k in range(GROUP):
            tiles += unfold([t.astype(F32) for t in tiles_of(landing[k])], count)
        for t, tile in enumerate(permute_chunks(tiles, back)):
            target[:, 128 * t : 128 * (t + 1)] = tile

    mix_sum.wait()

    def write_out(at):
        here = pl.ds(pl.multiple_of(OWN * d + at.start, at.size), at.size)
        out_o[at, :] = (mix_sum.value(at) + last_weight * s.y[here, :]).astype(BF)

    by_rows(OWN, 32, write_out)

    for one in sums:
        one.send_two()
    out_sum.send_mirror()
    in_sum.wait()

    def first_norm_back(at):
        grad = in_sum.value(at)
        normal, scale = standardize(s.x_all[d, at, :].astype(F32))
        back = norm_back(grad, s.norms[0:1, :], normal, scale)
        ig_o[at, :] = (s.dy[at, :] + back).astype(BF)

    by_rows(OWN, 32, first_norm_back)
    for one in sums:
        one.send_near()
    up_sum.finish()
    up_spread = spread(s.f_up, s.b_up, s.a_up)
    arrive(s.uzd.at[pl.ds(0, 3)], depth_z)
    s.uzd[4 + d] = (s.uzd[0] + s.uzd[1]) + (s.uzd[2] + s.uzd[3])
    for m, device in mates:
        copy_to(s.uzd.at[4 + d], s.uzd.at[4 + d], device, depth_d, depth_group)
    for one in sums:
        one.keep_own()
    out_sum.send_two_outside()
    out_sum.send_two_inside()
    out_sum.send_near()
    arrive(s.uzd.at[pl.ds(0, 3)], depth_d)
    dg_o[...] = (s.uzd[4] + s.uzd[5]) + (s.uzd[6] + s.uzd[7])

    arrive(s.fin.at[pl.ds(0, 11)], shared[3])
    for k in range(GROUP):
        s.q_sum[k] = (
            s.fin[12 + k].astype(F32) + s.fin[4 + k].astype(F32) + s.fin[k].astype(F32)
        )

    @pl.when(inside)
    def _():
        arrive(s.fin.at[pl.ds(0, 4)], shared[4])
        for k in range(GROUP):
            s.q_sum[k] += s.fin[8 + k].astype(F32)

    tiles = []
    for k in range(GROUP):
        tiles += unfold_qkv(tiles_of(s.q_sum[k]))
    for t, tile in enumerate(permute_chunks(tiles, QKV_BACK)):
        gq_o[:, 128 * t : 128 * (t + 1)] = tile
    collect(up_spread, s.a_up, 6, UP_BACK, gu_o)
    out_sum.finish()
    for t, tile in enumerate(unfold(tiles_of(s.f_out[:, :1152]), 6)):
        go_o[:, 128 * t : 128 * (t + 1)] = tile
    ng_o[...] = s.f_out[:8, 1152:]
    for group, view, condition in send_groups:
        wait = prepare(view, view, x_dev, 0, group).wait_send
        if condition is None:
            wait()
        else:
            pl.when(condition)(wait)
    assert used["send"] <= N_SENDS and used["arrival"] <= N_ARRIVALS, used


def finish_kernel(*refs):
    count = N_OUT - 2
    ins, refs = refs[:count], refs[count:]
    (norm, depth), refs = refs[:2], refs[2:]
    outs, (norm_o, depth_o), sems = refs[:count], refs[count : count + 2], refs[-1]
    copies = [pltpu.make_async_copy(a, b, sems.at[i]) for i, (a, b) in enumerate(zip(ins, outs))]
    for copy in copies:
        copy.start()
    norm_o[...] = norm[:4, :CHUNK]
    depth_o[...] = depth[:1, : GROUP + 1]
    for copy in copies:
        copy.wait()


def fused(
    block_input,
    history,
    cotangent,
    token_mask,
    qkv_weight,
    out_weight,
    up_weight,
    down_weight,
    norm_params,
    depth_weights,
):
    cosine, sine = tables()
    vmem = pl.BlockSpec(memory_space=pltpu.VMEM)
    smem = pl.BlockSpec(memory_space=pltpu.SMEM)
    hbm = pl.BlockSpec(memory_space=pltpu.HBM)
    shape = jax.ShapeDtypeStruct
    shapes = (
        shape((OWN, WIDTH), BF),
        shape((OWN, WIDTH), BF),
        shape((SEQ, WIDTH), BF),
        shape((CHUNK, 3 * WIDTH), F32),
        shape((CHUNK, WIDTH), F32),
        shape((CHUNK, 4 * WIDTH), F32),
        shape((BLOCK, WIDTH), F32),
        shape((8, 128), F32),
        shape((8, 128), F32),
    )
    outs = pl.pallas_call(
        fused_kernel,
        out_shape=tuple(pltpu.VMEM(one.shape, one.dtype) for one in shapes),
        in_specs=[hbm] * 3 + [vmem] + [hbm] * 4 + [vmem, smem] + [hbm] * 2,
        out_specs=[vmem] * 9,
        scratch_shapes=[pltpu.VMEM(dims, kind) for dims, kind in SCRATCH.values()]
        + [pltpu.SemaphoreType.DMA((n,)) for n in (N_SENDS, N_ARRIVALS, 9)],
        compiler_params=pltpu.CompilerParams(
            collective_id=0, has_side_effects=True, vmem_limit_bytes=VMEM_MIB * 2**20
        ),
        cost_estimate=pl.CostEstimate(flops=12 * 10**9, bytes_accessed=4 * 10**6, transcendentals=10**6),
    )(
        block_input,
        history.reshape(SEQ, WIDTH),
        cotangent,
        token_mask.reshape(1, OWN),
        qkv_weight,
        out_weight,
        up_weight,
        down_weight,
        norm_params,
        depth_weights,
        jnp.asarray(cosine),
        jnp.asarray(sine),
    )
    held = pl.pallas_call(
        finish_kernel,
        out_shape=shapes[:7] + (shape((4, CHUNK), F32), shape((1, GROUP + 1), F32)),
        in_specs=[vmem] * 9,
        out_specs=[hbm] * 7 + [vmem] * 2,
        scratch_shapes=[pltpu.SemaphoreType.DMA((7,))],
        compiler_params=pltpu.CompilerParams(vmem_limit_bytes=4 * 2**20),
    )(*outs)
    out, input_grad, history_grad, *grads, g_depth = held
    return (out, input_grad, history_grad.reshape(1, SEQ, WIDTH), *grads, g_depth.reshape(GROUP + 1))


def fits(mesh, block_input, history, up_weight):
    devices = ROWS * GROUP
    return (
        mesh.shape["rows"] == ROWS
        and mesh.shape["depth"] == GROUP
        and block_input.shape == (OWN * devices, WIDTH)
        and history.shape[0] == GROUP
        and up_weight.shape == (WIDTH, 4 * WIDTH)
    )


def solution(mesh):
    weights = P(("rows", "depth"), None)
    in_specs = (
        weights,
        P("depth", "rows", None),
        weights,
        P(("rows", "depth")),
        weights,
        weights,
        weights,
        weights,
        P(None, ("rows", "depth")),
        P(),
    )
    out_specs = (
        weights,
        weights,
        P("depth", "rows", None),
        weights,
        weights,
        weights,
        weights,
        P(None, ("rows", "depth")),
        P(),
    )

    def run(*args):
        body = fused if fits(mesh, args[0], args[1], args[6]) else local
        return jax.shard_map(
            body, mesh=mesh, in_specs=in_specs, out_specs=out_specs, check_vma=False
        )(*args)

    return run
```

```python
import functools

import jax
import jax.numpy as jnp
import numpy as np
from jax import lax
from jax.experimental import pallas as pl
from jax.experimental.pallas import tpu as pltpu
from jax.sharding import PartitionSpec as P

HEADS = 12
HD = 64


def norm_rows(value, gain, shift):
    center = value - jnp.mean(value, axis=-1, keepdims=True)
    spread = jnp.mean(center * center, axis=-1, keepdims=True)
    return center * lax.rsqrt(spread + 1e-05) * (1.0 + gain) + shift


def rotate(value, place, sign):
    half = value.shape[-1] // 2
    freq = 10000.0 ** (-jnp.arange(half, dtype=jnp.float32) / half)
    angle = place.astype(jnp.float32)[:, None] * freq[None, :]
    cosine = jnp.cos(angle)[:, None, :]
    sine = jnp.sin(angle)[:, None, :] * sign
    first = value[..., :half]
    second = value[..., half:]
    return jnp.concatenate(
        [first * cosine - second * sine, second * cosine + first * sine], axis=-1
    )


def block_scores(query, key_block, start, query_place, scale):
    block_len = key_block.shape[0]
    scores = (
        jnp.einsum("qhd,khd->hqk", query, key_block, preferred_element_type=jnp.float32) * scale
    )
    key_place = start + jnp.arange(block_len, dtype=jnp.int32)
    allowed = query_place[:, None] >= key_place[None, :]
    return (scores, allowed)


def local(
    block_input,
    history,
    cotangent,
    token_mask,
    qkv_weight,
    out_weight,
    up_weight,
    down_weight,
    norm_params,
    depth_weights,
):
    rows_tok, width = block_input.shape
    depth_count = lax.axis_size("depth")
    device_count = lax.axis_size("rows") * depth_count
    place_depth = lax.axis_index("depth")
    heads = HEADS
    head_size = HD
    scale = head_size ** (-0.5)
    seq_len = rows_tok * depth_count
    slot_count = history.shape[0]
    hist_total = slot_count * depth_count
    wide_qkv, wide_out, wide_up, wide_down, wide_norms = (
        lax.all_gather(qkv_weight, ("rows", "depth"), axis=0, tiled=True),
        lax.all_gather(out_weight, ("rows", "depth"), axis=0, tiled=True),
        lax.all_gather(up_weight, ("rows", "depth"), axis=0, tiled=True),
        lax.all_gather(down_weight, ("rows", "depth"), axis=0, tiled=True),
        lax.all_gather(
            norm_params.astype(jnp.bfloat16), ("rows", "depth"), axis=1, tiled=True
        ).astype(norm_params.dtype),
    )
    total = lax.psum(jnp.sum(token_mask), ("rows", "depth")).astype(jnp.float32)
    loss_scale = rows_tok * device_count / total
    float_input = block_input.astype(jnp.float32)
    place = place_depth * rows_tok + jnp.arange(rows_tok, dtype=jnp.int32)
    first = norm_rows(float_input, wide_norms[0], wide_norms[1]).astype(jnp.bfloat16)
    projected = jnp.dot(first, wide_qkv, preferred_element_type=jnp.float32)
    query = rotate(projected[:, :width].reshape(rows_tok, heads, head_size), place, 1.0).astype(
        jnp.bfloat16
    )
    keys = rotate(projected[:, width : 2 * width].reshape(rows_tok, heads, head_size), place, 1.0)
    keys = keys.astype(jnp.bfloat16).reshape(rows_tok, width)
    values = projected[:, 2 * width :].astype(jnp.bfloat16)
    all_keys, all_values = (
        lax.all_gather(keys, "depth", axis=0, tiled=True),
        lax.all_gather(values, "depth", axis=0, tiled=True),
    )
    block_len = min(512, seq_len)
    block_count = seq_len // block_len
    key_blocks = all_keys.reshape(block_count, block_len, heads, head_size)
    value_blocks = all_values.reshape(block_count, block_len, heads, head_size)
    starts = jnp.arange(block_count, dtype=jnp.int32) * block_len

    def peak_step(carry, item):
        peak, weight_sum = carry
        key_block, value_block, start = item
        scores, allowed = block_scores(query, key_block, start, place, scale)
        scores = jnp.where(allowed[None], scores, -1e30)
        new_peak = jnp.maximum(peak, jnp.max(scores, axis=-1))
        weight_sum = weight_sum * jnp.exp(peak - new_peak) + jnp.sum(
            jnp.exp(scores - new_peak[..., None]), axis=-1
        )
        return ((new_peak, weight_sum), None)

    start_carry = (
        jnp.full((heads, rows_tok), -1e30, jnp.float32),
        jnp.zeros((heads, rows_tok), jnp.float32),
    )
    (peak, weight_sum), _ = lax.scan(peak_step, start_carry, (key_blocks, value_blocks, starts))
    log_total = peak + jnp.log(weight_sum)

    def value_step(running, item):
        key_block, value_block, start = item
        scores, allowed = block_scores(query, key_block, start, place, scale)
        probs = jnp.where(allowed[None], jnp.exp(scores - log_total[..., None]), 0.0)
        running = running + jnp.einsum(
            "hqk,khd->qhd",
            probs.astype(jnp.bfloat16),
            value_block,
            preferred_element_type=jnp.float32,
        )
        return (running, None)

    running, _ = lax.scan(
        value_step,
        jnp.zeros((rows_tok, heads, head_size), jnp.float32),
        (key_blocks, value_blocks, starts),
    )
    mixed = running.reshape(rows_tok, width)
    mixed_low = mixed.astype(jnp.bfloat16)
    middle = float_input + jnp.dot(mixed_low, wide_out, preferred_element_type=jnp.float32)
    second = norm_rows(middle, wide_norms[2], wide_norms[3]).astype(jnp.bfloat16)
    upper = jnp.dot(second, wide_up, preferred_element_type=jnp.float32)
    active = jax.nn.gelu(upper).astype(jnp.bfloat16)
    block_out = middle + jnp.dot(active, wide_down, preferred_element_type=jnp.float32)
    own_alpha = lax.dynamic_slice_in_dim(depth_weights, place_depth * slot_count, slot_count)
    partial_mix = jnp.sum(own_alpha[:, None, None] * history.astype(jnp.float32), axis=0)
    mixture = lax.psum_scatter(
        partial_mix.astype(jnp.bfloat16), "depth", scatter_dimension=0, tiled=True
    ).astype(jnp.float32)
    output = (mixture + depth_weights[hist_total] * block_out).astype(jnp.bfloat16)
    grad_out = token_mask.astype(jnp.float32)[:, None] * cotangent.astype(jnp.float32) * loss_scale
    last_term = jnp.sum(grad_out * block_out)
    index_all = jnp.arange(hist_total + 1, dtype=jnp.int32)
    grad_rows = lax.all_gather(grad_out.astype(jnp.bfloat16), "depth", axis=0, tiled=True).astype(
        grad_out.dtype
    )
    history_grad = (own_alpha[:, None, None] * grad_rows[None]).astype(jnp.bfloat16)
    hist_terms = jnp.sum(history.astype(jnp.float32) * grad_rows[None], axis=(1, 2))
    own_index = place_depth * slot_count + jnp.arange(slot_count, dtype=jnp.int32)
    alpha_terms = jnp.sum(
        jnp.where(index_all[None, :] == own_index[:, None], hist_terms[:, None], 0.0), axis=0
    )
    alpha_terms = alpha_terms + jnp.where(index_all == hist_total, last_term, 0.0)
    depth_gradient = lax.psum(alpha_terms, ("rows", "depth"))
    wide_qkv, wide_out, wide_up, wide_down, wide_norms = (
        lax.all_gather(qkv_weight, ("rows", "depth"), axis=0, tiled=True),
        lax.all_gather(out_weight, ("rows", "depth"), axis=0, tiled=True),
        lax.all_gather(up_weight, ("rows", "depth"), axis=0, tiled=True),
        lax.all_gather(down_weight, ("rows", "depth"), axis=0, tiled=True),
        lax.all_gather(
            norm_params.astype(jnp.bfloat16), ("rows", "depth"), axis=1, tiled=True
        ).astype(norm_params.dtype),
    )
    block_grad = depth_weights[hist_total] * grad_out
    lower_grad = block_grad.astype(jnp.bfloat16)
    down_gradient = jnp.dot(active.T, lower_grad, preferred_element_type=jnp.float32)
    active_grad = jnp.dot(lower_grad, wide_down.T, preferred_element_type=jnp.float32)
    _, gelu_pull = jax.vjp(jax.nn.gelu, upper)
    upper_grad = gelu_pull(active_grad)[0].astype(jnp.bfloat16)
    up_gradient = jnp.dot(second.T, upper_grad, preferred_element_type=jnp.float32)
    second_grad = jnp.dot(upper_grad, wide_up.T, preferred_element_type=jnp.float32)
    _, norm_pull = jax.vjp(norm_rows, middle, wide_norms[2], wide_norms[3])
    middle_part, gain_two, shift_two = norm_pull(second_grad)
    middle_grad = block_grad + middle_part
    branch_grad = middle_grad.astype(jnp.bfloat16)
    out_gradient = jnp.dot(mixed_low.T, branch_grad, preferred_element_type=jnp.float32)
    mixed_grad = jnp.dot(branch_grad, wide_out.T, preferred_element_type=jnp.float32).astype(
        jnp.bfloat16
    )
    delta = jnp.sum(
        (mixed_grad.astype(jnp.float32) * mixed).reshape(rows_tok, heads, head_size), axis=-1
    ).T
    mixed_heads = mixed_grad.reshape(rows_tok, heads, head_size)

    def score_grads(
        query_rows, grad_rows, lse_rows, delta_rows, key_block, value_block, query_place, start
    ):
        scores, allowed = block_scores(query_rows, key_block, start, query_place, scale)
        probs = jnp.where(allowed[None], jnp.exp(scores - lse_rows[..., None]), 0.0)
        prob_grad = jnp.einsum(
            "qhd,khd->hqk", grad_rows, value_block, preferred_element_type=jnp.float32
        )
        score_grad = (probs * (prob_grad - delta_rows[..., None])).astype(jnp.bfloat16)
        return (probs, score_grad)

    def grad_step(query_total, item):
        key_block, value_block, start = item
        probs, score_grad = score_grads(
            query, mixed_heads, log_total, delta, key_block, value_block, place, start
        )
        query_total = (
            query_total
            + jnp.einsum("hqk,khd->qhd", score_grad, key_block, preferred_element_type=jnp.float32)
            * scale
        )
        key_part = (
            jnp.einsum("hqk,qhd->khd", score_grad, query, preferred_element_type=jnp.float32)
            * scale
        )
        value_part = jnp.einsum(
            "hqk,qhd->khd",
            probs.astype(jnp.bfloat16),
            mixed_heads,
            preferred_element_type=jnp.float32,
        )
        return (query_total, (key_part, value_part))

    query_total, (key_parts, value_parts) = lax.scan(
        grad_step,
        jnp.zeros((rows_tok, heads, head_size), jnp.float32),
        (key_blocks, value_blocks, starts),
    )
    key_sum, value_sum = (
        lax.psum_scatter(
            key_parts.reshape(seq_len, width).astype(jnp.bfloat16),
            "depth",
            scatter_dimension=0,
            tiled=True,
        ).astype(jnp.float32),
        lax.psum_scatter(
            value_parts.reshape(seq_len, width).astype(jnp.bfloat16),
            "depth",
            scatter_dimension=0,
            tiled=True,
        ).astype(jnp.float32),
    )
    query_grad = rotate(query_total, place, -1.0).reshape(rows_tok, width)
    key_grad = rotate(key_sum.reshape(rows_tok, heads, head_size), place, -1.0).reshape(
        rows_tok, width
    )
    projected_grad = jnp.concatenate([query_grad, key_grad, value_sum], axis=1).astype(jnp.bfloat16)
    qkv_gradient = jnp.dot(first.T, projected_grad, preferred_element_type=jnp.float32)
    first_grad = jnp.dot(projected_grad, wide_qkv.T, preferred_element_type=jnp.float32)
    _, first_pull = jax.vjp(norm_rows, float_input, wide_norms[0], wide_norms[1])
    input_part, gain_one, shift_one = first_pull(first_grad)
    input_grad = (middle_grad + input_part).astype(jnp.bfloat16)
    norms_full = jnp.stack([gain_one, shift_one, gain_two, shift_two])
    qkv_gradient, out_gradient, up_gradient, down_gradient, norm_gradient = (
        lax.psum_scatter(qkv_gradient, ("rows", "depth"), scatter_dimension=0, tiled=True),
        lax.psum_scatter(out_gradient, ("rows", "depth"), scatter_dimension=0, tiled=True),
        lax.psum_scatter(up_gradient, ("rows", "depth"), scatter_dimension=0, tiled=True),
        lax.psum_scatter(down_gradient, ("rows", "depth"), scatter_dimension=0, tiled=True),
        lax.psum_scatter(norms_full, ("rows", "depth"), scatter_dimension=1, tiled=True),
    )
    return (
        output,
        input_grad,
        history_grad,
        qkv_gradient,
        out_gradient,
        up_gradient,
        down_gradient,
        norm_gradient,
        depth_gradient,
    )

SEQ = 512
OWN = 128
WIDTH = 768
ROWS = 8
GROUP = 4
PACK = 640
BLOCK = WIDTH // ROWS
CHUNK = BLOCK // GROUP
QBLOCK = 256
BF = jnp.bfloat16
F32 = jnp.float32
MESH = pl.DeviceIdType.MESH


def dot(a, b, ca=1, cb=0):
    return lax.dot_general(a, b, (((ca,), (cb,)), ((), ())), preferred_element_type=F32)


def lane_id(shape):
    return lax.broadcasted_iota(jnp.int32, shape, len(shape) - 1)


def row_id(shape):
    return lax.broadcasted_iota(jnp.int32, shape, len(shape) - 2)


def tiles_of(value):
    return [value[:, 128 * i : 128 * (i + 1)] for i in range(value.shape[1] // 128)]


def permute_chunks(tiles, picks):
    group = lax.div(lane_id(tiles[0].shape), jnp.int32(32))
    out = []
    for t in range(len(picks) // 4):
        total, rolled = jnp.zeros_like(tiles[0]), {}
        for j in range(4):
            pick = picks[4 * t + j]
            if pick is None:
                continue
            source, place = divmod(pick, 4)
            shift = (j - place) * 32 % 128
            if (source, shift) not in rolled:
                value = tiles[source]
                rolled[source, shift] = pltpu.roll(value, shift, 1) if shift else value
            total = jnp.where(group == j, rolled[source, shift], total)
        out.append(total)
    return out


def fold(tiles):
    half = (len(tiles) + 1) // 2
    low = [t[16:] for t in tiles]
    if len(low) % 2:
        low.append(jnp.zeros_like(low[0]))
    return [t[:16] for t in tiles] + [
        jnp.concatenate([low[i], low[half + i]], axis=0) for i in range(half)
    ]


def unfold(tiles, count):
    half = (count + 1) // 2
    rest = tiles[count:]
    low = [rest[i][:8] for i in range(half)] + [rest[i][8:] for i in range(half)]
    return [jnp.concatenate([tiles[i], low[i]], axis=0) for i in range(count)]


def fold_qkv(tiles):
    t0, t1, t2, t3, t4 = tiles
    lane, lane8, lane16 = (lane_id((n, 128)) for n in (CHUNK, 8, 16))
    turned = pltpu.roll(t3, 96, 1)
    keys = jnp.where(lane < 96, t2, turned)
    extra = jnp.where(
        lane8 < 80,
        pltpu.roll(t2[:8], 96, 1),
        jnp.where(lane8 < 96, pltpu.roll(t2[8:16], 112, 1), t2[16:]),
    )
    right = jnp.concatenate([pltpu.roll(turned[16:], 64, 1), extra], axis=0)
    shared = jnp.where(lane16 < 64, turned[:16], right)
    return [t0[:16], t1[:16], t4[:16], keys[:16], shared] + [
        jnp.concatenate([a[16:], b[16:]], axis=0) for a, b in ((t0, t1), (t4, keys))
    ]


def unfold_qkv(tiles):
    u0, u1, u4, u3, shared, low01, low43 = tiles
    lane = lane_id((CHUNK, 128))
    t0 = jnp.concatenate([u0, low01[:8]], axis=0)
    t1 = jnp.concatenate([u1, low01[8:]], axis=0)
    t4 = jnp.concatenate([u4, low43[:8]], axis=0)
    keys = jnp.concatenate([u3, low43[8:]], axis=0)
    turned = jnp.concatenate([shared, pltpu.roll(shared[:8], 64, 1)], axis=0)
    t3 = jnp.where(lane < 32, pltpu.roll(keys, 32, 1), pltpu.roll(turned, 32, 1))
    t3 = jnp.where(lane < 96, t3, 0.0)
    extra = shared[8:]
    extra = jnp.concatenate([pltpu.roll(extra, 32, 1), pltpu.roll(extra, 16, 1), extra], axis=0)
    t2 = jnp.where(lane < 96, keys, jnp.where(lane < 112, extra, 0.0))
    return [t0, t1, t2, t3, t4]


def qkv_chunk(block, head, half):
    return 24 * block + 2 * head + half


def qkv_picks(d):
    heads = [3 * d + i for i in range(3)]
    picks = []
    for block in range(2):
        for half in range(2):
            picks += [qkv_chunk(block, h, half) for h in heads]
            picks.append(qkv_chunk(2, heads[2], half) if block == 0 else None)
    return picks + [qkv_chunk(2, h, half) for h in heads[:2] for half in range(2)]


def up_picks(d):
    return [3 * (GROUP * r + d) + j for r in range(ROWS) for j in range(3)]


def inverse_picks(per_device, count, tiles_each):
    back = [None] * count
    for d, picks in enumerate(per_device):
        for place, pick in enumerate(picks):
            if pick is not None:
                back[pick] = 4 * tiles_each * d + place
    return back


QKV_BACK = inverse_picks([qkv_picks(d) for d in range(GROUP)], 72, 5)
UP_BACK = inverse_picks([up_picks(d) for d in range(GROUP)], 96, 6)


def tables():
    half = HD // 2
    freq = np.float32(10000.0) ** (-np.arange(half, dtype=np.float32) / np.float32(half))
    angle = (np.arange(SEQ, dtype=np.float32)[:, None] * freq[None, :]).astype(np.float32)
    angle = angle.astype(np.float64)
    cosine, sine = np.ones((SEQ, 128), np.float32), np.zeros((SEQ, 128), np.float32)
    cosine[:, :96] = np.tile(np.cos(angle), (1, 3))
    sine[:, :96] = np.tile(np.sin(angle), (1, 3))
    return cosine, sine


def standardize(value):
    center = value - jnp.mean(value, axis=-1, keepdims=True)
    spread = jnp.mean(center * center, axis=-1, keepdims=True)
    scale = lax.rsqrt(spread + 1e-05)
    return center * scale, scale


def norm_back(grad, gain, normal, scale):
    part = grad * (1.0 + gain)
    inner = jnp.mean(part, axis=-1, keepdims=True)
    along = jnp.mean(part * normal, axis=-1, keepdims=True)
    return scale * (part - inner - normal * along)


def sublane_sum(value):
    return jnp.sum(value.reshape(value.shape[0] // 8, 8, value.shape[1]), axis=0)


SCRATCH = dict(
    hist=((SEQ, WIDTH), BF),
    cot=((OWN, WIDTH), BF),
    wq=((CHUNK, 3 * WIDTH), BF),
    wo=((CHUNK, WIDTH), BF),
    wu=((CHUNK, 4 * WIDTH), BF),
    cosine=((SEQ, 128), F32),
    sine=((SEQ, 128), F32),
    x_all=((GROUP, OWN, WIDTH), BF),
    c_all=((GROUP, OWN, WIDTH), BF),
    qp_s=((GROUP, 16, 896), BF),
    q_all=((ROWS * GROUP, 16, 896), BF),
    up_s=((GROUP, 16, 1152), BF),
    up_l=((GROUP, 16, 1152), BF),
    tmp=((BLOCK, WIDTH), F32),
    w_qkv=((WIDTH, PACK), BF),
    w_up=((WIDTH, WIDTH), BF),
    w_down=((WIDTH, WIDTH), BF),
    wo_l=((GROUP, 2, ROWS // 2, 16, 1152), BF),
    w_out=((WIDTH, WIDTH), BF),
    w_own=((256, WIDTH), BF),
    norms=((8, WIDTH), F32),
    normal=((SEQ, WIDTH), F32),
    h1=((SEQ, WIDTH), BF),
    qv=((SEQ, 256), BF),
    kk=((SEQ, 256), BF),
    v01=((SEQ, 128), BF),
    v_all=((SEQ, 256), BF),
    probs=((3, SEQ, SEQ), F32),
    o_l=((GROUP, 2, 384, 128), BF),
    ob=((SEQ, WIDTH), BF),
    y=((SEQ, WIDTH), F32),
    h2=((SEQ, WIDTH), BF),
    slope=((SEQ, WIDTH), F32),
    act=((SEQ, WIDTH), BF),
    dm=((SEQ, WIDTH), BF),
    g_down=((WIDTH, WIDTH), F32),
    g_up=((WIDTH, WIDTH), F32),
    g_out=((WIDTH, WIDTH), F32),
    g_qkv=((WIDTH, PACK), F32),
    du=((SEQ, WIDTH), BF),
    part=((SEQ, WIDTH), F32),
    part2=((SEQ, WIDTH), F32),
    dy=((OWN, WIDTH), F32),
    dyb=((GROUP, OWN, WIDTH), BF),
    dq=((SEQ, 256), F32),
    dk=((SEQ, 256), F32),
    dv=((SEQ, 256), F32),
    dqkv=((SEQ, PACK), BF),
    terms=((8, WIDTH), F32),
    terms2=((8, WIDTH), F32),
    t0=((8, WIDTH), F32),
    td=((4, 8, WIDTH), F32),
    ext=((ROWS, 16, 128), F32),
    u0=((8, 128), F32),
    u1=((8, 128), F32),
    uzd=((8, 8, 128), F32),
    fin=((16, 16, 896), BF),
    ps=((16, 16, 896), BF),
    q_sum=((GROUP, 16, 896), F32),
    a_up=((GROUP, 16, 1152), BF),
    f_down=((BLOCK, WIDTH), F32),
    f_up=((BLOCK, WIDTH), F32),
    f_out=((16, 1280), F32),
    b_up=((GROUP, 16, 1152), BF),
    gain_sum=((8, WIDTH), F32),
    shift_sum=((8, WIDTH), F32),
)
for _name, _rows, _cols in (
    ("down", BLOCK, WIDTH),
    ("up", BLOCK, WIDTH),
    ("out", 16, 1280),
):
    SCRATCH["st_" + _name] = ((8, _rows, _cols), BF)
    SCRATCH["xl_" + _name] = ((4, _rows, _cols), BF)
    SCRATCH["zl_" + _name] = ((3, _rows, _cols), BF)
    SCRATCH["nl_" + _name] = ((2, _rows, _cols), BF)
for _h in range(2):
    SCRATCH[f"st_qkv{_h}"] = ((6, BLOCK // 2, PACK), BF)
    SCRATCH[f"xl_qkv{_h}"] = ((4, BLOCK // 2, PACK), BF)
    for _name in ("cl", "zl"):
        SCRATCH[f"{_name}_qkv{_h}"] = ((BLOCK // 2, PACK), BF)
for _name in ("mix", "mid", "in"):
    SCRATCH["gs_" + _name] = ((3, OWN, WIDTH), BF)
    SCRATCH["l1_" + _name] = ((2, OWN, WIDTH), BF)
    SCRATCH["l2_" + _name] = ((OWN, WIDTH), BF)
N_SENDS = 32
N_ARRIVALS = 110
N_IN = 12
N_OUT = 9
VMEM_MIB = 60


class Names:
    pass


def fused_kernel(*refs):
    (x_hbm, hist_hbm, cot_hbm, mask, wq_hbm, wo_hbm, wu_hbm, wd_hbm) = refs[:8]
    (nrm, dw, cosine_hbm, sine_hbm) = refs[8:N_IN]
    results, (ng_o, dg_o) = refs[N_IN : N_IN + N_OUT - 2], refs[N_IN + N_OUT - 2 : N_IN + N_OUT]
    s = Names()
    for name, ref in zip(SCRATCH, refs[N_IN + N_OUT :]):
        setattr(s, name, ref)
    send_sems, recv_sems, local_sems = refs[-3:]

    r, d = lax.axis_index("rows"), lax.axis_index("depth")
    z, x = lax.div(r, 2), lax.rem(r, 2)
    yy, c = lax.div(d, 2), lax.rem(d, 2)
    other_x, other_c, other_y = 1 - x, 1 - c, 1 - yy
    x_dev = (2 * z + other_x, d)
    z_two, z_mirror, z_near = lax.rem(z + 2, 4), 3 - z, z + 1 - 2 * lax.rem(z, 2)
    two_dev, mirror_dev, near_dev = ((2 * zk + x, d) for zk in (z_two, z_mirror, z_near))
    inside = lax.rem(z + 1, 4) >= 2
    outside = jnp.logical_not(inside)
    core_d, y_d, far_d = 2 * yy + other_c, 2 * other_y + c, 2 * other_y + other_c
    core_dev, y_dev, far_dev = (r, core_d), (r, y_d), (r, far_d)
    mates = ((core_d, core_dev), (y_d, y_dev), (far_d, far_dev))
    used = {"send": 0, "arrival": 0}
    send_groups = []

    def arrivals(count=1):
        used["arrival"] += count
        return used["arrival"] - count

    def sends(view, condition=None):
        used["send"] += 1
        send_groups.append((used["send"] - 1, view, condition))
        return used["send"] - 1

    def prepare(src, dst, device, arrival, group):
        return pltpu.make_async_remote_copy(
            src_ref=src,
            dst_ref=dst,
            send_sem=send_sems.at[group],
            recv_sem=recv_sems.at[arrival],
            device_id=device,
            device_id_type=MESH,
        )

    def copy_to(src, dst, device, arrival, group, condition=None):
        copy = prepare(src, dst, device, arrival, group)
        if condition is None:
            copy.start()
        else:
            pl.when(condition)(copy.start)

    def arrive(view, arrival):
        prepare(view, view, x_dev, arrival, 0).wait_recv()

    def rows_at(ref, index, size):
        return ref.at[pl.ds(pl.multiple_of(index * size, size), size)]

    def by_rows(count, step, body):
        def one(i, carry):
            body(pl.ds(pl.multiple_of(i * step, step), step))
            return carry

        lax.fori_loop(0, count // step, one, 0)

    barrier = pltpu.get_barrier_semaphore()
    partners = [x_dev, core_dev, y_dev, far_dev]
    partners += [
        (2 * zk + x, m) for zk in (z_two, z_mirror, z_near) for m in (d, core_d, y_d, far_d)
    ]
    for device in partners:
        pl.semaphore_signal(barrier, inc=1, device_id=device, device_id_type=MESH)

    hist, cot, wq, wo, wu, cosine, sine = s.hist, s.cot, s.wq, s.wo, s.wu, s.cosine, s.sine
    loads = {}
    for name, source, target in (
        ("wq", wq_hbm, wq),
        ("x", x_hbm, s.x_all.at[d]),
        ("wo", wo_hbm, wo),
        ("wu", wu_hbm, wu),
        ("wd", wd_hbm, rows_at(s.w_down, r, BLOCK)),
        ("cot", cot_hbm, cot),
        ("cosine", cosine_hbm, cosine),
        ("sine", sine_hbm, sine),
        ("hist", hist_hbm, hist),
    ):
        loads[name] = pltpu.make_async_copy(source, target, local_sems.at[len(loads)])
        loads[name].start()
    out_o, ig_o, hg_o, gq_o, go_o, gu_o, gd_o = results


    class Gather:
        def __init__(self, piece, pieces, cross=False):
            self.piece, self.pieces, self.cross = piece, pieces, cross
            self.group, self.inner = sends(pieces(6)), sends(pieces(2), inside)
            self.two, self.near, self.mirror, self.along_x = (arrivals() for _ in range(4))
            self.own_x = arrivals() if cross else self.along_x

        def copy(self, zk, xk, device, arrival, inner=False, condition=None):
            piece = self.piece(zk, xk)
            group = self.inner if inner else self.group
            copy_to(piece, piece, device, arrival, group, condition)

        def send_two(self):
            self.copy(z, x, two_dev, self.two)

        def send_mirror(self):
            self.copy(z, x, mirror_dev, self.mirror, True, inside)

        def send_near(self, where=None):
            condition = None if where is None else outside if where else inside
            self.copy(z, x, near_dev, self.near, condition=condition)

        def send_x(self, zk=z):
            self.copy(zk, x, x_dev, self.along_x)

        def send_own_x(self):
            self.copy(z, x, x_dev, self.own_x)

        def arrive_near(self):
            arrive(self.piece(z_near, x), self.near)

        def forward_near(self):
            self.arrive_near()
            if not self.cross:
                self.send_x(z_near)

        def forward_cross(self):
            arrive(self.piece(z, other_x), self.own_x)
            self.copy(z, other_x, near_dev, self.along_x)

        def pass_two(self):
            arrive(self.piece(z_two, x), self.two)
            self.copy(z_two, x, near_dev, self.mirror, True, inside)

        def forward_two(self):
            self.pass_two()
            self.send_x(z_two)

        def forward_mirror(self):
            arrive(self.piece(z_mirror, x), self.mirror)
            self.send_x(z_mirror)

        def finish(self):
            arrive(self.pieces(3 if self.cross else 4), self.along_x)

    class GroupGather:
        def __init__(self, slab, slabs, group=None):
            self.slab, self.slabs = slab, slabs
            self.group = sends(slabs(3)) if group is None else group
            self.from_y, self.others = arrivals(), arrivals()

        def send(self):
            mine = self.slab(d)
            copy_to(mine, mine, core_dev, self.others, self.group)
            copy_to(mine, mine, y_dev, self.from_y, self.group)

        def relay(self):
            slab = self.slab(y_d)
            arrive(slab, self.from_y)
            copy_to(slab, slab, core_dev, self.others, self.group)

        def finish(self):
            arrive(self.slabs(2), self.others)

    class RowSum:
        def __init__(self, name, total, block, step, cross):
            staged = getattr(s, "st_" + name)
            self.xs, self.zs, self.ns = (
                [staged.at[i + j] for j in range(n)] for i, n in ((0, 4), (4, 2), (6, 2))
            )
            self.xs = staged.at[pl.ds(0, 4)]
            self.xl, self.zl, self.nl = (getattr(s, p + name) for p in ("xl_", "zl_", "nl_"))
            self.total = total
            self.block, self.step, self.cross = block, step, cross
            self.count = self.total.shape[0]
            self.group = sends(staged.at[pl.ds(0, 7)])
            self.along_x = {k: arrivals() for k in ("mirror", "two", "own")}
            if not cross:
                self.along_x["near"] = arrivals()
            self.crossing, self.near, self.two, self.mirror, self.passing = (
                arrivals() for _ in range(5)
            )

        def stage(self, target, index, *extras):
            def one(at):
                value = self.block(index, at)
                for ref in extras:
                    value = value + ref[at, :].astype(F32)
                target[at, :] = value.astype(BF)

            by_rows(self.count, self.step, one)

        def send_x(self, name, zk, *extras):
            self.stage(self.xs.at[zk], 2 * zk + other_x, *extras)
            copy_to(self.xs.at[zk], self.xl.at[zk], x_dev, self.along_x[name], self.group)

        def arrive_x(self, name, zk):
            arrive(self.xl.at[zk], self.along_x[name])

        def send(self, early_near=False):
            self.send_x("mirror", z_mirror)
            if self.cross:
                self.send_crossing()
            self.send_x("two", z_two)
            if self.cross and early_near:
                self.send_near()
            if not self.cross:
                self.send_x("near", z_near)
                self.send_x("own", z)

        def send_crossing(self):
            self.stage(self.ns[0], 2 * z_near + other_x)
            copy_to(self.ns[0], self.nl.at[0], near_dev, self.crossing, self.group)

        def send_own(self):
            arrive(self.nl.at[0], self.crossing)
            self.send_x("own", z, self.nl.at[0])

        def send_mirror(self):
            self.arrive_x("mirror", z_mirror)
            self.stage(self.zs[0], 2 * z_mirror + x, self.xl.at[z_mirror])
            copy_to(self.zs[0], self.zl.at[0], mirror_dev, self.mirror, self.group, inside)
            copy_to(self.zs[0], self.zl.at[2], near_dev, self.passing, self.group, outside)

        def send_two_outside(self):
            @pl.when(outside)
            def _():
                self.arrive_x("two", z_two)
                self.stage(self.zs[1], 2 * z_two + x, self.xl.at[z_two])
                copy_to(self.zs[1], self.zl.at[1], two_dev, self.two, self.group)

        def send_two_inside(self):
            @pl.when(inside)
            def _():
                self.arrive_x("two", z_two)
                arrive(self.zl.at[2], self.passing)
                self.stage(self.zs[1], 2 * z_two + x, self.xl.at[z_two], self.zl.at[2])
                copy_to(self.zs[1], self.zl.at[1], two_dev, self.two, self.group)

        def send_near(self):
            extras = ()
            if not self.cross:
                self.arrive_x("near", z_near)
                extras = (self.xl.at[z_near],)
            self.stage(self.ns[1], 2 * z_near + x, *extras)
            copy_to(self.ns[1], self.nl.at[1], near_dev, self.near, self.group)

        def finish(self):
            self.arrive_x("own", z)
            arrive(self.zl.at[1], self.two)
            arrive(self.nl.at[1], self.near)

            def add(at):
                self.total[at, :] = (
                    self.block(r, at)
                    + self.xl[z, at, :].astype(F32)
                    + self.zl[1, at, :].astype(F32)
                    + self.nl[1, at, :].astype(F32)
                )

            by_rows(self.count, self.step, add)

            @pl.when(inside)
            def _():
                arrive(self.zl.at[0], self.mirror)

                def add_mirror(at):
                    self.total[at, :] += self.zl[0, at, :].astype(F32)

                by_rows(self.count, self.step, add_mirror)

    class SpreadSum:
        def __init__(self, half, shared):
            staged = getattr(s, f"st_qkv{half}")
            self.xs, self.cs, self.zs = staged.at[pl.ds(0, 4)], staged.at[4], staged.at[5]
            self.xl, self.cl, self.zl = (getattr(s, f"{p}_qkv{half}") for p in ("xl", "cl", "zl"))
            self.half = half
            self.group = sends(staged.at[pl.ds(0, 4)])
            self.inner, self.outer, self.last, self.final, self.final_mirror = shared
            self.along_x = {k: arrivals() for k in ("mirror", "two", "near", "own")}
            self.crossing, self.passing = arrivals(), arrivals()

        def value(self, index, *extras):
            rows = BLOCK // 2
            start_row = pl.multiple_of((2 * index + self.half) * rows, rows)
            value = s.g_qkv[pl.ds(start_row, rows), :]
            for extra in extras:
                value = value + extra.astype(F32)
            return value

        def send_x(self, name, zk, *extras):
            self.xs[zk] = self.value(2 * zk + other_x, *extras).astype(BF)
            copy_to(self.xs.at[zk], self.xl.at[zk], x_dev, self.along_x[name], self.group)

        def arrive_x(self, name, zk):
            arrive(self.xl.at[zk], self.along_x[name])

        def send_crossing(self):
            @pl.when(inside)
            def _():
                self.cs[...] = self.value(2 * z_near + other_x).astype(BF)
                copy_to(self.cs, self.cl, near_dev, self.crossing, self.group)

        def send_third(self):
            pl.when(inside)(lambda: self.send_x("own", z))
            pl.when(outside)(lambda: self.send_x("near", z_near))

        def send_own_outside(self):
            @pl.when(outside)
            def _():
                arrive(self.cl, self.crossing)
                self.send_x("own", z, self.cl[...])

        def deliver(self, slot, zk, value):
            for j in range(2):
                to = 2 * self.half + j
                at = 8 * self.half + 2 * slot + j
                for t, tile in enumerate(fold_qkv(tiles_of(value[CHUNK * j : CHUNK * (j + 1)]))):
                    s.ps[at, :, 128 * t : 128 * (t + 1)] = tile.astype(BF)
                copy_to(
                    s.ps.at[at],
                    s.fin.at[GROUP * slot + d],
                    (2 * zk + x, to),
                    self.final_mirror if slot == 2 else self.final,
                    self.inner if slot == 2 else self.last,
                    inside if slot == 2 else d != to if slot == 3 else None,
                )
                if slot == 3:

                    @pl.when(d == to)
                    def _(at=at):
                        s.fin[GROUP * slot + d] = s.ps[at]

        def send_mirror(self):
            self.arrive_x("mirror", z_mirror)
            value = self.value(2 * z_mirror + x, self.xl[z_mirror])
            self.deliver(2, z_mirror, value)
            self.zs[...] = value.astype(BF)
            copy_to(self.zs, self.zl, near_dev, self.passing, self.outer, outside)

        def send_two(self):
            self.arrive_x("two", z_two)

            @pl.when(outside)
            def _():
                self.zl[...] = jnp.zeros((BLOCK // 2, PACK), BF)

            pl.when(inside)(lambda: arrive(self.zl, self.passing))
            self.deliver(0, z_two, self.value(2 * z_two + x, self.xl[z_two], self.zl[...]))

        def send_near(self):
            pl.when(inside)(lambda: self.deliver(1, z_near, self.value(2 * z_near + x)))

            @pl.when(outside)
            def _():
                self.arrive_x("near", z_near)
                self.deliver(1, z_near, self.value(2 * z_near + x, self.xl[z_near]))

        def keep_own(self):
            self.arrive_x("own", z)
            self.deliver(3, z, self.value(r, self.xl[z]))

    class GroupSum:
        def __init__(self, name, source, parts=1):
            staged = getattr(s, "gs_" + name)
            self.s1, self.s2 = staged.at[pl.ds(0, 2)], staged.at[2]
            self.l1, self.l2 = (getattr(s, p + name) for p in ("l1_", "l2_"))
            self.source, self.parts, self.size = source, parts, OWN // parts
            self.group = sends(staged)
            self.first, self.second = arrivals(parts), arrivals(parts)
            self.kept = arrivals()

        def block(self, index, at):
            return self.source[pl.ds(pl.multiple_of(index * OWN + at.start, at.size), at.size), :]

        def part(self, i):
            return pl.ds(self.size * i, self.size)

        def over(self, i, body):
            def shifted(at):
                body(pl.ds(pl.multiple_of(self.size * i + at.start, at.size), at.size))

            by_rows(self.size, 32, shifted)

        def send(self, i=0):
            for j, yj in enumerate((other_y, yy)):

                def stage(at):
                    self.s1[j, at, :] = self.block(2 * yj + other_c, at).astype(BF)

                self.over(i, stage)
                copy_to(
                    self.s1.at[j, self.part(i)],
                    self.l1.at[j, self.part(i)],
                    core_dev,
                    self.kept if j else self.first + i,
                    self.group,
                )

        def middle(self, i=0):
            arrive(self.l1.at[0, self.part(i)], self.first + i)

            def stage(at):
                value = self.block(2 * other_y + c, at) + self.l1[0, at, :].astype(F32)
                self.s2[at, :] = value.astype(BF)

            self.over(i, stage)
            copy_to(
                self.s2.at[self.part(i)],
                self.l2.at[self.part(i)],
                y_dev,
                self.second + i,
                self.group,
            )

        def wait(self, i=0):
            if i == 0:
                arrive(self.l1.at[1], self.kept)
            arrive(self.l2.at[self.part(i)], self.second + i)

        def value(self, at):
            return (
                self.block(d, at)
                + self.l1[1, at, :].astype(F32)
                + self.l2[at, :].astype(F32)
            )

    class PieceGather:
        def __init__(self):
            self.group = sends(s.q_all.at[pl.ds(0, 27)])
            self.inner = sends(s.q_all.at[pl.ds(0, 8)], inside)
            self.own, self.two, self.near, self.mirror = (arrivals(2) for _ in range(4))
            self.along_x = {k: arrivals() for k in ("own", "near", "two", "mirror")}

        def fan(self, zk, arrival, group, condition=None):
            for i, m in enumerate((d, core_d, y_d, far_d)):
                if i == 0 and zk is z:
                    continue
                copy_to(
                    s.qp_s.at[m],
                    s.q_all.at[GROUP * r + d],
                    (2 * zk + x, m),
                    arrival + i // 2,
                    group,
                    condition,
                )

        def slab(self, zk, xk, h):
            first = GROUP * (2 * zk + xk) + 2 * (other_y if h else yy)
            return s.q_all.at[pl.ds(pl.multiple_of(first, 2), 2)]

        def send(self):
            self.fan(z, self.own, self.group)
            self.fan(z_two, self.two, self.group)
            self.fan(z_near, self.near, self.group)
            self.fan(z_mirror, self.mirror, self.inner, inside)

        def send_x(self, name, zk, h):
            slab = self.slab(zk, x, h)
            copy_to(slab, slab, x_dev, self.along_x[name], self.group)

        def forward_own(self, h):
            if h:
                arrive(self.slab(z, x, h), self.own + h)
            else:
                arrive(s.q_all.at[GROUP * r + core_d], self.own)
            self.send_x("own", z, h)

        def forward_near(self, h):
            arrive(self.slab(z_near, x, h), self.near + h)
            self.send_x("near", z_near, h)

        def forward_two(self, h):
            slab = self.slab(z_two, x, h)
            arrive(slab, self.two + h)
            copy_to(slab, slab, near_dev, self.mirror + h, self.inner, inside)
            self.send_x("two", z_two, h)

        def forward_mirror(self, h):
            arrive(self.slab(z_mirror, x, h), self.mirror + h)
            self.send_x("mirror", z_mirror, h)

        def finish(self, name, zk):
            first = pl.multiple_of(GROUP * (2 * zk + other_x), GROUP)
            arrive(s.q_all.at[pl.ds(first, GROUP)], self.along_x[name])

    def assemble(landing, count, target, row):
        for k in range(GROUP):
            landed = landing[k][...] if isinstance(landing, list) else landing[k]
            tiles = [t.astype(F32) for t in tiles_of(landed)]
            for t, tile in enumerate(unfold_qkv(tiles) if count == 5 else unfold(tiles, count)):
                s.tmp[CHUNK * k : CHUNK * (k + 1), 128 * t : 128 * (t + 1)] = tile
        rows_at(target, row, BLOCK)[...] = s.tmp[:, : 128 * count].astype(BF)

    def assemble_qkv(row):
        assemble([s.q_all.at[GROUP * row + k] for k in range(GROUP)], 5, s.w_qkv, row)

    lane = lane_id((CHUNK, 128))
    eye = row_id((CHUNK, CHUNK)) == lane_id((CHUNK, CHUNK))
    extra = jnp.zeros((CHUNK, 128), F32)
    for k in range(4):
        column = jnp.sum(jnp.where(eye, nrm[k : k + 1, :], 0.0), axis=1, keepdims=True)
        high = column.astype(BF).astype(F32)
        extra = jnp.where(lane == 96 + k, high, extra)
        extra = jnp.where(lane == 100 + k, column - high, extra)
    mask_row = mask[...].astype(F32)
    ones = jnp.sum(mask_row, axis=1, keepdims=True)
    extra = jnp.where((lane == 104) & (row_id((CHUNK, 128)) == 0), ones, extra)

    loads["wq"].wait()
    wq_tiles = tiles_of(wq[...].astype(F32))
    for k in range(GROUP):
        tiles = permute_chunks(wq_tiles, qkv_picks(k))
        tiles[2] = tiles[2] + extra
        for t, tile in enumerate(fold_qkv(tiles)):
            s.qp_s[k, :, 128 * t : 128 * (t + 1)] = tile.astype(BF)
    s.q_all[GROUP * r + d] = s.qp_s[d]
    pl.semaphore_wait(barrier, len(partners))

    qkv_gather = PieceGather()
    qkv_gather.send()
    loads["wd"].wait()
    up_gather = Gather(
        lambda zk, xk: rows_at(s.w_up, 2 * zk + xk, BLOCK),
        lambda n: s.w_up.at[pl.ds(0, n * BLOCK)],
        cross=True,
    )
    downs = [
        Gather(
            lambda zk, xk, h=h: rows_at(s.w_down, 2 * (2 * zk + xk) + h, BLOCK // 2),
            lambda n: s.w_down.at[pl.ds(0, n * BLOCK // 2)],
            cross=h == 0,
        )
        for h in range(2)
    ]
    loads["wo"].wait()
    for t, tile in enumerate(fold(tiles_of(wo[...].astype(F32)))):
        s.wo_l[d, x, z, :, 128 * t : 128 * (t + 1)] = tile.astype(BF)
    out_gather = Gather(
        lambda zk, xk: s.wo_l.at[d, xk, zk],
        lambda n: s.wo_l.at[0, 0, pl.ds(0, n)] if n <= 4 else s.wo_l.at[0, :, pl.ds(0, n // 2)],
    )
    out_gather.send_two()
    out_gather.send_mirror()
    out_gather.send_near()
    out_gather.send_own_x()
    for half in downs:
        half.send_own_x()
    loads["wu"].wait()
    wu_tiles = tiles_of(wu[...].astype(F32))
    for k in range(GROUP):
        for t, tile in enumerate(fold(permute_chunks(wu_tiles, up_picks(k)))):
            s.up_s[k, :, 128 * t : 128 * (t + 1)] = tile.astype(BF)
    s.up_l[d] = s.up_s[d]
    up_arrival, up_group = arrivals(), sends(s.up_s.at[pl.ds(0, 3)])
    for m, device in mates:
        copy_to(s.up_s.at[m], s.up_l.at[d], device, up_arrival, up_group)
    loads["x"].wait()
    x_gather = GroupGather(lambda i: s.x_all.at[i], lambda n: s.x_all.at[pl.ds(0, n)])
    x_gather.send()
    diagonal = jnp.where(
        row_id((OWN, OWN)) == lane_id((OWN, OWN)), jnp.broadcast_to(mask_row, (OWN, OWN)), 0.0
    )
    loads["cot"].wait()
    s.c_all[d] = dot(diagonal.astype(BF), cot[...]).astype(BF)
    c_gather = GroupGather(lambda i: s.c_all.at[i], lambda n: s.c_all.at[pl.ds(0, n)])
    c_gather.send()

    def normalize(i):
        def one(at):
            normal, _ = standardize(s.x_all[i, at, :].astype(F32))
            s.normal[pl.ds(pl.multiple_of(OWN * i + at.start, at.size), at.size), :] = normal

        by_rows(OWN, 64, one)

    qkv_gather.forward_own(0)
    qkv_gather.forward_own(1)
    qkv_gather.forward_near(0)
    assemble_qkv(r)
    qkv_gather.forward_two(0)
    qkv_gather.forward_near(1)
    assemble_qkv(2 * z_near + x)
    qkv_gather.forward_two(1)
    out_gather.pass_two()
    assemble_qkv(2 * z_two + x)
    arrive(s.up_l.at[pl.ds(0, 3)], up_arrival)
    assemble(s.up_l, 6, s.w_up, r)
    up_gather.send_two()
    up_gather.send_near(True)
    qkv_gather.forward_mirror(0)
    x_gather.relay()
    qkv_gather.forward_mirror(1)
    up_gather.send_near(False)
    up_gather.send_mirror()
    for half in downs:
        half.send_two()
    downs[1].send_near()
    downs[0].send_near(True)
    out_gather.send_x(z_two)
    out_gather.forward_near()
    out_gather.forward_mirror()
    up_gather.send_own_x()
    columns = [
        GroupGather(lambda i, xk=xk: s.wo_l.at[i, xk], lambda n: s.wo_l.at[pl.ds(0, n), 0])
        for xk in (x, other_x)
    ]
    columns[0].send()
    assemble_qkv(2 * z_mirror + x)
    x_gather.finish()
    for i in range(GROUP):
        normalize(i)
    for name, zk in (("own", z), ("near", z_near), ("two", z_two)):
        qkv_gather.finish(name, zk)
        assemble_qkv(2 * zk + other_x)
    c_gather.relay()
    qkv_gather.finish("mirror", z_mirror)
    assemble_qkv(2 * z_mirror + other_x)

    lane = lane_id((8, 128))
    row = row_id((8, 128))
    pick = jnp.where((lane == 96 + row) | (lane == 100 + row), 1.0, 0.0)
    pick = jnp.where(row < 4, pick, jnp.where((row == 4) & (lane == 104), 1.0, 0.0))
    s.norms[...] = dot(pick.astype(BF), s.w_qkv[:, 256:384], 1, 1)
    total = jnp.sum(s.norms[4:5, :], axis=1, keepdims=True)
    loss_scale = (SEQ * ROWS) / total
    own_weight = dw[d]
    last_weight = dw[GROUP]

    def first_norm(at):
        value = s.normal[at, :] * (1.0 + s.norms[0:1, :]) + s.norms[1:2, :]
        s.h1[at, :] = value.astype(BF)

    by_rows(SEQ, 64, first_norm)

    def project(at):
        value = dot(s.h1[at, :], s.w_qkv[...])
        co, si = cosine[at, :], sine[at, :]
        for left, target in ((0, s.qv), (256, s.kk)):
            a, b = value[:, left : left + 128], value[:, left + 128 : left + 256]
            target[at, :128] = (a * co - b * si).astype(BF)
            target[at, 128:] = (b * co + a * si).astype(BF)
        s.v01[at, :] = value[:, 512:].astype(BF)

    loads["cosine"].wait()
    loads["sine"].wait()
    by_rows(SEQ, 256, project)

    lane2 = lax.div(lax.rem(lane_id((1, 256)), 128), jnp.int32(32))
    head_mask = [jnp.where(lane2 == h, 1.0, 0.0).astype(BF) for h in range(3)]
    tail_mask = jnp.where(lane2 == 3, 1.0, 0.0).astype(BF)
    half_id = lax.div(lane_id((1, 128)), jnp.int32(64))
    half_mask = [jnp.where(half_id == h, 1.0, 0.0).astype(BF) for h in range(2)]
    root = HD**-0.5
    o_gathers = [
        GroupGather(lambda i, b=b: s.o_l.at[i, b], lambda n: s.o_l.at[pl.ds(0, n), 0])
        for b in range(2)
    ]

    def attend(b):
        rows = slice(QBLOCK * b, QBLOCK * (b + 1))
        keys = QBLOCK * (b + 1)
        query = s.qv[rows, :]
        allowed = row_id((QBLOCK, keys)) + QBLOCK * b >= lane_id((QBLOCK, keys))
        first = jnp.zeros((QBLOCK, 128), F32)
        third = None
        for h in range(3):
            scores = dot(query * head_mask[h], s.kk[:keys, :], 1, 1) * root
            scores = jnp.where(allowed, scores, -1e30)
            raised = jnp.exp(scores - jnp.max(scores, axis=1, keepdims=True))
            probs = raised * (1.0 / jnp.sum(raised, axis=1, keepdims=True))
            s.probs[h, rows, :keys] = probs
            if h < 2:
                first = first + dot(probs.astype(BF), s.v01[:keys, :] * half_mask[h])
            else:
                third = dot(probs.astype(BF), s.qv[:keys, :])
            if b == 1 and h == 0:
                up_gather.forward_two()
                downs[0].send_near(False)
                for half in downs:
                    half.send_mirror()
            if b == 1 and h == 1:
                out_gather.finish()
                columns[1].send()
        s.o_l[d, b, :QBLOCK, :] = first.astype(BF)
        lane = lane_id((QBLOCK, 128))
        third = jnp.where(
            lane < 32, pltpu.roll(third[:, :128], 32, 1), pltpu.roll(third[:, 128:], 64, 1)
        )
        lane = lane_id((OWN, 128))
        third = jnp.where(lane < 64, third[:OWN], pltpu.roll(third[OWN:], 64, 1))
        s.o_l[d, b, QBLOCK:, :] = third.astype(BF)
        o_gathers[b].send()

    attend(1)
    columns[0].relay()
    attend(0)
    for h in range(3):
        s.probs[h, :QBLOCK, QBLOCK:] = jnp.zeros((QBLOCK, QBLOCK), F32)
    s.v_all[:, :128] = s.v01[...]

    def third_values(at):
        lane = lane_id((64, 128))
        low = pltpu.roll(s.qv[at, :128].astype(F32), 32, 1)
        high = pltpu.roll(s.qv[at, 128:].astype(F32), 64, 1)
        both = jnp.where(lane < 32, low, jnp.where(lane < 64, high, 0.0))
        s.v_all[at, 128:] = both.astype(BF)

    by_rows(SEQ, 64, third_values)
    up_gather.forward_cross()
    columns[1].relay()
    downs[1].forward_near()
    up_gather.forward_mirror()
    for column in columns:
        column.finish()
    for k in range(GROUP):
        for i in range(ROWS):
            tiles = [t.astype(F32) for t in tiles_of(s.wo_l[k, i % 2, i // 2])]
            at = CHUNK * (GROUP * i + k)
            for t, tile in enumerate(unfold(tiles, 6)):
                s.g_out[at : at + CHUNK, 128 * t : 128 * (t + 1)] = tile

    def out_place(head):
        k, h = divmod(head, 3)
        return 128 * k + 64 * h if h < 2 else 512 + 64 * k

    for head in range(HEADS):
        at = out_place(head)
        s.w_out[at : at + 64, :] = s.g_out[64 * head : 64 * head + 64, :].astype(BF)
    s.w_own[:128, :] = rows_at(s.w_out.at[pl.ds(0, 512)], d, 128)[...]
    s.w_own[128:192, :] = rows_at(s.w_out.at[pl.ds(512, 256)], d, 64)[...]
    s.w_own[192:, :] = jnp.zeros((64, WIDTH), BF)
    downs[0].forward_two()
    o_gathers[1].relay()
    c_gather.finish()

    loads["hist"].wait()
    s.terms[...] = jnp.zeros((8, WIDTH), F32)
    for i in range(GROUP):

        def loss_rows(at, i=i):
            here = pl.ds(pl.multiple_of(OWN * i + at.start, at.size), at.size)
            grad = s.c_all[i, at, :].astype(F32) * loss_scale
            s.dm[here, :] = (last_weight * grad).astype(BF)
            hg_o[here, :] = (own_weight * grad).astype(BF)
            s.terms[...] += sublane_sum(grad * hist[here, :].astype(F32))

        by_rows(OWN, 32, loss_rows)

    downs[1].forward_two()
    downs[0].forward_cross()
    for b in (1, 0):
        if b == 0:
            o_gathers[0].relay()
            downs[0].forward_mirror()
        o_gathers[b].finish()
        rows = slice(QBLOCK * b, QBLOCK * (b + 1))
        thirds = []
        for k in range(GROUP):
            s.ob[rows, 128 * k : 128 * (k + 1)] = s.o_l[k, b, :QBLOCK, :]
            thirds.append(s.o_l[k, b, QBLOCK:, :].astype(F32))
        lane = lane_id((OWN, 128))
        for p in range(2):
            even, odd = thirds[2 * p], thirds[2 * p + 1]
            top = jnp.where(lane < 64, even, pltpu.roll(odd, 64, 1))
            low = jnp.where(lane < 64, pltpu.roll(even, 64, 1), odd)
            cols = slice(512 + 128 * p, 640 + 128 * p)
            s.ob[QBLOCK * b : QBLOCK * b + OWN, cols] = top.astype(BF)
            s.ob[QBLOCK * b + OWN : QBLOCK * (b + 1), cols] = low.astype(BF)
        s.y[rows, :] = dot(s.ob[rows, :], s.w_out[...])
        for i in (2 * b, 2 * b + 1):

            def second_norm(at, i=i):
                here = pl.ds(pl.multiple_of(OWN * i + at.start, at.size), at.size)
                value = s.y[here, :] + s.x_all[i, at, :].astype(F32)
                s.y[here, :] = value
                normal, _ = standardize(value)
                value = normal * (1.0 + s.norms[2:3, :]) + s.norms[3:4, :]
                s.h2[here, :] = value.astype(BF)

            by_rows(OWN, 64, second_norm)

    downs[1].forward_mirror()
    up_gather.arrive_near()
    up_gather.finish()

    def widen(at):
        s.part[at, :] = dot(s.h2[at, :], s.w_up[...])

    by_rows(SEQ, 256, widen)

    rate = 0.7978845608028654

    def gate(at):
        u = s.part[at, :]
        bend = jnp.tanh(rate * (u + 0.044715 * u * u * u))
        s.act[at, :] = (0.5 * u * (1.0 + bend)).astype(BF)
        s.slope[at, :] = bend

    by_rows(SEQ, 32, gate)

    def gate_slope(at):
        u, bend = s.part[at, :], s.slope[at, :]
        inner = rate * (1.0 + 3 * 0.044715 * u * u)
        s.slope[at, :] = 0.5 * (1.0 + bend) + 0.5 * u * (1.0 - bend * bend) * inner

    def block_of(ref, shift=0):
        def block(index, at):
            start = pl.multiple_of(index * BLOCK + shift + at.start, at.size)
            return ref[pl.ds(start, at.size), :]

        return block

    for i in range(3):
        cols = slice(QBLOCK * i, QBLOCK * (i + 1))
        s.g_down[cols, :] = dot(s.act[:, cols], s.dm[...], 0, 0)
    down_sum = RowSum("down", s.f_down, block_of(s.g_down), 16, True)
    down_sum.send(early_near=True)
    by_rows(SEQ, 32, gate_slope)
    downs[0].arrive_near()
    for half in downs:
        half.finish()

    mid_sum = GroupSum("mid", s.part, 4)

    def quarter(ref, i, size=32):
        return jnp.concatenate(
            [ref[OWN * j + 32 * i : OWN * j + 32 * i + size, :] for j in range(GROUP)], axis=0
        )

    def put_quarter(ref, i, value, size=32):
        for j in range(GROUP):
            ref[OWN * j + 32 * i : OWN * j + 32 * i + size, :] = value[size * j : size * (j + 1)]

    for i in (0, 2):
        value = dot(quarter(s.dm, i, 64), s.w_down[...], 1, 1)
        value = (value * quarter(s.slope, i, 64)).astype(BF)
        put_quarter(s.du, i, value, 64)
        put_quarter(s.part, i, dot(value, s.w_up[...], 1, 1), 64)
        mid_sum.send(i)
        mid_sum.send(i + 1)
    for i in range(3):
        mid_sum.middle(i)
    down_sum.send_mirror()
    mid_sum.middle(3)
    down_sum.send_own()

    def up_part(i):
        cols = slice(QBLOCK * i, QBLOCK * (i + 1))
        s.g_up[cols, :] = dot(s.h2[:, cols], s.du[...], 0, 0)

    up_part(0)
    s.terms2[...] = jnp.zeros((8, WIDTH), F32)
    s.t0[...] = jnp.zeros((8, WIDTH), F32)

    def second_norm_back(at):
        here = pl.ds(pl.multiple_of(OWN * d + at.start, at.size), at.size)
        grad = mid_sum.value(at)
        value = s.y[here, :]
        normal, scale = standardize(value)
        loss = s.c_all[d, at, :].astype(F32) * loss_scale
        back = last_weight * loss + norm_back(grad, s.norms[2:3, :], normal, scale)
        s.dy[at, :] = back
        s.dyb[d, at, :] = back.astype(BF)
        s.t0[2:3, :] += jnp.sum(grad * normal, axis=0, keepdims=True)
        s.t0[3:4, :] += jnp.sum(grad, axis=0, keepdims=True)
        s.terms2[...] += sublane_sum(loss * value)

    up_sum = RowSum("up", s.f_up, block_of(s.g_up), 16, True)
    dy_gathers = []
    dy_group = sends(s.dyb.at[pl.ds(0, 3)])
    for i in range(4):
        mid_sum.wait(i)
        mid_sum.over(i, second_norm_back)
        dy_gathers.append(
            GroupGather(
                lambda j, i=i: s.dyb.at[j, mid_sum.part(i)],
                lambda n: s.dyb.at[pl.ds(0, n), mid_sum.part(0)],
                dy_group,
            )
        )
        dy_gathers[i].send()
        if i < 2:
            up_part(i + 1)
        if i == 2:
            up_sum.send()

    def block_out(at):
        value = dot(s.act[at, :], s.w_down[...])
        s.part2[at, :] = value

    by_rows(SEQ, 256, block_out)
    def mix_quarter(i):
        def mix(at):
            here = pl.ds(pl.multiple_of(OWN * i + at.start, at.size), at.size)
            value = s.part2[here, :]
            loss = s.c_all[i, at, :].astype(F32) * loss_scale
            s.terms2[...] += sublane_sum(loss * value)
            s.part2[here, :] = own_weight * hist[here, :].astype(F32) + last_weight * value

        by_rows(OWN, 32, mix)

    down_sum.send_two_outside()
    dy_gathers[0].relay()
    mix_quarter(0)
    mix_quarter(1)
    dy_gathers[1].relay()
    mix_quarter(2)
    mix_quarter(3)
    mix_sum = GroupSum("mix", s.part2)
    mix_sum.send()
    lane = lane_id((8, 128))
    own_term = jnp.sum(jnp.sum(s.terms[...], axis=0, keepdims=True), axis=1, keepdims=True)
    last_term = jnp.sum(jnp.sum(s.terms2[...], axis=0, keepdims=True), axis=1, keepdims=True)
    s.u0[...] = jnp.where(lane == d, own_term, jnp.where(lane == GROUP, last_term, 0.0))
    depth_x, depth_z, depth_d = (arrivals() for _ in range(3))
    depth_group = sends(s.uzd.at[pl.ds(0, 7)])
    copy_to(s.u0, s.u1, x_dev, depth_x, depth_group)
    down_sum.send_two_inside()

    head_scale = [jnp.where(lane2 == h, root, 0.0) for h in range(3)]
    lane = lax.div(lane_id((1, 256)), jnp.int32(64))
    head_lanes = [jnp.where(lane == h, 1.0, 0.0).astype(BF) for h in range(3)]
    for i in range(4):
        dy_gathers[i].finish()
        rows = s.dyb[:, 32 * i : 32 * (i + 1), :].reshape(OWN, WIDTH)
        grad = dot(rows, s.w_own[...], 1, 1).astype(BF)
        grad = jnp.concatenate([grad * m for m in head_lanes], axis=0)
        probs = jnp.concatenate([quarter(s.probs.at[h], i) for h in range(3)], axis=0)
        dp = dot(grad, s.v_all[...], 1, 1)
        delta = jnp.sum(dp * probs, axis=1, keepdims=True)
        ds = (probs * (dp - delta)).astype(BF)
        query = quarter(s.qv, i)
        query = jnp.concatenate([query * m for m in head_mask], axis=0)
        dk = dot(ds, query, 0, 0) * root
        dv = dot(probs.astype(BF), grad, 0, 0)
        if i == 0:
            s.dk[...] = dk
            s.dv[...] = dv
        else:
            s.dk[...] += dk
            s.dv[...] += dv
        dq = dot(ds, s.kk[...])
        dq = sum(dq[OWN * h : OWN * (h + 1)] * head_scale[h] for h in range(3))
        put_quarter(s.dq, i, dq)
        if i < 2:
            dy_gathers[i + 2].relay()
        if i == 1:
            up_sum.send_mirror()
            up_sum.send_own()
            mix_sum.middle()

    def turn_back(at):
        co, si = cosine[at, :], sine[at, :]
        lane = lane_id((64, 128))
        for left, source in ((0, s.dq), (256, s.dk)):
            a, b = source[at, :128], source[at, 128:]
            first, second = a * co + b * si, b * co - a * si
            if left == 0:
                third = s.dv[at, 128:]
                first = jnp.where(lane < 96, first, pltpu.roll(third, 96, 1))
                second = jnp.where(lane < 96, second, pltpu.roll(third, 64, 1))
            s.dqkv[at, left : left + 128] = first.astype(BF)
            s.dqkv[at, left + 128 : left + 256] = second.astype(BF)
        s.dqkv[at, 512:] = s.dv[at, :128].astype(BF)

    by_rows(SEQ, 64, turn_back)
    up_sum.send_two_outside()
    for i in range(3):
        cols = slice(QBLOCK * i, QBLOCK * (i + 1))
        s.g_qkv[cols, :] = dot(s.h1[:, cols], s.dqkv[...], 0, 0)
    shared = (
        sends(s.fin.at[pl.ds(0, 4)], inside),
        sends(s.st_qkv0.at[pl.ds(0, 2)], outside),
        sends(s.fin.at[pl.ds(0, 11)]),
        arrivals(),
        arrivals(),
    )
    sums = [SpreadSum(h, shared) for h in range(2)]
    for one in sums:
        one.send_x("mirror", z_mirror)
        one.send_crossing()
    for one in sums:
        one.send_x("two", z_two)
    for one in sums:
        one.send_third()
    arrive(s.u1, depth_x)
    s.uzd[z] = s.u0[...] + s.u1[...]
    for device in (two_dev, mirror_dev, near_dev):
        copy_to(s.uzd.at[z], s.uzd.at[z], device, depth_z, depth_group)

    def first_back(at):
        s.part[at, :] = dot(s.dqkv[at, :], s.w_qkv[...], 1, 1)

    by_rows(SEQ, 256, first_back)
    in_sum = GroupSum("in", s.part)
    in_sum.send()
    up_sum.send_two_inside()
    s.gain_sum[...] = jnp.zeros((8, WIDTH), F32)
    s.shift_sum[...] = jnp.zeros((8, WIDTH), F32)

    def first_norm_sums(at):
        grad = s.part[at, :]
        s.gain_sum[...] += sublane_sum(grad * s.normal[at, :])
        s.shift_sum[...] += sublane_sum(grad)

    by_rows(SEQ, 32, first_norm_sums)
    s.t0[0:1, :] = jnp.sum(s.gain_sum[...], axis=0, keepdims=True)
    s.t0[1:2, :] = jnp.sum(s.shift_sum[...], axis=0, keepdims=True)
    s.td[d] = s.t0[...]
    norm_arrival, norm_group = arrivals(), sends(s.td.at[pl.ds(0, 3)])
    for m, device in mates:
        copy_to(s.td.at[d], s.td.at[d], device, norm_arrival, norm_group)
    in_sum.middle()
    for p in range(3):
        cols = slice(QBLOCK * p, QBLOCK * (p + 1))
        value = dot(s.ob[:, cols], s.dyb[...].reshape(SEQ, WIDTH), 0, 0)
        for i in range(4):
            place = QBLOCK * p + 64 * i
            for head in range(HEADS):
                if out_place(head) == place:
                    s.g_out[64 * head : 64 * head + 64, :] = value[64 * i : 64 * i + 64]

    for one in sums:
        one.send_mirror()
    up_sum.send_near()
    arrive(s.td.at[pl.ds(0, 3)], norm_arrival)
    value = (s.td[0] + s.td[1]) + (s.td[2] + s.td[3])
    value = pltpu.roll(value, lax.rem(WIDTH - CHUNK * d, WIDTH), 1)
    for i in range(ROWS):
        shift = (WIDTH - BLOCK * i) % WIDTH
        shifted = pltpu.roll(value, shift, 1) if shift else value
        s.ext[i] = jnp.concatenate([shifted[:, :128], jnp.zeros((8, 128), F32)], axis=0)

    def out_block(index, at):
        start_row = pl.multiple_of((GROUP * index + d) * CHUNK, 8)
        tiles = tiles_of(s.g_out[pl.ds(start_row, CHUNK), :])
        return jnp.concatenate(fold(tiles) + [s.ext[index]], axis=1)

    out_sum = RowSum("out", s.f_out, out_block, 16, False)
    out_sum.send_x("mirror", z_mirror)
    out_sum.send_x("two", z_two)
    for one in sums:
        one.send_own_outside()
    out_sum.send_x("near", z_near)
    out_sum.send_x("own", z)

    down_sum.finish()
    gd_o[...] = s.f_down[...]
    def spread(total, staged, landing):
        arrival, group = arrivals(), sends(staged.at[pl.ds(0, 3)])
        for m, device in mates:
            rows = total[pl.ds(pl.multiple_of(CHUNK * m, CHUNK), CHUNK), :]
            for t, tile in enumerate(fold(tiles_of(rows))):
                staged[m, :, 128 * t : 128 * (t + 1)] = tile.astype(BF)
            copy_to(staged.at[m], landing.at[d], device, arrival, group)
        rows = total[pl.ds(pl.multiple_of(CHUNK * d, CHUNK), CHUNK), :]
        for t, tile in enumerate(fold(tiles_of(rows))):
            landing[d, :, 128 * t : 128 * (t + 1)] = tile.astype(BF)
        return arrival

    def collect(arrival, landing, count, back, target):
        arrive(landing.at[pl.ds(0, 3)], arrival)
        tiles = []
        for k in range(GROUP):
            tiles += unfold([t.astype(F32) for t in tiles_of(landing[k])], count)
        for t, tile in enumerate(permute_chunks(tiles, back)):
            target[:, 128 * t : 128 * (t + 1)] = tile

    mix_sum.wait()

    def write_out(at):
        here = pl.ds(pl.multiple_of(OWN * d + at.start, at.size), at.size)
        out_o[at, :] = (mix_sum.value(at) + last_weight * s.y[here, :]).astype(BF)

    by_rows(OWN, 32, write_out)

    for one in sums:
        one.send_two()
    out_sum.send_mirror()
    in_sum.wait()

    def first_norm_back(at):
        grad = in_sum.value(at)
        normal, scale = standardize(s.x_all[d, at, :].astype(F32))
        back = norm_back(grad, s.norms[0:1, :], normal, scale)
        ig_o[at, :] = (s.dy[at, :] + back).astype(BF)

    by_rows(OWN, 32, first_norm_back)
    for one in sums:
        one.send_near()
    up_sum.finish()
    up_spread = spread(s.f_up, s.b_up, s.a_up)
    arrive(s.uzd.at[pl.ds(0, 3)], depth_z)
    s.uzd[4 + d] = (s.uzd[0] + s.uzd[1]) + (s.uzd[2] + s.uzd[3])
    for m, device in mates:
        copy_to(s.uzd.at[4 + d], s.uzd.at[4 + d], device, depth_d, depth_group)
    for one in sums:
        one.keep_own()
    out_sum.send_two_outside()
    out_sum.send_two_inside()
    out_sum.send_near()
    arrive(s.uzd.at[pl.ds(0, 3)], depth_d)
    dg_o[...] = (s.uzd[4] + s.uzd[5]) + (s.uzd[6] + s.uzd[7])

    collect(up_spread, s.a_up, 6, UP_BACK, gu_o)

    arrive(s.fin.at[pl.ds(0, 11)], shared[3])
    for k in range(GROUP):
        s.q_sum[k] = (
            s.fin[12 + k].astype(F32) + s.fin[4 + k].astype(F32) + s.fin[k].astype(F32)
        )

    @pl.when(inside)
    def _():
        arrive(s.fin.at[pl.ds(0, 4)], shared[4])
        for k in range(GROUP):
            s.q_sum[k] += s.fin[8 + k].astype(F32)

    tiles = []
    for k in range(GROUP):
        tiles += unfold_qkv(tiles_of(s.q_sum[k]))
    for t, tile in enumerate(permute_chunks(tiles, QKV_BACK)):
        gq_o[:, 128 * t : 128 * (t + 1)] = tile
    out_sum.finish()
    for t, tile in enumerate(unfold(tiles_of(s.f_out[:, :1152]), 6)):
        go_o[:, 128 * t : 128 * (t + 1)] = tile
    ng_o[...] = s.f_out[:8, 1152:]
    for group, view, condition in send_groups:
        wait = prepare(view, view, x_dev, 0, group).wait_send
        if condition is None:
            wait()
        else:
            pl.when(condition)(wait)
    assert used["send"] <= N_SENDS and used["arrival"] <= N_ARRIVALS, used


def finish_kernel(*refs):
    count = N_OUT - 2
    ins, refs = refs[:count], refs[count:]
    (norm, depth), refs = refs[:2], refs[2:]
    outs, (norm_o, depth_o), sems = refs[:count], refs[count : count + 2], refs[-1]
    copies = [pltpu.make_async_copy(a, b, sems.at[i]) for i, (a, b) in enumerate(zip(ins, outs))]
    for copy in copies:
        copy.start()
    norm_o[...] = norm[:4, :CHUNK]
    depth_o[...] = depth[:1, : GROUP + 1]
    for copy in copies:
        copy.wait()


def fused(
    block_input,
    history,
    cotangent,
    token_mask,
    qkv_weight,
    out_weight,
    up_weight,
    down_weight,
    norm_params,
    depth_weights,
):
    cosine, sine = tables()
    vmem = pl.BlockSpec(memory_space=pltpu.VMEM)
    smem = pl.BlockSpec(memory_space=pltpu.SMEM)
    hbm = pl.BlockSpec(memory_space=pltpu.HBM)
    shape = jax.ShapeDtypeStruct
    shapes = (
        shape((OWN, WIDTH), BF),
        shape((OWN, WIDTH), BF),
        shape((SEQ, WIDTH), BF),
        shape((CHUNK, 3 * WIDTH), F32),
        shape((CHUNK, WIDTH), F32),
        shape((CHUNK, 4 * WIDTH), F32),
        shape((BLOCK, WIDTH), F32),
        shape((8, 128), F32),
        shape((8, 128), F32),
    )
    outs = pl.pallas_call(
        fused_kernel,
        out_shape=tuple(pltpu.VMEM(one.shape, one.dtype) for one in shapes),
        in_specs=[hbm] * 3 + [vmem] + [hbm] * 4 + [vmem, smem] + [hbm] * 2,
        out_specs=[vmem] * 9,
        scratch_shapes=[pltpu.VMEM(dims, kind) for dims, kind in SCRATCH.values()]
        + [pltpu.SemaphoreType.DMA((n,)) for n in (N_SENDS, N_ARRIVALS, 9)],
        compiler_params=pltpu.CompilerParams(
            collective_id=0, has_side_effects=True, vmem_limit_bytes=VMEM_MIB * 2**20
        ),
        cost_estimate=pl.CostEstimate(flops=12 * 10**9, bytes_accessed=4 * 10**6, transcendentals=10**6),
    )(
        block_input,
        history.reshape(SEQ, WIDTH),
        cotangent,
        token_mask.reshape(1, OWN),
        qkv_weight,
        out_weight,
        up_weight,
        down_weight,
        norm_params,
        depth_weights,
        jnp.asarray(cosine),
        jnp.asarray(sine),
    )
    held = pl.pallas_call(
        finish_kernel,
        out_shape=shapes[:7] + (shape((4, CHUNK), F32), shape((1, GROUP + 1), F32)),
        in_specs=[vmem] * 9,
        out_specs=[hbm] * 7 + [vmem] * 2,
        scratch_shapes=[pltpu.SemaphoreType.DMA((7,))],
        compiler_params=pltpu.CompilerParams(vmem_limit_bytes=4 * 2**20),
    )(*outs)
    out, input_grad, history_grad, *grads, g_depth = held
    return (out, input_grad, history_grad.reshape(1, SEQ, WIDTH), *grads, g_depth.reshape(GROUP + 1))


def fits(mesh, block_input, history, up_weight):
    devices = ROWS * GROUP
    return (
        mesh.shape["rows"] == ROWS
        and mesh.shape["depth"] == GROUP
        and block_input.shape == (OWN * devices, WIDTH)
        and history.shape[0] == GROUP
        and up_weight.shape == (WIDTH, 4 * WIDTH)
    )


def solution(mesh):
    weights = P(("rows", "depth"), None)
    in_specs = (
        weights,
        P("depth", "rows", None),
        weights,
        P(("rows", "depth")),
        weights,
        weights,
        weights,
        weights,
        P(None, ("rows", "depth")),
        P(),
    )
    out_specs = (
        weights,
        weights,
        P("depth", "rows", None),
        weights,
        weights,
        weights,
        weights,
        P(None, ("rows", "depth")),
        P(),
    )

    def run(*args):
        body = fused if fits(mesh, args[0], args[1], args[6]) else local
        return jax.shard_map(
            body, mesh=mesh, in_specs=in_specs, out_specs=out_specs, check_vma=False
        )(*args)

    return run
```

```python
import functools

import jax
import jax.numpy as jnp
import numpy as np
from jax import lax
from jax.experimental import pallas as pl
from jax.experimental.pallas import tpu as pltpu
from jax.sharding import PartitionSpec as P

HEADS = 12
HD = 64


def norm_rows(value, gain, shift):
    center = value - jnp.mean(value, axis=-1, keepdims=True)
    spread = jnp.mean(center * center, axis=-1, keepdims=True)
    return center * lax.rsqrt(spread + 1e-05) * (1.0 + gain) + shift


def rotate(value, place, sign):
    half = value.shape[-1] // 2
    freq = 10000.0 ** (-jnp.arange(half, dtype=jnp.float32) / half)
    angle = place.astype(jnp.float32)[:, None] * freq[None, :]
    cosine = jnp.cos(angle)[:, None, :]
    sine = jnp.sin(angle)[:, None, :] * sign
    first = value[..., :half]
    second = value[..., half:]
    return jnp.concatenate(
        [first * cosine - second * sine, second * cosine + first * sine], axis=-1
    )


def block_scores(query, key_block, start, query_place, scale):
    block_len = key_block.shape[0]
    scores = (
        jnp.einsum("qhd,khd->hqk", query, key_block, preferred_element_type=jnp.float32) * scale
    )
    key_place = start + jnp.arange(block_len, dtype=jnp.int32)
    allowed = query_place[:, None] >= key_place[None, :]
    return (scores, allowed)


def local(
    block_input,
    history,
    cotangent,
    token_mask,
    qkv_weight,
    out_weight,
    up_weight,
    down_weight,
    norm_params,
    depth_weights,
):
    rows_tok, width = block_input.shape
    depth_count = lax.axis_size("depth")
    device_count = lax.axis_size("rows") * depth_count
    place_depth = lax.axis_index("depth")
    heads = HEADS
    head_size = HD
    scale = head_size ** (-0.5)
    seq_len = rows_tok * depth_count
    slot_count = history.shape[0]
    hist_total = slot_count * depth_count
    wide_qkv, wide_out, wide_up, wide_down, wide_norms = (
        lax.all_gather(qkv_weight, ("rows", "depth"), axis=0, tiled=True),
        lax.all_gather(out_weight, ("rows", "depth"), axis=0, tiled=True),
        lax.all_gather(up_weight, ("rows", "depth"), axis=0, tiled=True),
        lax.all_gather(down_weight, ("rows", "depth"), axis=0, tiled=True),
        lax.all_gather(
            norm_params.astype(jnp.bfloat16), ("rows", "depth"), axis=1, tiled=True
        ).astype(norm_params.dtype),
    )
    total = lax.psum(jnp.sum(token_mask), ("rows", "depth")).astype(jnp.float32)
    loss_scale = rows_tok * device_count / total
    float_input = block_input.astype(jnp.float32)
    place = place_depth * rows_tok + jnp.arange(rows_tok, dtype=jnp.int32)
    first = norm_rows(float_input, wide_norms[0], wide_norms[1]).astype(jnp.bfloat16)
    projected = jnp.dot(first, wide_qkv, preferred_element_type=jnp.float32)
    query = rotate(projected[:, :width].reshape(rows_tok, heads, head_size), place, 1.0).astype(
        jnp.bfloat16
    )
    keys = rotate(projected[:, width : 2 * width].reshape(rows_tok, heads, head_size), place, 1.0)
    keys = keys.astype(jnp.bfloat16).reshape(rows_tok, width)
    values = projected[:, 2 * width :].astype(jnp.bfloat16)
    all_keys, all_values = (
        lax.all_gather(keys, "depth", axis=0, tiled=True),
        lax.all_gather(values, "depth", axis=0, tiled=True),
    )
    block_len = min(512, seq_len)
    block_count = seq_len // block_len
    key_blocks = all_keys.reshape(block_count, block_len, heads, head_size)
    value_blocks = all_values.reshape(block_count, block_len, heads, head_size)
    starts = jnp.arange(block_count, dtype=jnp.int32) * block_len

    def peak_step(carry, item):
        peak, weight_sum = carry
        key_block, value_block, start = item
        scores, allowed = block_scores(query, key_block, start, place, scale)
        scores = jnp.where(allowed[None], scores, -1e30)
        new_peak = jnp.maximum(peak, jnp.max(scores, axis=-1))
        weight_sum = weight_sum * jnp.exp(peak - new_peak) + jnp.sum(
            jnp.exp(scores - new_peak[..., None]), axis=-1
        )
        return ((new_peak, weight_sum), None)

    start_carry = (
        jnp.full((heads, rows_tok), -1e30, jnp.float32),
        jnp.zeros((heads, rows_tok), jnp.float32),
    )
    (peak, weight_sum), _ = lax.scan(peak_step, start_carry, (key_blocks, value_blocks, starts))
    log_total = peak + jnp.log(weight_sum)

    def value_step(running, item):
        key_block, value_block, start = item
        scores, allowed = block_scores(query, key_block, start, place, scale)
        probs = jnp.where(allowed[None], jnp.exp(scores - log_total[..., None]), 0.0)
        running = running + jnp.einsum(
            "hqk,khd->qhd",
            probs.astype(jnp.bfloat16),
            value_block,
            preferred_element_type=jnp.float32,
        )
        return (running, None)

    running, _ = lax.scan(
        value_step,
        jnp.zeros((rows_tok, heads, head_size), jnp.float32),
        (key_blocks, value_blocks, starts),
    )
    mixed = running.reshape(rows_tok, width)
    mixed_low = mixed.astype(jnp.bfloat16)
    middle = float_input + jnp.dot(mixed_low, wide_out, preferred_element_type=jnp.float32)
    second = norm_rows(middle, wide_norms[2], wide_norms[3]).astype(jnp.bfloat16)
    upper = jnp.dot(second, wide_up, preferred_element_type=jnp.float32)
    active = jax.nn.gelu(upper).astype(jnp.bfloat16)
    block_out = middle + jnp.dot(active, wide_down, preferred_element_type=jnp.float32)
    own_alpha = lax.dynamic_slice_in_dim(depth_weights, place_depth * slot_count, slot_count)
    partial_mix = jnp.sum(own_alpha[:, None, None] * history.astype(jnp.float32), axis=0)
    mixture = lax.psum_scatter(
        partial_mix.astype(jnp.bfloat16), "depth", scatter_dimension=0, tiled=True
    ).astype(jnp.float32)
    output = (mixture + depth_weights[hist_total] * block_out).astype(jnp.bfloat16)
    grad_out = token_mask.astype(jnp.float32)[:, None] * cotangent.astype(jnp.float32) * loss_scale
    last_term = jnp.sum(grad_out * block_out)
    index_all = jnp.arange(hist_total + 1, dtype=jnp.int32)
    grad_rows = lax.all_gather(grad_out.astype(jnp.bfloat16), "depth", axis=0, tiled=True).astype(
        grad_out.dtype
    )
    history_grad = (own_alpha[:, None, None] * grad_rows[None]).astype(jnp.bfloat16)
    hist_terms = jnp.sum(history.astype(jnp.float32) * grad_rows[None], axis=(1, 2))
    own_index = place_depth * slot_count + jnp.arange(slot_count, dtype=jnp.int32)
    alpha_terms = jnp.sum(
        jnp.where(index_all[None, :] == own_index[:, None], hist_terms[:, None], 0.0), axis=0
    )
    alpha_terms = alpha_terms + jnp.where(index_all == hist_total, last_term, 0.0)
    depth_gradient = lax.psum(alpha_terms, ("rows", "depth"))
    wide_qkv, wide_out, wide_up, wide_down, wide_norms = (
        lax.all_gather(qkv_weight, ("rows", "depth"), axis=0, tiled=True),
        lax.all_gather(out_weight, ("rows", "depth"), axis=0, tiled=True),
        lax.all_gather(up_weight, ("rows", "depth"), axis=0, tiled=True),
        lax.all_gather(down_weight, ("rows", "depth"), axis=0, tiled=True),
        lax.all_gather(
            norm_params.astype(jnp.bfloat16), ("rows", "depth"), axis=1, tiled=True
        ).astype(norm_params.dtype),
    )
    block_grad = depth_weights[hist_total] * grad_out
    lower_grad = block_grad.astype(jnp.bfloat16)
    down_gradient = jnp.dot(active.T, lower_grad, preferred_element_type=jnp.float32)
    active_grad = jnp.dot(lower_grad, wide_down.T, preferred_element_type=jnp.float32)
    _, gelu_pull = jax.vjp(jax.nn.gelu, upper)
    upper_grad = gelu_pull(active_grad)[0].astype(jnp.bfloat16)
    up_gradient = jnp.dot(second.T, upper_grad, preferred_element_type=jnp.float32)
    second_grad = jnp.dot(upper_grad, wide_up.T, preferred_element_type=jnp.float32)
    _, norm_pull = jax.vjp(norm_rows, middle, wide_norms[2], wide_norms[3])
    middle_part, gain_two, shift_two = norm_pull(second_grad)
    middle_grad = block_grad + middle_part
    branch_grad = middle_grad.astype(jnp.bfloat16)
    out_gradient = jnp.dot(mixed_low.T, branch_grad, preferred_element_type=jnp.float32)
    mixed_grad = jnp.dot(branch_grad, wide_out.T, preferred_element_type=jnp.float32).astype(
        jnp.bfloat16
    )
    delta = jnp.sum(
        (mixed_grad.astype(jnp.float32) * mixed).reshape(rows_tok, heads, head_size), axis=-1
    ).T
    mixed_heads = mixed_grad.reshape(rows_tok, heads, head_size)

    def score_grads(
        query_rows, grad_rows, lse_rows, delta_rows, key_block, value_block, query_place, start
    ):
        scores, allowed = block_scores(query_rows, key_block, start, query_place, scale)
        probs = jnp.where(allowed[None], jnp.exp(scores - lse_rows[..., None]), 0.0)
        prob_grad = jnp.einsum(
            "qhd,khd->hqk", grad_rows, value_block, preferred_element_type=jnp.float32
        )
        score_grad = (probs * (prob_grad - delta_rows[..., None])).astype(jnp.bfloat16)
        return (probs, score_grad)

    def grad_step(query_total, item):
        key_block, value_block, start = item
        probs, score_grad = score_grads(
            query, mixed_heads, log_total, delta, key_block, value_block, place, start
        )
        query_total = (
            query_total
            + jnp.einsum("hqk,khd->qhd", score_grad, key_block, preferred_element_type=jnp.float32)
            * scale
        )
        key_part = (
            jnp.einsum("hqk,qhd->khd", score_grad, query, preferred_element_type=jnp.float32)
            * scale
        )
        value_part = jnp.einsum(
            "hqk,qhd->khd",
            probs.astype(jnp.bfloat16),
            mixed_heads,
            preferred_element_type=jnp.float32,
        )
        return (query_total, (key_part, value_part))

    query_total, (key_parts, value_parts) = lax.scan(
        grad_step,
        jnp.zeros((rows_tok, heads, head_size), jnp.float32),
        (key_blocks, value_blocks, starts),
    )
    key_sum, value_sum = (
        lax.psum_scatter(
            key_parts.reshape(seq_len, width).astype(jnp.bfloat16),
            "depth",
            scatter_dimension=0,
            tiled=True,
        ).astype(jnp.float32),
        lax.psum_scatter(
            value_parts.reshape(seq_len, width).astype(jnp.bfloat16),
            "depth",
            scatter_dimension=0,
            tiled=True,
        ).astype(jnp.float32),
    )
    query_grad = rotate(query_total, place, -1.0).reshape(rows_tok, width)
    key_grad = rotate(key_sum.reshape(rows_tok, heads, head_size), place, -1.0).reshape(
        rows_tok, width
    )
    projected_grad = jnp.concatenate([query_grad, key_grad, value_sum], axis=1).astype(jnp.bfloat16)
    qkv_gradient = jnp.dot(first.T, projected_grad, preferred_element_type=jnp.float32)
    first_grad = jnp.dot(projected_grad, wide_qkv.T, preferred_element_type=jnp.float32)
    _, first_pull = jax.vjp(norm_rows, float_input, wide_norms[0], wide_norms[1])
    input_part, gain_one, shift_one = first_pull(first_grad)
    input_grad = (middle_grad + input_part).astype(jnp.bfloat16)
    norms_full = jnp.stack([gain_one, shift_one, gain_two, shift_two])
    qkv_gradient, out_gradient, up_gradient, down_gradient, norm_gradient = (
        lax.psum_scatter(qkv_gradient, ("rows", "depth"), scatter_dimension=0, tiled=True),
        lax.psum_scatter(out_gradient, ("rows", "depth"), scatter_dimension=0, tiled=True),
        lax.psum_scatter(up_gradient, ("rows", "depth"), scatter_dimension=0, tiled=True),
        lax.psum_scatter(down_gradient, ("rows", "depth"), scatter_dimension=0, tiled=True),
        lax.psum_scatter(norms_full, ("rows", "depth"), scatter_dimension=1, tiled=True),
    )
    return (
        output,
        input_grad,
        history_grad,
        qkv_gradient,
        out_gradient,
        up_gradient,
        down_gradient,
        norm_gradient,
        depth_gradient,
    )

SEQ = 512
OWN = 128
WIDTH = 768
ROWS = 8
GROUP = 4
PACK = 640
BLOCK = WIDTH // ROWS
CHUNK = BLOCK // GROUP
QBLOCK = 256
BF = jnp.bfloat16
F32 = jnp.float32
MESH = pl.DeviceIdType.MESH


def dot(a, b, ca=1, cb=0):
    return lax.dot_general(a, b, (((ca,), (cb,)), ((), ())), preferred_element_type=F32)


def lane_id(shape):
    return lax.broadcasted_iota(jnp.int32, shape, len(shape) - 1)


def row_id(shape):
    return lax.broadcasted_iota(jnp.int32, shape, len(shape) - 2)


def tiles_of(value):
    return [value[:, 128 * i : 128 * (i + 1)] for i in range(value.shape[1] // 128)]


def permute_chunks(tiles, picks):
    group = lax.div(lane_id(tiles[0].shape), jnp.int32(32))
    out = []
    for t in range(len(picks) // 4):
        total, rolled = jnp.zeros_like(tiles[0]), {}
        for j in range(4):
            pick = picks[4 * t + j]
            if pick is None:
                continue
            source, place = divmod(pick, 4)
            shift = (j - place) * 32 % 128
            if (source, shift) not in rolled:
                value = tiles[source]
                rolled[source, shift] = pltpu.roll(value, shift, 1) if shift else value
            total = jnp.where(group == j, rolled[source, shift], total)
        out.append(total)
    return out


def fold(tiles):
    half = (len(tiles) + 1) // 2
    low = [t[16:] for t in tiles]
    if len(low) % 2:
        low.append(jnp.zeros_like(low[0]))
    return [t[:16] for t in tiles] + [
        jnp.concatenate([low[i], low[half + i]], axis=0) for i in range(half)
    ]


def unfold(tiles, count):
    half = (count + 1) // 2
    rest = tiles[count:]
    low = [rest[i][:8] for i in range(half)] + [rest[i][8:] for i in range(half)]
    return [jnp.concatenate([tiles[i], low[i]], axis=0) for i in range(count)]


def fold_qkv(tiles):
    t0, t1, t2, t3, t4 = tiles
    lane, lane8, lane16 = (lane_id((n, 128)) for n in (CHUNK, 8, 16))
    turned = pltpu.roll(t3, 96, 1)
    keys = jnp.where(lane < 96, t2, turned)
    extra = jnp.where(
        lane8 < 80,
        pltpu.roll(t2[:8], 96, 1),
        jnp.where(lane8 < 96, pltpu.roll(t2[8:16], 112, 1), t2[16:]),
    )
    right = jnp.concatenate([pltpu.roll(turned[16:], 64, 1), extra], axis=0)
    shared = jnp.where(lane16 < 64, turned[:16], right)
    return [t0[:16], t1[:16], t4[:16], keys[:16], shared] + [
        jnp.concatenate([a[16:], b[16:]], axis=0) for a, b in ((t0, t1), (t4, keys))
    ]


def unfold_qkv(tiles):
    u0, u1, u4, u3, shared, low01, low43 = tiles
    lane = lane_id((CHUNK, 128))
    t0 = jnp.concatenate([u0, low01[:8]], axis=0)
    t1 = jnp.concatenate([u1, low01[8:]], axis=0)
    t4 = jnp.concatenate([u4, low43[:8]], axis=0)
    keys = jnp.concatenate([u3, low43[8:]], axis=0)
    turned = jnp.concatenate([shared, pltpu.roll(shared[:8], 64, 1)], axis=0)
    t3 = jnp.where(lane < 32, pltpu.roll(keys, 32, 1), pltpu.roll(turned, 32, 1))
    t3 = jnp.where(lane < 96, t3, 0.0)
    extra = shared[8:]
    extra = jnp.concatenate([pltpu.roll(extra, 32, 1), pltpu.roll(extra, 16, 1), extra], axis=0)
    t2 = jnp.where(lane < 96, keys, jnp.where(lane < 112, extra, 0.0))
    return [t0, t1, t2, t3, t4]


def qkv_chunk(block, head, half):
    return 24 * block + 2 * head + half


def qkv_picks(d):
    heads = [3 * d + i for i in range(3)]
    picks = []
    for block in range(2):
        for half in range(2):
            picks += [qkv_chunk(block, h, half) for h in heads]
            picks.append(qkv_chunk(2, heads[2], half) if block == 0 else None)
    return picks + [qkv_chunk(2, h, half) for h in heads[:2] for half in range(2)]


def up_picks(d):
    return [3 * (GROUP * r + d) + j for r in range(ROWS) for j in range(3)]


def inverse_picks(per_device, count, tiles_each):
    back = [None] * count
    for d, picks in enumerate(per_device):
        for place, pick in enumerate(picks):
            if pick is not None:
                back[pick] = 4 * tiles_each * d + place
    return back


QKV_BACK = inverse_picks([qkv_picks(d) for d in range(GROUP)], 72, 5)
UP_BACK = inverse_picks([up_picks(d) for d in range(GROUP)], 96, 6)


def tables():
    half = HD // 2
    freq = np.float32(10000.0) ** (-np.arange(half, dtype=np.float32) / np.float32(half))
    angle = (np.arange(SEQ, dtype=np.float32)[:, None] * freq[None, :]).astype(np.float32)
    angle = angle.astype(np.float64)
    cosine, sine = np.ones((SEQ, 128), np.float32), np.zeros((SEQ, 128), np.float32)
    cosine[:, :96] = np.tile(np.cos(angle), (1, 3))
    sine[:, :96] = np.tile(np.sin(angle), (1, 3))
    return cosine, sine


def standardize(value):
    center = value - jnp.mean(value, axis=-1, keepdims=True)
    spread = jnp.mean(center * center, axis=-1, keepdims=True)
    scale = lax.rsqrt(spread + 1e-05)
    return center * scale, scale


def norm_back(grad, gain, normal, scale):
    part = grad * (1.0 + gain)
    inner = jnp.mean(part, axis=-1, keepdims=True)
    along = jnp.mean(part * normal, axis=-1, keepdims=True)
    return scale * (part - inner - normal * along)


def sublane_sum(value):
    return jnp.sum(value.reshape(value.shape[0] // 8, 8, value.shape[1]), axis=0)


SCRATCH = dict(
    hist=((SEQ, WIDTH), BF),
    cot=((OWN, WIDTH), BF),
    wq=((CHUNK, 3 * WIDTH), BF),
    wo=((CHUNK, WIDTH), BF),
    wu=((CHUNK, 4 * WIDTH), BF),
    cosine=((SEQ, 128), F32),
    sine=((SEQ, 128), F32),
    x_all=((GROUP, OWN, WIDTH), BF),
    c_all=((GROUP, OWN, WIDTH), BF),
    qp_s=((GROUP, 16, 896), BF),
    q_all=((ROWS * GROUP, 16, 896), BF),
    up_s=((GROUP, 16, 1152), BF),
    up_l=((GROUP, 16, 1152), BF),
    tmp=((BLOCK, WIDTH), F32),
    w_qkv=((WIDTH, PACK), BF),
    w_up=((WIDTH, WIDTH), BF),
    w_down=((WIDTH, WIDTH), BF),
    wo_l=((GROUP, 2, ROWS // 2, 16, 1152), BF),
    w_out=((WIDTH, WIDTH), BF),
    w_own=((256, WIDTH), BF),
    norms=((8, WIDTH), F32),
    normal=((SEQ, WIDTH), F32),
    h1=((SEQ, WIDTH), BF),
    qv=((SEQ, 256), BF),
    kk=((SEQ, 256), BF),
    v01=((SEQ, 128), BF),
    v_all=((SEQ, 256), BF),
    probs=((3, SEQ, SEQ), F32),
    o_l=((GROUP, 2, 384, 128), BF),
    ob=((SEQ, WIDTH), BF),
    y=((SEQ, WIDTH), F32),
    h2=((SEQ, WIDTH), BF),
    slope=((SEQ, WIDTH), F32),
    act=((SEQ, WIDTH), BF),
    dm=((SEQ, WIDTH), BF),
    g_down=((WIDTH, WIDTH), F32),
    g_up=((WIDTH, WIDTH), F32),
    g_out=((WIDTH, WIDTH), F32),
    g_qkv=((WIDTH, PACK), F32),
    du=((SEQ, WIDTH), BF),
    part=((SEQ, WIDTH), F32),
    part2=((SEQ, WIDTH), F32),
    dy=((OWN, WIDTH), F32),
    dyb=((GROUP, OWN, WIDTH), BF),
    dq=((SEQ, 256), F32),
    dk=((SEQ, 256), F32),
    dv=((SEQ, 256), F32),
    dqkv=((SEQ, PACK), BF),
    terms=((8, WIDTH), F32),
    terms2=((8, WIDTH), F32),
    t0=((8, WIDTH), F32),
    td=((4, 8, WIDTH), F32),
    ext=((ROWS, 16, 128), F32),
    u0=((8, 128), F32),
    u1=((8, 128), F32),
    uzd=((8, 8, 128), F32),
    fin=((16, 16, 896), BF),
    ps=((16, 16, 896), BF),
    q_sum=((GROUP, 16, 896), F32),
    a_up=((GROUP, 16, 1152), BF),
    f_down=((BLOCK, WIDTH), F32),
    f_up=((BLOCK, WIDTH), F32),
    f_out=((16, 1280), F32),
    b_up=((GROUP, 16, 1152), BF),
    gain_sum=((8, WIDTH), F32),
    shift_sum=((8, WIDTH), F32),
)
for _name, _rows, _cols in (
    ("down", BLOCK, WIDTH),
    ("up", BLOCK, WIDTH),
    ("out", 16, 1280),
):
    SCRATCH["st_" + _name] = ((8, _rows, _cols), BF)
    SCRATCH["xl_" + _name] = ((4, _rows, _cols), BF)
    SCRATCH["zl_" + _name] = ((3, _rows, _cols), BF)
    SCRATCH["nl_" + _name] = ((2, _rows, _cols), BF)
for _h in range(2):
    SCRATCH[f"st_qkv{_h}"] = ((6, 2, 16, 896), BF)
    SCRATCH[f"xl_qkv{_h}"] = ((4, 2, 16, 896), BF)
    for _name in ("cl", "zl"):
        SCRATCH[f"{_name}_qkv{_h}"] = ((2, 16, 896), BF)
for _name in ("mix", "mid", "in"):
    SCRATCH["gs_" + _name] = ((3, OWN, WIDTH), BF)
    SCRATCH["l1_" + _name] = ((2, OWN, WIDTH), BF)
    SCRATCH["l2_" + _name] = ((OWN, WIDTH), BF)
N_SENDS = 32
N_ARRIVALS = 110
N_IN = 12
N_OUT = 9
VMEM_MIB = 60


class Names:
    pass


def fused_kernel(*refs):
    (x_hbm, hist_hbm, cot_hbm, mask, wq_hbm, wo_hbm, wu_hbm, wd_hbm) = refs[:8]
    (nrm, dw, cosine_hbm, sine_hbm) = refs[8:N_IN]
    results, (ng_o, dg_o) = refs[N_IN : N_IN + N_OUT - 2], refs[N_IN + N_OUT - 2 : N_IN + N_OUT]
    s = Names()
    for name, ref in zip(SCRATCH, refs[N_IN + N_OUT :]):
        setattr(s, name, ref)
    send_sems, recv_sems, local_sems = refs[-3:]

    r, d = lax.axis_index("rows"), lax.axis_index("depth")
    z, x = lax.div(r, 2), lax.rem(r, 2)
    yy, c = lax.div(d, 2), lax.rem(d, 2)
    other_x, other_c, other_y = 1 - x, 1 - c, 1 - yy
    x_dev = (2 * z + other_x, d)
    z_two, z_mirror, z_near = lax.rem(z + 2, 4), 3 - z, z + 1 - 2 * lax.rem(z, 2)
    two_dev, mirror_dev, near_dev = ((2 * zk + x, d) for zk in (z_two, z_mirror, z_near))
    inside = lax.rem(z + 1, 4) >= 2
    outside = jnp.logical_not(inside)
    core_d, y_d, far_d = 2 * yy + other_c, 2 * other_y + c, 2 * other_y + other_c
    core_dev, y_dev, far_dev = (r, core_d), (r, y_d), (r, far_d)
    mates = ((core_d, core_dev), (y_d, y_dev), (far_d, far_dev))
    used = {"send": 0, "arrival": 0}
    send_groups = []

    def arrivals(count=1):
        used["arrival"] += count
        return used["arrival"] - count

    def sends(view, condition=None):
        used["send"] += 1
        send_groups.append((used["send"] - 1, view, condition))
        return used["send"] - 1

    def prepare(src, dst, device, arrival, group):
        return pltpu.make_async_remote_copy(
            src_ref=src,
            dst_ref=dst,
            send_sem=send_sems.at[group],
            recv_sem=recv_sems.at[arrival],
            device_id=device,
            device_id_type=MESH,
        )

    def copy_to(src, dst, device, arrival, group, condition=None):
        copy = prepare(src, dst, device, arrival, group)
        if condition is None:
            copy.start()
        else:
            pl.when(condition)(copy.start)

    def arrive(view, arrival):
        prepare(view, view, x_dev, arrival, 0).wait_recv()

    def rows_at(ref, index, size):
        return ref.at[pl.ds(pl.multiple_of(index * size, size), size)]

    def by_rows(count, step, body):
        def one(i, carry):
            body(pl.ds(pl.multiple_of(i * step, step), step))
            return carry

        lax.fori_loop(0, count // step, one, 0)

    barrier = pltpu.get_barrier_semaphore()
    partners = [x_dev, core_dev, y_dev, far_dev]
    partners += [
        (2 * zk + x, m) for zk in (z_two, z_mirror, z_near) for m in (d, core_d, y_d, far_d)
    ]
    for device in partners:
        pl.semaphore_signal(barrier, inc=1, device_id=device, device_id_type=MESH)

    hist, cot, wq, wo, wu, cosine, sine = s.hist, s.cot, s.wq, s.wo, s.wu, s.cosine, s.sine
    loads = {}
    for name, source, target in (
        ("wq", wq_hbm, wq),
        ("x", x_hbm, s.x_all.at[d]),
        ("wo", wo_hbm, wo),
        ("wu", wu_hbm, wu),
        ("wd", wd_hbm, rows_at(s.w_down, r, BLOCK)),
        ("cot", cot_hbm, cot),
        ("cosine", cosine_hbm, cosine),
        ("sine", sine_hbm, sine),
        ("hist", hist_hbm, hist),
    ):
        loads[name] = pltpu.make_async_copy(source, target, local_sems.at[len(loads)])
        loads[name].start()
    out_o, ig_o, hg_o, gq_o, go_o, gu_o, gd_o = results


    class Gather:
        def __init__(self, piece, pieces, cross=False):
            self.piece, self.pieces, self.cross = piece, pieces, cross
            self.group, self.inner = sends(pieces(6)), sends(pieces(2), inside)
            self.two, self.near, self.mirror, self.along_x = (arrivals() for _ in range(4))
            self.own_x = arrivals() if cross else self.along_x

        def copy(self, zk, xk, device, arrival, inner=False, condition=None):
            piece = self.piece(zk, xk)
            group = self.inner if inner else self.group
            copy_to(piece, piece, device, arrival, group, condition)

        def send_two(self):
            self.copy(z, x, two_dev, self.two)

        def send_mirror(self):
            self.copy(z, x, mirror_dev, self.mirror, True, inside)

        def send_near(self, where=None):
            condition = None if where is None else outside if where else inside
            self.copy(z, x, near_dev, self.near, condition=condition)

        def send_x(self, zk=z):
            self.copy(zk, x, x_dev, self.along_x)

        def send_own_x(self):
            self.copy(z, x, x_dev, self.own_x)

        def arrive_near(self):
            arrive(self.piece(z_near, x), self.near)

        def forward_near(self):
            self.arrive_near()
            if not self.cross:
                self.send_x(z_near)

        def forward_cross(self):
            arrive(self.piece(z, other_x), self.own_x)
            self.copy(z, other_x, near_dev, self.along_x)

        def pass_two(self):
            arrive(self.piece(z_two, x), self.two)
            self.copy(z_two, x, near_dev, self.mirror, True, inside)

        def forward_two(self):
            self.pass_two()
            self.send_x(z_two)

        def forward_mirror(self):
            arrive(self.piece(z_mirror, x), self.mirror)
            self.send_x(z_mirror)

        def finish(self):
            arrive(self.pieces(3 if self.cross else 4), self.along_x)

    class GroupGather:
        def __init__(self, slab, slabs, group=None):
            self.slab, self.slabs = slab, slabs
            self.group = sends(slabs(3)) if group is None else group
            self.from_y, self.others = arrivals(), arrivals()

        def send(self):
            mine = self.slab(d)
            copy_to(mine, mine, core_dev, self.others, self.group)
            copy_to(mine, mine, y_dev, self.from_y, self.group)

        def relay(self):
            slab = self.slab(y_d)
            arrive(slab, self.from_y)
            copy_to(slab, slab, core_dev, self.others, self.group)

        def finish(self):
            arrive(self.slabs(2), self.others)

    class RowSum:
        def __init__(self, name, total, block, step, cross):
            staged = getattr(s, "st_" + name)
            self.xs, self.zs, self.ns = (
                [staged.at[i + j] for j in range(n)] for i, n in ((0, 4), (4, 2), (6, 2))
            )
            self.xs = staged.at[pl.ds(0, 4)]
            self.xl, self.zl, self.nl = (getattr(s, p + name) for p in ("xl_", "zl_", "nl_"))
            self.total = total
            self.block, self.step, self.cross = block, step, cross
            self.count = self.total.shape[0]
            self.group = sends(staged.at[pl.ds(0, 7)])
            self.along_x = {k: arrivals() for k in ("mirror", "two", "own")}
            if not cross:
                self.along_x["near"] = arrivals()
            self.crossing, self.near, self.two, self.mirror, self.passing = (
                arrivals() for _ in range(5)
            )

        def stage(self, target, index, *extras):
            def one(at):
                value = self.block(index, at)
                for ref in extras:
                    value = value + ref[at, :].astype(F32)
                target[at, :] = value.astype(BF)

            by_rows(self.count, self.step, one)

        def send_x(self, name, zk, *extras):
            self.stage(self.xs.at[zk], 2 * zk + other_x, *extras)
            copy_to(self.xs.at[zk], self.xl.at[zk], x_dev, self.along_x[name], self.group)

        def arrive_x(self, name, zk):
            arrive(self.xl.at[zk], self.along_x[name])

        def send(self, early_near=False):
            self.send_x("mirror", z_mirror)
            if self.cross:
                self.send_crossing()
            self.send_x("two", z_two)
            if self.cross and early_near:
                self.send_near()
            if not self.cross:
                self.send_x("near", z_near)
                self.send_x("own", z)

        def send_crossing(self):
            self.stage(self.ns[0], 2 * z_near + other_x)
            copy_to(self.ns[0], self.nl.at[0], near_dev, self.crossing, self.group)

        def send_own(self):
            arrive(self.nl.at[0], self.crossing)
            self.send_x("own", z, self.nl.at[0])

        def send_mirror(self):
            self.arrive_x("mirror", z_mirror)
            self.stage(self.zs[0], 2 * z_mirror + x, self.xl.at[z_mirror])
            copy_to(self.zs[0], self.zl.at[0], mirror_dev, self.mirror, self.group, inside)
            copy_to(self.zs[0], self.zl.at[2], near_dev, self.passing, self.group, outside)

        def send_two_outside(self):
            @pl.when(outside)
            def _():
                self.arrive_x("two", z_two)
                self.stage(self.zs[1], 2 * z_two + x, self.xl.at[z_two])
                copy_to(self.zs[1], self.zl.at[1], two_dev, self.two, self.group)

        def send_two_inside(self):
            @pl.when(inside)
            def _():
                self.arrive_x("two", z_two)
                arrive(self.zl.at[2], self.passing)
                self.stage(self.zs[1], 2 * z_two + x, self.xl.at[z_two], self.zl.at[2])
                copy_to(self.zs[1], self.zl.at[1], two_dev, self.two, self.group)

        def send_near(self):
            extras = ()
            if not self.cross:
                self.arrive_x("near", z_near)
                extras = (self.xl.at[z_near],)
            self.stage(self.ns[1], 2 * z_near + x, *extras)
            copy_to(self.ns[1], self.nl.at[1], near_dev, self.near, self.group)

        def finish(self):
            self.arrive_x("own", z)
            arrive(self.zl.at[1], self.two)
            arrive(self.nl.at[1], self.near)

            def add(at):
                self.total[at, :] = (
                    self.block(r, at)
                    + self.xl[z, at, :].astype(F32)
                    + self.zl[1, at, :].astype(F32)
                    + self.nl[1, at, :].astype(F32)
                )

            by_rows(self.count, self.step, add)

            @pl.when(inside)
            def _():
                arrive(self.zl.at[0], self.mirror)

                def add_mirror(at):
                    self.total[at, :] += self.zl[0, at, :].astype(F32)

                by_rows(self.count, self.step, add_mirror)

    class SpreadSum:
        def __init__(self, half, shared):
            staged = getattr(s, f"st_qkv{half}")
            self.xs, self.cs, self.zs = staged.at[pl.ds(0, 4)], staged.at[4], staged.at[5]
            self.xl, self.cl, self.zl = (getattr(s, f"{p}_qkv{half}") for p in ("xl", "cl", "zl"))
            self.half = half
            self.group = sends(staged.at[pl.ds(0, 4)])
            self.inner, self.outer, self.last, self.final, self.final_mirror = shared
            self.along_x = {k: arrivals() for k in ("mirror", "two", "near", "own")}
            self.crossing, self.passing = arrivals(), arrivals()

        def value(self, index, *extras):
            rows = BLOCK // 2
            start_row = pl.multiple_of((2 * index + self.half) * rows, rows)
            value = s.g_qkv[pl.ds(start_row, rows), :]
            pieces = [fold_qkv(tiles_of(value[CHUNK * j : CHUNK * (j + 1)])) for j in range(2)]
            pieces = [jnp.concatenate(tiles, axis=1) for tiles in pieces]
            for extra in extras:
                pieces = [piece + extra[j].astype(F32) for j, piece in enumerate(pieces)]
            return pieces

        def put(self, target, pieces):
            for j, piece in enumerate(pieces):
                target[j] = piece.astype(BF)

        def send_x(self, name, zk, *extras):
            self.put(self.xs.at[zk], self.value(2 * zk + other_x, *extras))
            copy_to(self.xs.at[zk], self.xl.at[zk], x_dev, self.along_x[name], self.group)

        def arrive_x(self, name, zk):
            arrive(self.xl.at[zk], self.along_x[name])

        def send_crossing(self):
            @pl.when(inside)
            def _():
                self.put(self.cs, self.value(2 * z_near + other_x))
                copy_to(self.cs, self.cl, near_dev, self.crossing, self.group)

        def send_third(self):
            pl.when(inside)(lambda: self.send_x("own", z))
            pl.when(outside)(lambda: self.send_x("near", z_near))

        def send_own_outside(self):
            @pl.when(outside)
            def _():
                arrive(self.cl, self.crossing)
                self.send_x("own", z, self.cl[...])

        def deliver(self, slot, zk, value):
            for j in range(2):
                to = 2 * self.half + j
                at = 8 * self.half + 2 * slot + j
                s.ps[at] = value[j].astype(BF)
                copy_to(
                    s.ps.at[at],
                    s.fin.at[GROUP * slot + d],
                    (2 * zk + x, to),
                    self.final_mirror if slot == 2 else self.final,
                    self.inner if slot == 2 else self.last,
                    inside if slot == 2 else d != to if slot == 3 else None,
                )
                if slot == 3:

                    @pl.when(d == to)
                    def _(at=at):
                        s.fin[GROUP * slot + d] = s.ps[at]

        def send_mirror(self):
            self.arrive_x("mirror", z_mirror)
            value = self.value(2 * z_mirror + x, self.xl[z_mirror])
            self.deliver(2, z_mirror, value)
            self.put(self.zs, value)
            copy_to(self.zs, self.zl, near_dev, self.passing, self.outer, outside)

        def send_two(self):
            self.arrive_x("two", z_two)

            @pl.when(outside)
            def _():
                self.zl[...] = jnp.zeros((2, 16, 896), BF)

            pl.when(inside)(lambda: arrive(self.zl, self.passing))
            self.deliver(0, z_two, self.value(2 * z_two + x, self.xl[z_two], self.zl[...]))

        def send_near(self):
            pl.when(inside)(lambda: self.deliver(1, z_near, self.value(2 * z_near + x)))

            @pl.when(outside)
            def _():
                self.arrive_x("near", z_near)
                self.deliver(1, z_near, self.value(2 * z_near + x, self.xl[z_near]))

        def keep_own(self):
            self.arrive_x("own", z)
            self.deliver(3, z, self.value(r, self.xl[z]))

    class GroupSum:
        def __init__(self, name, source, parts=1):
            staged = getattr(s, "gs_" + name)
            self.s1, self.s2 = staged.at[pl.ds(0, 2)], staged.at[2]
            self.l1, self.l2 = (getattr(s, p + name) for p in ("l1_", "l2_"))
            self.source, self.parts, self.size = source, parts, OWN // parts
            self.group = sends(staged)
            self.first, self.second = arrivals(parts), arrivals(parts)
            self.kept = arrivals()

        def block(self, index, at):
            return self.source[pl.ds(pl.multiple_of(index * OWN + at.start, at.size), at.size), :]

        def part(self, i):
            return pl.ds(self.size * i, self.size)

        def over(self, i, body):
            def shifted(at):
                body(pl.ds(pl.multiple_of(self.size * i + at.start, at.size), at.size))

            by_rows(self.size, 32, shifted)

        def send(self, i=0):
            for j, yj in enumerate((other_y, yy)):

                def stage(at):
                    self.s1[j, at, :] = self.block(2 * yj + other_c, at).astype(BF)

                self.over(i, stage)
                copy_to(
                    self.s1.at[j, self.part(i)],
                    self.l1.at[j, self.part(i)],
                    core_dev,
                    self.kept if j else self.first + i,
                    self.group,
                )

        def middle(self, i=0):
            arrive(self.l1.at[0, self.part(i)], self.first + i)

            def stage(at):
                value = self.block(2 * other_y + c, at) + self.l1[0, at, :].astype(F32)
                self.s2[at, :] = value.astype(BF)

            self.over(i, stage)
            copy_to(
                self.s2.at[self.part(i)],
                self.l2.at[self.part(i)],
                y_dev,
                self.second + i,
                self.group,
            )

        def wait(self, i=0):
            if i == 0:
                arrive(self.l1.at[1], self.kept)
            arrive(self.l2.at[self.part(i)], self.second + i)

        def value(self, at):
            return (
                self.block(d, at)
                + self.l1[1, at, :].astype(F32)
                + self.l2[at, :].astype(F32)
            )

    class PieceGather:
        def __init__(self):
            self.group = sends(s.q_all.at[pl.ds(0, 27)])
            self.inner = sends(s.q_all.at[pl.ds(0, 8)], inside)
            self.own, self.two, self.near, self.mirror = (arrivals(2) for _ in range(4))
            self.along_x = {k: arrivals() for k in ("own", "near", "two", "mirror")}

        def fan(self, zk, arrival, group, condition=None):
            for i, m in enumerate((d, core_d, y_d, far_d)):
                if i == 0 and zk is z:
                    continue
                copy_to(
                    s.qp_s.at[m],
                    s.q_all.at[GROUP * r + d],
                    (2 * zk + x, m),
                    arrival + i // 2,
                    group,
                    condition,
                )

        def slab(self, zk, xk, h):
            first = GROUP * (2 * zk + xk) + 2 * (other_y if h else yy)
            return s.q_all.at[pl.ds(pl.multiple_of(first, 2), 2)]

        def send(self):
            self.fan(z, self.own, self.group)
            self.fan(z_two, self.two, self.group)
            self.fan(z_near, self.near, self.group)
            self.fan(z_mirror, self.mirror, self.inner, inside)

        def send_x(self, name, zk, h):
            slab = self.slab(zk, x, h)
            copy_to(slab, slab, x_dev, self.along_x[name], self.group)

        def forward_own(self, h):
            if h:
                arrive(self.slab(z, x, h), self.own + h)
            else:
                arrive(s.q_all.at[GROUP * r + core_d], self.own)
            self.send_x("own", z, h)

        def forward_near(self, h):
            arrive(self.slab(z_near, x, h), self.near + h)
            self.send_x("near", z_near, h)

        def forward_two(self, h):
            slab = self.slab(z_two, x, h)
            arrive(slab, self.two + h)
            copy_to(slab, slab, near_dev, self.mirror + h, self.inner, inside)
            self.send_x("two", z_two, h)

        def forward_mirror(self, h):
            arrive(self.slab(z_mirror, x, h), self.mirror + h)
            self.send_x("mirror", z_mirror, h)

        def finish(self, name, zk):
            first = pl.multiple_of(GROUP * (2 * zk + other_x), GROUP)
            arrive(s.q_all.at[pl.ds(first, GROUP)], self.along_x[name])

    def assemble(landing, count, target, row):
        for k in range(GROUP):
            landed = landing[k][...] if isinstance(landing, list) else landing[k]
            tiles = [t.astype(F32) for t in tiles_of(landed)]
            for t, tile in enumerate(unfold_qkv(tiles) if count == 5 else unfold(tiles, count)):
                s.tmp[CHUNK * k : CHUNK * (k + 1), 128 * t : 128 * (t + 1)] = tile
        rows_at(target, row, BLOCK)[...] = s.tmp[:, : 128 * count].astype(BF)

    def assemble_qkv(row):
        assemble([s.q_all.at[GROUP * row + k] for k in range(GROUP)], 5, s.w_qkv, row)

    lane = lane_id((CHUNK, 128))
    eye = row_id((CHUNK, CHUNK)) == lane_id((CHUNK, CHUNK))
    extra = jnp.zeros((CHUNK, 128), F32)
    for k in range(4):
        column = jnp.sum(jnp.where(eye, nrm[k : k + 1, :], 0.0), axis=1, keepdims=True)
        high = column.astype(BF).astype(F32)
        extra = jnp.where(lane == 96 + k, high, extra)
        extra = jnp.where(lane == 100 + k, column - high, extra)
    mask_row = mask[...].astype(F32)
    ones = jnp.sum(mask_row, axis=1, keepdims=True)
    extra = jnp.where((lane == 104) & (row_id((CHUNK, 128)) == 0), ones, extra)

    loads["wq"].wait()
    wq_tiles = tiles_of(wq[...].astype(F32))
    for k in range(GROUP):
        tiles = permute_chunks(wq_tiles, qkv_picks(k))
        tiles[2] = tiles[2] + extra
        for t, tile in enumerate(fold_qkv(tiles)):
            s.qp_s[k, :, 128 * t : 128 * (t + 1)] = tile.astype(BF)
    s.q_all[GROUP * r + d] = s.qp_s[d]
    pl.semaphore_wait(barrier, len(partners))

    qkv_gather = PieceGather()
    qkv_gather.send()
    loads["wd"].wait()
    up_gather = Gather(
        lambda zk, xk: rows_at(s.w_up, 2 * zk + xk, BLOCK),
        lambda n: s.w_up.at[pl.ds(0, n * BLOCK)],
        cross=True,
    )
    downs = [
        Gather(
            lambda zk, xk, h=h: rows_at(s.w_down, 2 * (2 * zk + xk) + h, BLOCK // 2),
            lambda n: s.w_down.at[pl.ds(0, n * BLOCK // 2)],
            cross=h == 0,
        )
        for h in range(2)
    ]
    loads["wo"].wait()
    for t, tile in enumerate(fold(tiles_of(wo[...].astype(F32)))):
        s.wo_l[d, x, z, :, 128 * t : 128 * (t + 1)] = tile.astype(BF)
    out_gather = Gather(
        lambda zk, xk: s.wo_l.at[d, xk, zk],
        lambda n: s.wo_l.at[0, 0, pl.ds(0, n)] if n <= 4 else s.wo_l.at[0, :, pl.ds(0, n // 2)],
    )
    out_gather.send_two()
    out_gather.send_mirror()
    out_gather.send_near()
    out_gather.send_own_x()
    for half in downs:
        half.send_own_x()
    loads["wu"].wait()
    wu_tiles = tiles_of(wu[...].astype(F32))
    for k in range(GROUP):
        for t, tile in enumerate(fold(permute_chunks(wu_tiles, up_picks(k)))):
            s.up_s[k, :, 128 * t : 128 * (t + 1)] = tile.astype(BF)
    s.up_l[d] = s.up_s[d]
    up_arrival, up_group = arrivals(), sends(s.up_s.at[pl.ds(0, 3)])
    for m, device in mates:
        copy_to(s.up_s.at[m], s.up_l.at[d], device, up_arrival, up_group)
    loads["x"].wait()
    x_gather = GroupGather(lambda i: s.x_all.at[i], lambda n: s.x_all.at[pl.ds(0, n)])
    x_gather.send()
    diagonal = jnp.where(
        row_id((OWN, OWN)) == lane_id((OWN, OWN)), jnp.broadcast_to(mask_row, (OWN, OWN)), 0.0
    )
    loads["cot"].wait()
    s.c_all[d] = dot(diagonal.astype(BF), cot[...]).astype(BF)
    c_gather = GroupGather(lambda i: s.c_all.at[i], lambda n: s.c_all.at[pl.ds(0, n)])
    c_gather.send()

    def normalize(i):
        def one(at):
            normal, _ = standardize(s.x_all[i, at, :].astype(F32))
            s.normal[pl.ds(pl.multiple_of(OWN * i + at.start, at.size), at.size), :] = normal

        by_rows(OWN, 64, one)

    qkv_gather.forward_own(0)
    qkv_gather.forward_own(1)
    qkv_gather.forward_near(0)
    assemble_qkv(r)
    qkv_gather.forward_two(0)
    qkv_gather.forward_near(1)
    assemble_qkv(2 * z_near + x)
    qkv_gather.forward_two(1)
    out_gather.pass_two()
    assemble_qkv(2 * z_two + x)
    arrive(s.up_l.at[pl.ds(0, 3)], up_arrival)
    assemble(s.up_l, 6, s.w_up, r)
    up_gather.send_two()
    up_gather.send_near(True)
    qkv_gather.forward_mirror(0)
    x_gather.relay()
    qkv_gather.forward_mirror(1)
    up_gather.send_near(False)
    up_gather.send_mirror()
    for half in downs:
        half.send_two()
    downs[1].send_near()
    downs[0].send_near(True)
    out_gather.send_x(z_two)
    out_gather.forward_near()
    out_gather.forward_mirror()
    up_gather.send_own_x()
    columns = [
        GroupGather(lambda i, xk=xk: s.wo_l.at[i, xk], lambda n: s.wo_l.at[pl.ds(0, n), 0])
        for xk in (x, other_x)
    ]
    columns[0].send()
    assemble_qkv(2 * z_mirror + x)
    x_gather.finish()
    for i in range(GROUP):
        normalize(i)
    for name, zk in (("own", z), ("near", z_near), ("two", z_two)):
        qkv_gather.finish(name, zk)
        assemble_qkv(2 * zk + other_x)
    c_gather.relay()
    qkv_gather.finish("mirror", z_mirror)
    assemble_qkv(2 * z_mirror + other_x)

    lane = lane_id((8, 128))
    row = row_id((8, 128))
    pick = jnp.where((lane == 96 + row) | (lane == 100 + row), 1.0, 0.0)
    pick = jnp.where(row < 4, pick, jnp.where((row == 4) & (lane == 104), 1.0, 0.0))
    s.norms[...] = dot(pick.astype(BF), s.w_qkv[:, 256:384], 1, 1)
    total = jnp.sum(s.norms[4:5, :], axis=1, keepdims=True)
    loss_scale = (SEQ * ROWS) / total
    own_weight = dw[d]
    last_weight = dw[GROUP]

    def first_norm(at):
        value = s.normal[at, :] * (1.0 + s.norms[0:1, :]) + s.norms[1:2, :]
        s.h1[at, :] = value.astype(BF)

    by_rows(SEQ, 64, first_norm)

    def project(at):
        value = dot(s.h1[at, :], s.w_qkv[...])
        co, si = cosine[at, :], sine[at, :]
        for left, target in ((0, s.qv), (256, s.kk)):
            a, b = value[:, left : left + 128], value[:, left + 128 : left + 256]
            target[at, :128] = (a * co - b * si).astype(BF)
            target[at, 128:] = (b * co + a * si).astype(BF)
        s.v01[at, :] = value[:, 512:].astype(BF)

    loads["cosine"].wait()
    loads["sine"].wait()
    by_rows(SEQ, 256, project)

    lane2 = lax.div(lax.rem(lane_id((1, 256)), 128), jnp.int32(32))
    head_mask = [jnp.where(lane2 == h, 1.0, 0.0).astype(BF) for h in range(3)]
    tail_mask = jnp.where(lane2 == 3, 1.0, 0.0).astype(BF)
    half_id = lax.div(lane_id((1, 128)), jnp.int32(64))
    half_mask = [jnp.where(half_id == h, 1.0, 0.0).astype(BF) for h in range(2)]
    root = HD**-0.5
    o_gathers = [
        GroupGather(lambda i, b=b: s.o_l.at[i, b], lambda n: s.o_l.at[pl.ds(0, n), 0])
        for b in range(2)
    ]

    def attend(b):
        rows = slice(QBLOCK * b, QBLOCK * (b + 1))
        keys = QBLOCK * (b + 1)
        query = s.qv[rows, :]
        allowed = row_id((QBLOCK, keys)) + QBLOCK * b >= lane_id((QBLOCK, keys))
        first = jnp.zeros((QBLOCK, 128), F32)
        third = None
        for h in range(3):
            scores = dot(query * head_mask[h], s.kk[:keys, :], 1, 1) * root
            scores = jnp.where(allowed, scores, -1e30)
            raised = jnp.exp(scores - jnp.max(scores, axis=1, keepdims=True))
            probs = raised * (1.0 / jnp.sum(raised, axis=1, keepdims=True))
            s.probs[h, rows, :keys] = probs
            if h < 2:
                first = first + dot(probs.astype(BF), s.v01[:keys, :] * half_mask[h])
            else:
                third = dot(probs.astype(BF), s.qv[:keys, :])
            if b == 1 and h == 0:
                up_gather.forward_two()
                downs[0].send_near(False)
                for half in downs:
                    half.send_mirror()
            if b == 1 and h == 1:
                out_gather.finish()
                columns[1].send()
        s.o_l[d, b, :QBLOCK, :] = first.astype(BF)
        lane = lane_id((QBLOCK, 128))
        third = jnp.where(
            lane < 32, pltpu.roll(third[:, :128], 32, 1), pltpu.roll(third[:, 128:], 64, 1)
        )
        lane = lane_id((OWN, 128))
        third = jnp.where(lane < 64, third[:OWN], pltpu.roll(third[OWN:], 64, 1))
        s.o_l[d, b, QBLOCK:, :] = third.astype(BF)
        o_gathers[b].send()

    attend(1)
    columns[0].relay()
    attend(0)
    for h in range(3):
        s.probs[h, :QBLOCK, QBLOCK:] = jnp.zeros((QBLOCK, QBLOCK), F32)
    s.v_all[:, :128] = s.v01[...]

    def third_values(at):
        lane = lane_id((64, 128))
        low = pltpu.roll(s.qv[at, :128].astype(F32), 32, 1)
        high = pltpu.roll(s.qv[at, 128:].astype(F32), 64, 1)
        both = jnp.where(lane < 32, low, jnp.where(lane < 64, high, 0.0))
        s.v_all[at, 128:] = both.astype(BF)

    by_rows(SEQ, 64, third_values)
    up_gather.forward_cross()
    columns[1].relay()
    downs[1].forward_near()
    up_gather.forward_mirror()
    for column in columns:
        column.finish()
    for k in range(GROUP):
        for i in range(ROWS):
            tiles = [t.astype(F32) for t in tiles_of(s.wo_l[k, i % 2, i // 2])]
            at = CHUNK * (GROUP * i + k)
            for t, tile in enumerate(unfold(tiles, 6)):
                s.g_out[at : at + CHUNK, 128 * t : 128 * (t + 1)] = tile

    def out_place(head):
        k, h = divmod(head, 3)
        return 128 * k + 64 * h if h < 2 else 512 + 64 * k

    for head in range(HEADS):
        at = out_place(head)
        s.w_out[at : at + 64, :] = s.g_out[64 * head : 64 * head + 64, :].astype(BF)
    s.w_own[:128, :] = rows_at(s.w_out.at[pl.ds(0, 512)], d, 128)[...]
    s.w_own[128:192, :] = rows_at(s.w_out.at[pl.ds(512, 256)], d, 64)[...]
    s.w_own[192:, :] = jnp.zeros((64, WIDTH), BF)
    downs[0].forward_two()
    o_gathers[1].relay()
    c_gather.finish()

    loads["hist"].wait()
    s.terms[...] = jnp.zeros((8, WIDTH), F32)
    for i in range(GROUP):

        def loss_rows(at, i=i):
            here = pl.ds(pl.multiple_of(OWN * i + at.start, at.size), at.size)
            grad = s.c_all[i, at, :].astype(F32) * loss_scale
            s.dm[here, :] = (last_weight * grad).astype(BF)
            hg_o[here, :] = (own_weight * grad).astype(BF)
            s.terms[...] += sublane_sum(grad * hist[here, :].astype(F32))

        by_rows(OWN, 32, loss_rows)

    downs[1].forward_two()
    downs[0].forward_cross()
    for b in (1, 0):
        if b == 0:
            o_gathers[0].relay()
            downs[0].forward_mirror()
        o_gathers[b].finish()
        rows = slice(QBLOCK * b, QBLOCK * (b + 1))
        thirds = []
        for k in range(GROUP):
            s.ob[rows, 128 * k : 128 * (k + 1)] = s.o_l[k, b, :QBLOCK, :]
            thirds.append(s.o_l[k, b, QBLOCK:, :].astype(F32))
        lane = lane_id((OWN, 128))
        for p in range(2):
            even, odd = thirds[2 * p], thirds[2 * p + 1]
            top = jnp.where(lane < 64, even, pltpu.roll(odd, 64, 1))
            low = jnp.where(lane < 64, pltpu.roll(even, 64, 1), odd)
            cols = slice(512 + 128 * p, 640 + 128 * p)
            s.ob[QBLOCK * b : QBLOCK * b + OWN, cols] = top.astype(BF)
            s.ob[QBLOCK * b + OWN : QBLOCK * (b + 1), cols] = low.astype(BF)
        s.y[rows, :] = dot(s.ob[rows, :], s.w_out[...])
        for i in (2 * b, 2 * b + 1):

            def second_norm(at, i=i):
                here = pl.ds(pl.multiple_of(OWN * i + at.start, at.size), at.size)
                value = s.y[here, :] + s.x_all[i, at, :].astype(F32)
                s.y[here, :] = value
                normal, _ = standardize(value)
                value = normal * (1.0 + s.norms[2:3, :]) + s.norms[3:4, :]
                s.h2[here, :] = value.astype(BF)

            by_rows(OWN, 64, second_norm)

    downs[1].forward_mirror()
    up_gather.arrive_near()
    up_gather.finish()

    def widen(at):
        s.part[at, :] = dot(s.h2[at, :], s.w_up[...])

    by_rows(SEQ, 256, widen)

    rate = 0.7978845608028654

    def gate(at):
        u = s.part[at, :]
        bend = jnp.tanh(rate * (u + 0.044715 * u * u * u))
        s.act[at, :] = (0.5 * u * (1.0 + bend)).astype(BF)
        s.slope[at, :] = bend

    by_rows(SEQ, 32, gate)

    def gate_slope(at):
        u, bend = s.part[at, :], s.slope[at, :]
        inner = rate * (1.0 + 3 * 0.044715 * u * u)
        s.slope[at, :] = 0.5 * (1.0 + bend) + 0.5 * u * (1.0 - bend * bend) * inner

    def block_of(ref, shift=0):
        def block(index, at):
            start = pl.multiple_of(index * BLOCK + shift + at.start, at.size)
            return ref[pl.ds(start, at.size), :]

        return block

    for i in range(3):
        cols = slice(QBLOCK * i, QBLOCK * (i + 1))
        s.g_down[cols, :] = dot(s.act[:, cols], s.dm[...], 0, 0)
    down_sum = RowSum("down", s.f_down, block_of(s.g_down), 16, True)
    down_sum.send(early_near=True)
    by_rows(SEQ, 32, gate_slope)
    downs[0].arrive_near()
    for half in downs:
        half.finish()

    mid_sum = GroupSum("mid", s.part, 4)

    def quarter(ref, i, size=32):
        return jnp.concatenate(
            [ref[OWN * j + 32 * i : OWN * j + 32 * i + size, :] for j in range(GROUP)], axis=0
        )

    def put_quarter(ref, i, value, size=32):
        for j in range(GROUP):
            ref[OWN * j + 32 * i : OWN * j + 32 * i + size, :] = value[size * j : size * (j + 1)]

    for i in (0, 2):
        value = dot(quarter(s.dm, i, 64), s.w_down[...], 1, 1)
        value = (value * quarter(s.slope, i, 64)).astype(BF)
        put_quarter(s.du, i, value, 64)
        put_quarter(s.part, i, dot(value, s.w_up[...], 1, 1), 64)
        mid_sum.send(i)
        mid_sum.send(i + 1)
    for i in range(3):
        mid_sum.middle(i)
    down_sum.send_mirror()
    mid_sum.middle(3)
    down_sum.send_own()

    def up_part(i):
        cols = slice(QBLOCK * i, QBLOCK * (i + 1))
        s.g_up[cols, :] = dot(s.h2[:, cols], s.du[...], 0, 0)

    up_part(0)
    s.terms2[...] = jnp.zeros((8, WIDTH), F32)
    s.t0[...] = jnp.zeros((8, WIDTH), F32)

    def second_norm_back(at):
        here = pl.ds(pl.multiple_of(OWN * d + at.start, at.size), at.size)
        grad = mid_sum.value(at)
        value = s.y[here, :]
        normal, scale = standardize(value)
        loss = s.c_all[d, at, :].astype(F32) * loss_scale
        back = last_weight * loss + norm_back(grad, s.norms[2:3, :], normal, scale)
        s.dy[at, :] = back
        s.dyb[d, at, :] = back.astype(BF)
        s.t0[2:3, :] += jnp.sum(grad * normal, axis=0, keepdims=True)
        s.t0[3:4, :] += jnp.sum(grad, axis=0, keepdims=True)
        s.terms2[...] += sublane_sum(loss * value)

    up_sum = RowSum("up", s.f_up, block_of(s.g_up), 16, True)
    dy_gathers = []
    dy_group = sends(s.dyb.at[pl.ds(0, 3)])
    for i in range(4):
        mid_sum.wait(i)
        mid_sum.over(i, second_norm_back)
        dy_gathers.append(
            GroupGather(
                lambda j, i=i: s.dyb.at[j, mid_sum.part(i)],
                lambda n: s.dyb.at[pl.ds(0, n), mid_sum.part(0)],
                dy_group,
            )
        )
        dy_gathers[i].send()
        if i < 2:
            up_part(i + 1)
        if i == 2:
            up_sum.send()

    def block_out(at):
        value = dot(s.act[at, :], s.w_down[...])
        s.part2[at, :] = value

    by_rows(SEQ, 256, block_out)
    def mix_quarter(i):
        def mix(at):
            here = pl.ds(pl.multiple_of(OWN * i + at.start, at.size), at.size)
            value = s.part2[here, :]
            loss = s.c_all[i, at, :].astype(F32) * loss_scale
            s.terms2[...] += sublane_sum(loss * value)
            s.part2[here, :] = own_weight * hist[here, :].astype(F32) + last_weight * value

        by_rows(OWN, 32, mix)

    down_sum.send_two_outside()
    dy_gathers[0].relay()
    mix_quarter(0)
    mix_quarter(1)
    dy_gathers[1].relay()
    mix_quarter(2)
    mix_quarter(3)
    mix_sum = GroupSum("mix", s.part2)
    mix_sum.send()
    lane = lane_id((8, 128))
    own_term = jnp.sum(jnp.sum(s.terms[...], axis=0, keepdims=True), axis=1, keepdims=True)
    last_term = jnp.sum(jnp.sum(s.terms2[...], axis=0, keepdims=True), axis=1, keepdims=True)
    s.u0[...] = jnp.where(lane == d, own_term, jnp.where(lane == GROUP, last_term, 0.0))
    depth_x, depth_z, depth_d = (arrivals() for _ in range(3))
    depth_group = sends(s.uzd.at[pl.ds(0, 7)])
    copy_to(s.u0, s.u1, x_dev, depth_x, depth_group)
    down_sum.send_two_inside()

    head_scale = [jnp.where(lane2 == h, root, 0.0) for h in range(3)]
    lane = lax.div(lane_id((1, 256)), jnp.int32(64))
    head_lanes = [jnp.where(lane == h, 1.0, 0.0).astype(BF) for h in range(3)]
    for i in range(4):
        dy_gathers[i].finish()
        rows = s.dyb[:, 32 * i : 32 * (i + 1), :].reshape(OWN, WIDTH)
        grad = dot(rows, s.w_own[...], 1, 1).astype(BF)
        grad = jnp.concatenate([grad * m for m in head_lanes], axis=0)
        probs = jnp.concatenate([quarter(s.probs.at[h], i) for h in range(3)], axis=0)
        dp = dot(grad, s.v_all[...], 1, 1)
        delta = jnp.sum(dp * probs, axis=1, keepdims=True)
        ds = (probs * (dp - delta)).astype(BF)
        query = quarter(s.qv, i)
        query = jnp.concatenate([query * m for m in head_mask], axis=0)
        dk = dot(ds, query, 0, 0) * root
        dv = dot(probs.astype(BF), grad, 0, 0)
        if i == 0:
            s.dk[...] = dk
            s.dv[...] = dv
        else:
            s.dk[...] += dk
            s.dv[...] += dv
        dq = dot(ds, s.kk[...])
        dq = sum(dq[OWN * h : OWN * (h + 1)] * head_scale[h] for h in range(3))
        put_quarter(s.dq, i, dq)
        if i < 2:
            dy_gathers[i + 2].relay()
        if i == 1:
            up_sum.send_mirror()
            up_sum.send_own()
            mix_sum.middle()

    def turn_back(at):
        co, si = cosine[at, :], sine[at, :]
        lane = lane_id((64, 128))
        for left, source in ((0, s.dq), (256, s.dk)):
            a, b = source[at, :128], source[at, 128:]
            first, second = a * co + b * si, b * co - a * si
            if left == 0:
                third = s.dv[at, 128:]
                first = jnp.where(lane < 96, first, pltpu.roll(third, 96, 1))
                second = jnp.where(lane < 96, second, pltpu.roll(third, 64, 1))
            s.dqkv[at, left : left + 128] = first.astype(BF)
            s.dqkv[at, left + 128 : left + 256] = second.astype(BF)
        s.dqkv[at, 512:] = s.dv[at, :128].astype(BF)

    by_rows(SEQ, 64, turn_back)
    up_sum.send_two_outside()
    for i in range(3):
        cols = slice(QBLOCK * i, QBLOCK * (i + 1))
        s.g_qkv[cols, :] = dot(s.h1[:, cols], s.dqkv[...], 0, 0)
    shared = (
        sends(s.fin.at[pl.ds(0, 4)], inside),
        sends(s.st_qkv0.at[pl.ds(0, 2)], outside),
        sends(s.fin.at[pl.ds(0, 11)]),
        arrivals(),
        arrivals(),
    )
    sums = [SpreadSum(h, shared) for h in range(2)]
    for one in sums:
        one.send_x("mirror", z_mirror)
        one.send_crossing()
    for one in sums:
        one.send_x("two", z_two)
    for one in sums:
        one.send_third()
    arrive(s.u1, depth_x)
    s.uzd[z] = s.u0[...] + s.u1[...]
    for device in (two_dev, mirror_dev, near_dev):
        copy_to(s.uzd.at[z], s.uzd.at[z], device, depth_z, depth_group)

    def first_back(at):
        s.part[at, :] = dot(s.dqkv[at, :], s.w_qkv[...], 1, 1)

    by_rows(SEQ, 256, first_back)
    in_sum = GroupSum("in", s.part)
    in_sum.send()
    up_sum.send_two_inside()
    s.gain_sum[...] = jnp.zeros((8, WIDTH), F32)
    s.shift_sum[...] = jnp.zeros((8, WIDTH), F32)

    def first_norm_sums(at):
        grad = s.part[at, :]
        s.gain_sum[...] += sublane_sum(grad * s.normal[at, :])
        s.shift_sum[...] += sublane_sum(grad)

    by_rows(SEQ, 32, first_norm_sums)
    s.t0[0:1, :] = jnp.sum(s.gain_sum[...], axis=0, keepdims=True)
    s.t0[1:2, :] = jnp.sum(s.shift_sum[...], axis=0, keepdims=True)
    s.td[d] = s.t0[...]
    norm_arrival, norm_group = arrivals(), sends(s.td.at[pl.ds(0, 3)])
    for m, device in mates:
        copy_to(s.td.at[d], s.td.at[d], device, norm_arrival, norm_group)
    in_sum.middle()
    for p in range(3):
        cols = slice(QBLOCK * p, QBLOCK * (p + 1))
        value = dot(s.ob[:, cols], s.dyb[...].reshape(SEQ, WIDTH), 0, 0)
        for i in range(4):
            place = QBLOCK * p + 64 * i
            for head in range(HEADS):
                if out_place(head) == place:
                    s.g_out[64 * head : 64 * head + 64, :] = value[64 * i : 64 * i + 64]

    for one in sums:
        one.send_mirror()
    up_sum.send_near()
    arrive(s.td.at[pl.ds(0, 3)], norm_arrival)
    value = (s.td[0] + s.td[1]) + (s.td[2] + s.td[3])
    value = pltpu.roll(value, lax.rem(WIDTH - CHUNK * d, WIDTH), 1)
    for i in range(ROWS):
        shift = (WIDTH - BLOCK * i) % WIDTH
        shifted = pltpu.roll(value, shift, 1) if shift else value
        s.ext[i] = jnp.concatenate([shifted[:, :128], jnp.zeros((8, 128), F32)], axis=0)

    def out_block(index, at):
        start_row = pl.multiple_of((GROUP * index + d) * CHUNK, 8)
        tiles = tiles_of(s.g_out[pl.ds(start_row, CHUNK), :])
        return jnp.concatenate(fold(tiles) + [s.ext[index]], axis=1)

    out_sum = RowSum("out", s.f_out, out_block, 16, False)
    out_sum.send_x("mirror", z_mirror)
    out_sum.send_x("two", z_two)
    for one in sums:
        one.send_own_outside()
    out_sum.send_x("near", z_near)
    out_sum.send_x("own", z)

    down_sum.finish()
    gd_o[...] = s.f_down[...]
    def spread(total, staged, landing):
        arrival, group = arrivals(), sends(staged.at[pl.ds(0, 3)])
        for m, device in mates:
            rows = total[pl.ds(pl.multiple_of(CHUNK * m, CHUNK), CHUNK), :]
            for t, tile in enumerate(fold(tiles_of(rows))):
                staged[m, :, 128 * t : 128 * (t + 1)] = tile.astype(BF)
            copy_to(staged.at[m], landing.at[d], device, arrival, group)
        rows = total[pl.ds(pl.multiple_of(CHUNK * d, CHUNK), CHUNK), :]
        for t, tile in enumerate(fold(tiles_of(rows))):
            landing[d, :, 128 * t : 128 * (t + 1)] = tile.astype(BF)
        return arrival

    def collect(arrival, landing, count, back, target):
        arrive(landing.at[pl.ds(0, 3)], arrival)
        tiles = []
        for k in range(GROUP):
            tiles += unfold([t.astype(F32) for t in tiles_of(landing[k])], count)
        for t, tile in enumerate(permute_chunks(tiles, back)):
            target[:, 128 * t : 128 * (t + 1)] = tile

    mix_sum.wait()

    def write_out(at):
        here = pl.ds(pl.multiple_of(OWN * d + at.start, at.size), at.size)
        out_o[at, :] = (mix_sum.value(at) + last_weight * s.y[here, :]).astype(BF)

    by_rows(OWN, 32, write_out)

    for one in sums:
        one.send_two()
    out_sum.send_mirror()
    in_sum.wait()

    def first_norm_back(at):
        grad = in_sum.value(at)
        normal, scale = standardize(s.x_all[d, at, :].astype(F32))
        back = norm_back(grad, s.norms[0:1, :], normal, scale)
        ig_o[at, :] = (s.dy[at, :] + back).astype(BF)

    by_rows(OWN, 32, first_norm_back)
    for one in sums:
        one.send_near()
    arrive(s.uzd.at[pl.ds(0, 3)], depth_z)
    s.uzd[4 + d] = (s.uzd[0] + s.uzd[1]) + (s.uzd[2] + s.uzd[3])
    for m, device in mates:
        copy_to(s.uzd.at[4 + d], s.uzd.at[4 + d], device, depth_d, depth_group)
    for one in sums:
        one.keep_own()
    up_sum.finish()
    up_spread = spread(s.f_up, s.b_up, s.a_up)
    out_sum.send_two_outside()
    out_sum.send_two_inside()
    out_sum.send_near()
    arrive(s.uzd.at[pl.ds(0, 3)], depth_d)
    dg_o[...] = (s.uzd[4] + s.uzd[5]) + (s.uzd[6] + s.uzd[7])

    collect(up_spread, s.a_up, 6, UP_BACK, gu_o)

    arrive(s.fin.at[pl.ds(0, 11)], shared[3])
    for k in range(GROUP):
        s.q_sum[k] = (
            s.fin[12 + k].astype(F32) + s.fin[4 + k].astype(F32) + s.fin[k].astype(F32)
        )

    @pl.when(inside)
    def _():
        arrive(s.fin.at[pl.ds(0, 4)], shared[4])
        for k in range(GROUP):
            s.q_sum[k] += s.fin[8 + k].astype(F32)

    tiles = []
    for k in range(GROUP):
        tiles += unfold_qkv(tiles_of(s.q_sum[k]))
    for t, tile in enumerate(permute_chunks(tiles, QKV_BACK)):
        gq_o[:, 128 * t : 128 * (t + 1)] = tile
    out_sum.finish()
    for t, tile in enumerate(unfold(tiles_of(s.f_out[:, :1152]), 6)):
        go_o[:, 128 * t : 128 * (t + 1)] = tile
    ng_o[...] = s.f_out[:8, 1152:]
    for group, view, condition in send_groups:
        wait = prepare(view, view, x_dev, 0, group).wait_send
        if condition is None:
            wait()
        else:
            pl.when(condition)(wait)
    assert used["send"] <= N_SENDS and used["arrival"] <= N_ARRIVALS, used


def finish_kernel(*refs):
    count = N_OUT - 2
    ins, refs = refs[:count], refs[count:]
    (norm, depth), refs = refs[:2], refs[2:]
    outs, (norm_o, depth_o), sems = refs[:count], refs[count : count + 2], refs[-1]
    copies = [pltpu.make_async_copy(a, b, sems.at[i]) for i, (a, b) in enumerate(zip(ins, outs))]
    for copy in copies:
        copy.start()
    norm_o[...] = norm[:4, :CHUNK]
    depth_o[...] = depth[:1, : GROUP + 1]
    for copy in copies:
        copy.wait()


def fused(
    block_input,
    history,
    cotangent,
    token_mask,
    qkv_weight,
    out_weight,
    up_weight,
    down_weight,
    norm_params,
    depth_weights,
):
    cosine, sine = tables()
    vmem = pl.BlockSpec(memory_space=pltpu.VMEM)
    smem = pl.BlockSpec(memory_space=pltpu.SMEM)
    hbm = pl.BlockSpec(memory_space=pltpu.HBM)
    shape = jax.ShapeDtypeStruct
    shapes = (
        shape((OWN, WIDTH), BF),
        shape((OWN, WIDTH), BF),
        shape((SEQ, WIDTH), BF),
        shape((CHUNK, 3 * WIDTH), F32),
        shape((CHUNK, WIDTH), F32),
        shape((CHUNK, 4 * WIDTH), F32),
        shape((BLOCK, WIDTH), F32),
        shape((8, 128), F32),
        shape((8, 128), F32),
    )
    outs = pl.pallas_call(
        fused_kernel,
        out_shape=tuple(pltpu.VMEM(one.shape, one.dtype) for one in shapes),
        in_specs=[hbm] * 3 + [vmem] + [hbm] * 4 + [vmem, smem] + [hbm] * 2,
        out_specs=[vmem] * 9,
        scratch_shapes=[pltpu.VMEM(dims, kind) for dims, kind in SCRATCH.values()]
        + [pltpu.SemaphoreType.DMA((n,)) for n in (N_SENDS, N_ARRIVALS, 9)],
        compiler_params=pltpu.CompilerParams(
            collective_id=0, has_side_effects=True, vmem_limit_bytes=VMEM_MIB * 2**20
        ),
        cost_estimate=pl.CostEstimate(flops=12 * 10**9, bytes_accessed=4 * 10**6, transcendentals=10**6),
    )(
        block_input,
        history.reshape(SEQ, WIDTH),
        cotangent,
        token_mask.reshape(1, OWN),
        qkv_weight,
        out_weight,
        up_weight,
        down_weight,
        norm_params,
        depth_weights,
        jnp.asarray(cosine),
        jnp.asarray(sine),
    )
    held = pl.pallas_call(
        finish_kernel,
        out_shape=shapes[:7] + (shape((4, CHUNK), F32), shape((1, GROUP + 1), F32)),
        in_specs=[vmem] * 9,
        out_specs=[hbm] * 7 + [vmem] * 2,
        scratch_shapes=[pltpu.SemaphoreType.DMA((7,))],
        compiler_params=pltpu.CompilerParams(vmem_limit_bytes=4 * 2**20),
    )(*outs)
    out, input_grad, history_grad, *grads, g_depth = held
    return (out, input_grad, history_grad.reshape(1, SEQ, WIDTH), *grads, g_depth.reshape(GROUP + 1))


def fits(mesh, block_input, history, up_weight):
    devices = ROWS * GROUP
    return (
        mesh.shape["rows"] == ROWS
        and mesh.shape["depth"] == GROUP
        and block_input.shape == (OWN * devices, WIDTH)
        and history.shape[0] == GROUP
        and up_weight.shape == (WIDTH, 4 * WIDTH)
    )


def solution(mesh):
    weights = P(("rows", "depth"), None)
    in_specs = (
        weights,
        P("depth", "rows", None),
        weights,
        P(("rows", "depth")),
        weights,
        weights,
        weights,
        weights,
        P(None, ("rows", "depth")),
        P(),
    )
    out_specs = (
        weights,
        weights,
        P("depth", "rows", None),
        weights,
        weights,
        weights,
        weights,
        P(None, ("rows", "depth")),
        P(),
    )

    def run(*args):
        body = fused if fits(mesh, args[0], args[1], args[6]) else local
        return jax.shard_map(
            body, mesh=mesh, in_specs=in_specs, out_specs=out_specs, check_vma=False
        )(*args)

    return run
```
